32 devices in a mesh: rep: 2 (over y), sec: 4 (over x, core), tp: 4 (over z).
Axes of the slice: x: 2, y: 2, z: 4, core: 2. Of those that a mesh axis runs over, the one named last changes fastest.
Arguments:
- resid: bfloat16 [96, 5120], P(('rep', 'tp'), 'sec'), parts along dimension 0, may hold values from -6 to 6
- query: bfloat16 [96, 5120], P(('rep', 'tp'), 'sec'), parts along dimension 0, may hold values from -120 to 120
- new_kv: bfloat16 [96, 2048], P(('rep', 'tp'), 'sec'), parts along dimension 0, may hold values from -4 to 4
- key_cache: bfloat16 [96, 224, 1024], P(('rep', 'sec', 'tp')), parts along dimension 0, may hold values from -4 to 4
- cached_value_rows: bfloat16 [96, 224, 1024], P(('rep', 'sec', 'tp')), parts along dimension 0, may hold values from -6 to 6
- cache_len: int32 [96], P(('rep', 'sec', 'tp')), parts along dimension 0, may hold values from 1 to 224, as said below
- assign: int32 [96], P('rep'), parts along dimension 0, may hold values from 0 to 11, as said below
- out_weight: bfloat16 [5120, 5120], P('tp', 'sec'), may hold values from -0.078125 to 0.078125
- norm_gain: bfloat16 [5120], P('sec'), may hold values from 0.099609375 to 1.8984375
- gate_weight: bfloat16 [5120, 16384], P('sec', 'tp'), may hold values from -0.078125 to 0.078125
- up_weight: bfloat16 [5120, 16384], P('sec', 'tp'), may hold values from -0.078125 to 0.078125
- down_weight: bfloat16 [16384, 5120], P('tp', 'sec'), may hold values from -0.046875 to 0.046875
Outputs:
- layer_out: bfloat16 [96, 5120], P(('rep', 'tp'), 'sec'), parts along dimension 0
The draws below stay inside these ranges and needn't reach their ends.
There are 2 independent parts, one for each index of `rep`. The reference program is written for one: setup_inputs(seed, part) draws one part's arguments, and reference() takes and returns one part's arrays. A program takes and returns all parts, laid end to end along the dimension named above; an argument that names none is the same for every part. Nothing has to cross between parts.
Inputs may be any that keep to these rules, and one draw needn't show every extreme that they name: `assign`: each block of 12 consecutive requests names every slot 0 to 11 exactly once. `cache_len`: some cache slot has all 224 positions valid.
All inputs are finite; a program needn't handle non-finite values.
Results may differ from the reference program's by a relative error of at most 0.025.
Values may be sent and summed in bfloat16 or wider, within the bound.
No kernel may reach another device: no remote copies, remote signals or barrier semaphores. Data moves between devices by JAX's collectives and lax.ppermute only.
A program may use at most 64 MiB of HBM per device.

```python
import math
import jax
import jax.numpy as jnp
from jax import lax

D = 5120
QUERY_HEADS = 40
KEY_VALUE_HEADS = 8
HEAD_WIDTH = 128
FFW = 16384
CACHE_SLOTS = 224
REQ_DEV = 3
GROUP = 12
REQUEST_COUNT = 48
N_SEC = 4
N_TP = 4


def clipped_normal_sample(key, array_shape):
    return jax.random.truncated_normal(key, -4.0, 4.0, array_shape, jnp.float32)


def newest_pairs(key):
    return clipped_normal_sample(jax.random.fold_in(key, 101), (REQUEST_COUNT, KEY_VALUE_HEADS, 2, HEAD_WIDTH))


def slot_table(key):
    groups = REQUEST_COUNT // GROUP
    group_keys = jax.random.split(jax.random.fold_in(key, 7), groups)
    orders = jax.vmap(lambda group_key: jax.random.permutation(group_key, GROUP))(group_keys)
    return orders.reshape(REQUEST_COUNT).astype(jnp.int32)


def draw_assign(key, part):
    return slot_table(key)


def draw_new_kv(key, part):
    key_value_pairs = newest_pairs(key)
    return key_value_pairs.reshape(REQUEST_COUNT, 2 * KEY_VALUE_HEADS * HEAD_WIDTH).astype(jnp.bfloat16)


def draw_query(key, part):
    group_query = QUERY_HEADS // KEY_VALUE_HEADS
    incoming_keys = newest_pairs(key)[:, :, 0]
    array_shape = (REQUEST_COUNT, KEY_VALUE_HEADS, group_query, HEAD_WIDTH)
    result = clipped_normal_sample(jax.random.fold_in(key, 102), array_shape) + 0.3 * incoming_keys[:, :, None, :]
    return result.reshape(REQUEST_COUNT, QUERY_HEADS * HEAD_WIDTH).astype(jnp.bfloat16)


def draw_key_cache(key, part):
    array_shape = (REQUEST_COUNT, CACHE_SLOTS, KEY_VALUE_HEADS * HEAD_WIDTH)
    base = clipped_normal_sample(jax.random.fold_in(key, 103), array_shape)
    return base.astype(jnp.bfloat16)


def draw_cache_len(key, part):
    lengths = jax.random.randint(jax.random.fold_in(key, 9), (REQUEST_COUNT,), 1, CACHE_SLOTS + 1, jnp.int32)
    longest = jax.random.randint(jax.random.fold_in(key, 10), (), 0, REQUEST_COUNT, jnp.int32)
    return lengths.at[longest].set(CACHE_SLOTS)


def level_of(rng, shape, shards, smallest, high):
    level = 1.0
    for dim, parts in shards:
        heights = jax.random.uniform(jax.random.fold_in(jax.random.fold_in(rng, 6), dim), (parts,), jnp.float32, smallest / len(shards), high / len(shards))
        level = level * jnp.repeat(jnp.exp(heights), shape[dim] // parts).reshape((-1,) + (1,) * (len(shape) - 1 - dim))
    return level


def normal_values(own_key, shape, scale, limit, shards=(), kind=jnp.bfloat16):
    values = jax.random.normal(own_key, shape, jnp.float32) * scale
    if len(shards) > 0:
        values = level_of(own_key, shape, shards, -0.22, 0.18) * values
    return jnp.clip(values, min=-limit, max=limit).astype(kind)


def setup_inputs(seed: int = 0, part: int = 0) -> dict:
    seeds = jax.random.split(jax.random.key(seed), 13)
    part_splits = jax.random.split(jax.random.fold_in(seeds[12], part), 13)
    resid = normal_values(part_splits[0], (REQUEST_COUNT, D), 1.0, 6.0, ((0, 4), (1, 4)))
    query = draw_query(jax.random.fold_in(jax.random.fold_in(seeds[12], part), 71), part)
    new_kv = draw_new_kv(jax.random.fold_in(jax.random.fold_in(seeds[12], part), 71), part)
    key_cache = draw_key_cache(jax.random.fold_in(jax.random.fold_in(seeds[12], part), 71), part)
    cached_value_rows = normal_values(part_splits[4], (REQUEST_COUNT, CACHE_SLOTS, KEY_VALUE_HEADS * HEAD_WIDTH), 1.0, 6.0, ((0, 16),))
    cache_len = draw_cache_len(jax.random.fold_in(jax.random.fold_in(seeds[12], part), 71), part)
    assign = draw_assign(jax.random.fold_in(jax.random.fold_in(seeds[12], part), 71), part)
    out_weight = normal_values(seeds[7], (QUERY_HEADS * HEAD_WIDTH, D), (QUERY_HEADS * HEAD_WIDTH) ** -0.5, 0.078125, ((0, 4), (1, 4)))
    norm_gain = jnp.clip(1.0 + 0.18 * jax.random.normal(seeds[8], (D,), jnp.float32), 0.099609375, 1.8984375).astype(jnp.bfloat16)
    gate_weight = normal_values(seeds[9], (D, FFW), D ** -0.5, 0.078125, ((0, 4), (1, 4)))
    up_weight = normal_values(seeds[10], (D, FFW), D ** -0.5, 0.078125, ((0, 4), (1, 4)))
    down_weight = normal_values(seeds[11], (FFW, D), FFW ** -0.5, 0.046875, ((0, 4), (1, 4)))
    return {"resid": resid, "query": query, "new_kv": new_kv, "key_cache": key_cache, "cached_value_rows": cached_value_rows, "cache_len": cache_len, "assign": assign, "out_weight": out_weight, "norm_gain": norm_gain, "gate_weight": gate_weight, "up_weight": up_weight, "down_weight": down_weight}


def attend_block(query_rows, key_value_pairs, stored_keys, stored_values, lengths):
    cache_slots = query_rows.shape[0]
    group_query = QUERY_HEADS // KEY_VALUE_HEADS
    query_head_rows = query_rows.astype(jnp.float32).reshape(cache_slots, KEY_VALUE_HEADS, group_query, HEAD_WIDTH)
    paired_heads = key_value_pairs.astype(jnp.float32).reshape(cache_slots, KEY_VALUE_HEADS, 2, HEAD_WIDTH)
    fresh_keys = paired_heads[:, :, 0]
    fresh_values = paired_heads[:, :, 1]
    earlier_keys = stored_keys.astype(jnp.float32).reshape(cache_slots, CACHE_SLOTS, KEY_VALUE_HEADS, HEAD_WIDTH)
    earlier_values = stored_values.astype(jnp.float32).reshape(cache_slots, CACHE_SLOTS, KEY_VALUE_HEADS, HEAD_WIDTH)
    scaling = 1.0 / math.sqrt(HEAD_WIDTH)
    past_scores = jnp.einsum('rkgd,rlkd->rkgl', query_head_rows, earlier_keys) * scaling
    fresh_scores = jnp.einsum('rkgd,rkd->rkg', query_head_rows, fresh_keys) * scaling
    valid = jnp.arange(CACHE_SLOTS, dtype=jnp.int32)[None, :] < lengths[:, None]
    past_scores = jnp.where(valid[:, None, None, :], past_scores, -1e+30)
    highest = jnp.maximum(lax.optimization_barrier(jnp.max(past_scores, axis=-1)), fresh_scores)
    past_exp = jnp.exp(past_scores - highest[..., None])
    fresh_exp = jnp.exp(fresh_scores - highest)
    denominator = lax.optimization_barrier(jnp.sum(past_exp, axis=-1)) + fresh_exp
    past_weights = lax.optimization_barrier((past_exp / denominator[..., None]).astype(jnp.bfloat16)).astype(jnp.float32)
    fresh_weights = lax.optimization_barrier((fresh_exp / denominator).astype(jnp.bfloat16)).astype(jnp.float32)
    mixed = jnp.einsum('rkgl,rlkd->rkgd', past_weights, earlier_values)
    mixed = mixed + fresh_weights[..., None] * fresh_values[:, :, None, :]
    return mixed.reshape(cache_slots, QUERY_HEADS * HEAD_WIDTH).astype(jnp.bfloat16)

def block_sum(left, right, pieces):
    width = left.shape[1] // pieces

    def add_block(index, total):
        lhs = lax.dynamic_slice_in_dim(left, index * width, width, 1)
        rhs = lax.dynamic_slice_in_dim(right, index * width, width, 0)
        term = jnp.dot(lhs, rhs, preferred_element_type=jnp.float32)
        term = lax.optimization_barrier(term.astype(jnp.bfloat16)).astype(jnp.float32)
        return total + term
    start_total = jnp.zeros((left.shape[0], right.shape[1]), jnp.float32)
    return lax.fori_loop(0, pieces, add_block, start_total)

def reference(resid, query, new_kv, key_cache, cached_value_rows, cache_len, assign, out_weight, norm_gain, gate_weight, up_weight, down_weight):
    request_ids = jnp.arange(REQUEST_COUNT, dtype=jnp.int32)
    slot_row = (assign // REQ_DEV * N_TP + request_ids // GROUP) * REQ_DEV + assign % REQ_DEV
    blocks = REQUEST_COUNT // GROUP

    def one_block(index):
        first = (index * GROUP).astype(jnp.int32)
        chosen = lax.dynamic_slice_in_dim(slot_row, first, GROUP)
        query_rows = lax.dynamic_slice_in_dim(query, first, GROUP, 0)
        key_value_pairs = lax.dynamic_slice_in_dim(new_kv, first, GROUP, 0)
        return attend_block(query_rows, key_value_pairs, key_cache[chosen], cached_value_rows[chosen], cache_len[chosen])
    attended = lax.map(one_block, jnp.arange(blocks, dtype=jnp.int32)).reshape(REQUEST_COUNT, QUERY_HEADS * HEAD_WIDTH)
    attn_out = block_sum(attended, out_weight, N_TP)
    stream = resid.astype(jnp.float32) + attn_out
    inverse = lax.rsqrt(lax.optimization_barrier(jnp.mean(stream * stream, axis=1)) + 1e-06)
    normed = (stream * inverse[:, None] * norm_gain.astype(jnp.float32)[None, :]).astype(jnp.bfloat16)
    gate = block_sum(normed, gate_weight, N_SEC)
    upper = block_sum(normed, up_weight, N_SEC)
    hidden = (jax.nn.silu(gate) * upper).astype(jnp.bfloat16)
    ff_out = block_sum(hidden, down_weight, N_TP)
    return (stream + ff_out).astype(jnp.bfloat16)
```

```python
import math

import jax
import jax.numpy as jnp
from jax import lax
from jax.sharding import PartitionSpec as P

D = 5120
QUERY_HEADS = 40
KEY_VALUE_HEADS = 8
HEAD_WIDTH = 128
CACHE_SLOTS = 224


def attend_slots(query_rows, key_value_pairs, stored_keys, stored_values, lengths):
    cache_slots = query_rows.shape[0]
    group_query = QUERY_HEADS // KEY_VALUE_HEADS
    query_head_rows = query_rows.reshape(cache_slots, KEY_VALUE_HEADS, group_query, HEAD_WIDTH)
    paired_heads = key_value_pairs.reshape(cache_slots, KEY_VALUE_HEADS, 2, HEAD_WIDTH)
    fresh_keys = paired_heads[:, :, 0]
    fresh_values = paired_heads[:, :, 1]
    earlier_keys = stored_keys.reshape(cache_slots, CACHE_SLOTS, KEY_VALUE_HEADS, HEAD_WIDTH)
    earlier_values = stored_values.reshape(cache_slots, CACHE_SLOTS, KEY_VALUE_HEADS, HEAD_WIDTH)
    scaling = 1.0 / math.sqrt(HEAD_WIDTH)
    past_scores = (
        jnp.einsum(
            "rkgd,rlkd->rkgl", query_head_rows, earlier_keys, preferred_element_type=jnp.float32
        )
        * scaling
    )
    fresh_scores = (
        jnp.einsum("rkgd,rkd->rkg", query_head_rows, fresh_keys, preferred_element_type=jnp.float32)
        * scaling
    )
    valid = lax.broadcasted_iota(jnp.int32, (cache_slots, CACHE_SLOTS), 1) < lengths[:, None]
    past_scores = jnp.where(valid[:, None, None, :], past_scores, -1e30)
    highest = jnp.maximum(jnp.max(past_scores, axis=-1), fresh_scores)
    past_exp = jnp.exp(past_scores - highest[..., None])
    fresh_exp = jnp.exp(fresh_scores - highest)
    denominator = jnp.sum(past_exp, axis=-1) + fresh_exp
    past_weights = (past_exp / denominator[..., None]).astype(jnp.bfloat16)
    fresh_weights = (fresh_exp / denominator).astype(jnp.bfloat16)
    mixed = jnp.einsum(
        "rkgl,rlkd->rkgd", past_weights, earlier_values, preferred_element_type=jnp.float32
    )
    mixed = (
        mixed
        + fresh_weights.astype(jnp.float32)[..., None]
        * fresh_values.astype(jnp.float32)[:, :, None, :]
    )
    return mixed.reshape(cache_slots, QUERY_HEADS * HEAD_WIDTH).astype(jnp.bfloat16)


def gated_units(values, width):
    return (jax.nn.silu(values[:, :width]) * values[:, width:]).astype(jnp.bfloat16)


def received(blocks, axis):
    count = lax.axis_size(axis)
    result = [blocks[0]]
    for step in range(1, count):
        result.append(lax.ppermute(blocks[step], axis, [(i, i ^ step) for i in range(count)]))
    return result


def local(
    resid,
    query,
    new_kv,
    key_cache,
    cached_value_rows,
    cache_len,
    assign,
    out_weight,
    norm_gain,
    gate_weight,
    up_weight,
    down_weight,
):
    group = query.shape[0]
    per_device = key_cache.shape[0]
    tp_index = lax.axis_index("tp")
    sec_index = lax.axis_index("sec")
    tp_count = lax.axis_size("tp")
    sec_count = lax.axis_size("sec")
    local_slots = lax.dynamic_slice_in_dim(assign, tp_index * group, group)
    resid_f32 = resid.astype(jnp.float32)
    features = resid.shape[1]
    width = gate_weight.shape[1]
    rows = group * tp_count // sec_count

    tokens = jnp.concatenate([query, new_kv], axis=1)
    blocks = []
    for step in range(sec_count):
        wanted = (sec_index ^ step) * per_device + lax.iota(jnp.int32, per_device)
        picker = (local_slots[None, :] == wanted[:, None]).astype(jnp.bfloat16)
        blocks.append(jnp.dot(picker, tokens, preferred_element_type=jnp.float32).astype(jnp.bfloat16))
    pieces = jnp.stack(received(blocks, "sec"))
    pieces = jnp.take(pieces, sec_index ^ lax.iota(jnp.int32, sec_count), axis=0)
    my_query = pieces[:, :, : query.shape[1]].transpose(1, 0, 2).reshape(per_device, -1)
    my_pairs = pieces[:, :, query.shape[1] :].transpose(1, 0, 2).reshape(per_device, -1)
    attended = attend_slots(my_query, my_pairs, key_cache, cached_value_rows, cache_len)

    head_block = out_weight.shape[0]
    blocks = [
        lax.dynamic_slice_in_dim(attended, (tp_index ^ step) * head_block, head_block, 1)
        for step in range(tp_count)
    ]
    mine = jnp.stack(received(blocks, "tp"))
    everyone = jnp.stack(received([mine] * sec_count, "sec"))
    everyone = jnp.take(everyone, sec_index ^ lax.iota(jnp.int32, sec_count), axis=0)
    everyone = everyone.transpose(1, 0, 2, 3).reshape(tp_count, group, head_block)
    parts = jnp.dot(everyone.reshape(tp_count * group, head_block), out_weight, preferred_element_type=jnp.float32)
    parts = parts.astype(jnp.bfloat16).reshape(tp_count, group, features)
    shares = received([parts[step] for step in range(tp_count)], "tp")
    attn_out = sum(share.astype(jnp.float32) for share in shares)
    attn_out = jnp.take(attn_out, local_slots, axis=0)
    stream = resid_f32 + attn_out

    scaled = (stream * norm_gain.astype(jnp.float32)[None, :]).astype(jnp.bfloat16)
    squares = jnp.broadcast_to(jnp.sum(stream * stream, axis=1, keepdims=True), (group, 128))
    piece = jnp.concatenate(received([scaled] * tp_count, "tp"), axis=0)
    square_parts = jnp.concatenate(received([squares] * tp_count, "tp"), axis=0)
    square_parts = square_parts.reshape(sec_count, rows, 128)
    gate_part = jnp.dot(piece, gate_weight, preferred_element_type=jnp.float32)
    up_part = jnp.dot(piece, up_weight, preferred_element_type=jnp.float32)
    projected = jnp.concatenate([gate_part, up_part], axis=1).astype(jnp.bfloat16)
    projected = projected.reshape(sec_count, rows, 2 * width)
    blocks = [lax.dynamic_index_in_dim(projected, sec_index ^ step, 0, False) for step in range(sec_count)]
    share = sum(block.astype(jnp.float32) for block in received(blocks, "sec"))
    blocks = [lax.dynamic_index_in_dim(square_parts, sec_index ^ step, 0, False) for step in range(sec_count)]
    total = sum(received(blocks, "sec"))
    inverse = lax.rsqrt(total[:, :1] / D + 1e-06)
    hidden = gated_units(share * inverse, width)
    hidden = jnp.stack(received([hidden] * sec_count, "sec"))
    hidden = jnp.take(hidden, sec_index ^ lax.iota(jnp.int32, sec_count), axis=0).reshape(-1, width)
    parts = jnp.dot(hidden, down_weight, preferred_element_type=jnp.float32).astype(jnp.bfloat16)
    parts = parts.reshape(tp_count, group, features)
    shares = received([parts[step] for step in range(tp_count)], "tp")
    ff_out = sum(share.astype(jnp.float32) for share in shares)
    return (stream + ff_out).astype(jnp.bfloat16)


def solution(mesh):
    return jax.shard_map(
        local,
        mesh=mesh,
        in_specs=(
            P(("rep", "tp"), "sec"),
            P(("rep", "tp"), "sec"),
            P(("rep", "tp"), "sec"),
            P(("rep", "sec", "tp"), None, None),
            P(("rep", "sec", "tp"), None, None),
            P(("rep", "sec", "tp")),
            P("rep"),
            P("tp", "sec"),
            P("sec"),
            P("sec", "tp"),
            P("sec", "tp"),
            P("tp", "sec"),
        ),
        out_specs=P(("rep", "tp"), "sec"),
        check_vma=False,
    )
```

```python
import functools
import math

import jax
import jax.numpy as jnp
from jax import lax
from jax.experimental import pallas as pl
from jax.experimental.pallas import tpu as pltpu
from jax.sharding import PartitionSpec as P

D = 5120
QUERY_HEADS = 40
KEY_VALUE_HEADS = 8
HEAD_WIDTH = 128
CACHE_SLOTS = 224


def attend_slots(query_rows, key_value_pairs, stored_keys, stored_values, lengths):
    cache_slots = query_rows.shape[0]
    group_query = QUERY_HEADS // KEY_VALUE_HEADS
    query_head_rows = query_rows.reshape(cache_slots, KEY_VALUE_HEADS, group_query, HEAD_WIDTH)
    paired_heads = key_value_pairs.reshape(cache_slots, KEY_VALUE_HEADS, 2, HEAD_WIDTH)
    fresh_keys = paired_heads[:, :, 0]
    fresh_values = paired_heads[:, :, 1]
    earlier_keys = stored_keys.reshape(cache_slots, CACHE_SLOTS, KEY_VALUE_HEADS, HEAD_WIDTH)
    earlier_values = stored_values.reshape(cache_slots, CACHE_SLOTS, KEY_VALUE_HEADS, HEAD_WIDTH)
    scaling = 1.0 / math.sqrt(HEAD_WIDTH)
    past_scores = (
        jnp.einsum(
            "rkgd,rlkd->rkgl", query_head_rows, earlier_keys, preferred_element_type=jnp.float32
        )
        * scaling
    )
    fresh_scores = (
        jnp.einsum("rkgd,rkd->rkg", query_head_rows, fresh_keys, preferred_element_type=jnp.float32)
        * scaling
    )
    valid = lax.broadcasted_iota(jnp.int32, (cache_slots, CACHE_SLOTS), 1) < lengths[:, None]
    past_scores = jnp.where(valid[:, None, None, :], past_scores, -1e30)
    highest = jnp.maximum(jnp.max(past_scores, axis=-1), fresh_scores)
    past_exp = jnp.exp(past_scores - highest[..., None])
    fresh_exp = jnp.exp(fresh_scores - highest)
    denominator = jnp.sum(past_exp, axis=-1) + fresh_exp
    past_weights = (past_exp / denominator[..., None]).astype(jnp.bfloat16)
    fresh_weights = (fresh_exp / denominator).astype(jnp.bfloat16)
    mixed = jnp.einsum(
        "rkgl,rlkd->rkgd", past_weights, earlier_values, preferred_element_type=jnp.float32
    )
    mixed = (
        mixed
        + fresh_weights.astype(jnp.float32)[..., None]
        * fresh_values.astype(jnp.float32)[:, :, None, :]
    )
    return mixed.reshape(cache_slots, QUERY_HEADS * HEAD_WIDTH).astype(jnp.bfloat16)


def gated_units(values, width):
    return (jax.nn.silu(values[:, :width]) * values[:, width:]).astype(jnp.bfloat16)


def received(blocks, axis):
    count = lax.axis_size(axis)
    result = [blocks[0]]
    for step in range(1, count):
        result.append(lax.ppermute(blocks[step], axis, [(i, i ^ step) for i in range(count)]))
    return result


def local(
    resid,
    query,
    new_kv,
    key_cache,
    cached_value_rows,
    cache_len,
    assign,
    out_weight,
    norm_gain,
    gate_weight,
    up_weight,
    down_weight,
):
    group = query.shape[0]
    per_device = key_cache.shape[0]
    tp_index = lax.axis_index("tp")
    sec_index = lax.axis_index("sec")
    tp_count = lax.axis_size("tp")
    sec_count = lax.axis_size("sec")
    local_slots = lax.dynamic_slice_in_dim(assign, tp_index * group, group)
    resid_f32 = resid.astype(jnp.float32)
    features = resid.shape[1]
    width = gate_weight.shape[1]
    rows = group * tp_count // sec_count

    tokens = jnp.concatenate([query, new_kv], axis=1)
    blocks = []
    for step in range(sec_count):
        wanted = (sec_index ^ step) * per_device + lax.iota(jnp.int32, per_device)
        picker = (local_slots[None, :] == wanted[:, None]).astype(jnp.bfloat16)
        blocks.append(jnp.dot(picker, tokens, preferred_element_type=jnp.float32).astype(jnp.bfloat16))
    pieces = jnp.stack(received(blocks, "sec"))
    pieces = jnp.take(pieces, sec_index ^ lax.iota(jnp.int32, sec_count), axis=0)
    my_query = pieces[:, :, : query.shape[1]].transpose(1, 0, 2).reshape(per_device, -1)
    my_pairs = pieces[:, :, query.shape[1] :].transpose(1, 0, 2).reshape(per_device, -1)
    attended = attend_slots(my_query, my_pairs, key_cache, cached_value_rows, cache_len)

    head_block = out_weight.shape[0]
    blocks = [
        lax.dynamic_slice_in_dim(attended, (tp_index ^ step) * head_block, head_block, 1)
        for step in range(tp_count)
    ]
    mine = jnp.stack(received(blocks, "tp"))
    everyone = jnp.stack(received([mine] * sec_count, "sec"))
    everyone = jnp.take(everyone, sec_index ^ lax.iota(jnp.int32, sec_count), axis=0)
    everyone = everyone.transpose(1, 0, 2, 3).reshape(tp_count, group, head_block)
    parts = jnp.dot(everyone.reshape(tp_count * group, head_block), out_weight, preferred_element_type=jnp.float32)
    parts = parts.astype(jnp.bfloat16).reshape(tp_count, group, features)
    shares = received([parts[step] for step in range(tp_count)], "tp")
    attn_out = sum(share.astype(jnp.float32) for share in shares)
    attn_out = jnp.take(attn_out, local_slots, axis=0)
    stream = resid_f32 + attn_out

    scaled = (stream * norm_gain.astype(jnp.float32)[None, :]).astype(jnp.bfloat16)
    squares = jnp.broadcast_to(jnp.sum(stream * stream, axis=1, keepdims=True), (group, 128))
    piece = jnp.concatenate(received([scaled] * tp_count, "tp"), axis=0)
    square_parts = jnp.concatenate(received([squares] * tp_count, "tp"), axis=0)
    square_parts = square_parts.reshape(sec_count, rows, 128)
    gate_part = jnp.dot(piece, gate_weight, preferred_element_type=jnp.float32)
    up_part = jnp.dot(piece, up_weight, preferred_element_type=jnp.float32)
    projected = jnp.concatenate([gate_part, up_part], axis=1).astype(jnp.bfloat16)
    projected = projected.reshape(sec_count, rows, 2 * width)
    blocks = [lax.dynamic_index_in_dim(projected, sec_index ^ step, 0, False) for step in range(sec_count)]
    share = sum(block.astype(jnp.float32) for block in received(blocks, "sec"))
    blocks = [lax.dynamic_index_in_dim(square_parts, sec_index ^ step, 0, False) for step in range(sec_count)]
    total = sum(received(blocks, "sec"))
    inverse = lax.rsqrt(total[:, :1] / D + 1e-06)
    hidden = gated_units(share * inverse, width)
    hidden = jnp.stack(received([hidden] * sec_count, "sec"))
    hidden = jnp.take(hidden, sec_index ^ lax.iota(jnp.int32, sec_count), axis=0).reshape(-1, width)
    parts = jnp.dot(hidden, down_weight, preferred_element_type=jnp.float32).astype(jnp.bfloat16)
    parts = parts.reshape(tp_count, group, features)
    shares = received([parts[step] for step in range(tp_count)], "tp")
    ff_out = sum(share.astype(jnp.float32) for share in shares)
    return (stream + ff_out).astype(jnp.bfloat16)


MIB = 1024 * 1024


def call(kernel, outs, operands, scratch=(), smem=(), resident=(), flops=0, moved=0, limit=8):
    specs = []
    placed = []
    for place, operand in enumerate(operands):
        space = pltpu.SMEM if place in smem else pltpu.VMEM
        specs.append(pl.BlockSpec(memory_space=space))
        placed.append(in_vmem(operand) if place in resident else operand)
    return pl.pallas_call(
        kernel,
        out_shape=[jax.ShapeDtypeStruct(shape, dtype) for shape, dtype in outs],
        in_specs=specs,
        out_specs=[pl.BlockSpec(memory_space=pltpu.VMEM) for _ in outs],
        scratch_shapes=list(scratch),
        compiler_params=pltpu.CompilerParams(vmem_limit_bytes=limit * MIB),
        cost_estimate=pl.CostEstimate(flops=flops, bytes_accessed=moved, transcendentals=0),
    )(*placed)


def in_vmem(operand):
    return pltpu.with_memory_space_constraint(operand, pltpu.VMEM)


def swap(value, axis, step):
    count = lax.axis_size(axis)
    return lax.ppermute(value, axis, [(i, i ^ step) for i in range(count)])


def pick_kernel(per_device, group, heads, query_a, pairs_a, query_b, pairs_b, assign, keep, send, rows):
    sec, tp = lax.axis_index("sec"), lax.axis_index("tp")
    odd = (sec & 1) == 1
    slots = jnp.zeros((1, group), jnp.int32)
    for index in range(assign.shape[1] // group):
        slots = jnp.where(tp == index, assign[:, index * group : (index + 1) * group], slots)
    line = lax.broadcasted_iota(jnp.int32, (16, group), 0)
    wanted = jnp.where(line < 8, sec * per_device + line, (sec ^ 2) * per_device + line - 8)
    inside = (line & 7) < per_device
    picker = jnp.where(inside & (jnp.broadcast_to(slots, (16, group)) == wanted), 1.0, 0.0).astype(jnp.bfloat16)

    def picked(ref):
        return jnp.dot(picker, ref[...], preferred_element_type=jnp.float32)

    mine_q, mine_p, other_q, other_p = picked(query_a), picked(pairs_a), picked(query_b), picked(pairs_b)
    both = (
        (jnp.where(odd, other_q, mine_q), jnp.where(odd, other_p, mine_p)),
        (jnp.where(odd, mine_q, other_q), jnp.where(odd, mine_p, other_p)),
    )
    rows[...] = jnp.zeros_like(rows)
    width = HEAD_WIDTH
    for side in range(2):
        for place, (queries, pairs) in enumerate(both):
            for j in range(per_device):
                base = j * 32 + place * 16
                line = side * 8 + j
                for h in range(heads):
                    rows[side, base + h : base + h + 1, :] = queries[line : line + 1, h * width : (h + 1) * width]
                for h in range(pairs.shape[1] // width):
                    at = base + heads + h
                    rows[side, at : at + 1, :] = pairs[line : line + 1, h * width : (h + 1) * width]
    keep[...] = rows[0].astype(jnp.bfloat16)
    send[...] = rows[1].astype(jnp.bfloat16)


def attend_kernel(per_device, heads, lengths, mine, other, keys, values, keep, send, total):
    sec, tp = lax.axis_index("sec"), lax.axis_index("tp")
    high = (sec >> 1) == 1
    share = heads // 2
    first, second = mine[...], other[...]
    halves = (jnp.where(high, second, first), jnp.where(high, first, second))
    slots = keys.shape[1]
    width = HEAD_WIDTH
    scaling = 1.0 / math.sqrt(width)
    line = lax.broadcasted_iota(jnp.int32, (16, width), 0)
    upper = line < share
    place = lax.broadcasted_iota(jnp.int32, (16, slots), 1)
    total[...] = jnp.zeros_like(total)
    for j in range(per_device):
        valid = place < lengths[j]
        for b in range(4):
            base = j * 32 + (b & 1) * 16
            block = halves[b >> 1][base : base + 16]
            wide = block.astype(jnp.float32)
            zero = jnp.zeros_like(wide)
            left = jnp.where(upper, wide, zero).astype(jnp.bfloat16)
            right = jnp.where(upper, zero, wide).astype(jnp.bfloat16)
            both = jnp.concatenate([left, right], axis=1)
            columns = slice(b * 2 * width, (b + 1) * 2 * width)
            past = lax.dot_general(
                both, keys[j, :, columns], (((1,), (1,)), ((), ())), preferred_element_type=jnp.float32
            )
            past = jnp.where(valid, past * scaling, -1e30)
            new_key = jnp.where(upper, wide[heads : heads + 1], wide[heads + 2 : heads + 3])
            new_value = jnp.where(upper, wide[heads + 1 : heads + 2], wide[heads + 3 : heads + 4])
            fresh = jnp.sum(wide * new_key, axis=1, keepdims=True) * scaling
            highest = jnp.maximum(jnp.max(past, axis=1, keepdims=True), fresh)
            past_exp = jnp.exp(past - highest)
            fresh_exp = jnp.exp(fresh - highest)
            inverse = 1.0 / (jnp.sum(past_exp, axis=1, keepdims=True) + fresh_exp)
            weights = (past_exp * inverse).astype(jnp.bfloat16)
            fresh_weight = (fresh_exp * inverse).astype(jnp.bfloat16).astype(jnp.float32)
            mixed = jnp.dot(weights, values[j, :, columns], preferred_element_type=jnp.float32)
            mixed = jnp.where(upper, mixed[:, :width], mixed[:, width:]) + fresh_weight * new_value
            side = (b & 1) ^ (tp & 1)
            for h in range(heads):
                total[side, b >> 1, j : j + 1, h * width : (h + 1) * width] = mixed[h : h + 1]
    keep[...] = total[0, :, 0:4].astype(jnp.bfloat16)
    send[...] = total[1, :, 0:4].astype(jnp.bfloat16)


def forward_kernel(mine, other, send):
    away = (lax.axis_index("tp") >> 1) ^ 1
    send[0] = mine[away]
    send[1] = other[away]


def gather_kernel(mine, other, far, out, rows):
    here = lax.axis_index("tp") >> 1
    rows[0:4] = mine[here].astype(jnp.float32)
    rows[4:8] = other[here].astype(jnp.float32)
    rows[8:12] = far[0].astype(jnp.float32)
    rows[12:16] = far[1].astype(jnp.float32)
    out[...] = rows[...].astype(jnp.bfloat16)


def group_order(group, shape, axis):
    place = lax.broadcasted_iota(jnp.int32, shape, axis)
    number = jnp.zeros(shape, jnp.int32)
    for limit in range(1, 4):
        number = number + jnp.where(place >= limit * group, 1, 0)
    return (((number & 1) << 1) | (number >> 1)) * group + place - number * group


def project_kernel(per_device, group, first, second, third, fourth, assign, weight, keep, send, product):
    sec, tp = lax.axis_index("sec"), lax.axis_index("tp")
    count = assign.shape[1]
    lines = jnp.concatenate([first[...], second[...], third[...], fourth[...]], axis=0)
    line = lax.broadcasted_iota(jnp.int32, (64, count), 0)
    request = lax.broadcasted_iota(jnp.int32, (64, count), 1)
    number = jnp.zeros((64, count), jnp.int32)
    for limit in range(1, 4):
        number = number + jnp.where(request >= limit * group, 1, 0)
    slot = (sec ^ (line >> 4)) * per_device + (line & 3)
    match = (number == (tp ^ ((line >> 2) & 3))) & (jnp.broadcast_to(assign[...], (64, count)) == slot)
    match = jnp.where(match & ((line & 3) < per_device), 1.0, 0.0).astype(jnp.bfloat16)
    order = group_order(group, (count, count), 1) == lax.broadcasted_iota(jnp.int32, (count, count), 0)
    order = jnp.where(order, 1.0, 0.0).astype(jnp.bfloat16)
    match = jnp.dot(match, order, preferred_element_type=jnp.float32).astype(jnp.bfloat16)
    ordered = lax.dot_general(match, lines, (((0,), (0,)), ((), ())), preferred_element_type=jnp.float32)
    ordered = ordered.astype(jnp.bfloat16)
    product[...] = jnp.dot(ordered, weight[...], preferred_element_type=jnp.float32)
    half = count // 2
    odd = tp & 1
    keep[...] = product[pl.ds(pl.multiple_of(odd * half, 8), half), :]
    send[...] = product[pl.ds(pl.multiple_of((1 - odd) * half, 8), half), :].astype(jnp.bfloat16)


def add_resid_kernel(mine, other, resid, keep, send):
    tp = lax.axis_index("tp")
    group = resid.shape[0]
    line = lax.broadcasted_iota(jnp.int32, (2 * group, group), 0)
    match = line == lax.broadcasted_iota(jnp.int32, (2 * group, group), 1) + (tp >> 1) * group
    match = jnp.where(match, 1.0, 0.0).astype(jnp.bfloat16)
    total = mine[...] + other[...].astype(jnp.float32)
    total = total + jnp.dot(match, resid[...], preferred_element_type=jnp.float32)
    keep[...] = total
    send[...] = total.astype(jnp.bfloat16)


def stream_kernel(mine, other, stream, send):
    total = mine[...] + other[...].astype(jnp.float32)
    stream[...] = total
    send[...] = total.astype(jnp.bfloat16)


def gate_up_kernel(chunk, mine, other, gain, gate, up, keep, send, lines):
    sec, tp = lax.axis_index("sec"), lax.axis_index("tp")
    half = mine.shape[0]
    mine_at = (tp ^ sec) & 1
    lines[mine_at] = mine[...].astype(jnp.float32)
    lines[1 - mine_at] = other[...].astype(jnp.float32)
    stream = jnp.concatenate([lines[0], lines[1]], axis=0)
    squares = jnp.sum(stream * stream, axis=1, keepdims=True)
    features = (stream * gain[...].astype(jnp.float32)).astype(jnp.bfloat16)
    width = gate.shape[1] // 2
    for part in range(2):
        for kind, weight in enumerate((gate, up)):
            for start in range(0, width, chunk):
                column = part * width + start
                product = jnp.dot(features, weight[:, column : column + chunk], preferred_element_type=jnp.float32)
                at = kind * width + start
                keep[part, :, at : at + chunk] = product[:half]
                send[part, :, at : at + chunk] = product[half:].astype(jnp.bfloat16)
        keep[part, :, 2 * width :] = jnp.broadcast_to(squares[:half], (half, 128))
        send[part, :, 2 * width :] = two_terms(squares[half:])


def two_terms(column):
    shape = (column.shape[0], 128)
    column = jnp.broadcast_to(column, shape)
    coarse = column.astype(jnp.bfloat16).astype(jnp.float32)
    lane = lax.broadcasted_iota(jnp.int32, shape, 1)
    return jnp.where(lane < 64, coarse, column - coarse).astype(jnp.bfloat16)


def one_column(terms):
    return terms[:, 0:1].astype(jnp.float32) + terms[:, 64:65].astype(jnp.float32)


def pair_sum_kernel(mine, other, keep, send):
    here = lax.axis_index("sec") >> 1
    width = mine.shape[2] - 128
    for target, part in ((send, 1 - here), (keep, here)):
        total = mine[part, :, :width] + other[part, :, :width].astype(jnp.float32)
        target[:, :width] = total.astype(target.dtype)
    squares = mine[0, :, width:] + one_column(other[0, :, width:])
    keep[:, width:] = squares
    send[:, width:] = two_terms(squares[:, 0:1])


def hidden_kernel(features, mine, other, hidden):
    width = (mine.shape[1] - 128) // 2
    squares = mine[:, 2 * width : 2 * width + 1] + one_column(other[:, 2 * width :])
    inverse = lax.rsqrt(squares / features + 1e-06)
    gate = (mine[:, :width] + other[:, :width].astype(jnp.float32)) * inverse
    up = (mine[:, width : 2 * width] + other[:, width : 2 * width].astype(jnp.float32)) * inverse
    hidden[...] = (gate / (1.0 + jnp.exp(-gate)) * up).astype(jnp.bfloat16)


def down_first_kernel(mine, other, weight, out):
    here = lax.axis_index("sec") >> 1
    lines = jnp.concatenate([mine[...].astype(jnp.float32), other[...].astype(jnp.float32)], axis=0)
    lines = lines.astype(jnp.bfloat16)
    depth = lines.shape[1]
    rows = weight[pl.ds(pl.multiple_of(here * depth, depth), depth), :]
    out[...] = jnp.dot(lines, rows, preferred_element_type=jnp.float32)


def down_second_kernel(mine, other, before, weight, keep, send, product):
    sec, tp = lax.axis_index("sec"), lax.axis_index("tp")
    away = 1 - (sec >> 1)
    lines = jnp.concatenate([mine[...].astype(jnp.float32), other[...].astype(jnp.float32)], axis=0)
    lines = lines.astype(jnp.bfloat16)
    depth = lines.shape[1]
    rows = weight[pl.ds(pl.multiple_of(away * depth, depth), depth), :]
    product[...] = before[...] + jnp.dot(lines, rows, preferred_element_type=jnp.float32)
    half = product.shape[0] // 2
    at = (sec ^ tp) & 1
    keep[...] = product[pl.ds(pl.multiple_of(at * half, 8), half), :]
    send[...] = product[pl.ds(pl.multiple_of((1 - at) * half, 8), half), :].astype(jnp.bfloat16)


def share_kernel(mine, other, stream, keep, send):
    high = (lax.axis_index("tp") >> 1) == 1
    group = keep.shape[0]
    total = mine[...] + other[...].astype(jnp.float32)
    lower, upper = total[:group], total[group:]
    send[...] = jnp.where(high, lower, upper).astype(jnp.bfloat16)
    total = total + stream[...]
    keep[...] = jnp.where(high, total[group:], total[:group])


def finish_kernel(mine, other, out):
    out[...] = (mine[...] + other[...].astype(jnp.float32)).astype(jnp.bfloat16)


def local_pairs(
    resid,
    query,
    new_kv,
    key_cache,
    cached_value_rows,
    cache_len,
    assign,
    out_weight,
    norm_gain,
    gate_weight,
    up_weight,
    down_weight,
):
    f32, bf16 = jnp.float32, jnp.bfloat16
    group, features = resid.shape
    per_device = key_cache.shape[0]
    heads = query.shape[1] // HEAD_WIDTH
    head_block = out_weight.shape[0]
    width = gate_weight.shape[1]
    half = 2 * group
    assign = assign.reshape(1, -1)
    gain = norm_gain.reshape(1, -1)

    query_b, pairs_b = swap(query, "sec", 1), swap(new_kv, "sec", 1)
    lines = 32 * per_device
    mine, away = call(
        functools.partial(pick_kernel, per_device, group, heads),
        [((lines, HEAD_WIDTH), bf16)] * 2,
        (query, new_kv, query_b, pairs_b, assign),
        [pltpu.VMEM((2, lines, HEAD_WIDTH), f32)],
    )
    other = swap(away, "sec", 2)
    mine, away = call(
        functools.partial(attend_kernel, per_device, heads),
        [((2, 4, head_block), bf16)] * 2,
        (cache_len, mine, other, key_cache, cached_value_rows),
        [pltpu.VMEM((2, 2, 8, head_block), f32)],
        smem=(0,),
        resident=(3, 4),
    )

    other = swap(away, "tp", 1)
    (away,) = call(forward_kernel, [((2, 4, head_block), bf16)], (mine, other))
    far = swap(away, "tp", 2)
    (block,) = call(
        gather_kernel, [((16, head_block), bf16)], (mine, other, far), [pltpu.VMEM((16, head_block), f32)]
    )
    blocks = [block] + [swap(block, "sec", step) for step in range(1, 4)]
    mine, away = call(
        functools.partial(project_kernel, per_device, group),
        [((half, features), f32), ((half, features), bf16)],
        (*blocks, assign, out_weight),
        [pltpu.VMEM((2 * half, features), f32)],
        resident=(5,),
    )
    other = swap(away, "tp", 1)
    mine, away = call(
        add_resid_kernel, [((half, features), f32), ((half, features), bf16)], (mine, other, resid)
    )
    other = swap(away, "tp", 2)
    stream, mine = call(stream_kernel, [((half, features), f32), ((half, features), bf16)], (mine, other))
    other = swap(mine, "tp", 1)

    wide = (2, half, width + 128)
    mine, away = call(
        functools.partial(gate_up_kernel, min(512, width // 2)),
        [(wide, f32), (wide, bf16)],
        (mine, other, gain, gate_weight, up_weight),
        [pltpu.VMEM((2, half, features), f32)],
        resident=(3, 4),
    )
    other = swap(away, "sec", 1)
    mine, away = call(pair_sum_kernel, [(wide[1:], f32), (wide[1:], bf16)], (mine, other))
    other = swap(away, "sec", 2)
    (hidden,) = call(
        functools.partial(hidden_kernel, features * lax.axis_size("sec")), [((half, width // 2), bf16)], (mine, other)
    )
    across = swap(hidden, "sec", 2)
    beside = swap(hidden, "sec", 1)
    corner = swap(across, "sec", 1)
    (before,) = call(down_first_kernel, [((2 * half, features), f32)], (hidden, beside, down_weight), resident=(2,))
    mine, away = call(
        down_second_kernel,
        [((half, features), f32), ((half, features), bf16)],
        (across, corner, before, down_weight),
        [pltpu.VMEM((2 * half, features), f32)],
        resident=(3,),
    )
    other = swap(away, "tp", 1)
    mine, away = call(share_kernel, [((group, features), f32), ((group, features), bf16)], (mine, other, stream))
    other = swap(away, "tp", 2)
    (out,) = call(finish_kernel, [((group, features), bf16)], (mine, other))
    return out


def solution(mesh):
    small = mesh.shape["sec"] == 4 and mesh.shape["tp"] == 4
    return jax.shard_map(
        local_pairs if small else local,
        mesh=mesh,
        in_specs=(
            P(("rep", "tp"), "sec"),
            P(("rep", "tp"), "sec"),
            P(("rep", "tp"), "sec"),
            P(("rep", "sec", "tp"), None, None),
            P(("rep", "sec", "tp"), None, None),
            P(("rep", "sec", "tp")),
            P("rep"),
            P("tp", "sec"),
            P("sec"),
            P("sec", "tp"),
            P("sec", "tp"),
            P("tp", "sec"),
        ),
        out_specs=P(("rep", "tp"), "sec"),
        check_vma=False,
    )
```

```python
import functools
import math

import jax
import jax.numpy as jnp
from jax import lax
from jax.experimental import pallas as pl
from jax.experimental.pallas import tpu as pltpu
from jax.sharding import PartitionSpec as P

D = 5120
QUERY_HEADS = 40
KEY_VALUE_HEADS = 8
HEAD_WIDTH = 128
CACHE_SLOTS = 224


def attend_slots(query_rows, key_value_pairs, stored_keys, stored_values, lengths):
    cache_slots = query_rows.shape[0]
    group_query = QUERY_HEADS // KEY_VALUE_HEADS
    query_head_rows = query_rows.reshape(cache_slots, KEY_VALUE_HEADS, group_query, HEAD_WIDTH)
    paired_heads = key_value_pairs.reshape(cache_slots, KEY_VALUE_HEADS, 2, HEAD_WIDTH)
    fresh_keys = paired_heads[:, :, 0]
    fresh_values = paired_heads[:, :, 1]
    earlier_keys = stored_keys.reshape(cache_slots, CACHE_SLOTS, KEY_VALUE_HEADS, HEAD_WIDTH)
    earlier_values = stored_values.reshape(cache_slots, CACHE_SLOTS, KEY_VALUE_HEADS, HEAD_WIDTH)
    scaling = 1.0 / math.sqrt(HEAD_WIDTH)
    past_scores = (
        jnp.einsum(
            "rkgd,rlkd->rkgl", query_head_rows, earlier_keys, preferred_element_type=jnp.float32
        )
        * scaling
    )
    fresh_scores = (
        jnp.einsum("rkgd,rkd->rkg", query_head_rows, fresh_keys, preferred_element_type=jnp.float32)
        * scaling
    )
    valid = lax.broadcasted_iota(jnp.int32, (cache_slots, CACHE_SLOTS), 1) < lengths[:, None]
    past_scores = jnp.where(valid[:, None, None, :], past_scores, -1e30)
    highest = jnp.maximum(jnp.max(past_scores, axis=-1), fresh_scores)
    past_exp = jnp.exp(past_scores - highest[..., None])
    fresh_exp = jnp.exp(fresh_scores - highest)
    denominator = jnp.sum(past_exp, axis=-1) + fresh_exp
    past_weights = (past_exp / denominator[..., None]).astype(jnp.bfloat16)
    fresh_weights = (fresh_exp / denominator).astype(jnp.bfloat16)
    mixed = jnp.einsum(
        "rkgl,rlkd->rkgd", past_weights, earlier_values, preferred_element_type=jnp.float32
    )
    mixed = (
        mixed
        + fresh_weights.astype(jnp.float32)[..., None]
        * fresh_values.astype(jnp.float32)[:, :, None, :]
    )
    return mixed.reshape(cache_slots, QUERY_HEADS * HEAD_WIDTH).astype(jnp.bfloat16)


def gated_units(values, width):
    return (jax.nn.silu(values[:, :width]) * values[:, width:]).astype(jnp.bfloat16)


def received(blocks, axis):
    count = lax.axis_size(axis)
    result = [blocks[0]]
    for step in range(1, count):
        result.append(lax.ppermute(blocks[step], axis, [(i, i ^ step) for i in range(count)]))
    return result


def local(
    resid,
    query,
    new_kv,
    key_cache,
    cached_value_rows,
    cache_len,
    assign,
    out_weight,
    norm_gain,
    gate_weight,
    up_weight,
    down_weight,
):
    group = query.shape[0]
    per_device = key_cache.shape[0]
    tp_index = lax.axis_index("tp")
    sec_index = lax.axis_index("sec")
    tp_count = lax.axis_size("tp")
    sec_count = lax.axis_size("sec")
    local_slots = lax.dynamic_slice_in_dim(assign, tp_index * group, group)
    resid_f32 = resid.astype(jnp.float32)
    features = resid.shape[1]
    width = gate_weight.shape[1]
    rows = group * tp_count // sec_count

    tokens = jnp.concatenate([query, new_kv], axis=1)
    blocks = []
    for step in range(sec_count):
        wanted = (sec_index ^ step) * per_device + lax.iota(jnp.int32, per_device)
        picker = (local_slots[None, :] == wanted[:, None]).astype(jnp.bfloat16)
        blocks.append(jnp.dot(picker, tokens, preferred_element_type=jnp.float32).astype(jnp.bfloat16))
    pieces = jnp.stack(received(blocks, "sec"))
    pieces = jnp.take(pieces, sec_index ^ lax.iota(jnp.int32, sec_count), axis=0)
    my_query = pieces[:, :, : query.shape[1]].transpose(1, 0, 2).reshape(per_device, -1)
    my_pairs = pieces[:, :, query.shape[1] :].transpose(1, 0, 2).reshape(per_device, -1)
    attended = attend_slots(my_query, my_pairs, key_cache, cached_value_rows, cache_len)

    head_block = out_weight.shape[0]
    blocks = [
        lax.dynamic_slice_in_dim(attended, (tp_index ^ step) * head_block, head_block, 1)
        for step in range(tp_count)
    ]
    mine = jnp.stack(received(blocks, "tp"))
    everyone = jnp.stack(received([mine] * sec_count, "sec"))
    everyone = jnp.take(everyone, sec_index ^ lax.iota(jnp.int32, sec_count), axis=0)
    everyone = everyone.transpose(1, 0, 2, 3).reshape(tp_count, group, head_block)
    parts = jnp.dot(everyone.reshape(tp_count * group, head_block), out_weight, preferred_element_type=jnp.float32)
    parts = parts.astype(jnp.bfloat16).reshape(tp_count, group, features)
    shares = received([parts[step] for step in range(tp_count)], "tp")
    attn_out = sum(share.astype(jnp.float32) for share in shares)
    attn_out = jnp.take(attn_out, local_slots, axis=0)
    stream = resid_f32 + attn_out

    scaled = (stream * norm_gain.astype(jnp.float32)[None, :]).astype(jnp.bfloat16)
    squares = jnp.broadcast_to(jnp.sum(stream * stream, axis=1, keepdims=True), (group, 128))
    piece = jnp.concatenate(received([scaled] * tp_count, "tp"), axis=0)
    square_parts = jnp.concatenate(received([squares] * tp_count, "tp"), axis=0)
    square_parts = square_parts.reshape(sec_count, rows, 128)
    gate_part = jnp.dot(piece, gate_weight, preferred_element_type=jnp.float32)
    up_part = jnp.dot(piece, up_weight, preferred_element_type=jnp.float32)
    projected = jnp.concatenate([gate_part, up_part], axis=1).astype(jnp.bfloat16)
    projected = projected.reshape(sec_count, rows, 2 * width)
    blocks = [lax.dynamic_index_in_dim(projected, sec_index ^ step, 0, False) for step in range(sec_count)]
    share = sum(block.astype(jnp.float32) for block in received(blocks, "sec"))
    blocks = [lax.dynamic_index_in_dim(square_parts, sec_index ^ step, 0, False) for step in range(sec_count)]
    total = sum(received(blocks, "sec"))
    inverse = lax.rsqrt(total[:, :1] / D + 1e-06)
    hidden = gated_units(share * inverse, width)
    hidden = jnp.stack(received([hidden] * sec_count, "sec"))
    hidden = jnp.take(hidden, sec_index ^ lax.iota(jnp.int32, sec_count), axis=0).reshape(-1, width)
    parts = jnp.dot(hidden, down_weight, preferred_element_type=jnp.float32).astype(jnp.bfloat16)
    parts = parts.reshape(tp_count, group, features)
    shares = received([parts[step] for step in range(tp_count)], "tp")
    ff_out = sum(share.astype(jnp.float32) for share in shares)
    return (stream + ff_out).astype(jnp.bfloat16)


MIB = 1024 * 1024


def call(kernel, outs, operands, scratch=(), smem=(), resident=(), micros=4, limit=8):
    specs = []
    placed = []
    for place, operand in enumerate(operands):
        space = pltpu.SMEM if place in smem else pltpu.VMEM
        specs.append(pl.BlockSpec(memory_space=space))
        placed.append(in_vmem(operand) if place in resident else operand)
    return pl.pallas_call(
        kernel,
        out_shape=[jax.ShapeDtypeStruct(shape, dtype) for shape, dtype in outs],
        in_specs=specs,
        out_specs=[pl.BlockSpec(memory_space=pltpu.VMEM) for _ in outs],
        scratch_shapes=list(scratch),
        compiler_params=pltpu.CompilerParams(vmem_limit_bytes=limit * MIB),
        cost_estimate=pl.CostEstimate(flops=micros * 10**9, bytes_accessed=0, transcendentals=0),
    )(*placed)


def in_vmem(operand):
    return pltpu.with_memory_space_constraint(operand, pltpu.VMEM)


def swap(value, axis, step):
    count = lax.axis_size(axis)
    return lax.ppermute(value, axis, [(i, i ^ step) for i in range(count)])


def pick_kernel(per_device, group, heads, query_a, pairs_a, query_b, pairs_b, assign, keep, send, rows):
    sec, tp = lax.axis_index("sec"), lax.axis_index("tp")
    odd = (sec & 1) == 1
    slots = jnp.zeros((1, group), jnp.int32)
    for index in range(assign.shape[1] // group):
        slots = jnp.where(tp == index, assign[:, index * group : (index + 1) * group], slots)
    line = lax.broadcasted_iota(jnp.int32, (16, group), 0)
    wanted = jnp.where(line < 8, sec * per_device + line, (sec ^ 2) * per_device + line - 8)
    inside = (line & 7) < per_device
    picker = jnp.where(inside & (jnp.broadcast_to(slots, (16, group)) == wanted), 1.0, 0.0).astype(jnp.bfloat16)

    def picked(ref):
        return jnp.dot(picker, ref[...], preferred_element_type=jnp.float32)

    mine_q, mine_p, other_q, other_p = picked(query_a), picked(pairs_a), picked(query_b), picked(pairs_b)
    both = (
        (jnp.where(odd, other_q, mine_q), jnp.where(odd, other_p, mine_p)),
        (jnp.where(odd, mine_q, other_q), jnp.where(odd, mine_p, other_p)),
    )
    rows[...] = jnp.zeros_like(rows)
    width = HEAD_WIDTH
    for side in range(2):
        for place, (queries, pairs) in enumerate(both):
            for j in range(per_device):
                base = j * 32 + place * 16
                line = side * 8 + j
                for h in range(heads):
                    rows[side, base + h : base + h + 1, :] = queries[line : line + 1, h * width : (h + 1) * width]
                for h in range(pairs.shape[1] // width):
                    at = base + heads + h
                    rows[side, at : at + 1, :] = pairs[line : line + 1, h * width : (h + 1) * width]
    keep[...] = rows[0].astype(jnp.bfloat16)
    send[...] = rows[1].astype(jnp.bfloat16)


def attend_kernel(per_device, heads, lengths, mine, other, keys, values, keep, send, total):
    sec, tp = lax.axis_index("sec"), lax.axis_index("tp")
    high = (sec >> 1) == 1
    share = heads // 2
    first, second = mine[...], other[...]
    halves = (jnp.where(high, second, first), jnp.where(high, first, second))
    slots = keys.shape[1]
    width = HEAD_WIDTH
    scaling = 1.0 / math.sqrt(width)
    line = lax.broadcasted_iota(jnp.int32, (16, width), 0)
    upper = line < share
    place = lax.broadcasted_iota(jnp.int32, (16, slots), 1)
    total[...] = jnp.zeros_like(total)
    for j in range(per_device):
        valid = place < lengths[j]
        for b in range(4):
            base = j * 32 + (b & 1) * 16
            block = halves[b >> 1][base : base + 16]
            wide = block.astype(jnp.float32)
            zero = jnp.zeros_like(wide)
            left = jnp.where(upper, wide, zero).astype(jnp.bfloat16)
            right = jnp.where(upper, zero, wide).astype(jnp.bfloat16)
            both = jnp.concatenate([left, right], axis=1)
            columns = slice(b * 2 * width, (b + 1) * 2 * width)
            past = lax.dot_general(
                both, keys[j, :, columns], (((1,), (1,)), ((), ())), preferred_element_type=jnp.float32
            )
            past = jnp.where(valid, past * scaling, -1e30)
            new_key = jnp.where(upper, wide[heads : heads + 1], wide[heads + 2 : heads + 3])
            new_value = jnp.where(upper, wide[heads + 1 : heads + 2], wide[heads + 3 : heads + 4])
            fresh = jnp.sum(wide * new_key, axis=1, keepdims=True) * scaling
            highest = jnp.maximum(jnp.max(past, axis=1, keepdims=True), fresh)
            past_exp = jnp.exp(past - highest)
            fresh_exp = jnp.exp(fresh - highest)
            inverse = 1.0 / (jnp.sum(past_exp, axis=1, keepdims=True) + fresh_exp)
            weights = (past_exp * inverse).astype(jnp.bfloat16)
            fresh_weight = (fresh_exp * inverse).astype(jnp.bfloat16).astype(jnp.float32)
            mixed = jnp.dot(weights, values[j, :, columns], preferred_element_type=jnp.float32)
            mixed = jnp.where(upper, mixed[:, :width], mixed[:, width:]) + fresh_weight * new_value
            side = (b & 1) ^ (tp & 1)
            for h in range(heads):
                total[side, b >> 1, j : j + 1, h * width : (h + 1) * width] = mixed[h : h + 1]
    keep[...] = total[0, :, 0:4].astype(jnp.bfloat16)
    send[...] = total[1, :, 0:4].astype(jnp.bfloat16)


def forward_kernel(mine, other, send):
    away = (lax.axis_index("tp") >> 1) ^ 1
    send[0] = mine[away]
    send[1] = other[away]


def gather_kernel(mine, other, far, out, rows):
    here = lax.axis_index("tp") >> 1
    rows[0:4] = mine[here].astype(jnp.float32)
    rows[4:8] = other[here].astype(jnp.float32)
    rows[8:12] = far[0].astype(jnp.float32)
    rows[12:16] = far[1].astype(jnp.float32)
    out[...] = rows[...].astype(jnp.bfloat16)


def group_order(group, shape, axis):
    place = lax.broadcasted_iota(jnp.int32, shape, axis)
    number = jnp.zeros(shape, jnp.int32)
    for limit in range(1, 4):
        number = number + jnp.where(place >= limit * group, 1, 0)
    return (((number & 1) << 1) | (number >> 1)) * group + place - number * group


def project_kernel(per_device, group, first, second, third, fourth, assign, weight, keep, send, product):
    sec, tp = lax.axis_index("sec"), lax.axis_index("tp")
    count = assign.shape[1]
    lines = jnp.concatenate([first[...], second[...], third[...], fourth[...]], axis=0)
    line = lax.broadcasted_iota(jnp.int32, (64, count), 0)
    request = lax.broadcasted_iota(jnp.int32, (64, count), 1)
    number = jnp.zeros((64, count), jnp.int32)
    for limit in range(1, 4):
        number = number + jnp.where(request >= limit * group, 1, 0)
    slot = (sec ^ (line >> 4)) * per_device + (line & 3)
    match = (number == (tp ^ ((line >> 2) & 3))) & (jnp.broadcast_to(assign[...], (64, count)) == slot)
    match = jnp.where(match & ((line & 3) < per_device), 1.0, 0.0).astype(jnp.bfloat16)
    order = group_order(group, (count, count), 1) == lax.broadcasted_iota(jnp.int32, (count, count), 0)
    order = jnp.where(order, 1.0, 0.0).astype(jnp.bfloat16)
    match = jnp.dot(match, order, preferred_element_type=jnp.float32).astype(jnp.bfloat16)
    ordered = lax.dot_general(match, lines, (((0,), (0,)), ((), ())), preferred_element_type=jnp.float32)
    ordered = ordered.astype(jnp.bfloat16)
    product[...] = jnp.dot(ordered, weight[...], preferred_element_type=jnp.float32)
    half = count // 2
    odd = tp & 1
    keep[...] = product[pl.ds(pl.multiple_of(odd * half, 8), half), :]
    send[...] = product[pl.ds(pl.multiple_of((1 - odd) * half, 8), half), :].astype(jnp.bfloat16)


def add_resid_kernel(mine, other, resid, keep, send):
    tp = lax.axis_index("tp")
    group = resid.shape[0]
    line = lax.broadcasted_iota(jnp.int32, (2 * group, group), 0)
    match = line == lax.broadcasted_iota(jnp.int32, (2 * group, group), 1) + (tp >> 1) * group
    match = jnp.where(match, 1.0, 0.0).astype(jnp.bfloat16)
    total = mine[...] + other[...].astype(jnp.float32)
    total = total + jnp.dot(match, resid[...], preferred_element_type=jnp.float32)
    keep[...] = total
    send[...] = total.astype(jnp.bfloat16)


def stream_kernel(mine, other, stream, send):
    total = mine[...] + other[...].astype(jnp.float32)
    stream[...] = total
    send[...] = total.astype(jnp.bfloat16)


def gate_up_kernel(chunk, mine, other, gain, gate, up, keep, send, lines):
    sec, tp = lax.axis_index("sec"), lax.axis_index("tp")
    half = mine.shape[0]
    mine_at = (tp ^ sec) & 1
    lines[mine_at] = mine[...].astype(jnp.float32)
    lines[1 - mine_at] = other[...].astype(jnp.float32)
    stream = jnp.concatenate([lines[0], lines[1]], axis=0)
    squares = jnp.sum(stream * stream, axis=1, keepdims=True)
    features = (stream * gain[...].astype(jnp.float32)).astype(jnp.bfloat16)
    width = gate.shape[1] // 2
    for part in range(2):
        for kind, weight in enumerate((gate, up)):
            for start in range(0, width, chunk):
                column = part * width + start
                product = jnp.dot(features, weight[:, column : column + chunk], preferred_element_type=jnp.float32)
                at = kind * width + start
                keep[part, :, at : at + chunk] = product[:half]
                send[part, :, at : at + chunk] = product[half:].astype(jnp.bfloat16)
        keep[part, :, 2 * width :] = jnp.broadcast_to(squares[:half], (half, 128))
        send[part, :, 2 * width :] = two_terms(squares[half:])


def two_terms(column):
    shape = (column.shape[0], 128)
    column = jnp.broadcast_to(column, shape)
    coarse = column.astype(jnp.bfloat16).astype(jnp.float32)
    lane = lax.broadcasted_iota(jnp.int32, shape, 1)
    return jnp.where(lane < 64, coarse, column - coarse).astype(jnp.bfloat16)


def one_column(terms):
    return terms[:, 0:1].astype(jnp.float32) + terms[:, 64:65].astype(jnp.float32)


def pair_sum_kernel(mine, other, keep, send):
    here = lax.axis_index("sec") >> 1
    width = mine.shape[2] - 128
    for target, part in ((send, 1 - here), (keep, here)):
        total = mine[part, :, :width] + other[part, :, :width].astype(jnp.float32)
        target[:, :width] = total.astype(target.dtype)
    squares = mine[0, :, width:] + one_column(other[0, :, width:])
    keep[:, width:] = squares
    send[:, width:] = two_terms(squares[:, 0:1])


def hidden_kernel(features, mine, other, hidden):
    width = (mine.shape[1] - 128) // 2
    squares = mine[:, 2 * width : 2 * width + 1] + one_column(other[:, 2 * width :])
    inverse = lax.rsqrt(squares / features + 1e-06)
    gate = (mine[:, :width] + other[:, :width].astype(jnp.float32)) * inverse
    up = (mine[:, width : 2 * width] + other[:, width : 2 * width].astype(jnp.float32)) * inverse
    hidden[...] = (gate / (1.0 + jnp.exp(-gate)) * up).astype(jnp.bfloat16)


def down_first_kernel(mine, other, weight, out):
    here = lax.axis_index("sec") >> 1
    lines = jnp.concatenate([mine[...].astype(jnp.float32), other[...].astype(jnp.float32)], axis=0)
    lines = lines.astype(jnp.bfloat16)
    depth = lines.shape[1]
    rows = weight[pl.ds(pl.multiple_of(here * depth, depth), depth), :]
    out[...] = jnp.dot(lines, rows, preferred_element_type=jnp.float32)


def down_second_kernel(mine, other, before, weight, keep, send, product):
    sec, tp = lax.axis_index("sec"), lax.axis_index("tp")
    away = 1 - (sec >> 1)
    lines = jnp.concatenate([mine[...].astype(jnp.float32), other[...].astype(jnp.float32)], axis=0)
    lines = lines.astype(jnp.bfloat16)
    depth = lines.shape[1]
    rows = weight[pl.ds(pl.multiple_of(away * depth, depth), depth), :]
    product[...] = before[...] + jnp.dot(lines, rows, preferred_element_type=jnp.float32)
    half = product.shape[0] // 2
    at = (sec ^ tp) & 1
    keep[...] = product[pl.ds(pl.multiple_of(at * half, 8), half), :]
    send[...] = product[pl.ds(pl.multiple_of((1 - at) * half, 8), half), :].astype(jnp.bfloat16)


def share_kernel(mine, other, stream, keep, send):
    high = (lax.axis_index("tp") >> 1) == 1
    group = keep.shape[0]
    total = mine[...] + other[...].astype(jnp.float32)
    lower, upper = total[:group], total[group:]
    send[...] = jnp.where(high, lower, upper).astype(jnp.bfloat16)
    total = total + stream[...]
    keep[...] = jnp.where(high, total[group:], total[:group])


def finish_kernel(mine, other, out):
    out[...] = (mine[...] + other[...].astype(jnp.float32)).astype(jnp.bfloat16)


def local_pairs(
    resid,
    query,
    new_kv,
    key_cache,
    cached_value_rows,
    cache_len,
    assign,
    out_weight,
    norm_gain,
    gate_weight,
    up_weight,
    down_weight,
):
    f32, bf16 = jnp.float32, jnp.bfloat16
    group, features = resid.shape
    per_device = key_cache.shape[0]
    heads = query.shape[1] // HEAD_WIDTH
    head_block = out_weight.shape[0]
    width = gate_weight.shape[1]
    half = 2 * group
    assign = assign.reshape(1, -1)
    gain = norm_gain.reshape(1, -1)

    query_b, pairs_b = swap(query, "sec", 1), swap(new_kv, "sec", 1)
    lines = 32 * per_device
    mine, away = call(
        functools.partial(pick_kernel, per_device, group, heads),
        [((lines, HEAD_WIDTH), bf16)] * 2,
        (query, new_kv, query_b, pairs_b, assign),
        [pltpu.VMEM((2, lines, HEAD_WIDTH), f32)],
    )
    other = swap(away, "sec", 2)
    mine, away = call(
        functools.partial(attend_kernel, per_device, heads),
        [((2, 4, head_block), bf16)] * 2,
        (cache_len, mine, other, key_cache, cached_value_rows),
        [pltpu.VMEM((2, 2, 8, head_block), f32)],
        smem=(0,),
        resident=(3, 4),
    )

    other = swap(away, "tp", 1)
    (away,) = call(forward_kernel, [((2, 4, head_block), bf16)], (mine, other))
    far = swap(away, "tp", 2)
    (block,) = call(
        gather_kernel, [((16, head_block), bf16)], (mine, other, far), [pltpu.VMEM((16, head_block), f32)]
    )
    blocks = [block] + [swap(block, "sec", step) for step in range(1, 4)]
    mine, away = call(
        functools.partial(project_kernel, per_device, group),
        [((half, features), f32), ((half, features), bf16)],
        (*blocks, assign, out_weight),
        [pltpu.VMEM((2 * half, features), f32)],
        resident=(5,),
    )
    other = swap(away, "tp", 1)
    mine, away = call(
        add_resid_kernel, [((half, features), f32), ((half, features), bf16)], (mine, other, resid)
    )
    other = swap(away, "tp", 2)
    stream, mine = call(stream_kernel, [((half, features), f32), ((half, features), bf16)], (mine, other))
    other = swap(mine, "tp", 1)

    wide = (2, half, width + 128)
    mine, away = call(
        functools.partial(gate_up_kernel, min(512, width // 2)),
        [(wide, f32), (wide, bf16)],
        (mine, other, gain, gate_weight, up_weight),
        [pltpu.VMEM((2, half, features), f32)],
        resident=(3, 4),
    )
    other = swap(away, "sec", 1)
    mine, away = call(pair_sum_kernel, [(wide[1:], f32), (wide[1:], bf16)], (mine, other))
    other = swap(away, "sec", 2)
    (hidden,) = call(
        functools.partial(hidden_kernel, features * lax.axis_size("sec")), [((half, width // 2), bf16)], (mine, other)
    )
    across = swap(hidden, "sec", 2)
    beside = swap(hidden, "sec", 1)
    corner = swap(across, "sec", 1)
    (before,) = call(down_first_kernel, [((2 * half, features), f32)], (hidden, beside, down_weight), resident=(2,))
    mine, away = call(
        down_second_kernel,
        [((half, features), f32), ((half, features), bf16)],
        (across, corner, before, down_weight),
        [pltpu.VMEM((2 * half, features), f32)],
        resident=(3,),
    )
    other = swap(away, "tp", 1)
    mine, away = call(share_kernel, [((group, features), f32), ((group, features), bf16)], (mine, other, stream))
    other = swap(away, "tp", 2)
    (out,) = call(finish_kernel, [((group, features), bf16)], (mine, other))
    return out


def solution(mesh):
    small = mesh.shape["sec"] == 4 and mesh.shape["tp"] == 4
    return jax.shard_map(
        local_pairs if small else local,
        mesh=mesh,
        in_specs=(
            P(("rep", "tp"), "sec"),
            P(("rep", "tp"), "sec"),
            P(("rep", "tp"), "sec"),
            P(("rep", "sec", "tp"), None, None),
            P(("rep", "sec", "tp"), None, None),
            P(("rep", "sec", "tp")),
            P("rep"),
            P("tp", "sec"),
            P("sec"),
            P("sec", "tp"),
            P("sec", "tp"),
            P("tp", "sec"),
        ),
        out_specs=P(("rep", "tp"), "sec"),
        check_vma=False,
    )
```

```python
import functools
import math

import jax
import jax.numpy as jnp
from jax import lax
from jax.experimental import pallas as pl
from jax.experimental.pallas import tpu as pltpu
from jax.sharding import PartitionSpec as P

D = 5120
QUERY_HEADS = 40
KEY_VALUE_HEADS = 8
HEAD_WIDTH = 128
CACHE_SLOTS = 224


def attend_slots(query_rows, key_value_pairs, stored_keys, stored_values, lengths):
    cache_slots = query_rows.shape[0]
    group_query = QUERY_HEADS // KEY_VALUE_HEADS
    query_head_rows = query_rows.reshape(cache_slots, KEY_VALUE_HEADS, group_query, HEAD_WIDTH)
    paired_heads = key_value_pairs.reshape(cache_slots, KEY_VALUE_HEADS, 2, HEAD_WIDTH)
    fresh_keys = paired_heads[:, :, 0]
    fresh_values = paired_heads[:, :, 1]
    earlier_keys = stored_keys.reshape(cache_slots, CACHE_SLOTS, KEY_VALUE_HEADS, HEAD_WIDTH)
    earlier_values = stored_values.reshape(cache_slots, CACHE_SLOTS, KEY_VALUE_HEADS, HEAD_WIDTH)
    scaling = 1.0 / math.sqrt(HEAD_WIDTH)
    past_scores = (
        jnp.einsum(
            "rkgd,rlkd->rkgl", query_head_rows, earlier_keys, preferred_element_type=jnp.float32
        )
        * scaling
    )
    fresh_scores = (
        jnp.einsum("rkgd,rkd->rkg", query_head_rows, fresh_keys, preferred_element_type=jnp.float32)
        * scaling
    )
    valid = lax.broadcasted_iota(jnp.int32, (cache_slots, CACHE_SLOTS), 1) < lengths[:, None]
    past_scores = jnp.where(valid[:, None, None, :], past_scores, -1e30)
    highest = jnp.maximum(jnp.max(past_scores, axis=-1), fresh_scores)
    past_exp = jnp.exp(past_scores - highest[..., None])
    fresh_exp = jnp.exp(fresh_scores - highest)
    denominator = jnp.sum(past_exp, axis=-1) + fresh_exp
    past_weights = (past_exp / denominator[..., None]).astype(jnp.bfloat16)
    fresh_weights = (fresh_exp / denominator).astype(jnp.bfloat16)
    mixed = jnp.einsum(
        "rkgl,rlkd->rkgd", past_weights, earlier_values, preferred_element_type=jnp.float32
    )
    mixed = (
        mixed
        + fresh_weights.astype(jnp.float32)[..., None]
        * fresh_values.astype(jnp.float32)[:, :, None, :]
    )
    return mixed.reshape(cache_slots, QUERY_HEADS * HEAD_WIDTH).astype(jnp.bfloat16)


def gated_units(values, width):
    return (jax.nn.silu(values[:, :width]) * values[:, width:]).astype(jnp.bfloat16)


def received(blocks, axis):
    count = lax.axis_size(axis)
    result = [blocks[0]]
    for step in range(1, count):
        result.append(lax.ppermute(blocks[step], axis, [(i, i ^ step) for i in range(count)]))
    return result


def local(
    resid,
    query,
    new_kv,
    key_cache,
    cached_value_rows,
    cache_len,
    assign,
    out_weight,
    norm_gain,
    gate_weight,
    up_weight,
    down_weight,
):
    group = query.shape[0]
    per_device = key_cache.shape[0]
    tp_index = lax.axis_index("tp")
    sec_index = lax.axis_index("sec")
    tp_count = lax.axis_size("tp")
    sec_count = lax.axis_size("sec")
    local_slots = lax.dynamic_slice_in_dim(assign, tp_index * group, group)
    resid_f32 = resid.astype(jnp.float32)
    features = resid.shape[1]
    width = gate_weight.shape[1]
    rows = group * tp_count // sec_count

    tokens = jnp.concatenate([query, new_kv], axis=1)
    blocks = []
    for step in range(sec_count):
        wanted = (sec_index ^ step) * per_device + lax.iota(jnp.int32, per_device)
        picker = (local_slots[None, :] == wanted[:, None]).astype(jnp.bfloat16)
        blocks.append(jnp.dot(picker, tokens, preferred_element_type=jnp.float32).astype(jnp.bfloat16))
    pieces = jnp.stack(received(blocks, "sec"))
    pieces = jnp.take(pieces, sec_index ^ lax.iota(jnp.int32, sec_count), axis=0)
    my_query = pieces[:, :, : query.shape[1]].transpose(1, 0, 2).reshape(per_device, -1)
    my_pairs = pieces[:, :, query.shape[1] :].transpose(1, 0, 2).reshape(per_device, -1)
    attended = attend_slots(my_query, my_pairs, key_cache, cached_value_rows, cache_len)

    head_block = out_weight.shape[0]
    blocks = [
        lax.dynamic_slice_in_dim(attended, (tp_index ^ step) * head_block, head_block, 1)
        for step in range(tp_count)
    ]
    mine = jnp.stack(received(blocks, "tp"))
    everyone = jnp.stack(received([mine] * sec_count, "sec"))
    everyone = jnp.take(everyone, sec_index ^ lax.iota(jnp.int32, sec_count), axis=0)
    everyone = everyone.transpose(1, 0, 2, 3).reshape(tp_count, group, head_block)
    parts = jnp.dot(everyone.reshape(tp_count * group, head_block), out_weight, preferred_element_type=jnp.float32)
    parts = parts.astype(jnp.bfloat16).reshape(tp_count, group, features)
    shares = received([parts[step] for step in range(tp_count)], "tp")
    attn_out = sum(share.astype(jnp.float32) for share in shares)
    attn_out = jnp.take(attn_out, local_slots, axis=0)
    stream = resid_f32 + attn_out

    scaled = (stream * norm_gain.astype(jnp.float32)[None, :]).astype(jnp.bfloat16)
    squares = jnp.broadcast_to(jnp.sum(stream * stream, axis=1, keepdims=True), (group, 128))
    piece = jnp.concatenate(received([scaled] * tp_count, "tp"), axis=0)
    square_parts = jnp.concatenate(received([squares] * tp_count, "tp"), axis=0)
    square_parts = square_parts.reshape(sec_count, rows, 128)
    gate_part = jnp.dot(piece, gate_weight, preferred_element_type=jnp.float32)
    up_part = jnp.dot(piece, up_weight, preferred_element_type=jnp.float32)
    projected = jnp.concatenate([gate_part, up_part], axis=1).astype(jnp.bfloat16)
    projected = projected.reshape(sec_count, rows, 2 * width)
    blocks = [lax.dynamic_index_in_dim(projected, sec_index ^ step, 0, False) for step in range(sec_count)]
    share = sum(block.astype(jnp.float32) for block in received(blocks, "sec"))
    blocks = [lax.dynamic_index_in_dim(square_parts, sec_index ^ step, 0, False) for step in range(sec_count)]
    total = sum(received(blocks, "sec"))
    inverse = lax.rsqrt(total[:, :1] / D + 1e-06)
    hidden = gated_units(share * inverse, width)
    hidden = jnp.stack(received([hidden] * sec_count, "sec"))
    hidden = jnp.take(hidden, sec_index ^ lax.iota(jnp.int32, sec_count), axis=0).reshape(-1, width)
    parts = jnp.dot(hidden, down_weight, preferred_element_type=jnp.float32).astype(jnp.bfloat16)
    parts = parts.reshape(tp_count, group, features)
    shares = received([parts[step] for step in range(tp_count)], "tp")
    ff_out = sum(share.astype(jnp.float32) for share in shares)
    return (stream + ff_out).astype(jnp.bfloat16)


MIB = 1024 * 1024


def call(kernel, outs, operands, scratch=(), smem=(), resident=(), remote=(), micros=4, limit=8):
    specs = []
    placed = []
    for place, operand in enumerate(operands):
        space = pltpu.SMEM if place in smem else pltpu.HBM if place in remote else pltpu.VMEM
        specs.append(pl.BlockSpec(memory_space=space))
        if place in resident or place in remote:
            operand = constrained(operand, space)
        placed.append(operand)
    return pl.pallas_call(
        kernel,
        out_shape=[jax.ShapeDtypeStruct(shape, dtype) for shape, dtype in outs],
        in_specs=specs,
        out_specs=[pl.BlockSpec(memory_space=pltpu.VMEM) for _ in outs],
        scratch_shapes=list(scratch),
        compiler_params=pltpu.CompilerParams(vmem_limit_bytes=limit * MIB),
        cost_estimate=pl.CostEstimate(flops=micros * 10**9, bytes_accessed=0, transcendentals=0),
    )(*placed)


def constrained(operand, space):
    return pltpu.with_memory_space_constraint(operand, space)


def swap(value, axis, step):
    if isinstance(axis, tuple):
        count = lax.axis_size(axis[1])
        total = lax.axis_size(axis[0]) * count
        step = step[0] * count + step[1]
    else:
        total = lax.axis_size(axis)
    return lax.ppermute(value, axis, [(i, i ^ step) for i in range(total)])


def slot_picker(per_device, group, assign):
    sec, tp = lax.axis_index("sec"), lax.axis_index("tp")
    slots = jnp.zeros((1, group), jnp.int32)
    for index in range(assign.shape[1] // group):
        slots = jnp.where(tp == index, assign[:, index * group : (index + 1) * group], slots)
    line = lax.broadcasted_iota(jnp.int32, (16, group), 0)
    wanted = jnp.where(line < 8, sec * per_device + line, (sec ^ 3) * per_device + line - 8)
    inside = (line & 7) < per_device
    return jnp.where(inside & (jnp.broadcast_to(slots, (16, group)) == wanted), 1.0, 0.0).astype(jnp.bfloat16)


def split_heads(per_device, picker, query, pairs, rows):
    queries = jnp.dot(picker, query[...], preferred_element_type=jnp.float32)
    others = jnp.dot(picker, pairs[...], preferred_element_type=jnp.float32)
    width = HEAD_WIDTH
    heads = query.shape[1] // width
    rows[...] = jnp.zeros_like(rows)
    for side in range(2):
        for j in range(per_device):
            line = side * 8 + j
            for h in range(heads):
                rows[side, j * 16 + h : j * 16 + h + 1, :] = queries[line : line + 1, h * width : (h + 1) * width]
            for h in range(pairs.shape[1] // width):
                at = j * 16 + heads + h
                rows[side, at : at + 1, :] = others[line : line + 1, h * width : (h + 1) * width]


def pick_own_kernel(per_device, group, query, pairs, assign, out, query_here, pairs_here, assign_here, rows, sems):
    copies = [
        pltpu.make_async_copy(source, target, sems.at[index])
        for index, (source, target) in enumerate(
            ((query, query_here), (pairs, pairs_here), (assign, assign_here))
        )
    ]
    for copy in copies:
        copy.start()
    for copy in copies:
        copy.wait()
    split_heads(per_device, slot_picker(per_device, group, assign_here), query_here, pairs_here, rows)
    out[...] = rows[...].astype(jnp.bfloat16)


def pick_other_kernel(per_device, group, own, query, pairs, assign, keep, send, rows):
    split_heads(per_device, slot_picker(per_device, group, assign), query, pairs, rows)
    here = lax.axis_index("sec") & 1
    keep[here] = own[0]
    keep[1 - here] = rows[0].astype(jnp.bfloat16)
    send[here] = own[1]
    send[1 - here] = rows[1].astype(jnp.bfloat16)


def attend_kernel(flip, per_device, heads, lengths, mine, other, keys, values, out, total):
    sec, tp = lax.axis_index("sec"), lax.axis_index("tp")
    chip = sec >> 1
    parity = (tp & 1) ^ flip
    share = heads // 2
    slots = keys.shape[1]
    width = HEAD_WIDTH
    scaling = 1.0 / math.sqrt(width)
    line = lax.broadcasted_iota(jnp.int32, (16, width), 0)
    upper = line < share
    place = lax.broadcasted_iota(jnp.int32, (16, slots), 1)
    near, far = mine[parity].astype(jnp.float32), other[parity].astype(jnp.float32)
    sources = (jnp.where(chip == 0, near, far), jnp.where(chip == 0, far, near))
    work = [(i, j) for i in range(2) for j in range(per_device)]
    past, fresh, new_values, columns = [], [], [], []
    for i, j in work:
        wide = sources[i][j * 16 : (j + 1) * 16]
        zero = jnp.zeros_like(wide)
        both = jnp.concatenate([jnp.where(upper, wide, zero), jnp.where(upper, zero, wide)], axis=1)
        column = pl.ds(pl.multiple_of((2 * i + parity) * 2 * width, 2 * width), 2 * width)
        columns.append(column)
        scores = lax.dot_general(
            both.astype(jnp.bfloat16),
            keys[j, :, column],
            (((1,), (1,)), ((), ())),
            preferred_element_type=jnp.float32,
        )
        past.append(jnp.where(place < lengths[j], scores * scaling, -1e30))
        new_key = jnp.where(upper, wide[heads : heads + 1], wide[heads + 2 : heads + 3])
        new_values.append(jnp.where(upper, wide[heads + 1 : heads + 2], wide[heads + 3 : heads + 4]))
        fresh.append(wide * new_key)
    past = jnp.concatenate(past, axis=0)
    fresh = jnp.sum(jnp.concatenate(fresh, axis=0), axis=1, keepdims=True) * scaling
    highest = jnp.maximum(jnp.max(past, axis=1, keepdims=True), fresh)
    past_exp = jnp.exp(past - highest)
    fresh_exp = jnp.exp(fresh - highest)
    inverse = 1.0 / (jnp.sum(past_exp, axis=1, keepdims=True) + fresh_exp)
    weights = (past_exp * inverse).astype(jnp.bfloat16)
    fresh_weight = (fresh_exp * inverse).astype(jnp.bfloat16).astype(jnp.float32)
    total[...] = jnp.zeros_like(total)
    for index, (i, j) in enumerate(work):
        lines = slice(index * 16, (index + 1) * 16)
        mixed = jnp.dot(weights[lines], values[j, :, columns[index]], preferred_element_type=jnp.float32)
        mixed = jnp.where(upper, mixed[:, :width], mixed[:, width:]) + fresh_weight[lines] * new_values[index]
        for h in range(heads):
            total[i, j : j + 1, h * width : (h + 1) * width] = mixed[h : h + 1]
    out[...] = total[:, 0:4].astype(jnp.bfloat16)


def forward_kernel(mine, other, send):
    away = (lax.axis_index("tp") >> 1) ^ 1
    send[0] = mine[away]
    send[1] = other[away]


def gather_kernel(mine, other, far, out, rows):
    here = lax.axis_index("tp") >> 1
    rows[0:4] = mine[here].astype(jnp.float32)
    rows[4:8] = other[here].astype(jnp.float32)
    rows[8:12] = far[0].astype(jnp.float32)
    rows[12:16] = far[1].astype(jnp.float32)
    out[...] = rows[...].astype(jnp.bfloat16)


def project_kernel(per_device, group, own, beside, across, corner, assign, resid, weight, keep, send):
    sec, tp = lax.axis_index("sec"), lax.axis_index("tp")
    count = assign.shape[1]
    lines = jnp.concatenate([own[...], beside[...], across[...], corner[...]], axis=0)
    line = lax.broadcasted_iota(jnp.int32, (64, count), 0)
    request = lax.broadcasted_iota(jnp.int32, (64, count), 1)
    number = jnp.zeros((64, count), jnp.int32)
    for limit in range(1, 4):
        number = number + jnp.where(request >= limit * group, 1, 0)
    block, place = line >> 4, (line >> 2) & 3
    from_sec = sec ^ block ^ (block >> 1) ^ ((place ^ (place >> 1)) & 1)
    slot = from_sec * per_device + (line & 3)
    match = (number == (tp ^ place)) & (jnp.broadcast_to(assign[...], (64, count)) == slot)
    match = jnp.where(match & ((line & 3) < per_device), 1.0, 0.0).astype(jnp.bfloat16)
    ordered = lax.dot_general(match, lines, (((0,), (0,)), ((), ())), preferred_element_type=jnp.float32)
    total = jnp.dot(ordered.astype(jnp.bfloat16), weight[...], preferred_element_type=jnp.float32)
    line = lax.broadcasted_iota(jnp.int32, (count, group), 0)
    match = line == lax.broadcasted_iota(jnp.int32, (count, group), 1) + tp * group
    match = jnp.where(match, 1.0, 0.0).astype(jnp.bfloat16)
    total = total + jnp.dot(match, resid[...], preferred_element_type=jnp.float32)
    keep[...] = total
    send[...] = total.astype(jnp.bfloat16)


def add_kernel(mine, other, keep, send):
    total = mine[...] + other[...].astype(jnp.float32)
    keep[...] = total
    send[...] = total.astype(jnp.bfloat16)


def row_half():
    sec = lax.axis_index("sec")
    return (sec ^ (sec >> 1)) & 1


def products(features, gate, up, part, chunk, keep, send):
    half = keep.shape[0]
    width = gate.shape[1] // 2
    for kind, weight in enumerate((gate, up)):
        for start in range(0, width, chunk):
            column = pl.ds(pl.multiple_of(part * width + start, chunk), chunk)
            product = jnp.dot(features, weight[:, column], preferred_element_type=jnp.float32)
            at = kind * width + start
            keep[:, at : at + chunk] = product[:half]
            send[:, at : at + chunk] = product[half:].astype(jnp.bfloat16)


def gate_up_first_kernel(chunk, mine, other, gain, gate, up, keep, send, features, stream, halves, groups):
    sec, tp = lax.axis_index("sec"), lax.axis_index("tp")
    half = mine.shape[0] // 2
    total = mine[...] + other[...].astype(jnp.float32)
    group = stream.shape[0]
    for index in range(mine.shape[0] // group):
        groups[index, 0:group] = total[index * group : (index + 1) * group]
    stream[...] = groups[tp, 0:group]
    halves[0] = total[:half]
    halves[1] = total[half:]
    first = row_half()
    total = jnp.concatenate([halves[first], halves[1 - first]], axis=0)
    squares = jnp.sum(total * total, axis=1, keepdims=True)
    scaled = (total * gain[...].astype(jnp.float32)).astype(jnp.bfloat16)
    features[...] = scaled
    products(scaled, gate, up, 1 - (sec >> 1), chunk, keep, send)
    width = gate.shape[1]
    keep[:, width:] = jnp.broadcast_to(squares[:half], (half, 128))
    send[:, width:] = two_terms(squares[half:])


def gate_up_second_kernel(chunk, features, gate, up, keep, send):
    products(features[...], gate, up, lax.axis_index("sec") >> 1, chunk, keep, send)


def two_terms(column):
    shape = (column.shape[0], 128)
    column = jnp.broadcast_to(column, shape)
    coarse = column.astype(jnp.bfloat16).astype(jnp.float32)
    lane = lax.broadcasted_iota(jnp.int32, shape, 1)
    return jnp.where(lane < 64, coarse, column - coarse).astype(jnp.bfloat16)


def one_column(terms):
    return terms[:, 0:1].astype(jnp.float32) + terms[:, 64:65].astype(jnp.float32)


def pair_sum_kernel(mine, other, send, squares):
    width = mine.shape[1] - 128
    total = mine[:, :width] + other[:, :width].astype(jnp.float32)
    send[:, :width] = total.astype(jnp.bfloat16)
    both = mine[:, width:] + one_column(other[:, width:])
    squares[...] = both
    send[:, width:] = two_terms(both[:, 0:1])


def hidden_kernel(features, mine, beside, across, squares, hidden):
    width = mine.shape[1] // 2
    total = squares[:, 0:1] + one_column(across[:, 2 * width :])
    inverse = lax.rsqrt(total / features + 1e-06)

    def summed(columns):
        here = mine[:, columns] + beside[:, columns].astype(jnp.float32)
        return (here + across[:, columns].astype(jnp.float32)) * inverse

    gate, up = summed(slice(0, width)), summed(slice(width, 2 * width))
    hidden[...] = (gate / (1.0 + jnp.exp(-gate)) * up).astype(jnp.bfloat16)


def down_lines(mine, other):
    lines = jnp.concatenate([mine[...].astype(jnp.float32), other[...].astype(jnp.float32)], axis=0)
    return lines.astype(jnp.bfloat16)


def down_first_kernel(mine, other, weight, out):
    here = lax.axis_index("sec") >> 1
    depth = mine.shape[1]
    rows = weight[pl.ds(pl.multiple_of(here * depth, depth), depth), :]
    out[...] = jnp.dot(down_lines(mine, other), rows, preferred_element_type=jnp.float32)


def down_second_kernel(mine, other, before, weight, keep, first, second, third, groups):
    tp = lax.axis_index("tp")
    away = 1 - (lax.axis_index("sec") >> 1)
    depth = mine.shape[1]
    rows = weight[pl.ds(pl.multiple_of(away * depth, depth), depth), :]
    product = before[...] + jnp.dot(down_lines(mine, other), rows, preferred_element_type=jnp.float32)
    group = keep.shape[0]
    for index in range(product.shape[0] // group):
        groups[index, 0:group] = product[index * group : (index + 1) * group]
    here = tp ^ (2 * row_half())
    keep[...] = groups[here, 0:group]
    for step, target in enumerate((first, second, third)):
        target[...] = groups[here ^ (step + 1), 0:group].astype(jnp.bfloat16)


def finish_kernel(stream, mine, first, second, third, out):
    total = stream[...] + mine[...]
    for other in (first, second, third):
        total = total + other[...].astype(jnp.float32)
    out[...] = total.astype(jnp.bfloat16)


def local_pairs(
    resid,
    query,
    new_kv,
    key_cache,
    cached_value_rows,
    cache_len,
    assign,
    out_weight,
    norm_gain,
    gate_weight,
    up_weight,
    down_weight,
):
    f32, bf16 = jnp.float32, jnp.bfloat16
    group, features = resid.shape
    per_device = key_cache.shape[0]
    heads = query.shape[1] // HEAD_WIDTH
    head_block = out_weight.shape[0]
    width = gate_weight.shape[1]
    half = 2 * group
    assign = assign.reshape(1, -1)
    gain = norm_gain.reshape(1, -1)

    query_b, pairs_b = swap(query, "sec", 1), swap(new_kv, "sec", 1)
    block = (2, 16 * per_device, HEAD_WIDTH)
    (own,) = call(
        functools.partial(pick_own_kernel, per_device, group),
        [(block, bf16)],
        (query, new_kv, assign),
        [
            pltpu.VMEM(query.shape, bf16),
            pltpu.VMEM(new_kv.shape, bf16),
            pltpu.VMEM(assign.shape, jnp.int32),
            pltpu.VMEM(block, f32),
            pltpu.SemaphoreType.DMA((3,)),
        ],
        remote=(0, 1, 2),
    )
    mine, away = call(
        functools.partial(pick_other_kernel, per_device, group),
        [(block, bf16)] * 2,
        (own, query_b, pairs_b, assign),
        [pltpu.VMEM(block, f32)],
    )
    other = swap(away, "sec", 3)
    sent, kept = [
        call(
            functools.partial(attend_kernel, flip, per_device, heads),
            [((2, 4, head_block), bf16)],
            (cache_len, mine, other, key_cache, cached_value_rows),
            [pltpu.VMEM((2, 8, head_block), f32)],
            smem=(0,),
            resident=(3, 4),
        )[0]
        for flip in (1, 0)
    ]

    other = swap(sent, ("sec", "tp"), (1, 1))
    (away,) = call(forward_kernel, [((2, 4, head_block), bf16)], (kept, other))
    far = swap(away, ("sec", "tp"), (1, 2))
    (own,) = call(
        gather_kernel, [((16, head_block), bf16)], (kept, other, far), [pltpu.VMEM((16, head_block), f32)]
    )
    across = swap(own, "sec", 3)
    beside = swap(own, "sec", 1)
    corner = swap(across, "sec", 1)
    pair = [((2 * half, features), f32), ((2 * half, features), bf16)]
    mine, away = call(
        functools.partial(project_kernel, per_device, group),
        pair,
        (own, beside, across, corner, assign, resid, out_weight),
        resident=(6,),
    )
    mine, away = call(add_kernel, pair, (mine, swap(away, "tp", 1)))
    other = swap(away, "tp", 2)

    chunk = min(512, width // 2)
    mine, away, lines, stream = call(
        functools.partial(gate_up_first_kernel, chunk),
        [
            ((half, width + 128), f32),
            ((half, width + 128), bf16),
            ((2 * half, features), bf16),
            ((group, features), f32),
        ],
        (mine, other, gain, gate_weight, up_weight),
        [pltpu.VMEM((2, half, features), f32), pltpu.VMEM((4, 16, features), f32)],
        resident=(3, 4),
    )
    away, squares = call(
        pair_sum_kernel, [((half, width + 128), bf16), ((half, 128), f32)], (mine, swap(away, "sec", 1))
    )
    across = swap(away, "sec", 3)
    mine, away = call(
        functools.partial(gate_up_second_kernel, chunk),
        [((half, width), f32), ((half, width), bf16)],
        (lines, gate_weight, up_weight),
        resident=(1, 2),
    )
    beside = swap(away, "sec", 1)
    (hidden,) = call(
        functools.partial(hidden_kernel, features * lax.axis_size("sec")),
        [((half, width // 2), bf16)],
        (mine, beside, across, squares),
    )
    across = swap(hidden, "sec", 3)
    beside = swap(hidden, "sec", 1)
    corner = swap(across, "sec", 1)
    (before,) = call(down_first_kernel, [((2 * half, features), f32)], (hidden, beside, down_weight), resident=(2,))
    mine, *parts = call(
        down_second_kernel,
        [((group, features), f32)] + [((group, features), bf16)] * 3,
        (across, corner, before, down_weight),
        [pltpu.VMEM((4, 16, features), f32)],
        resident=(3,),
    )
    parts = [swap(part, "tp", step + 1) for step, part in enumerate(parts)]
    (out,) = call(finish_kernel, [((group, features), bf16)], (stream, mine, *parts))
    return out


def solution(mesh):
    small = mesh.shape["sec"] == 4 and mesh.shape["tp"] == 4
    return jax.shard_map(
        local_pairs if small else local,
        mesh=mesh,
        in_specs=(
            P(("rep", "tp"), "sec"),
            P(("rep", "tp"), "sec"),
            P(("rep", "tp"), "sec"),
            P(("rep", "sec", "tp"), None, None),
            P(("rep", "sec", "tp"), None, None),
            P(("rep", "sec", "tp")),
            P("rep"),
            P("tp", "sec"),
            P("sec"),
            P("sec", "tp"),
            P("sec", "tp"),
            P("tp", "sec"),
        ),
        out_specs=P(("rep", "tp"), "sec"),
        check_vma=False,
    )
```

```python
import functools
import math

import jax
import jax.numpy as jnp
from jax import lax
from jax.experimental import pallas as pl
from jax.experimental.pallas import tpu as pltpu
from jax.sharding import PartitionSpec as P

D = 5120
QUERY_HEADS = 40
KEY_VALUE_HEADS = 8
HEAD_WIDTH = 128
CACHE_SLOTS = 224


def attend_slots(query_rows, key_value_pairs, stored_keys, stored_values, lengths):
    cache_slots = query_rows.shape[0]
    group_query = QUERY_HEADS // KEY_VALUE_HEADS
    query_head_rows = query_rows.reshape(cache_slots, KEY_VALUE_HEADS, group_query, HEAD_WIDTH)
    paired_heads = key_value_pairs.reshape(cache_slots, KEY_VALUE_HEADS, 2, HEAD_WIDTH)
    fresh_keys = paired_heads[:, :, 0]
    fresh_values = paired_heads[:, :, 1]
    earlier_keys = stored_keys.reshape(cache_slots, CACHE_SLOTS, KEY_VALUE_HEADS, HEAD_WIDTH)
    earlier_values = stored_values.reshape(cache_slots, CACHE_SLOTS, KEY_VALUE_HEADS, HEAD_WIDTH)
    scaling = 1.0 / math.sqrt(HEAD_WIDTH)
    past_scores = (
        jnp.einsum(
            "rkgd,rlkd->rkgl", query_head_rows, earlier_keys, preferred_element_type=jnp.float32
        )
        * scaling
    )
    fresh_scores = (
        jnp.einsum("rkgd,rkd->rkg", query_head_rows, fresh_keys, preferred_element_type=jnp.float32)
        * scaling
    )
    valid = lax.broadcasted_iota(jnp.int32, (cache_slots, CACHE_SLOTS), 1) < lengths[:, None]
    past_scores = jnp.where(valid[:, None, None, :], past_scores, -1e30)
    highest = jnp.maximum(jnp.max(past_scores, axis=-1), fresh_scores)
    past_exp = jnp.exp(past_scores - highest[..., None])
    fresh_exp = jnp.exp(fresh_scores - highest)
    denominator = jnp.sum(past_exp, axis=-1) + fresh_exp
    past_weights = (past_exp / denominator[..., None]).astype(jnp.bfloat16)
    fresh_weights = (fresh_exp / denominator).astype(jnp.bfloat16)
    mixed = jnp.einsum(
        "rkgl,rlkd->rkgd", past_weights, earlier_values, preferred_element_type=jnp.float32
    )
    mixed = (
        mixed
        + fresh_weights.astype(jnp.float32)[..., None]
        * fresh_values.astype(jnp.float32)[:, :, None, :]
    )
    return mixed.reshape(cache_slots, QUERY_HEADS * HEAD_WIDTH).astype(jnp.bfloat16)


def gated_units(values, width):
    return (jax.nn.silu(values[:, :width]) * values[:, width:]).astype(jnp.bfloat16)


def received(blocks, axis):
    count = lax.axis_size(axis)
    result = [blocks[0]]
    for step in range(1, count):
        result.append(lax.ppermute(blocks[step], axis, [(i, i ^ step) for i in range(count)]))
    return result


def local(
    resid,
    query,
    new_kv,
    key_cache,
    cached_value_rows,
    cache_len,
    assign,
    out_weight,
    norm_gain,
    gate_weight,
    up_weight,
    down_weight,
):
    group = query.shape[0]
    per_device = key_cache.shape[0]
    tp_index = lax.axis_index("tp")
    sec_index = lax.axis_index("sec")
    tp_count = lax.axis_size("tp")
    sec_count = lax.axis_size("sec")
    local_slots = lax.dynamic_slice_in_dim(assign, tp_index * group, group)
    resid_f32 = resid.astype(jnp.float32)
    features = resid.shape[1]
    width = gate_weight.shape[1]
    rows = group * tp_count // sec_count

    tokens = jnp.concatenate([query, new_kv], axis=1)
    blocks = []
    for step in range(sec_count):
        wanted = (sec_index ^ step) * per_device + lax.iota(jnp.int32, per_device)
        picker = (local_slots[None, :] == wanted[:, None]).astype(jnp.bfloat16)
        blocks.append(jnp.dot(picker, tokens, preferred_element_type=jnp.float32).astype(jnp.bfloat16))
    pieces = jnp.stack(received(blocks, "sec"))
    pieces = jnp.take(pieces, sec_index ^ lax.iota(jnp.int32, sec_count), axis=0)
    my_query = pieces[:, :, : query.shape[1]].transpose(1, 0, 2).reshape(per_device, -1)
    my_pairs = pieces[:, :, query.shape[1] :].transpose(1, 0, 2).reshape(per_device, -1)
    attended = attend_slots(my_query, my_pairs, key_cache, cached_value_rows, cache_len)

    head_block = out_weight.shape[0]
    blocks = [
        lax.dynamic_slice_in_dim(attended, (tp_index ^ step) * head_block, head_block, 1)
        for step in range(tp_count)
    ]
    mine = jnp.stack(received(blocks, "tp"))
    everyone = jnp.stack(received([mine] * sec_count, "sec"))
    everyone = jnp.take(everyone, sec_index ^ lax.iota(jnp.int32, sec_count), axis=0)
    everyone = everyone.transpose(1, 0, 2, 3).reshape(tp_count, group, head_block)
    parts = jnp.dot(everyone.reshape(tp_count * group, head_block), out_weight, preferred_element_type=jnp.float32)
    parts = parts.astype(jnp.bfloat16).reshape(tp_count, group, features)
    shares = received([parts[step] for step in range(tp_count)], "tp")
    attn_out = sum(share.astype(jnp.float32) for share in shares)
    attn_out = jnp.take(attn_out, local_slots, axis=0)
    stream = resid_f32 + attn_out

    scaled = (stream * norm_gain.astype(jnp.float32)[None, :]).astype(jnp.bfloat16)
    squares = jnp.broadcast_to(jnp.sum(stream * stream, axis=1, keepdims=True), (group, 128))
    piece = jnp.concatenate(received([scaled] * tp_count, "tp"), axis=0)
    square_parts = jnp.concatenate(received([squares] * tp_count, "tp"), axis=0)
    square_parts = square_parts.reshape(sec_count, rows, 128)
    gate_part = jnp.dot(piece, gate_weight, preferred_element_type=jnp.float32)
    up_part = jnp.dot(piece, up_weight, preferred_element_type=jnp.float32)
    projected = jnp.concatenate([gate_part, up_part], axis=1).astype(jnp.bfloat16)
    projected = projected.reshape(sec_count, rows, 2 * width)
    blocks = [lax.dynamic_index_in_dim(projected, sec_index ^ step, 0, False) for step in range(sec_count)]
    share = sum(block.astype(jnp.float32) for block in received(blocks, "sec"))
    blocks = [lax.dynamic_index_in_dim(square_parts, sec_index ^ step, 0, False) for step in range(sec_count)]
    total = sum(received(blocks, "sec"))
    inverse = lax.rsqrt(total[:, :1] / D + 1e-06)
    hidden = gated_units(share * inverse, width)
    hidden = jnp.stack(received([hidden] * sec_count, "sec"))
    hidden = jnp.take(hidden, sec_index ^ lax.iota(jnp.int32, sec_count), axis=0).reshape(-1, width)
    parts = jnp.dot(hidden, down_weight, preferred_element_type=jnp.float32).astype(jnp.bfloat16)
    parts = parts.reshape(tp_count, group, features)
    shares = received([parts[step] for step in range(tp_count)], "tp")
    ff_out = sum(share.astype(jnp.float32) for share in shares)
    return (stream + ff_out).astype(jnp.bfloat16)


MIB = 1024 * 1024


def call(kernel, outs, operands, scratch=(), smem=(), resident=(), remote=(), micros=4, limit=8):
    specs = []
    placed = []
    for place, operand in enumerate(operands):
        space = pltpu.SMEM if place in smem else pltpu.HBM if place in remote else pltpu.VMEM
        specs.append(pl.BlockSpec(memory_space=space))
        if place in resident or place in remote:
            operand = constrained(operand, space)
        placed.append(operand)
    return pl.pallas_call(
        kernel,
        out_shape=[jax.ShapeDtypeStruct(shape, dtype) for shape, dtype in outs],
        in_specs=specs,
        out_specs=[pl.BlockSpec(memory_space=pltpu.VMEM) for _ in outs],
        scratch_shapes=list(scratch),
        compiler_params=pltpu.CompilerParams(vmem_limit_bytes=limit * MIB),
        cost_estimate=pl.CostEstimate(flops=micros * 10**9, bytes_accessed=0, transcendentals=0),
    )(*placed)


def constrained(operand, space):
    return pltpu.with_memory_space_constraint(operand, space)


def swap(value, axis, step):
    if isinstance(axis, tuple):
        count = lax.axis_size(axis[1])
        total = lax.axis_size(axis[0]) * count
        step = step[0] * count + step[1]
    else:
        total = lax.axis_size(axis)
    return lax.ppermute(value, axis, [(i, i ^ step) for i in range(total)])


def slot_picker(per_device, group, assign):
    sec, tp = lax.axis_index("sec"), lax.axis_index("tp")
    slots = jnp.zeros((1, group), jnp.int32)
    for index in range(assign.shape[1] // group):
        slots = jnp.where(tp == index, assign[:, index * group : (index + 1) * group], slots)
    line = lax.broadcasted_iota(jnp.int32, (16, group), 0)
    wanted = jnp.where(line < 8, sec * per_device + line, (sec ^ 3) * per_device + line - 8)
    inside = (line & 7) < per_device
    return jnp.where(inside & (jnp.broadcast_to(slots, (16, group)) == wanted), 1.0, 0.0).astype(jnp.bfloat16)


def split_heads(per_device, picker, query, pairs, rows):
    queries = jnp.dot(picker, query[...], preferred_element_type=jnp.float32)
    others = jnp.dot(picker, pairs[...], preferred_element_type=jnp.float32)
    width = HEAD_WIDTH
    heads = query.shape[1] // width
    rows[...] = jnp.zeros_like(rows)
    for side in range(2):
        for j in range(per_device):
            line = side * 8 + j
            for h in range(heads):
                rows[side, j * 16 + h : j * 16 + h + 1, :] = queries[line : line + 1, h * width : (h + 1) * width]
            for h in range(pairs.shape[1] // width):
                at = j * 16 + heads + h
                rows[side, at : at + 1, :] = others[line : line + 1, h * width : (h + 1) * width]


def pick_own_kernel(per_device, group, query, pairs, assign, out, query_here, pairs_here, assign_here, rows, sems):
    copies = [
        pltpu.make_async_copy(source, target, sems.at[index])
        for index, (source, target) in enumerate(
            ((query, query_here), (pairs, pairs_here), (assign, assign_here))
        )
    ]
    for copy in copies:
        copy.start()
    for copy in copies:
        copy.wait()
    split_heads(per_device, slot_picker(per_device, group, assign_here), query_here, pairs_here, rows)
    out[...] = rows[...].astype(jnp.bfloat16)


def pick_other_kernel(per_device, group, own, query, pairs, assign, keep, send, rows):
    split_heads(per_device, slot_picker(per_device, group, assign), query, pairs, rows)
    here = lax.axis_index("sec") & 1
    keep[here] = own[0]
    keep[1 - here] = rows[0].astype(jnp.bfloat16)
    send[here] = own[1]
    send[1 - here] = rows[1].astype(jnp.bfloat16)


def attend_blocks(per_device, heads, lengths, chip, source, keys, values, target, first):
    share = heads // 2
    slots = keys.shape[1]
    width = HEAD_WIDTH
    scaling = 1.0 / math.sqrt(width)
    line = lax.broadcasted_iota(jnp.int32, (16, width), 0)
    upper = line < share
    place = lax.broadcasted_iota(jnp.int32, (16, slots), 1)
    work = [(i, j) for i in range(2) for j in range(per_device)]
    past, fresh, new_values, columns = [], [], [], []
    for i, j in work:
        wide = source[i, j * 16 : (j + 1) * 16].astype(jnp.float32)
        zero = jnp.zeros_like(wide)
        both = jnp.concatenate([jnp.where(upper, wide, zero), jnp.where(upper, zero, wide)], axis=1)
        column = pl.ds(pl.multiple_of((2 * chip + i) * 2 * width, 2 * width), 2 * width)
        columns.append(column)
        scores = lax.dot_general(
            both.astype(jnp.bfloat16),
            keys[j, :, column],
            (((1,), (1,)), ((), ())),
            preferred_element_type=jnp.float32,
        )
        past.append(jnp.where(place < lengths[j], scores * scaling, -1e30))
        new_key = jnp.where(upper, wide[heads : heads + 1], wide[heads + 2 : heads + 3])
        new_values.append(jnp.where(upper, wide[heads + 1 : heads + 2], wide[heads + 3 : heads + 4]))
        fresh.append(wide * new_key)
    past = jnp.concatenate(past, axis=0)
    fresh = jnp.sum(jnp.concatenate(fresh, axis=0), axis=1, keepdims=True) * scaling
    highest = jnp.maximum(jnp.max(past, axis=1, keepdims=True), fresh)
    past_exp = jnp.exp(past - highest)
    fresh_exp = jnp.exp(fresh - highest)
    inverse = 1.0 / (jnp.sum(past_exp, axis=1, keepdims=True) + fresh_exp)
    weights = (past_exp * inverse).astype(jnp.bfloat16)
    fresh_weight = (fresh_exp * inverse).astype(jnp.bfloat16).astype(jnp.float32)
    for index, (i, j) in enumerate(work):
        lines = slice(index * 16, (index + 1) * 16)
        mixed = jnp.dot(weights[lines], values[j, :, columns[index]], preferred_element_type=jnp.float32)
        mixed = jnp.where(upper, mixed[:, :width], mixed[:, width:]) + fresh_weight[lines] * new_values[index]
        for h in range(heads):
            target[first + i, j : j + 1, h * width : (h + 1) * width] = mixed[h : h + 1]


def attend_near_kernel(per_device, heads, lengths, source, keys, values, out):
    out[...] = jnp.zeros_like(out)
    attend_blocks(per_device, heads, lengths, lax.axis_index("sec") >> 1, source, keys, values, out, 0)


def attend_far_kernel(per_device, heads, lengths, source, near, keys, values, own, first, second, third, total):
    chip = lax.axis_index("sec") >> 1
    tp = lax.axis_index("tp")
    total[...] = jnp.zeros_like(total)
    total[2 * chip] = near[0]
    total[2 * chip + 1] = near[1]
    attend_blocks(per_device, heads, lengths, 1 - chip, source, keys, values, total, 2 * (1 - chip))
    for step, target in enumerate((own, first, second, third)):
        target[...] = total[tp ^ step, 0:4].astype(jnp.bfloat16)


def gather_kernel(own, first, second, third, out, rows):
    for step, part in enumerate((own, first, second, third)):
        rows[4 * step : 4 * step + 4] = part[...].astype(jnp.float32)
    out[...] = rows[...].astype(jnp.bfloat16)


def project_kernel(per_device, group, own, beside, across, corner, assign, resid, weight, *outs):
    sec, tp = lax.axis_index("sec"), lax.axis_index("tp")
    count = assign.shape[1]
    lines = jnp.concatenate([own[...], beside[...], across[...], corner[...]], axis=0)
    line = lax.broadcasted_iota(jnp.int32, (64, count), 0)
    request = lax.broadcasted_iota(jnp.int32, (64, count), 1)
    number = jnp.zeros((64, count), jnp.int32)
    for limit in range(1, 4):
        number = number + jnp.where(request >= limit * group, 1, 0)
    block, place = line >> 4, (line >> 2) & 3
    from_sec = sec ^ block ^ (block >> 1) ^ jnp.where(place > 0, 1, 0)
    slot = from_sec * per_device + (line & 3)
    match = (number == (tp ^ place)) & (jnp.broadcast_to(assign[...], (64, count)) == slot)
    match = jnp.where(match & ((line & 3) < per_device), 1.0, 0.0).astype(jnp.bfloat16)
    ordered = lax.dot_general(match, lines, (((0,), (0,)), ((), ())), preferred_element_type=jnp.float32)
    total = jnp.dot(ordered.astype(jnp.bfloat16), weight[...], preferred_element_type=jnp.float32)
    line = lax.broadcasted_iota(jnp.int32, (count, group), 0)
    match = line == lax.broadcasted_iota(jnp.int32, (count, group), 1) + tp * group
    match = jnp.where(match, 1.0, 0.0).astype(jnp.bfloat16)
    total = total + jnp.dot(match, resid[...], preferred_element_type=jnp.float32)
    half = count // 2
    for index in range(2):
        rows = total[index * half : (index + 1) * half]
        outs[2 * index][...] = rows
        outs[2 * index + 1][...] = rows.astype(jnp.bfloat16)


def add_kernel(mine, other, keep, send):
    total = mine[...] + other[...].astype(jnp.float32)
    keep[...] = total
    send[...] = total.astype(jnp.bfloat16)


def row_half():
    sec = lax.axis_index("sec")
    return (sec ^ (sec >> 1)) & 1


def products(features, gate, up, part, chunk, keep, send):
    half = keep.shape[0]
    width = gate.shape[1] // 2
    for kind, weight in enumerate((gate, up)):
        for start in range(0, width, chunk):
            column = pl.ds(pl.multiple_of(part * width + start, chunk), chunk)
            product = jnp.dot(features, weight[:, column], preferred_element_type=jnp.float32)
            at = kind * width + start
            keep[:, at : at + chunk] = product[:half]
            send[:, at : at + chunk] = product[half:].astype(jnp.bfloat16)


def gate_up_first_kernel(
    chunk, mine_a, other_a, mine_b, other_b, gain, gate, up, keep, send, features, stream, halves, groups
):
    sec, tp = lax.axis_index("sec"), lax.axis_index("tp")
    half = mine_a.shape[0]
    group = stream.shape[0]
    halves[0] = mine_a[...] + other_a[...].astype(jnp.float32)
    halves[1] = mine_b[...] + other_b[...].astype(jnp.float32)
    for index in range(2 * half // group):
        at = index * group % half
        groups[index, 0:group] = halves[index * group // half, at : at + group]
    stream[...] = groups[tp, 0:group]
    first = row_half()
    total = jnp.concatenate([halves[first], halves[1 - first]], axis=0)
    squares = jnp.sum(total * total, axis=1, keepdims=True)
    scaled = (total * gain[...].astype(jnp.float32)).astype(jnp.bfloat16)
    features[...] = scaled
    products(scaled, gate, up, 1 - (sec >> 1), chunk, keep, send)
    width = gate.shape[1]
    keep[:, width:] = jnp.broadcast_to(squares[:half], (half, 128))
    send[:, width:] = two_terms(squares[half:])


def gate_up_second_kernel(chunk, features, gate, up, keep, send):
    products(features[...], gate, up, lax.axis_index("sec") >> 1, chunk, keep, send)


def two_terms(column):
    shape = (column.shape[0], 128)
    column = jnp.broadcast_to(column, shape)
    coarse = column.astype(jnp.bfloat16).astype(jnp.float32)
    lane = lax.broadcasted_iota(jnp.int32, shape, 1)
    return jnp.where(lane < 64, coarse, column - coarse).astype(jnp.bfloat16)


def one_column(terms):
    return terms[:, 0:1].astype(jnp.float32) + terms[:, 64:65].astype(jnp.float32)


def pair_sum_kernel(mine, other, send, squares):
    width = mine.shape[1] - 128
    total = mine[:, :width] + other[:, :width].astype(jnp.float32)
    send[:, :width] = total.astype(jnp.bfloat16)
    both = mine[:, width:] + one_column(other[:, width:])
    squares[...] = both
    send[:, width:] = two_terms(both[:, 0:1])


def hidden_kernel(features, mine, beside, across, squares, hidden):
    width = mine.shape[1] // 2
    total = squares[:, 0:1] + one_column(across[:, 2 * width :])
    inverse = lax.rsqrt(total / features + 1e-06)

    def summed(columns):
        here = mine[:, columns] + beside[:, columns].astype(jnp.float32)
        return (here + across[:, columns].astype(jnp.float32)) * inverse

    gate, up = summed(slice(0, width)), summed(slice(width, 2 * width))
    hidden[...] = (gate / (1.0 + jnp.exp(-gate)) * up).astype(jnp.bfloat16)


def down_lines(mine, other):
    lines = jnp.concatenate([mine[...].astype(jnp.float32), other[...].astype(jnp.float32)], axis=0)
    return lines.astype(jnp.bfloat16)


def down_first_kernel(mine, other, weight, out):
    here = lax.axis_index("sec") >> 1
    depth = mine.shape[1]
    rows = weight[pl.ds(pl.multiple_of(here * depth, depth), depth), :]
    out[...] = jnp.dot(down_lines(mine, other), rows, preferred_element_type=jnp.float32)


def down_second_kernel(mine, other, before, weight, keep, first, second, third, groups):
    tp = lax.axis_index("tp")
    away = 1 - (lax.axis_index("sec") >> 1)
    depth = mine.shape[1]
    rows = weight[pl.ds(pl.multiple_of(away * depth, depth), depth), :]
    product = before[...] + jnp.dot(down_lines(mine, other), rows, preferred_element_type=jnp.float32)
    group = keep.shape[0]
    for index in range(product.shape[0] // group):
        groups[index, 0:group] = product[index * group : (index + 1) * group]
    here = tp ^ (2 * row_half())
    keep[...] = groups[here, 0:group]
    for step, target in enumerate((first, second, third)):
        target[...] = groups[here ^ (step + 1), 0:group].astype(jnp.bfloat16)


def finish_kernel(stream, mine, first, second, third, out):
    total = stream[...] + mine[...]
    for other in (first, second, third):
        total = total + other[...].astype(jnp.float32)
    out[...] = total.astype(jnp.bfloat16)


def local_pairs(
    resid,
    query,
    new_kv,
    key_cache,
    cached_value_rows,
    cache_len,
    assign,
    out_weight,
    norm_gain,
    gate_weight,
    up_weight,
    down_weight,
):
    f32, bf16 = jnp.float32, jnp.bfloat16
    group, features = resid.shape
    per_device = key_cache.shape[0]
    heads = query.shape[1] // HEAD_WIDTH
    head_block = out_weight.shape[0]
    width = gate_weight.shape[1]
    half = 2 * group
    assign = assign.reshape(1, -1)
    gain = norm_gain.reshape(1, -1)

    query_b, pairs_b = swap(query, "sec", 1), swap(new_kv, "sec", 1)
    block = (2, 16 * per_device, HEAD_WIDTH)
    (own,) = call(
        functools.partial(pick_own_kernel, per_device, group),
        [(block, bf16)],
        (query, new_kv, assign),
        [
            pltpu.VMEM(query.shape, bf16),
            pltpu.VMEM(new_kv.shape, bf16),
            pltpu.VMEM(assign.shape, jnp.int32),
            pltpu.VMEM(block, f32),
            pltpu.SemaphoreType.DMA((3,)),
        ],
        remote=(0, 1, 2),
    )
    mine, away = call(
        functools.partial(pick_other_kernel, per_device, group),
        [(block, bf16)] * 2,
        (own, query_b, pairs_b, assign),
        [pltpu.VMEM(block, f32)],
    )
    other = swap(away, "sec", 3)
    caches = (key_cache, cached_value_rows)
    (near,) = call(
        functools.partial(attend_near_kernel, per_device, heads),
        [((2, 4, head_block), f32)],
        (cache_len, mine, *caches),
        smem=(0,),
        resident=(2, 3),
    )
    own, *parts = call(
        functools.partial(attend_far_kernel, per_device, heads),
        [((4, head_block), bf16)] * 4,
        (cache_len, other, near, *caches),
        [pltpu.VMEM((4, 4, head_block), f32)],
        smem=(0,),
        resident=(3, 4),
    )

    parts = [swap(part, ("sec", "tp"), (1, step + 1)) for step, part in enumerate(parts)]
    (own,) = call(gather_kernel, [((16, head_block), bf16)], (own, *parts), [pltpu.VMEM((16, head_block), f32)])
    across = swap(own, "sec", 3)
    beside = swap(own, "sec", 1)
    corner = swap(across, "sec", 1)
    pair = [((half, features), f32), ((half, features), bf16)]
    mine_a, away_a, mine_b, away_b = call(
        functools.partial(project_kernel, per_device, group),
        pair * 2,
        (own, beside, across, corner, assign, resid, out_weight),
        resident=(6,),
    )
    mine_a, away_a = call(add_kernel, pair, (mine_a, swap(away_a, "tp", 1)))
    mine_b, away_b = call(add_kernel, pair, (mine_b, swap(away_b, "tp", 2)))
    other_a, other_b = swap(away_a, "tp", 2), swap(away_b, "tp", 1)

    chunk = min(512, width // 2)
    mine, away, lines, stream = call(
        functools.partial(gate_up_first_kernel, chunk),
        [
            ((half, width + 128), f32),
            ((half, width + 128), bf16),
            ((2 * half, features), bf16),
            ((group, features), f32),
        ],
        (mine_a, other_a, mine_b, other_b, gain, gate_weight, up_weight),
        [pltpu.VMEM((2, half, features), f32), pltpu.VMEM((4, 16, features), f32)],
        resident=(5, 6),
    )
    away, squares = call(
        pair_sum_kernel, [((half, width + 128), bf16), ((half, 128), f32)], (mine, swap(away, "sec", 1))
    )
    across = swap(away, "sec", 3)
    mine, away = call(
        functools.partial(gate_up_second_kernel, chunk),
        [((half, width), f32), ((half, width), bf16)],
        (lines, gate_weight, up_weight),
        resident=(1, 2),
    )
    beside = swap(away, "sec", 1)
    (hidden,) = call(
        functools.partial(hidden_kernel, features * lax.axis_size("sec")),
        [((half, width // 2), bf16)],
        (mine, beside, across, squares),
    )
    across = swap(hidden, "sec", 3)
    beside = swap(hidden, "sec", 1)
    corner = swap(across, "sec", 1)
    (before,) = call(down_first_kernel, [((2 * half, features), f32)], (hidden, beside, down_weight), resident=(2,))
    mine, *parts = call(
        down_second_kernel,
        [((group, features), f32)] + [((group, features), bf16)] * 3,
        (across, corner, before, down_weight),
        [pltpu.VMEM((4, 16, features), f32)],
        resident=(3,),
    )
    parts = [swap(part, "tp", step + 1) for step, part in enumerate(parts)]
    (out,) = call(finish_kernel, [((group, features), bf16)], (stream, mine, *parts))
    return out


def solution(mesh):
    small = mesh.shape["sec"] == 4 and mesh.shape["tp"] == 4
    return jax.shard_map(
        local_pairs if small else local,
        mesh=mesh,
        in_specs=(
            P(("rep", "tp"), "sec"),
            P(("rep", "tp"), "sec"),
            P(("rep", "tp"), "sec"),
            P(("rep", "sec", "tp"), None, None),
            P(("rep", "sec", "tp"), None, None),
            P(("rep", "sec", "tp")),
            P("rep"),
            P("tp", "sec"),
            P("sec"),
            P("sec", "tp"),
            P("sec", "tp"),
            P("tp", "sec"),
        ),
        out_specs=P(("rep", "tp"), "sec"),
        check_vma=False,
    )
```

```python
import functools
import math

import jax
import jax.numpy as jnp
from jax import lax
from jax.experimental import pallas as pl
from jax.experimental.pallas import tpu as pltpu
from jax.sharding import PartitionSpec as P

D = 5120
QUERY_HEADS = 40
KEY_VALUE_HEADS = 8
HEAD_WIDTH = 128
CACHE_SLOTS = 224


def attend_slots(query_rows, key_value_pairs, stored_keys, stored_values, lengths):
    cache_slots = query_rows.shape[0]
    group_query = QUERY_HEADS // KEY_VALUE_HEADS
    query_head_rows = query_rows.reshape(cache_slots, KEY_VALUE_HEADS, group_query, HEAD_WIDTH)
    paired_heads = key_value_pairs.reshape(cache_slots, KEY_VALUE_HEADS, 2, HEAD_WIDTH)
    fresh_keys = paired_heads[:, :, 0]
    fresh_values = paired_heads[:, :, 1]
    earlier_keys = stored_keys.reshape(cache_slots, CACHE_SLOTS, KEY_VALUE_HEADS, HEAD_WIDTH)
    earlier_values = stored_values.reshape(cache_slots, CACHE_SLOTS, KEY_VALUE_HEADS, HEAD_WIDTH)
    scaling = 1.0 / math.sqrt(HEAD_WIDTH)
    past_scores = (
        jnp.einsum(
            "rkgd,rlkd->rkgl", query_head_rows, earlier_keys, preferred_element_type=jnp.float32
        )
        * scaling
    )
    fresh_scores = (
        jnp.einsum("rkgd,rkd->rkg", query_head_rows, fresh_keys, preferred_element_type=jnp.float32)
        * scaling
    )
    valid = lax.broadcasted_iota(jnp.int32, (cache_slots, CACHE_SLOTS), 1) < lengths[:, None]
    past_scores = jnp.where(valid[:, None, None, :], past_scores, -1e30)
    highest = jnp.maximum(jnp.max(past_scores, axis=-1), fresh_scores)
    past_exp = jnp.exp(past_scores - highest[..., None])
    fresh_exp = jnp.exp(fresh_scores - highest)
    denominator = jnp.sum(past_exp, axis=-1) + fresh_exp
    past_weights = (past_exp / denominator[..., None]).astype(jnp.bfloat16)
    fresh_weights = (fresh_exp / denominator).astype(jnp.bfloat16)
    mixed = jnp.einsum(
        "rkgl,rlkd->rkgd", past_weights, earlier_values, preferred_element_type=jnp.float32
    )
    mixed = (
        mixed
        + fresh_weights.astype(jnp.float32)[..., None]
        * fresh_values.astype(jnp.float32)[:, :, None, :]
    )
    return mixed.reshape(cache_slots, QUERY_HEADS * HEAD_WIDTH).astype(jnp.bfloat16)


def gated_units(values, width):
    return (jax.nn.silu(values[:, :width]) * values[:, width:]).astype(jnp.bfloat16)


def received(blocks, axis):
    count = lax.axis_size(axis)
    result = [blocks[0]]
    for step in range(1, count):
        result.append(lax.ppermute(blocks[step], axis, [(i, i ^ step) for i in range(count)]))
    return result


def local(
    resid,
    query,
    new_kv,
    key_cache,
    cached_value_rows,
    cache_len,
    assign,
    out_weight,
    norm_gain,
    gate_weight,
    up_weight,
    down_weight,
):
    group = query.shape[0]
    per_device = key_cache.shape[0]
    tp_index = lax.axis_index("tp")
    sec_index = lax.axis_index("sec")
    tp_count = lax.axis_size("tp")
    sec_count = lax.axis_size("sec")
    local_slots = lax.dynamic_slice_in_dim(assign, tp_index * group, group)
    resid_f32 = resid.astype(jnp.float32)
    features = resid.shape[1]
    width = gate_weight.shape[1]
    rows = group * tp_count // sec_count

    tokens = jnp.concatenate([query, new_kv], axis=1)
    blocks = []
    for step in range(sec_count):
        wanted = (sec_index ^ step) * per_device + lax.iota(jnp.int32, per_device)
        picker = (local_slots[None, :] == wanted[:, None]).astype(jnp.bfloat16)
        blocks.append(jnp.dot(picker, tokens, preferred_element_type=jnp.float32).astype(jnp.bfloat16))
    pieces = jnp.stack(received(blocks, "sec"))
    pieces = jnp.take(pieces, sec_index ^ lax.iota(jnp.int32, sec_count), axis=0)
    my_query = pieces[:, :, : query.shape[1]].transpose(1, 0, 2).reshape(per_device, -1)
    my_pairs = pieces[:, :, query.shape[1] :].transpose(1, 0, 2).reshape(per_device, -1)
    attended = attend_slots(my_query, my_pairs, key_cache, cached_value_rows, cache_len)

    head_block = out_weight.shape[0]
    blocks = [
        lax.dynamic_slice_in_dim(attended, (tp_index ^ step) * head_block, head_block, 1)
        for step in range(tp_count)
    ]
    mine = jnp.stack(received(blocks, "tp"))
    everyone = jnp.stack(received([mine] * sec_count, "sec"))
    everyone = jnp.take(everyone, sec_index ^ lax.iota(jnp.int32, sec_count), axis=0)
    everyone = everyone.transpose(1, 0, 2, 3).reshape(tp_count, group, head_block)
    parts = jnp.dot(everyone.reshape(tp_count * group, head_block), out_weight, preferred_element_type=jnp.float32)
    parts = parts.astype(jnp.bfloat16).reshape(tp_count, group, features)
    shares = received([parts[step] for step in range(tp_count)], "tp")
    attn_out = sum(share.astype(jnp.float32) for share in shares)
    attn_out = jnp.take(attn_out, local_slots, axis=0)
    stream = resid_f32 + attn_out

    scaled = (stream * norm_gain.astype(jnp.float32)[None, :]).astype(jnp.bfloat16)
    squares = jnp.broadcast_to(jnp.sum(stream * stream, axis=1, keepdims=True), (group, 128))
    piece = jnp.concatenate(received([scaled] * tp_count, "tp"), axis=0)
    square_parts = jnp.concatenate(received([squares] * tp_count, "tp"), axis=0)
    square_parts = square_parts.reshape(sec_count, rows, 128)
    gate_part = jnp.dot(piece, gate_weight, preferred_element_type=jnp.float32)
    up_part = jnp.dot(piece, up_weight, preferred_element_type=jnp.float32)
    projected = jnp.concatenate([gate_part, up_part], axis=1).astype(jnp.bfloat16)
    projected = projected.reshape(sec_count, rows, 2 * width)
    blocks = [lax.dynamic_index_in_dim(projected, sec_index ^ step, 0, False) for step in range(sec_count)]
    share = sum(block.astype(jnp.float32) for block in received(blocks, "sec"))
    blocks = [lax.dynamic_index_in_dim(square_parts, sec_index ^ step, 0, False) for step in range(sec_count)]
    total = sum(received(blocks, "sec"))
    inverse = lax.rsqrt(total[:, :1] / D + 1e-06)
    hidden = gated_units(share * inverse, width)
    hidden = jnp.stack(received([hidden] * sec_count, "sec"))
    hidden = jnp.take(hidden, sec_index ^ lax.iota(jnp.int32, sec_count), axis=0).reshape(-1, width)
    parts = jnp.dot(hidden, down_weight, preferred_element_type=jnp.float32).astype(jnp.bfloat16)
    parts = parts.reshape(tp_count, group, features)
    shares = received([parts[step] for step in range(tp_count)], "tp")
    ff_out = sum(share.astype(jnp.float32) for share in shares)
    return (stream + ff_out).astype(jnp.bfloat16)


MIB = 1024 * 1024


def call(kernel, outs, operands, scratch=(), smem=(), resident=(), remote=(), micros=2, limit=8):
    specs = []
    placed = []
    for place, operand in enumerate(operands):
        space = pltpu.SMEM if place in smem else pltpu.HBM if place in remote else pltpu.VMEM
        specs.append(pl.BlockSpec(memory_space=space))
        if place in resident or place in remote:
            operand = constrained(operand, space)
        placed.append(operand)
    return pl.pallas_call(
        kernel,
        out_shape=[jax.ShapeDtypeStruct(shape, dtype) for shape, dtype in outs],
        in_specs=specs,
        out_specs=[pl.BlockSpec(memory_space=pltpu.VMEM) for _ in outs],
        scratch_shapes=list(scratch),
        compiler_params=pltpu.CompilerParams(vmem_limit_bytes=limit * MIB),
        cost_estimate=pl.CostEstimate(flops=micros * 10**9, bytes_accessed=0, transcendentals=0),
    )(*placed)


def constrained(operand, space):
    return pltpu.with_memory_space_constraint(operand, space)


def swap(value, axis, step):
    if isinstance(axis, tuple):
        count = lax.axis_size(axis[1])
        total = lax.axis_size(axis[0]) * count
        step = step[0] * count + step[1]
    else:
        total = lax.axis_size(axis)
    return lax.ppermute(value, axis, [(i, i ^ step) for i in range(total)])


def slot_picker(per_device, group, assign):
    sec, tp = lax.axis_index("sec"), lax.axis_index("tp")
    slots = jnp.zeros((1, group), jnp.int32)
    for index in range(assign.shape[1] // group):
        slots = jnp.where(tp == index, assign[:, index * group : (index + 1) * group], slots)
    line = lax.broadcasted_iota(jnp.int32, (16, group), 0)
    wanted = jnp.where(line < 8, sec * per_device + line, (sec ^ 3) * per_device + line - 8)
    inside = (line & 7) < per_device
    return jnp.where(inside & (jnp.broadcast_to(slots, (16, group)) == wanted), 1.0, 0.0).astype(jnp.bfloat16)


def split_heads(per_device, picker, query, pairs, rows):
    queries = jnp.dot(picker, query[...], preferred_element_type=jnp.float32)
    others = jnp.dot(picker, pairs[...], preferred_element_type=jnp.float32)
    width = HEAD_WIDTH
    heads = query.shape[1] // width
    rows[...] = jnp.zeros_like(rows)
    for side in range(2):
        for j in range(per_device):
            line = side * 8 + j
            for h in range(heads):
                rows[side, j * 16 + h : j * 16 + h + 1, :] = queries[line : line + 1, h * width : (h + 1) * width]
            for h in range(pairs.shape[1] // width):
                at = j * 16 + heads + h
                rows[side, at : at + 1, :] = others[line : line + 1, h * width : (h + 1) * width]


def pick_own_kernel(per_device, group, query, pairs, assign, out, query_here, pairs_here, assign_here, rows, sems):
    copies = [
        pltpu.make_async_copy(source, target, sems.at[index])
        for index, (source, target) in enumerate(
            ((query, query_here), (pairs, pairs_here), (assign, assign_here))
        )
    ]
    for copy in copies:
        copy.start()
    for copy in copies:
        copy.wait()
    split_heads(per_device, slot_picker(per_device, group, assign_here), query_here, pairs_here, rows)
    out[...] = rows[...].astype(jnp.bfloat16)


def pick_other_kernel(per_device, group, own, query, pairs, assign, keep, send, rows):
    split_heads(per_device, slot_picker(per_device, group, assign), query, pairs, rows)
    here = lax.axis_index("sec") & 1
    keep[here] = own[0]
    keep[1 - here] = rows[0].astype(jnp.bfloat16)
    send[here] = own[1]
    send[1 - here] = rows[1].astype(jnp.bfloat16)


def attend_blocks(per_device, heads, lengths, chip, source, keys, values, target, first):
    share = heads // 2
    slots = keys.shape[1]
    width = HEAD_WIDTH
    scaling = 1.0 / math.sqrt(width)
    line = lax.broadcasted_iota(jnp.int32, (16, width), 0)
    upper = line < share
    place = lax.broadcasted_iota(jnp.int32, (16, slots), 1)
    work = [(i, j) for i in range(2) for j in range(per_device)]
    past, fresh, new_values, columns = [], [], [], []
    for i, j in work:
        wide = source[i, j * 16 : (j + 1) * 16].astype(jnp.float32)
        zero = jnp.zeros_like(wide)
        both = jnp.concatenate([jnp.where(upper, wide, zero), jnp.where(upper, zero, wide)], axis=1)
        column = pl.ds(pl.multiple_of((2 * chip + i) * 2 * width, 2 * width), 2 * width)
        columns.append(column)
        scores = lax.dot_general(
            both.astype(jnp.bfloat16),
            keys[j, :, column],
            (((1,), (1,)), ((), ())),
            preferred_element_type=jnp.float32,
        )
        past.append(jnp.where(place < lengths[j], scores * scaling, -1e30))
        new_key = jnp.where(upper, wide[heads : heads + 1], wide[heads + 2 : heads + 3])
        new_values.append(jnp.where(upper, wide[heads + 1 : heads + 2], wide[heads + 3 : heads + 4]))
        fresh.append(wide * new_key)
    past = jnp.concatenate(past, axis=0)
    fresh = jnp.sum(jnp.concatenate(fresh, axis=0), axis=1, keepdims=True) * scaling
    highest = jnp.maximum(jnp.max(past, axis=1, keepdims=True), fresh)
    past_exp = jnp.exp(past - highest)
    fresh_exp = jnp.exp(fresh - highest)
    inverse = 1.0 / (jnp.sum(past_exp, axis=1, keepdims=True) + fresh_exp)
    weights = (past_exp * inverse).astype(jnp.bfloat16)
    fresh_weight = (fresh_exp * inverse).astype(jnp.bfloat16).astype(jnp.float32)
    for index, (i, j) in enumerate(work):
        lines = slice(index * 16, (index + 1) * 16)
        mixed = jnp.dot(weights[lines], values[j, :, columns[index]], preferred_element_type=jnp.float32)
        mixed = jnp.where(upper, mixed[:, :width], mixed[:, width:]) + fresh_weight[lines] * new_values[index]
        for h in range(heads):
            target[first + i, j : j + 1, h * width : (h + 1) * width] = mixed[h : h + 1]


def attend_near_kernel(per_device, heads, lengths, source, keys, values, out):
    out[...] = jnp.zeros_like(out)
    attend_blocks(per_device, heads, lengths, lax.axis_index("sec") >> 1, source, keys, values, out, 0)


def attend_far_kernel(per_device, heads, lengths, source, near, keys, values, own, first, second, third, total):
    chip = lax.axis_index("sec") >> 1
    tp = lax.axis_index("tp")
    total[...] = jnp.zeros_like(total)
    total[2 * chip] = near[0]
    total[2 * chip + 1] = near[1]
    attend_blocks(per_device, heads, lengths, 1 - chip, source, keys, values, total, 2 * (1 - chip))
    for step, target in enumerate((own, first, second, third)):
        target[...] = total[tp ^ step, 0:4].astype(jnp.bfloat16)


def gather_kernel(third, second, first, own, out, rows):
    for step, part in enumerate((own, first, second, third)):
        rows[4 * step : 4 * step + 4] = part[...].astype(jnp.float32)
    out[...] = rows[...].astype(jnp.bfloat16)


def project_kernel(per_device, group, own, beside, across, corner, assign, resid, weight, *outs):
    sec, tp = lax.axis_index("sec"), lax.axis_index("tp")
    count = assign.shape[1]
    lines = jnp.concatenate([own[...], beside[...], across[...], corner[...]], axis=0)
    line = lax.broadcasted_iota(jnp.int32, (64, count), 0)
    request = lax.broadcasted_iota(jnp.int32, (64, count), 1)
    number = jnp.zeros((64, count), jnp.int32)
    for limit in range(1, 4):
        number = number + jnp.where(request >= limit * group, 1, 0)
    block, place = line >> 4, (line >> 2) & 3
    from_sec = sec ^ block ^ (block >> 1) ^ jnp.where(place > 0, 1, 0)
    slot = from_sec * per_device + (line & 3)
    match = (number == (tp ^ place)) & (jnp.broadcast_to(assign[...], (64, count)) == slot)
    match = jnp.where(match & ((line & 3) < per_device), 1.0, 0.0).astype(jnp.bfloat16)
    ordered = lax.dot_general(match, lines, (((0,), (0,)), ((), ())), preferred_element_type=jnp.float32)
    total = jnp.dot(ordered.astype(jnp.bfloat16), weight[...], preferred_element_type=jnp.float32)
    line = lax.broadcasted_iota(jnp.int32, (count, group), 0)
    match = line == lax.broadcasted_iota(jnp.int32, (count, group), 1) + tp * group
    match = jnp.where(match, 1.0, 0.0).astype(jnp.bfloat16)
    total = total + jnp.dot(match, resid[...], preferred_element_type=jnp.float32)
    half = count // 2
    for index in range(2):
        rows = total[index * half : (index + 1) * half]
        outs[2 * index][...] = rows
        outs[2 * index + 1][...] = rows.astype(jnp.bfloat16)


def add_kernel(mine, other, keep, send):
    total = mine[...] + other[...].astype(jnp.float32)
    keep[...] = total
    send[...] = total.astype(jnp.bfloat16)


def row_half():
    sec = lax.axis_index("sec")
    return (sec ^ (sec >> 1)) & 1


def products(features, gate, up, part, chunk, keep, send):
    half = keep.shape[0]
    width = gate.shape[1] // 2
    for kind, weight in enumerate((gate, up)):
        for start in range(0, width, chunk):
            column = pl.ds(pl.multiple_of(part * width + start, chunk), chunk)
            product = jnp.dot(features, weight[:, column], preferred_element_type=jnp.float32)
            at = kind * width + start
            keep[:, at : at + chunk] = product[:half]
            send[:, at : at + chunk] = product[half:].astype(jnp.bfloat16)


def gate_up_first_kernel(
    chunk, mine_a, other_a, mine_b, other_b, gain, gate, up, keep, send, features, stream, halves, groups
):
    sec, tp = lax.axis_index("sec"), lax.axis_index("tp")
    half = mine_a.shape[0]
    group = stream.shape[0]
    halves[0] = mine_a[...] + other_a[...].astype(jnp.float32)
    halves[1] = mine_b[...] + other_b[...].astype(jnp.float32)
    for index in range(2 * half // group):
        at = index * group % half
        groups[index, 0:group] = halves[index * group // half, at : at + group]
    stream[...] = groups[tp, 0:group]
    first = row_half()
    total = jnp.concatenate([halves[first], halves[1 - first]], axis=0)
    squares = jnp.sum(total * total, axis=1, keepdims=True)
    scaled = (total * gain[...].astype(jnp.float32)).astype(jnp.bfloat16)
    features[...] = scaled
    products(scaled, gate, up, 1 - (sec >> 1), chunk, keep, send)
    width = gate.shape[1]
    keep[:, width:] = jnp.broadcast_to(squares[:half], (half, 128))
    send[:, width:] = two_terms(squares[half:])


def gate_up_second_kernel(chunk, features, gate, up, keep, send):
    products(features[...], gate, up, lax.axis_index("sec") >> 1, chunk, keep, send)


def two_terms(column):
    shape = (column.shape[0], 128)
    column = jnp.broadcast_to(column, shape)
    coarse = column.astype(jnp.bfloat16).astype(jnp.float32)
    lane = lax.broadcasted_iota(jnp.int32, shape, 1)
    return jnp.where(lane < 64, coarse, column - coarse).astype(jnp.bfloat16)


def one_column(terms):
    return terms[:, 0:1].astype(jnp.float32) + terms[:, 64:65].astype(jnp.float32)


def pair_sum_kernel(mine, other, send, squares):
    width = mine.shape[1] - 128
    total = mine[:, :width] + other[:, :width].astype(jnp.float32)
    send[:, :width] = total.astype(jnp.bfloat16)
    both = mine[:, width:] + one_column(other[:, width:])
    squares[...] = both
    send[:, width:] = two_terms(both[:, 0:1])


def hidden_kernel(features, mine, beside, across, squares, hidden):
    width = mine.shape[1] // 2
    total = squares[:, 0:1] + one_column(across[:, 2 * width :])
    inverse = lax.rsqrt(total / features + 1e-06)

    def summed(columns):
        here = mine[:, columns] + beside[:, columns].astype(jnp.float32)
        return (here + across[:, columns].astype(jnp.float32)) * inverse

    gate, up = summed(slice(0, width)), summed(slice(width, 2 * width))
    hidden[...] = (gate / (1.0 + jnp.exp(-gate)) * up).astype(jnp.bfloat16)


def down_lines(mine, other):
    lines = jnp.concatenate([mine[...].astype(jnp.float32), other[...].astype(jnp.float32)], axis=0)
    return lines.astype(jnp.bfloat16)


def down_first_kernel(mine, other, weight, out):
    here = lax.axis_index("sec") >> 1
    depth = mine.shape[1]
    rows = weight[pl.ds(pl.multiple_of(here * depth, depth), depth), :]
    out[...] = jnp.dot(down_lines(mine, other), rows, preferred_element_type=jnp.float32)


def down_second_kernel(mine, other, before, weight, keep, first, second, third, groups):
    tp = lax.axis_index("tp")
    away = 1 - (lax.axis_index("sec") >> 1)
    depth = mine.shape[1]
    rows = weight[pl.ds(pl.multiple_of(away * depth, depth), depth), :]
    product = before[...] + jnp.dot(down_lines(mine, other), rows, preferred_element_type=jnp.float32)
    group = keep.shape[0]
    for index in range(product.shape[0] // group):
        groups[index, 0:group] = product[index * group : (index + 1) * group]
    here = tp ^ (2 * row_half())
    keep[...] = groups[here, 0:group]
    for step, target in enumerate((first, second, third)):
        target[...] = groups[here ^ (step + 1), 0:group].astype(jnp.bfloat16)


def finish_kernel(third, second, first, stream, mine, out):
    total = stream[...] + mine[...]
    for other in (first, second, third):
        total = total + other[...].astype(jnp.float32)
    out[...] = total.astype(jnp.bfloat16)


def local_pairs(
    resid,
    query,
    new_kv,
    key_cache,
    cached_value_rows,
    cache_len,
    assign,
    out_weight,
    norm_gain,
    gate_weight,
    up_weight,
    down_weight,
):
    f32, bf16 = jnp.float32, jnp.bfloat16
    group, features = resid.shape
    per_device = key_cache.shape[0]
    heads = query.shape[1] // HEAD_WIDTH
    head_block = out_weight.shape[0]
    width = gate_weight.shape[1]
    half = 2 * group
    assign = assign.reshape(1, -1)
    gain = norm_gain.reshape(1, -1)

    query_b, pairs_b = swap(query, "sec", 1), swap(new_kv, "sec", 1)
    block = (2, 16 * per_device, HEAD_WIDTH)
    (own,) = call(
        functools.partial(pick_own_kernel, per_device, group),
        [(block, bf16)],
        (query, new_kv, assign),
        [
            pltpu.VMEM(query.shape, bf16),
            pltpu.VMEM(new_kv.shape, bf16),
            pltpu.VMEM(assign.shape, jnp.int32),
            pltpu.VMEM(block, f32),
            pltpu.SemaphoreType.DMA((3,)),
        ],
        remote=(0, 1, 2),
    )
    mine, away = call(
        functools.partial(pick_other_kernel, per_device, group),
        [(block, bf16)] * 2,
        (own, query_b, pairs_b, assign),
        [pltpu.VMEM(block, f32)],
    )
    other = swap(away, "sec", 3)
    caches = (key_cache, cached_value_rows)
    (near,) = call(
        functools.partial(attend_near_kernel, per_device, heads),
        [((2, 4, head_block), f32)],
        (cache_len, mine, *caches),
        smem=(0,),
        resident=(2, 3),
    )
    own, *parts = call(
        functools.partial(attend_far_kernel, per_device, heads),
        [((4, head_block), bf16)] * 4,
        (cache_len, other, near, *caches),
        [pltpu.VMEM((4, 4, head_block), f32)],
        smem=(0,),
        resident=(3, 4),
    )

    parts = [swap(parts[step - 1], ("sec", "tp"), (1, step)) for step in (3, 2, 1)]
    (own,) = call(gather_kernel, [((16, head_block), bf16)], (*parts, own), [pltpu.VMEM((16, head_block), f32)])
    across = swap(own, "sec", 3)
    beside = swap(own, "sec", 1)
    corner = swap(across, "sec", 1)
    pair = [((half, features), f32), ((half, features), bf16)]
    mine_a, away_a, mine_b, away_b = call(
        functools.partial(project_kernel, per_device, group),
        pair * 2,
        (own, beside, across, corner, assign, resid, out_weight),
        resident=(6,),
    )
    mine_a, away_a = call(add_kernel, pair, (mine_a, swap(away_a, "tp", 1)))
    mine_b, away_b = call(add_kernel, pair, (mine_b, swap(away_b, "tp", 2)))
    other_a, other_b = swap(away_a, "tp", 2), swap(away_b, "tp", 1)

    chunk = min(512, width // 2)
    mine, away, lines, stream = call(
        functools.partial(gate_up_first_kernel, chunk),
        [
            ((half, width + 128), f32),
            ((half, width + 128), bf16),
            ((2 * half, features), bf16),
            ((group, features), f32),
        ],
        (mine_a, other_a, mine_b, other_b, gain, gate_weight, up_weight),
        [pltpu.VMEM((2, half, features), f32), pltpu.VMEM((4, 16, features), f32)],
        resident=(5, 6),
    )
    away, squares = call(
        pair_sum_kernel, [((half, width + 128), bf16), ((half, 128), f32)], (mine, swap(away, "sec", 1))
    )
    across = swap(away, "sec", 3)
    mine, away = call(
        functools.partial(gate_up_second_kernel, chunk),
        [((half, width), f32), ((half, width), bf16)],
        (lines, gate_weight, up_weight),
        resident=(1, 2),
    )
    beside = swap(away, "sec", 1)
    (hidden,) = call(
        functools.partial(hidden_kernel, features * lax.axis_size("sec")),
        [((half, width // 2), bf16)],
        (mine, beside, across, squares),
    )
    across = swap(hidden, "sec", 3)
    beside = swap(hidden, "sec", 1)
    corner = swap(across, "sec", 1)
    (before,) = call(down_first_kernel, [((2 * half, features), f32)], (hidden, beside, down_weight), resident=(2,))
    mine, *parts = call(
        down_second_kernel,
        [((group, features), f32)] + [((group, features), bf16)] * 3,
        (across, corner, before, down_weight),
        [pltpu.VMEM((4, 16, features), f32)],
        resident=(3,),
    )
    parts = [swap(parts[step - 1], "tp", step) for step in (3, 2, 1)]
    (out,) = call(finish_kernel, [((group, features), bf16)], (*parts, stream, mine))
    return out


def solution(mesh):
    small = mesh.shape["sec"] == 4 and mesh.shape["tp"] == 4
    return jax.shard_map(
        local_pairs if small else local,
        mesh=mesh,
        in_specs=(
            P(("rep", "tp"), "sec"),
            P(("rep", "tp"), "sec"),
            P(("rep", "tp"), "sec"),
            P(("rep", "sec", "tp"), None, None),
            P(("rep", "sec", "tp"), None, None),
            P(("rep", "sec", "tp")),
            P("rep"),
            P("tp", "sec"),
            P("sec"),
            P("sec", "tp"),
            P("sec", "tp"),
            P("tp", "sec"),
        ),
        out_specs=P(("rep", "tp"), "sec"),
        check_vma=False,
    )
```

```python
import functools
import math

import jax
import jax.numpy as jnp
from jax import lax
from jax.experimental import pallas as pl
from jax.experimental.pallas import tpu as pltpu
from jax.sharding import PartitionSpec as P

D = 5120
QUERY_HEADS = 40
KEY_VALUE_HEADS = 8
HEAD_WIDTH = 128
CACHE_SLOTS = 224


def attend_slots(query_rows, key_value_pairs, stored_keys, stored_values, lengths):
    cache_slots = query_rows.shape[0]
    group_query = QUERY_HEADS // KEY_VALUE_HEADS
    query_head_rows = query_rows.reshape(cache_slots, KEY_VALUE_HEADS, group_query, HEAD_WIDTH)
    paired_heads = key_value_pairs.reshape(cache_slots, KEY_VALUE_HEADS, 2, HEAD_WIDTH)
    fresh_keys = paired_heads[:, :, 0]
    fresh_values = paired_heads[:, :, 1]
    earlier_keys = stored_keys.reshape(cache_slots, CACHE_SLOTS, KEY_VALUE_HEADS, HEAD_WIDTH)
    earlier_values = stored_values.reshape(cache_slots, CACHE_SLOTS, KEY_VALUE_HEADS, HEAD_WIDTH)
    scaling = 1.0 / math.sqrt(HEAD_WIDTH)
    past_scores = (
        jnp.einsum(
            "rkgd,rlkd->rkgl", query_head_rows, earlier_keys, preferred_element_type=jnp.float32
        )
        * scaling
    )
    fresh_scores = (
        jnp.einsum("rkgd,rkd->rkg", query_head_rows, fresh_keys, preferred_element_type=jnp.float32)
        * scaling
    )
    valid = lax.broadcasted_iota(jnp.int32, (cache_slots, CACHE_SLOTS), 1) < lengths[:, None]
    past_scores = jnp.where(valid[:, None, None, :], past_scores, -1e30)
    highest = jnp.maximum(jnp.max(past_scores, axis=-1), fresh_scores)
    past_exp = jnp.exp(past_scores - highest[..., None])
    fresh_exp = jnp.exp(fresh_scores - highest)
    denominator = jnp.sum(past_exp, axis=-1) + fresh_exp
    past_weights = (past_exp / denominator[..., None]).astype(jnp.bfloat16)
    fresh_weights = (fresh_exp / denominator).astype(jnp.bfloat16)
    mixed = jnp.einsum(
        "rkgl,rlkd->rkgd", past_weights, earlier_values, preferred_element_type=jnp.float32
    )
    mixed = (
        mixed
        + fresh_weights.astype(jnp.float32)[..., None]
        * fresh_values.astype(jnp.float32)[:, :, None, :]
    )
    return mixed.reshape(cache_slots, QUERY_HEADS * HEAD_WIDTH).astype(jnp.bfloat16)


def gated_units(values, width):
    return (jax.nn.silu(values[:, :width]) * values[:, width:]).astype(jnp.bfloat16)


def received(blocks, axis):
    count = lax.axis_size(axis)
    result = [blocks[0]]
    for step in range(1, count):
        result.append(lax.ppermute(blocks[step], axis, [(i, i ^ step) for i in range(count)]))
    return result


def local(
    resid,
    query,
    new_kv,
    key_cache,
    cached_value_rows,
    cache_len,
    assign,
    out_weight,
    norm_gain,
    gate_weight,
    up_weight,
    down_weight,
):
    group = query.shape[0]
    per_device = key_cache.shape[0]
    tp_index = lax.axis_index("tp")
    sec_index = lax.axis_index("sec")
    tp_count = lax.axis_size("tp")
    sec_count = lax.axis_size("sec")
    local_slots = lax.dynamic_slice_in_dim(assign, tp_index * group, group)
    resid_f32 = resid.astype(jnp.float32)
    features = resid.shape[1]
    width = gate_weight.shape[1]
    rows = group * tp_count // sec_count

    tokens = jnp.concatenate([query, new_kv], axis=1)
    blocks = []
    for step in range(sec_count):
        wanted = (sec_index ^ step) * per_device + lax.iota(jnp.int32, per_device)
        picker = (local_slots[None, :] == wanted[:, None]).astype(jnp.bfloat16)
        blocks.append(jnp.dot(picker, tokens, preferred_element_type=jnp.float32).astype(jnp.bfloat16))
    pieces = jnp.stack(received(blocks, "sec"))
    pieces = jnp.take(pieces, sec_index ^ lax.iota(jnp.int32, sec_count), axis=0)
    my_query = pieces[:, :, : query.shape[1]].transpose(1, 0, 2).reshape(per_device, -1)
    my_pairs = pieces[:, :, query.shape[1] :].transpose(1, 0, 2).reshape(per_device, -1)
    attended = attend_slots(my_query, my_pairs, key_cache, cached_value_rows, cache_len)

    head_block = out_weight.shape[0]
    blocks = [
        lax.dynamic_slice_in_dim(attended, (tp_index ^ step) * head_block, head_block, 1)
        for step in range(tp_count)
    ]
    mine = jnp.stack(received(blocks, "tp"))
    everyone = jnp.stack(received([mine] * sec_count, "sec"))
    everyone = jnp.take(everyone, sec_index ^ lax.iota(jnp.int32, sec_count), axis=0)
    everyone = everyone.transpose(1, 0, 2, 3).reshape(tp_count, group, head_block)
    parts = jnp.dot(everyone.reshape(tp_count * group, head_block), out_weight, preferred_element_type=jnp.float32)
    parts = parts.astype(jnp.bfloat16).reshape(tp_count, group, features)
    shares = received([parts[step] for step in range(tp_count)], "tp")
    attn_out = sum(share.astype(jnp.float32) for share in shares)
    attn_out = jnp.take(attn_out, local_slots, axis=0)
    stream = resid_f32 + attn_out

    scaled = (stream * norm_gain.astype(jnp.float32)[None, :]).astype(jnp.bfloat16)
    squares = jnp.broadcast_to(jnp.sum(stream * stream, axis=1, keepdims=True), (group, 128))
    piece = jnp.concatenate(received([scaled] * tp_count, "tp"), axis=0)
    square_parts = jnp.concatenate(received([squares] * tp_count, "tp"), axis=0)
    square_parts = square_parts.reshape(sec_count, rows, 128)
    gate_part = jnp.dot(piece, gate_weight, preferred_element_type=jnp.float32)
    up_part = jnp.dot(piece, up_weight, preferred_element_type=jnp.float32)
    projected = jnp.concatenate([gate_part, up_part], axis=1).astype(jnp.bfloat16)
    projected = projected.reshape(sec_count, rows, 2 * width)
    blocks = [lax.dynamic_index_in_dim(projected, sec_index ^ step, 0, False) for step in range(sec_count)]
    share = sum(block.astype(jnp.float32) for block in received(blocks, "sec"))
    blocks = [lax.dynamic_index_in_dim(square_parts, sec_index ^ step, 0, False) for step in range(sec_count)]
    total = sum(received(blocks, "sec"))
    inverse = lax.rsqrt(total[:, :1] / D + 1e-06)
    hidden = gated_units(share * inverse, width)
    hidden = jnp.stack(received([hidden] * sec_count, "sec"))
    hidden = jnp.take(hidden, sec_index ^ lax.iota(jnp.int32, sec_count), axis=0).reshape(-1, width)
    parts = jnp.dot(hidden, down_weight, preferred_element_type=jnp.float32).astype(jnp.bfloat16)
    parts = parts.reshape(tp_count, group, features)
    shares = received([parts[step] for step in range(tp_count)], "tp")
    ff_out = sum(share.astype(jnp.float32) for share in shares)
    return (stream + ff_out).astype(jnp.bfloat16)


MIB = 1024 * 1024


def call(kernel, outs, operands, scratch=(), smem=(), resident=(), remote=(), free=(), micros=2, limit=8):
    specs = []
    placed = []
    for place, operand in enumerate(operands):
        space = pltpu.SMEM if place in smem else pltpu.HBM if place in remote else pltpu.VMEM
        space = pl.ANY if place in free else space
        specs.append(pl.BlockSpec(memory_space=space))
        if place in resident or place in remote:
            operand = constrained(operand, space)
        placed.append(operand)
    return pl.pallas_call(
        kernel,
        out_shape=[jax.ShapeDtypeStruct(shape, dtype) for shape, dtype in outs],
        in_specs=specs,
        out_specs=[pl.BlockSpec(memory_space=pltpu.VMEM) for _ in outs],
        scratch_shapes=list(scratch),
        compiler_params=pltpu.CompilerParams(vmem_limit_bytes=limit * MIB),
        cost_estimate=pl.CostEstimate(flops=micros * 10**9, bytes_accessed=0, transcendentals=0),
    )(*placed)


def copy_kernel(value, earlier, out):
    out[...] = value[...]


def after(value, earlier):
    (value,) = call(copy_kernel, [(value.shape, value.dtype)], (value, earlier), free=(1,))
    return value


def constrained(operand, space):
    return pltpu.with_memory_space_constraint(operand, space)


def swap(value, axis, step):
    if isinstance(axis, tuple):
        count = lax.axis_size(axis[1])
        total = lax.axis_size(axis[0]) * count
        step = step[0] * count + step[1]
    else:
        total = lax.axis_size(axis)
    return lax.ppermute(value, axis, [(i, i ^ step) for i in range(total)])


def group_slots(group, assign):
    tp = lax.axis_index("tp")
    slots = jnp.zeros((1, group), jnp.int32)
    for index in range(assign.shape[1] // group):
        slots = jnp.where(tp == index, assign[:, index * group : (index + 1) * group], slots)
    return slots


def slot_picker(per_device, slots):
    sec = lax.axis_index("sec")
    group = slots.shape[1]
    line = lax.broadcasted_iota(jnp.int32, (16, group), 0)
    wanted = jnp.where(line < 8, sec * per_device + line, (sec ^ 3) * per_device + line - 8)
    inside = (line & 7) < per_device
    return jnp.where(inside & (jnp.broadcast_to(slots, (16, group)) == wanted), 1.0, 0.0).astype(jnp.bfloat16)


def split_heads(per_device, picker, query, pairs, rows):
    queries = jnp.dot(picker, query[...], preferred_element_type=jnp.float32)
    others = jnp.dot(picker, pairs[...], preferred_element_type=jnp.float32)
    width = HEAD_WIDTH
    heads = query.shape[1] // width
    rows[...] = jnp.zeros_like(rows)
    for side in range(2):
        for j in range(per_device):
            line = side * 8 + j
            for h in range(heads):
                rows[side, j * 16 + h : j * 16 + h + 1, :] = queries[line : line + 1, h * width : (h + 1) * width]
            for h in range(pairs.shape[1] // width):
                at = j * 16 + heads + h
                rows[side, at : at + 1, :] = others[line : line + 1, h * width : (h + 1) * width]


def pick_own_kernel(
    per_device, group, query, pairs, assign, out, picker, query_here, pairs_here, assign_here, rows, sems
):
    copies = [
        pltpu.make_async_copy(source, target, sems.at[index])
        for index, (source, target) in enumerate(
            ((query, query_here), (pairs, pairs_here), (assign, assign_here))
        )
    ]
    for copy in copies:
        copy.start()
    for copy in copies:
        copy.wait()
    picker[...] = slot_picker(per_device, group_slots(group, assign_here))
    split_heads(per_device, picker[...], query_here, pairs_here, rows)
    out[...] = rows[...].astype(jnp.bfloat16)


def pick_other_kernel(per_device, own, picker, query, pairs, keep, send, rows):
    split_heads(per_device, picker[...], query, pairs, rows)
    here = lax.axis_index("sec") & 1
    keep[here] = own[0]
    keep[1 - here] = rows[0].astype(jnp.bfloat16)
    send[here] = own[1]
    send[1 - here] = rows[1].astype(jnp.bfloat16)


def attend_blocks(per_device, heads, lengths, chip, source, keys, values, target, first):
    share = heads // 2
    slots = keys.shape[1]
    width = HEAD_WIDTH
    scaling = 1.0 / math.sqrt(width)
    line = lax.broadcasted_iota(jnp.int32, (16, width), 0)
    upper = line < share
    place = lax.broadcasted_iota(jnp.int32, (16, slots), 1)
    work = [(i, j) for i in range(2) for j in range(per_device)]
    past, fresh, new_values, columns = [], [], [], []
    for i, j in work:
        wide = source[i, j * 16 : (j + 1) * 16].astype(jnp.float32)
        zero = jnp.zeros_like(wide)
        both = jnp.concatenate([jnp.where(upper, wide, zero), jnp.where(upper, zero, wide)], axis=1)
        column = pl.ds(pl.multiple_of((2 * chip + i) * 2 * width, 2 * width), 2 * width)
        columns.append(column)
        scores = lax.dot_general(
            both.astype(jnp.bfloat16),
            keys[j, :, column],
            (((1,), (1,)), ((), ())),
            preferred_element_type=jnp.float32,
        )
        past.append(jnp.where(place < lengths[j], scores * scaling, -1e30))
        new_key = jnp.where(upper, wide[heads : heads + 1], wide[heads + 2 : heads + 3])
        new_values.append(jnp.where(upper, wide[heads + 1 : heads + 2], wide[heads + 3 : heads + 4]))
        fresh.append(wide * new_key)
    past = jnp.concatenate(past, axis=0)
    fresh = jnp.sum(jnp.concatenate(fresh, axis=0), axis=1, keepdims=True) * scaling
    highest = jnp.maximum(jnp.max(past, axis=1, keepdims=True), fresh)
    past_exp = jnp.exp(past - highest)
    fresh_exp = jnp.exp(fresh - highest)
    inverse = 1.0 / (jnp.sum(past_exp, axis=1, keepdims=True) + fresh_exp)
    weights = (past_exp * inverse).astype(jnp.bfloat16)
    fresh_weight = (fresh_exp * inverse).astype(jnp.bfloat16).astype(jnp.float32)
    for index, (i, j) in enumerate(work):
        lines = slice(index * 16, (index + 1) * 16)
        mixed = jnp.dot(weights[lines], values[j, :, columns[index]], preferred_element_type=jnp.float32)
        mixed = jnp.where(upper, mixed[:, :width], mixed[:, width:]) + fresh_weight[lines] * new_values[index]
        for h in range(heads):
            target[first + i, j : j + 1, h * width : (h + 1) * width] = mixed[h : h + 1]


def attend_near_kernel(per_device, heads, lengths, source, keys, values, out):
    out[...] = jnp.zeros_like(out)
    attend_blocks(per_device, heads, lengths, lax.axis_index("sec") >> 1, source, keys, values, out, 0)


def attend_far_kernel(per_device, heads, lengths, source, near, keys, values, own, first, second, third, total):
    chip = lax.axis_index("sec") >> 1
    tp = lax.axis_index("tp")
    total[...] = jnp.zeros_like(total)
    total[2 * chip] = near[0]
    total[2 * chip + 1] = near[1]
    attend_blocks(per_device, heads, lengths, 1 - chip, source, keys, values, total, 2 * (1 - chip))
    for step, target in enumerate((own, first, second, third)):
        target[...] = total[tp ^ step, 0:4].astype(jnp.bfloat16)


def gather_kernel(third, second, first, own, out, rows):
    for step, part in enumerate((own, first, second, third)):
        rows[4 * step : 4 * step + 4] = part[...].astype(jnp.float32)
    out[...] = rows[...].astype(jnp.bfloat16)


def project_kernel(far, per_device, first, second, assign, resid, weight, keep, send):
    sec, tp = lax.axis_index("sec"), lax.axis_index("tp")
    base = sec ^ (3 * far)
    share = 2 * per_device
    count = keep.shape[0]
    lines = jnp.concatenate([first[...], second[...]], axis=0)
    shape = (count, lines.shape[0])
    line = lax.broadcasted_iota(jnp.int32, shape, 1)
    place, index = (line >> 2) & 3, line & 3
    from_sec = base ^ (line >> 4) ^ jnp.where(place > 0, 1, 0)
    row = (tp ^ place) * share + (from_sec & 1) * per_device + index
    match = (lax.broadcasted_iota(jnp.int32, shape, 0) == row) & (index < per_device)
    match = jnp.where(match, 1.0, 0.0).astype(jnp.bfloat16)
    ordered = jnp.dot(match, lines, preferred_element_type=jnp.float32).astype(jnp.bfloat16)
    total = jnp.dot(ordered, weight[...], preferred_element_type=jnp.float32)
    group = resid.shape[0]
    slots = jnp.broadcast_to(group_slots(group, assign), (count, group)) - share * (base >> 1)
    match = lax.broadcasted_iota(jnp.int32, (count, group), 0) == slots + tp * share
    match = jnp.where(match & (slots >= 0) & (slots < share), 1.0, 0.0).astype(jnp.bfloat16)
    total = total + jnp.dot(match, resid[...], preferred_element_type=jnp.float32)
    keep[...] = total
    send[...] = total.astype(jnp.bfloat16)


def add_kernel(mine, other, keep, send):
    total = mine[...] + other[...].astype(jnp.float32)
    keep[...] = total
    send[...] = total.astype(jnp.bfloat16)


def row_half():
    sec = lax.axis_index("sec")
    return (sec ^ (sec >> 1)) & 1


def products(features, gate, up, part, chunk, keep, send):
    half = keep.shape[0]
    width = gate.shape[1] // 2
    for kind, weight in enumerate((gate, up)):
        for start in range(0, width, chunk):
            column = pl.ds(pl.multiple_of(part * width + start, chunk), chunk)
            product = jnp.dot(features, weight[:, column], preferred_element_type=jnp.float32)
            at = kind * width + start
            keep[:, at : at + chunk] = product[:half]
            send[:, at : at + chunk] = product[half:].astype(jnp.bfloat16)


def to_groups(first, second, groups):
    share = first.shape[0] // groups.shape[0]
    for index in range(groups.shape[0]):
        lines = slice(index * share, (index + 1) * share)
        groups[index, 0:share] = first[lines]
        groups[index, share : 2 * share] = second[lines]


def gate_up_first_kernel(
    chunk, near, near_other, far, far_other, gain, gate, up, keep, send, features, stream, halves, groups
):
    sec, tp = lax.axis_index("sec"), lax.axis_index("tp")
    chip = sec >> 1
    half = near.shape[0]
    halves[chip] = near[...] + near_other[...].astype(jnp.float32)
    halves[1 - chip] = far[...] + far_other[...].astype(jnp.float32)
    to_groups(halves[0], halves[1], groups)
    stream[...] = groups[tp, 0 : stream.shape[0]]
    first = row_half()
    total = jnp.concatenate([halves[first], halves[1 - first]], axis=0)
    squares = jnp.sum(total * total, axis=1, keepdims=True)
    scaled = (total * gain[...].astype(jnp.float32)).astype(jnp.bfloat16)
    features[...] = scaled
    products(scaled, gate, up, 1 - (sec >> 1), chunk, keep, send)
    width = gate.shape[1]
    keep[:, width:] = jnp.broadcast_to(squares[:half], (half, 128))
    send[:, width:] = two_terms(squares[half:])


def gate_up_second_kernel(chunk, features, gate, up, keep, send):
    products(features[...], gate, up, lax.axis_index("sec") >> 1, chunk, keep, send)


def two_terms(column):
    shape = (column.shape[0], 128)
    column = jnp.broadcast_to(column, shape)
    coarse = column.astype(jnp.bfloat16).astype(jnp.float32)
    lane = lax.broadcasted_iota(jnp.int32, shape, 1)
    return jnp.where(lane < 64, coarse, column - coarse).astype(jnp.bfloat16)


def one_column(terms):
    return terms[:, 0:1].astype(jnp.float32) + terms[:, 64:65].astype(jnp.float32)


def pair_sum_kernel(mine, other, send, squares):
    width = mine.shape[1] - 128
    total = mine[:, :width] + other[:, :width].astype(jnp.float32)
    send[:, :width] = total.astype(jnp.bfloat16)
    both = mine[:, width:] + one_column(other[:, width:])
    squares[...] = both
    send[:, width:] = two_terms(both[:, 0:1])


def hidden_kernel(features, mine, beside, across, squares, hidden):
    width = mine.shape[1] // 2
    total = squares[:, 0:1] + one_column(across[:, 2 * width :])
    inverse = lax.rsqrt(total / features + 1e-06)

    def summed(columns):
        here = mine[:, columns] + beside[:, columns].astype(jnp.float32)
        return (here + across[:, columns].astype(jnp.float32)) * inverse

    gate, up = summed(slice(0, width)), summed(slice(width, 2 * width))
    hidden[...] = (gate / (1.0 + jnp.exp(-gate)) * up).astype(jnp.bfloat16)


def down_lines(mine, other):
    lines = jnp.concatenate([mine[...].astype(jnp.float32), other[...].astype(jnp.float32)], axis=0)
    return lines.astype(jnp.bfloat16)


def down_first_kernel(mine, other, weight, out):
    here = lax.axis_index("sec") >> 1
    depth = mine.shape[1]
    rows = weight[pl.ds(pl.multiple_of(here * depth, depth), depth), :]
    out[...] = jnp.dot(down_lines(mine, other), rows, preferred_element_type=jnp.float32)


def down_second_kernel(mine, other, before, weight, keep, first, second, third, groups):
    tp = lax.axis_index("tp")
    away = 1 - (lax.axis_index("sec") >> 1)
    depth = mine.shape[1]
    rows = weight[pl.ds(pl.multiple_of(away * depth, depth), depth), :]
    product = before[...] + jnp.dot(down_lines(mine, other), rows, preferred_element_type=jnp.float32)
    group = keep.shape[0]
    half = product.shape[0] // 2
    swapped = row_half() == 1
    lower, upper = product[:half], product[half:]
    to_groups(jnp.where(swapped, upper, lower), jnp.where(swapped, lower, upper), groups)
    keep[...] = groups[tp, 0:group]
    for step, target in enumerate((first, second, third)):
        target[...] = groups[tp ^ (step + 1), 0:group].astype(jnp.bfloat16)


def finish_kernel(third, second, first, stream, mine, assign, out):
    total = stream[...] + mine[...]
    for other in (first, second, third):
        total = total + other[...].astype(jnp.float32)
    group = out.shape[0]
    slots = jnp.broadcast_to(group_slots(group, assign), (group, group))
    match = jnp.where(lax.broadcasted_iota(jnp.int32, (group, group), 0) == slots, 1.0, 0.0).astype(jnp.bfloat16)
    coarse = total.astype(jnp.bfloat16)
    fine = (total - coarse.astype(jnp.float32)).astype(jnp.bfloat16)
    ordered = [
        lax.dot_general(match, term, (((0,), (0,)), ((), ())), preferred_element_type=jnp.float32)
        for term in (coarse, fine)
    ]
    out[...] = (ordered[0] + ordered[1]).astype(jnp.bfloat16)


def local_pairs(
    resid,
    query,
    new_kv,
    key_cache,
    cached_value_rows,
    cache_len,
    assign,
    out_weight,
    norm_gain,
    gate_weight,
    up_weight,
    down_weight,
):
    f32, bf16 = jnp.float32, jnp.bfloat16
    group, features = resid.shape
    per_device = key_cache.shape[0]
    heads = query.shape[1] // HEAD_WIDTH
    head_block = out_weight.shape[0]
    width = gate_weight.shape[1]
    half = 2 * group
    assign = assign.reshape(1, -1)
    gain = norm_gain.reshape(1, -1)

    query_b, pairs_b = swap(query, "sec", 1), swap(new_kv, "sec", 1)
    block = (2, 16 * per_device, HEAD_WIDTH)
    own, picker = call(
        functools.partial(pick_own_kernel, per_device, group),
        [(block, bf16), ((16, group), bf16)],
        (query, new_kv, assign),
        [
            pltpu.VMEM(query.shape, bf16),
            pltpu.VMEM(new_kv.shape, bf16),
            pltpu.VMEM(assign.shape, jnp.int32),
            pltpu.VMEM(block, f32),
            pltpu.SemaphoreType.DMA((3,)),
        ],
        remote=(0, 1, 2),
    )
    mine, away = call(
        functools.partial(pick_other_kernel, per_device),
        [(block, bf16)] * 2,
        (own, picker, query_b, pairs_b),
        [pltpu.VMEM(block, f32)],
    )
    other = swap(away, "sec", 3)
    caches = (key_cache, cached_value_rows)
    (near,) = call(
        functools.partial(attend_near_kernel, per_device, heads),
        [((2, 4, head_block), f32)],
        (cache_len, mine, *caches),
        smem=(0,),
        resident=(2, 3),
    )
    own, *parts = call(
        functools.partial(attend_far_kernel, per_device, heads),
        [((4, head_block), bf16)] * 4,
        (cache_len, other, near, *caches),
        [pltpu.VMEM((4, 4, head_block), f32)],
        smem=(0,),
        resident=(3, 4),
    )

    parts = [swap(parts[step - 1], ("sec", "tp"), (1, step)) for step in (3, 2, 1)]
    (own,) = call(gather_kernel, [((16, head_block), bf16)], (*parts, own), [pltpu.VMEM((16, head_block), f32)])
    across = swap(own, "sec", 3)
    beside = swap(own, "sec", 1)

    pair = [((half, features), f32), ((half, features), bf16)]

    def project(far, *lines):
        return call(
            functools.partial(project_kernel, far, per_device), pair, (*lines, assign, resid, out_weight), resident=(4,)
        )

    def tp_sum(mine, away):
        mine, away = call(add_kernel, pair, (mine, swap(away, "tp", 1)))
        return mine, swap(away, "tp", 2)

    near = project(0, own, beside)
    corner = swap(after(across, near[1]), "sec", 1)
    far = project(1, across, corner)
    sums = tp_sum(*near) + tp_sum(*far)

    chunk = min(512, width // 2)
    mine, away, lines, stream = call(
        functools.partial(gate_up_first_kernel, chunk),
        [
            ((half, width + 128), f32),
            ((half, width + 128), bf16),
            ((2 * half, features), bf16),
            ((group, features), f32),
        ],
        (*sums, gain, gate_weight, up_weight),
        [pltpu.VMEM((2, half, features), f32), pltpu.VMEM((4, 16, features), f32)],
        resident=(5, 6),
    )
    away, squares = call(
        pair_sum_kernel, [((half, width + 128), bf16), ((half, 128), f32)], (mine, swap(away, "sec", 1))
    )
    across = swap(away, "sec", 3)
    mine, away = call(
        functools.partial(gate_up_second_kernel, chunk),
        [((half, width), f32), ((half, width), bf16)],
        (lines, gate_weight, up_weight),
        resident=(1, 2),
    )
    beside = swap(away, "sec", 1)
    (hidden,) = call(
        functools.partial(hidden_kernel, features * lax.axis_size("sec")),
        [((half, width // 2), bf16)],
        (mine, beside, across, squares),
    )
    across = swap(hidden, "sec", 3)
    beside = swap(hidden, "sec", 1)
    corner = swap(across, "sec", 1)
    (before,) = call(down_first_kernel, [((2 * half, features), f32)], (hidden, beside, down_weight), resident=(2,))
    mine, *parts = call(
        down_second_kernel,
        [((group, features), f32)] + [((group, features), bf16)] * 3,
        (across, corner, before, down_weight),
        [pltpu.VMEM((4, 16, features), f32)],
        resident=(3,),
    )
    parts = [swap(parts[step - 1], "tp", step) for step in (3, 2, 1)]
    (out,) = call(finish_kernel, [((group, features), bf16)], (*parts, stream, mine, assign))
    return out


def solution(mesh):
    small = mesh.shape["sec"] == 4 and mesh.shape["tp"] == 4
    return jax.shard_map(
        local_pairs if small else local,
        mesh=mesh,
        in_specs=(
            P(("rep", "tp"), "sec"),
            P(("rep", "tp"), "sec"),
            P(("rep", "tp"), "sec"),
            P(("rep", "sec", "tp"), None, None),
            P(("rep", "sec", "tp"), None, None),
            P(("rep", "sec", "tp")),
            P("rep"),
            P("tp", "sec"),
            P("sec"),
            P("sec", "tp"),
            P("sec", "tp"),
            P("tp", "sec"),
        ),
        out_specs=P(("rep", "tp"), "sec"),
        check_vma=False,
    )
```

```python
import functools
import math

import jax
import jax.numpy as jnp
from jax import lax
from jax.experimental import pallas as pl
from jax.experimental.pallas import tpu as pltpu
from jax.sharding import PartitionSpec as P

D = 5120
QUERY_HEADS = 40
KEY_VALUE_HEADS = 8
HEAD_WIDTH = 128
CACHE_SLOTS = 224


def attend_slots(query_rows, key_value_pairs, stored_keys, stored_values, lengths):
    cache_slots = query_rows.shape[0]
    group_query = QUERY_HEADS // KEY_VALUE_HEADS
    query_head_rows = query_rows.reshape(cache_slots, KEY_VALUE_HEADS, group_query, HEAD_WIDTH)
    paired_heads = key_value_pairs.reshape(cache_slots, KEY_VALUE_HEADS, 2, HEAD_WIDTH)
    fresh_keys = paired_heads[:, :, 0]
    fresh_values = paired_heads[:, :, 1]
    earlier_keys = stored_keys.reshape(cache_slots, CACHE_SLOTS, KEY_VALUE_HEADS, HEAD_WIDTH)
    earlier_values = stored_values.reshape(cache_slots, CACHE_SLOTS, KEY_VALUE_HEADS, HEAD_WIDTH)
    scaling = 1.0 / math.sqrt(HEAD_WIDTH)
    past_scores = (
        jnp.einsum(
            "rkgd,rlkd->rkgl", query_head_rows, earlier_keys, preferred_element_type=jnp.float32
        )
        * scaling
    )
    fresh_scores = (
        jnp.einsum("rkgd,rkd->rkg", query_head_rows, fresh_keys, preferred_element_type=jnp.float32)
        * scaling
    )
    valid = lax.broadcasted_iota(jnp.int32, (cache_slots, CACHE_SLOTS), 1) < lengths[:, None]
    past_scores = jnp.where(valid[:, None, None, :], past_scores, -1e30)
    highest = jnp.maximum(jnp.max(past_scores, axis=-1), fresh_scores)
    past_exp = jnp.exp(past_scores - highest[..., None])
    fresh_exp = jnp.exp(fresh_scores - highest)
    denominator = jnp.sum(past_exp, axis=-1) + fresh_exp
    past_weights = (past_exp / denominator[..., None]).astype(jnp.bfloat16)
    fresh_weights = (fresh_exp / denominator).astype(jnp.bfloat16)
    mixed = jnp.einsum(
        "rkgl,rlkd->rkgd", past_weights, earlier_values, preferred_element_type=jnp.float32
    )
    mixed = (
        mixed
        + fresh_weights.astype(jnp.float32)[..., None]
        * fresh_values.astype(jnp.float32)[:, :, None, :]
    )
    return mixed.reshape(cache_slots, QUERY_HEADS * HEAD_WIDTH).astype(jnp.bfloat16)


def gated_units(values, width):
    return (jax.nn.silu(values[:, :width]) * values[:, width:]).astype(jnp.bfloat16)


def received(blocks, axis):
    count = lax.axis_size(axis)
    result = [blocks[0]]
    for step in range(1, count):
        result.append(lax.ppermute(blocks[step], axis, [(i, i ^ step) for i in range(count)]))
    return result


def local(
    resid,
    query,
    new_kv,
    key_cache,
    cached_value_rows,
    cache_len,
    assign,
    out_weight,
    norm_gain,
    gate_weight,
    up_weight,
    down_weight,
):
    group = query.shape[0]
    per_device = key_cache.shape[0]
    tp_index = lax.axis_index("tp")
    sec_index = lax.axis_index("sec")
    tp_count = lax.axis_size("tp")
    sec_count = lax.axis_size("sec")
    local_slots = lax.dynamic_slice_in_dim(assign, tp_index * group, group)
    resid_f32 = resid.astype(jnp.float32)
    features = resid.shape[1]
    width = gate_weight.shape[1]
    rows = group * tp_count // sec_count

    tokens = jnp.concatenate([query, new_kv], axis=1)
    blocks = []
    for step in range(sec_count):
        wanted = (sec_index ^ step) * per_device + lax.iota(jnp.int32, per_device)
        picker = (local_slots[None, :] == wanted[:, None]).astype(jnp.bfloat16)
        blocks.append(jnp.dot(picker, tokens, preferred_element_type=jnp.float32).astype(jnp.bfloat16))
    pieces = jnp.stack(received(blocks, "sec"))
    pieces = jnp.take(pieces, sec_index ^ lax.iota(jnp.int32, sec_count), axis=0)
    my_query = pieces[:, :, : query.shape[1]].transpose(1, 0, 2).reshape(per_device, -1)
    my_pairs = pieces[:, :, query.shape[1] :].transpose(1, 0, 2).reshape(per_device, -1)
    attended = attend_slots(my_query, my_pairs, key_cache, cached_value_rows, cache_len)

    head_block = out_weight.shape[0]
    blocks = [
        lax.dynamic_slice_in_dim(attended, (tp_index ^ step) * head_block, head_block, 1)
        for step in range(tp_count)
    ]
    mine = jnp.stack(received(blocks, "tp"))
    everyone = jnp.stack(received([mine] * sec_count, "sec"))
    everyone = jnp.take(everyone, sec_index ^ lax.iota(jnp.int32, sec_count), axis=0)
    everyone = everyone.transpose(1, 0, 2, 3).reshape(tp_count, group, head_block)
    parts = jnp.dot(everyone.reshape(tp_count * group, head_block), out_weight, preferred_element_type=jnp.float32)
    parts = parts.astype(jnp.bfloat16).reshape(tp_count, group, features)
    shares = received([parts[step] for step in range(tp_count)], "tp")
    attn_out = sum(share.astype(jnp.float32) for share in shares)
    attn_out = jnp.take(attn_out, local_slots, axis=0)
    stream = resid_f32 + attn_out

    scaled = (stream * norm_gain.astype(jnp.float32)[None, :]).astype(jnp.bfloat16)
    squares = jnp.broadcast_to(jnp.sum(stream * stream, axis=1, keepdims=True), (group, 128))
    piece = jnp.concatenate(received([scaled] * tp_count, "tp"), axis=0)
    square_parts = jnp.concatenate(received([squares] * tp_count, "tp"), axis=0)
    square_parts = square_parts.reshape(sec_count, rows, 128)
    gate_part = jnp.dot(piece, gate_weight, preferred_element_type=jnp.float32)
    up_part = jnp.dot(piece, up_weight, preferred_element_type=jnp.float32)
    projected = jnp.concatenate([gate_part, up_part], axis=1).astype(jnp.bfloat16)
    projected = projected.reshape(sec_count, rows, 2 * width)
    blocks = [lax.dynamic_index_in_dim(projected, sec_index ^ step, 0, False) for step in range(sec_count)]
    share = sum(block.astype(jnp.float32) for block in received(blocks, "sec"))
    blocks = [lax.dynamic_index_in_dim(square_parts, sec_index ^ step, 0, False) for step in range(sec_count)]
    total = sum(received(blocks, "sec"))
    inverse = lax.rsqrt(total[:, :1] / D + 1e-06)
    hidden = gated_units(share * inverse, width)
    hidden = jnp.stack(received([hidden] * sec_count, "sec"))
    hidden = jnp.take(hidden, sec_index ^ lax.iota(jnp.int32, sec_count), axis=0).reshape(-1, width)
    parts = jnp.dot(hidden, down_weight, preferred_element_type=jnp.float32).astype(jnp.bfloat16)
    parts = parts.reshape(tp_count, group, features)
    shares = received([parts[step] for step in range(tp_count)], "tp")
    ff_out = sum(share.astype(jnp.float32) for share in shares)
    return (stream + ff_out).astype(jnp.bfloat16)


MIB = 1024 * 1024


def call(kernel, outs, operands, scratch=(), smem=(), resident=(), remote=(), free=(), micros=2, limit=8):
    specs = []
    placed = []
    for place, operand in enumerate(operands):
        space = pltpu.SMEM if place in smem else pltpu.HBM if place in remote else pltpu.VMEM
        space = pl.ANY if place in free else space
        specs.append(pl.BlockSpec(memory_space=space))
        if place in resident or place in remote:
            operand = constrained(operand, space)
        placed.append(operand)
    return pl.pallas_call(
        kernel,
        out_shape=[jax.ShapeDtypeStruct(shape, dtype) for shape, dtype in outs],
        in_specs=specs,
        out_specs=[pl.BlockSpec(memory_space=pltpu.VMEM) for _ in outs],
        scratch_shapes=list(scratch),
        compiler_params=pltpu.CompilerParams(vmem_limit_bytes=limit * MIB),
        cost_estimate=pl.CostEstimate(flops=micros * 10**9, bytes_accessed=0, transcendentals=0),
    )(*placed)


def copy_kernel(value, earlier, out):
    out[...] = value[...]


def after(value, earlier):
    (value,) = call(copy_kernel, [(value.shape, value.dtype)], (value, earlier), free=(1,), micros=0)
    return value


def constrained(operand, space):
    return pltpu.with_memory_space_constraint(operand, space)


def swap(value, axis, step):
    if isinstance(axis, tuple):
        count = lax.axis_size(axis[1])
        total = lax.axis_size(axis[0]) * count
        step = step[0] * count + step[1]
    else:
        total = lax.axis_size(axis)
    return lax.ppermute(value, axis, [(i, i ^ step) for i in range(total)])


def group_slots(group, assign):
    tp = lax.axis_index("tp")
    slots = jnp.zeros((1, group), jnp.int32)
    for index in range(assign.shape[1] // group):
        slots = jnp.where(tp == index, assign[:, index * group : (index + 1) * group], slots)
    return slots


def slot_picker(per_device, slots):
    sec = lax.axis_index("sec")
    group = slots.shape[1]
    line = lax.broadcasted_iota(jnp.int32, (16, group), 0)
    wanted = jnp.where(line < 8, sec * per_device + line, (sec ^ 3) * per_device + line - 8)
    inside = (line & 7) < per_device
    return jnp.where(inside & (jnp.broadcast_to(slots, (16, group)) == wanted), 1.0, 0.0).astype(jnp.bfloat16)


def split_heads(per_device, picker, query, pairs, rows):
    queries = jnp.dot(picker, query[...], preferred_element_type=jnp.float32)
    others = jnp.dot(picker, pairs[...], preferred_element_type=jnp.float32)
    width = HEAD_WIDTH
    heads = query.shape[1] // width
    rows[...] = jnp.zeros_like(rows)
    for side in range(2):
        for j in range(per_device):
            line = side * 8 + j
            for h in range(heads):
                rows[side, j * 16 + h : j * 16 + h + 1, :] = queries[line : line + 1, h * width : (h + 1) * width]
            for h in range(pairs.shape[1] // width):
                at = j * 16 + heads + h
                rows[side, at : at + 1, :] = others[line : line + 1, h * width : (h + 1) * width]


def pick_own_kernel(
    per_device, group, query, pairs, assign, out, picker, query_here, pairs_here, assign_here, rows, sems
):
    copies = [
        pltpu.make_async_copy(source, target, sems.at[index])
        for index, (source, target) in enumerate(
            ((query, query_here), (pairs, pairs_here), (assign, assign_here))
        )
    ]
    for copy in copies:
        copy.start()
    for copy in copies:
        copy.wait()
    picker[...] = slot_picker(per_device, group_slots(group, assign_here))
    split_heads(per_device, picker[...], query_here, pairs_here, rows)
    out[...] = rows[...].astype(jnp.bfloat16)


def pick_other_kernel(per_device, own, picker, query, pairs, keep, send, rows):
    split_heads(per_device, picker[...], query, pairs, rows)
    here = lax.axis_index("sec") & 1
    keep[here] = own[0]
    keep[1 - here] = rows[0].astype(jnp.bfloat16)
    send[here] = own[1]
    send[1 - here] = rows[1].astype(jnp.bfloat16)


def attend_blocks(per_device, heads, lengths, chip, source, keys, values, target, first):
    share = heads // 2
    slots = keys.shape[1]
    width = HEAD_WIDTH
    scaling = 1.0 / math.sqrt(width)
    line = lax.broadcasted_iota(jnp.int32, (16, width), 0)
    upper = line < share
    place = lax.broadcasted_iota(jnp.int32, (16, slots), 1)
    work = [(i, j) for i in range(2) for j in range(per_device)]
    past, fresh, new_values, columns = [], [], [], []
    for i, j in work:
        wide = source[i, j * 16 : (j + 1) * 16].astype(jnp.float32)
        zero = jnp.zeros_like(wide)
        both = jnp.concatenate([jnp.where(upper, wide, zero), jnp.where(upper, zero, wide)], axis=1)
        column = pl.ds(pl.multiple_of((2 * chip + i) * 2 * width, 2 * width), 2 * width)
        columns.append(column)
        scores = lax.dot_general(
            both.astype(jnp.bfloat16),
            keys[j, :, column],
            (((1,), (1,)), ((), ())),
            preferred_element_type=jnp.float32,
        )
        past.append(jnp.where(place < lengths[j], scores * scaling, -1e30))
        new_key = jnp.where(upper, wide[heads : heads + 1], wide[heads + 2 : heads + 3])
        new_values.append(jnp.where(upper, wide[heads + 1 : heads + 2], wide[heads + 3 : heads + 4]))
        fresh.append(wide * new_key)
    past = jnp.concatenate(past, axis=0)
    fresh = jnp.sum(jnp.concatenate(fresh, axis=0), axis=1, keepdims=True) * scaling
    highest = jnp.maximum(jnp.max(past, axis=1, keepdims=True), fresh)
    past_exp = jnp.exp(past - highest)
    fresh_exp = jnp.exp(fresh - highest)
    inverse = 1.0 / (jnp.sum(past_exp, axis=1, keepdims=True) + fresh_exp)
    weights = (past_exp * inverse).astype(jnp.bfloat16)
    fresh_weight = (fresh_exp * inverse).astype(jnp.bfloat16).astype(jnp.float32)
    for index, (i, j) in enumerate(work):
        lines = slice(index * 16, (index + 1) * 16)
        mixed = jnp.dot(weights[lines], values[j, :, columns[index]], preferred_element_type=jnp.float32)
        mixed = jnp.where(upper, mixed[:, :width], mixed[:, width:]) + fresh_weight[lines] * new_values[index]
        for h in range(heads):
            target[first + i, j : j + 1, h * width : (h + 1) * width] = mixed[h : h + 1]


def attend_near_kernel(per_device, heads, lengths, source, keys, values, assign, out, order):
    shape = order.shape
    slots = jnp.broadcast_to(group_slots(shape[0], assign), shape)
    line = lax.broadcasted_iota(jnp.int32, shape, 0)
    match = jnp.where(line == slots, 1.0, 0.0).astype(jnp.bfloat16)
    same = jnp.where(line == lax.broadcasted_iota(jnp.int32, shape, 1), 1.0, 0.0).astype(jnp.bfloat16)
    order[...] = lax.dot_general(
        match, same, (((0,), (0,)), ((), ())), preferred_element_type=jnp.float32
    ).astype(jnp.bfloat16)
    out[...] = jnp.zeros_like(out)
    attend_blocks(per_device, heads, lengths, lax.axis_index("sec") >> 1, source, keys, values, out, 0)


def attend_far_kernel(per_device, heads, lengths, source, near, keys, values, own, first, second, third, total):
    chip = lax.axis_index("sec") >> 1
    tp = lax.axis_index("tp")
    total[...] = jnp.zeros_like(total)
    total[2 * chip] = near[0]
    total[2 * chip + 1] = near[1]
    attend_blocks(per_device, heads, lengths, 1 - chip, source, keys, values, total, 2 * (1 - chip))
    for step, target in enumerate((own, first, second, third)):
        target[...] = total[tp ^ step, 0:4].astype(jnp.bfloat16)


def gather_kernel(third, second, first, own, out, rows):
    for step, part in enumerate((own, first, second, third)):
        rows[4 * step : 4 * step + 4] = part[...].astype(jnp.float32)
    out[...] = rows[...].astype(jnp.bfloat16)


def project_kernel(far, per_device, first, second, assign, resid, weight, keep, send):
    sec, tp = lax.axis_index("sec"), lax.axis_index("tp")
    base = sec ^ (3 * far)
    share = 2 * per_device
    count = keep.shape[0]
    lines = jnp.concatenate([first[...], second[...]], axis=0)
    shape = (count, lines.shape[0])
    line = lax.broadcasted_iota(jnp.int32, shape, 1)
    place, index = (line >> 2) & 3, line & 3
    from_sec = base ^ (line >> 4) ^ jnp.where(place > 0, 1, 0)
    row = (tp ^ place) * share + (from_sec & 1) * per_device + index
    match = (lax.broadcasted_iota(jnp.int32, shape, 0) == row) & (index < per_device)
    match = jnp.where(match, 1.0, 0.0).astype(jnp.bfloat16)
    ordered = jnp.dot(match, lines, preferred_element_type=jnp.float32).astype(jnp.bfloat16)
    total = jnp.dot(ordered, weight[...], preferred_element_type=jnp.float32)
    group = resid.shape[0]
    slots = jnp.broadcast_to(group_slots(group, assign), (count, group)) - share * (base >> 1)
    match = lax.broadcasted_iota(jnp.int32, (count, group), 0) == slots + tp * share
    match = jnp.where(match & (slots >= 0) & (slots < share), 1.0, 0.0).astype(jnp.bfloat16)
    total = total + jnp.dot(match, resid[...], preferred_element_type=jnp.float32)
    keep[...] = total
    send[...] = total.astype(jnp.bfloat16)


def add_kernel(mine, other, keep, send):
    total = mine[...] + other[...].astype(jnp.float32)
    keep[...] = total
    send[...] = total.astype(jnp.bfloat16)


def row_half():
    sec = lax.axis_index("sec")
    return (sec ^ (sec >> 1)) & 1


def products(features, gate, up, unit, units, chunk, keep, send):
    half = keep.shape[0]
    for kind, weight in enumerate((gate, up)):
        for start in range(0, units, chunk):
            column = pl.ds(pl.multiple_of(unit + start, chunk), chunk)
            product = jnp.dot(features, weight[:, column], preferred_element_type=jnp.float32)
            at = kind * units + start
            keep[:, at : at + chunk] = product[:half]
            send[:, at : at + chunk] = product[half:].astype(jnp.bfloat16)


def to_groups(first, second, groups):
    share = first.shape[0] // groups.shape[0]
    for index in range(groups.shape[0]):
        lines = slice(index * share, (index + 1) * share)
        groups[index, 0:share] = first[lines]
        groups[index, share : 2 * share] = second[lines]


def gate_up_first_kernel(
    chunk, near, near_other, far, far_other, gain, gate, up, keep, send, features, stream, halves, groups
):
    sec, tp = lax.axis_index("sec"), lax.axis_index("tp")
    chip = sec >> 1
    half = near.shape[0]
    halves[chip] = near[...] + near_other[...].astype(jnp.float32)
    halves[1 - chip] = far[...] + far_other[...].astype(jnp.float32)
    to_groups(halves[0], halves[1], groups)
    stream[...] = groups[tp, 0 : stream.shape[0]]
    first = row_half()
    total = jnp.concatenate([halves[first], halves[1 - first]], axis=0)
    squares = jnp.sum(total * total, axis=1, keepdims=True)
    scaled = (total * gain[...].astype(jnp.float32)).astype(jnp.bfloat16)
    features[...] = scaled
    units = (keep.shape[1] - 128) // 2
    products(scaled, gate, up, (1 - (sec >> 1)) * (gate.shape[1] // 2), units, chunk, keep, send)
    keep[:, 2 * units :] = jnp.broadcast_to(squares[:half], (half, 128))
    send[:, 2 * units :] = two_terms(squares[half:])


def gate_up_more_kernel(chunk, part, features, gate, up, earlier, keep, send):
    units = keep.shape[1] // 2
    width = gate.shape[1] // 2
    away = 1 - (lax.axis_index("sec") >> 1)
    first = away * width + width - units if part else (1 - away) * width
    products(features[...], gate, up, first, units, chunk, keep, send)


def two_terms(column):
    shape = (column.shape[0], 128)
    column = jnp.broadcast_to(column, shape)
    coarse = column.astype(jnp.bfloat16).astype(jnp.float32)
    lane = lax.broadcasted_iota(jnp.int32, shape, 1)
    return jnp.where(lane < 64, coarse, column - coarse).astype(jnp.bfloat16)


def one_column(terms):
    return terms[:, 0:1].astype(jnp.float32) + terms[:, 64:65].astype(jnp.float32)


def pair_sum_kernel(mine, other, send, squares):
    width = mine.shape[1] - 128
    total = mine[:, :width] + other[:, :width].astype(jnp.float32)
    send[:, :width] = total.astype(jnp.bfloat16)
    both = mine[:, width:] + one_column(other[:, width:])
    squares[...] = both
    send[:, width:] = two_terms(both[:, 0:1])


def add_send_kernel(mine, other, earlier, send):
    send[...] = (mine[...] + other[...].astype(jnp.float32)).astype(jnp.bfloat16)


def scale_kernel(features, squares, first, second, scale):
    width = first.shape[1] - 128
    total = squares[:, 0:1] + one_column(first[:, width:])
    scale[...] = jnp.broadcast_to(lax.rsqrt(total / features + 1e-06), scale.shape)


def hidden_kernel(mine, beside, first, second, scale, hidden):
    width = mine.shape[1] // 2
    units = width // 2
    factor = scale[:, 0:1]
    for index, across in enumerate((first, second)):

        def summed(kind):
            here = slice(kind * width + index * units, kind * width + (index + 1) * units)
            there = across[:, kind * units : (kind + 1) * units].astype(jnp.float32)
            return (mine[:, here] + beside[:, here].astype(jnp.float32) + there) * factor

        gate, up = summed(0), summed(1)
        hidden[:, index * units : (index + 1) * units] = (gate / (1.0 + jnp.exp(-gate)) * up).astype(jnp.bfloat16)


def down_product(away, mine, other, weight):
    here = (lax.axis_index("sec") >> 1) ^ away
    lines = jnp.concatenate([mine[...].astype(jnp.float32), other[...].astype(jnp.float32)], axis=0)
    depth = lines.shape[1]
    rows = weight[pl.ds(pl.multiple_of(here * depth, depth), depth), :]
    return jnp.dot(lines.astype(jnp.bfloat16), rows, preferred_element_type=jnp.float32)


def down_first_kernel(mine, other, weight, out):
    out[...] = down_product(0, mine, other, weight)


def down_second_kernel(mine, other, before, weight, keep, first, second, third, groups):
    tp = lax.axis_index("tp")
    product = before[...] + down_product(1, mine, other, weight)
    group = keep.shape[0]
    half = product.shape[0] // 2
    swapped = row_half() == 1
    lower, upper = product[:half], product[half:]
    to_groups(jnp.where(swapped, upper, lower), jnp.where(swapped, lower, upper), groups)
    keep[...] = groups[tp, 0:group]
    for step, target in enumerate((first, second, third)):
        target[...] = groups[tp ^ (step + 1), 0:group].astype(jnp.bfloat16)


def finish_kernel(third, second, first, stream, mine, order, out):
    total = stream[...] + mine[...]
    for other in (first, second, third):
        total = total + other[...].astype(jnp.float32)
    coarse = total.astype(jnp.bfloat16)
    fine = (total - coarse.astype(jnp.float32)).astype(jnp.bfloat16)
    ordered = [jnp.dot(order[...], term, preferred_element_type=jnp.float32) for term in (coarse, fine)]
    out[...] = (ordered[0] + ordered[1]).astype(jnp.bfloat16)


def local_pairs(
    resid,
    query,
    new_kv,
    key_cache,
    cached_value_rows,
    cache_len,
    assign,
    out_weight,
    norm_gain,
    gate_weight,
    up_weight,
    down_weight,
):
    f32, bf16 = jnp.float32, jnp.bfloat16
    group, features = resid.shape
    per_device = key_cache.shape[0]
    heads = query.shape[1] // HEAD_WIDTH
    head_block = out_weight.shape[0]
    width = gate_weight.shape[1]
    half = 2 * group
    assign = assign.reshape(1, -1)
    gain = norm_gain.reshape(1, -1)

    query_b, pairs_b = swap(query, "sec", 1), swap(new_kv, "sec", 1)
    block = (2, 16 * per_device, HEAD_WIDTH)
    own, picker = call(
        functools.partial(pick_own_kernel, per_device, group),
        [(block, bf16), ((16, group), bf16)],
        (query, new_kv, assign),
        [
            pltpu.VMEM(query.shape, bf16),
            pltpu.VMEM(new_kv.shape, bf16),
            pltpu.VMEM(assign.shape, jnp.int32),
            pltpu.VMEM(block, f32),
            pltpu.SemaphoreType.DMA((3,)),
        ],
        remote=(0, 1, 2),
    )
    mine, away = call(
        functools.partial(pick_other_kernel, per_device),
        [(block, bf16)] * 2,
        (own, picker, query_b, pairs_b),
        [pltpu.VMEM(block, f32)],
    )
    other = swap(away, "sec", 3)
    caches = (key_cache, cached_value_rows)
    near, order = call(
        functools.partial(attend_near_kernel, per_device, heads),
        [((2, 4, head_block), f32), ((group, group), bf16)],
        (cache_len, mine, *caches, assign),
        smem=(0,),
        resident=(2, 3),
    )
    own, *parts = call(
        functools.partial(attend_far_kernel, per_device, heads),
        [((4, head_block), bf16)] * 4,
        (cache_len, other, near, *caches),
        [pltpu.VMEM((4, 4, head_block), f32)],
        smem=(0,),
        resident=(3, 4),
    )

    parts = [swap(parts[step - 1], ("sec", "tp"), (1, step)) for step in (3, 2, 1)]
    (own,) = call(gather_kernel, [((16, head_block), bf16)], (*parts, own), [pltpu.VMEM((16, head_block), f32)])
    across = swap(own, "sec", 3)
    beside = swap(own, "sec", 1)

    pair = [((half, features), f32), ((half, features), bf16)]

    def project(far, *lines):
        return call(
            functools.partial(project_kernel, far, per_device), pair, (*lines, assign, resid, out_weight), resident=(4,), micros=0 if far else 2
        )

    def tp_sum(mine, away):
        mine, away = call(add_kernel, pair, (mine, swap(away, "tp", 1)))
        return mine, swap(away, "tp", 2)

    near = project(0, own, beside)
    corner = swap(after(across, near[1]), "sec", 1)
    far = project(1, across, corner)
    sums = tp_sum(*near) + tp_sum(*far)

    units = width // 4
    chunk = min(512, units)
    weights = (gate_weight, up_weight)
    mine, away, lines, stream = call(
        functools.partial(gate_up_first_kernel, chunk),
        [
            ((half, 2 * units + 128), f32),
            ((half, 2 * units + 128), bf16),
            ((2 * half, features), bf16),
            ((group, features), f32),
        ],
        (*sums, gain, *weights),
        [pltpu.VMEM((2, half, features), f32), pltpu.VMEM((4, 16, features), f32)],
        resident=(5, 6),
        micros=2,
    )
    beside = swap(away, "sec", 1)
    mine_b, away_b = call(
        functools.partial(gate_up_more_kernel, chunk, 1),
        [((half, 2 * units), f32), ((half, 2 * units), bf16)],
        (lines, *weights, away),
        resident=(1, 2),
        free=(3,),
        micros=0,
    )
    beside_b = swap(away_b, "sec", 1)
    away, squares = call(
        pair_sum_kernel, [((half, 2 * units + 128), bf16), ((half, 128), f32)], (mine, beside), micros=0
    )
    across = [swap(away, "sec", 3)]
    (away,) = call(add_send_kernel, [((half, 2 * units), bf16)], (mine_b, beside_b, away), free=(2,), micros=0)
    across += [swap(away, "sec", 3)]
    mine, away = call(
        functools.partial(gate_up_more_kernel, chunk, 0),
        [((half, 4 * units), f32), ((half, 4 * units), bf16)],
        (lines, *weights, away),
        resident=(1, 2),
        free=(3,),
        micros=0,
    )
    beside = swap(away, "sec", 1)
    (scale,) = call(
        functools.partial(scale_kernel, features * lax.axis_size("sec")),
        [((half, 128), f32)],
        (squares, *across),
        free=(2,),
        micros=4,
    )
    (hidden,) = call(hidden_kernel, [((half, 2 * units), bf16)], (mine, beside, *across, scale), micros=0)
    across = swap(hidden, "sec", 3)
    beside = swap(hidden, "sec", 1)
    corner = swap(across, "sec", 1)
    (before,) = call(
        down_first_kernel, [((2 * half, features), f32)], (hidden, beside, down_weight), resident=(2,), micros=2
    )
    mine, *parts = call(
        down_second_kernel,
        [((group, features), f32)] + [((group, features), bf16)] * 3,
        (across, corner, before, down_weight),
        [pltpu.VMEM((4, 16, features), f32)],
        resident=(3,),
    )
    parts = [swap(parts[step - 1], "tp", step) for step in (3, 2, 1)]
    (out,) = call(finish_kernel, [((group, features), bf16)], (*parts, stream, mine, order))
    return out


def solution(mesh):
    small = mesh.shape["sec"] == 4 and mesh.shape["tp"] == 4
    return jax.shard_map(
        local_pairs if small else local,
        mesh=mesh,
        in_specs=(
            P(("rep", "tp"), "sec"),
            P(("rep", "tp"), "sec"),
            P(("rep", "tp"), "sec"),
            P(("rep", "sec", "tp"), None, None),
            P(("rep", "sec", "tp"), None, None),
            P(("rep", "sec", "tp")),
            P("rep"),
            P("tp", "sec"),
            P("sec"),
            P("sec", "tp"),
            P("sec", "tp"),
            P("tp", "sec"),
        ),
        out_specs=P(("rep", "tp"), "sec"),
        check_vma=False,
    )
```

```python
import functools
import math

import jax
import jax.numpy as jnp
from jax import lax
from jax.experimental import pallas as pl
from jax.experimental.pallas import tpu as pltpu
from jax.sharding import PartitionSpec as P

D = 5120
QUERY_HEADS = 40
KEY_VALUE_HEADS = 8
HEAD_WIDTH = 128
CACHE_SLOTS = 224


def attend_slots(query_rows, key_value_pairs, stored_keys, stored_values, lengths):
    cache_slots = query_rows.shape[0]
    group_query = QUERY_HEADS // KEY_VALUE_HEADS
    query_head_rows = query_rows.reshape(cache_slots, KEY_VALUE_HEADS, group_query, HEAD_WIDTH)
    paired_heads = key_value_pairs.reshape(cache_slots, KEY_VALUE_HEADS, 2, HEAD_WIDTH)
    fresh_keys = paired_heads[:, :, 0]
    fresh_values = paired_heads[:, :, 1]
    earlier_keys = stored_keys.reshape(cache_slots, CACHE_SLOTS, KEY_VALUE_HEADS, HEAD_WIDTH)
    earlier_values = stored_values.reshape(cache_slots, CACHE_SLOTS, KEY_VALUE_HEADS, HEAD_WIDTH)
    scaling = 1.0 / math.sqrt(HEAD_WIDTH)
    past_scores = (
        jnp.einsum(
            "rkgd,rlkd->rkgl", query_head_rows, earlier_keys, preferred_element_type=jnp.float32
        )
        * scaling
    )
    fresh_scores = (
        jnp.einsum("rkgd,rkd->rkg", query_head_rows, fresh_keys, preferred_element_type=jnp.float32)
        * scaling
    )
    valid = lax.broadcasted_iota(jnp.int32, (cache_slots, CACHE_SLOTS), 1) < lengths[:, None]
    past_scores = jnp.where(valid[:, None, None, :], past_scores, -1e30)
    highest = jnp.maximum(jnp.max(past_scores, axis=-1), fresh_scores)
    past_exp = jnp.exp(past_scores - highest[..., None])
    fresh_exp = jnp.exp(fresh_scores - highest)
    denominator = jnp.sum(past_exp, axis=-1) + fresh_exp
    past_weights = (past_exp / denominator[..., None]).astype(jnp.bfloat16)
    fresh_weights = (fresh_exp / denominator).astype(jnp.bfloat16)
    mixed = jnp.einsum(
        "rkgl,rlkd->rkgd", past_weights, earlier_values, preferred_element_type=jnp.float32
    )
    mixed = (
        mixed
        + fresh_weights.astype(jnp.float32)[..., None]
        * fresh_values.astype(jnp.float32)[:, :, None, :]
    )
    return mixed.reshape(cache_slots, QUERY_HEADS * HEAD_WIDTH).astype(jnp.bfloat16)


def gated_units(values, width):
    return (jax.nn.silu(values[:, :width]) * values[:, width:]).astype(jnp.bfloat16)


def received(blocks, axis):
    count = lax.axis_size(axis)
    result = [blocks[0]]
    for step in range(1, count):
        result.append(lax.ppermute(blocks[step], axis, [(i, i ^ step) for i in range(count)]))
    return result


def local(
    resid,
    query,
    new_kv,
    key_cache,
    cached_value_rows,
    cache_len,
    assign,
    out_weight,
    norm_gain,
    gate_weight,
    up_weight,
    down_weight,
):
    group = query.shape[0]
    per_device = key_cache.shape[0]
    tp_index = lax.axis_index("tp")
    sec_index = lax.axis_index("sec")
    tp_count = lax.axis_size("tp")
    sec_count = lax.axis_size("sec")
    local_slots = lax.dynamic_slice_in_dim(assign, tp_index * group, group)
    resid_f32 = resid.astype(jnp.float32)
    features = resid.shape[1]
    width = gate_weight.shape[1]
    rows = group * tp_count // sec_count

    tokens = jnp.concatenate([query, new_kv], axis=1)
    blocks = []
    for step in range(sec_count):
        wanted = (sec_index ^ step) * per_device + lax.iota(jnp.int32, per_device)
        picker = (local_slots[None, :] == wanted[:, None]).astype(jnp.bfloat16)
        blocks.append(jnp.dot(picker, tokens, preferred_element_type=jnp.float32).astype(jnp.bfloat16))
    pieces = jnp.stack(received(blocks, "sec"))
    pieces = jnp.take(pieces, sec_index ^ lax.iota(jnp.int32, sec_count), axis=0)
    my_query = pieces[:, :, : query.shape[1]].transpose(1, 0, 2).reshape(per_device, -1)
    my_pairs = pieces[:, :, query.shape[1] :].transpose(1, 0, 2).reshape(per_device, -1)
    attended = attend_slots(my_query, my_pairs, key_cache, cached_value_rows, cache_len)

    head_block = out_weight.shape[0]
    blocks = [
        lax.dynamic_slice_in_dim(attended, (tp_index ^ step) * head_block, head_block, 1)
        for step in range(tp_count)
    ]
    mine = jnp.stack(received(blocks, "tp"))
    everyone = jnp.stack(received([mine] * sec_count, "sec"))
    everyone = jnp.take(everyone, sec_index ^ lax.iota(jnp.int32, sec_count), axis=0)
    everyone = everyone.transpose(1, 0, 2, 3).reshape(tp_count, group, head_block)
    parts = jnp.dot(everyone.reshape(tp_count * group, head_block), out_weight, preferred_element_type=jnp.float32)
    parts = parts.astype(jnp.bfloat16).reshape(tp_count, group, features)
    shares = received([parts[step] for step in range(tp_count)], "tp")
    attn_out = sum(share.astype(jnp.float32) for share in shares)
    attn_out = jnp.take(attn_out, local_slots, axis=0)
    stream = resid_f32 + attn_out

    scaled = (stream * norm_gain.astype(jnp.float32)[None, :]).astype(jnp.bfloat16)
    squares = jnp.broadcast_to(jnp.sum(stream * stream, axis=1, keepdims=True), (group, 128))
    piece = jnp.concatenate(received([scaled] * tp_count, "tp"), axis=0)
    square_parts = jnp.concatenate(received([squares] * tp_count, "tp"), axis=0)
    square_parts = square_parts.reshape(sec_count, rows, 128)
    gate_part = jnp.dot(piece, gate_weight, preferred_element_type=jnp.float32)
    up_part = jnp.dot(piece, up_weight, preferred_element_type=jnp.float32)
    projected = jnp.concatenate([gate_part, up_part], axis=1).astype(jnp.bfloat16)
    projected = projected.reshape(sec_count, rows, 2 * width)
    blocks = [lax.dynamic_index_in_dim(projected, sec_index ^ step, 0, False) for step in range(sec_count)]
    share = sum(block.astype(jnp.float32) for block in received(blocks, "sec"))
    blocks = [lax.dynamic_index_in_dim(square_parts, sec_index ^ step, 0, False) for step in range(sec_count)]
    total = sum(received(blocks, "sec"))
    inverse = lax.rsqrt(total[:, :1] / D + 1e-06)
    hidden = gated_units(share * inverse, width)
    hidden = jnp.stack(received([hidden] * sec_count, "sec"))
    hidden = jnp.take(hidden, sec_index ^ lax.iota(jnp.int32, sec_count), axis=0).reshape(-1, width)
    parts = jnp.dot(hidden, down_weight, preferred_element_type=jnp.float32).astype(jnp.bfloat16)
    parts = parts.reshape(tp_count, group, features)
    shares = received([parts[step] for step in range(tp_count)], "tp")
    ff_out = sum(share.astype(jnp.float32) for share in shares)
    return (stream + ff_out).astype(jnp.bfloat16)


MIB = 1024 * 1024


def call(kernel, outs, operands, scratch=(), smem=(), resident=(), remote=(), free=(), nanos=2000, limit=8):
    specs = []
    placed = []
    for place, operand in enumerate(operands):
        space = pltpu.SMEM if place in smem else pltpu.HBM if place in remote else pltpu.VMEM
        space = pl.ANY if place in free else space
        specs.append(pl.BlockSpec(memory_space=space))
        if place in resident or place in remote:
            operand = constrained(operand, space)
        placed.append(operand)
    return pl.pallas_call(
        kernel,
        out_shape=[jax.ShapeDtypeStruct(shape, dtype) for shape, dtype in outs],
        in_specs=specs,
        out_specs=[pl.BlockSpec(memory_space=pltpu.VMEM) for _ in outs],
        scratch_shapes=list(scratch),
        compiler_params=pltpu.CompilerParams(vmem_limit_bytes=limit * MIB),
        cost_estimate=pl.CostEstimate(flops=nanos * 10**6, bytes_accessed=0, transcendentals=0),
    )(*placed)


def copy_kernel(value, earlier, out):
    out[...] = value[...]


def after(value, earlier):
    (value,) = call(copy_kernel, [(value.shape, value.dtype)], (value, earlier), free=(1,), nanos=0)
    return value


def constrained(operand, space):
    return pltpu.with_memory_space_constraint(operand, space)


def swap(value, axis, step):
    if isinstance(axis, tuple):
        count = lax.axis_size(axis[1])
        total = lax.axis_size(axis[0]) * count
        step = step[0] * count + step[1]
    else:
        total = lax.axis_size(axis)
    return lax.ppermute(value, axis, [(i, i ^ step) for i in range(total)])


def group_slots(group, assign):
    tp = lax.axis_index("tp")
    slots = jnp.zeros((1, group), jnp.int32)
    for index in range(assign.shape[1] // group):
        slots = jnp.where(tp == index, assign[:, index * group : (index + 1) * group], slots)
    return slots


def slot_picker(per_device, slots):
    sec = lax.axis_index("sec")
    group = slots.shape[1]
    line = lax.broadcasted_iota(jnp.int32, (16, group), 0)
    wanted = jnp.where(line < 8, sec * per_device + line, (sec ^ 3) * per_device + line - 8)
    inside = (line & 7) < per_device
    return jnp.where(inside & (jnp.broadcast_to(slots, (16, group)) == wanted), 1.0, 0.0).astype(jnp.bfloat16)


def split_heads(per_device, picker, query, pairs, rows):
    queries = jnp.dot(picker, query[...], preferred_element_type=jnp.float32)
    others = jnp.dot(picker, pairs[...], preferred_element_type=jnp.float32)
    width = HEAD_WIDTH
    heads = query.shape[1] // width
    rows[...] = jnp.zeros_like(rows)
    for side in range(2):
        for j in range(per_device):
            line = side * 8 + j
            for h in range(heads):
                rows[side, j * 16 + h : j * 16 + h + 1, :] = queries[line : line + 1, h * width : (h + 1) * width]
            for h in range(pairs.shape[1] // width):
                at = j * 16 + heads + h
                rows[side, at : at + 1, :] = others[line : line + 1, h * width : (h + 1) * width]


def pick_own_kernel(
    per_device, group, query, pairs, assign, out, picker, query_here, pairs_here, assign_here, rows, sems
):
    copies = [
        pltpu.make_async_copy(source, target, sems.at[index])
        for index, (source, target) in enumerate(
            ((query, query_here), (pairs, pairs_here), (assign, assign_here))
        )
    ]
    for copy in copies:
        copy.start()
    copies[2].wait()
    picker[...] = slot_picker(per_device, group_slots(group, assign_here))
    copies[0].wait()
    copies[1].wait()
    split_heads(per_device, picker[...], query_here, pairs_here, rows)
    out[...] = rows[...].astype(jnp.bfloat16)


def pick_other_kernel(per_device, own, picker, query, pairs, keep, send, rows):
    split_heads(per_device, picker[...], query, pairs, rows)
    here = lax.axis_index("sec") & 1
    keep[here] = own[0]
    keep[1 - here] = rows[0].astype(jnp.bfloat16)
    send[here] = own[1]
    send[1 - here] = rows[1].astype(jnp.bfloat16)


def attend_blocks(per_device, heads, lengths, chip, source, keys, values, target, first):
    share = heads // 2
    slots = keys.shape[1]
    width = HEAD_WIDTH
    scaling = 1.0 / math.sqrt(width)
    line = lax.broadcasted_iota(jnp.int32, (16, width), 0)
    upper = line < share
    place = lax.broadcasted_iota(jnp.int32, (16, slots), 1)
    work = [(i, j) for i in range(2) for j in range(per_device)]
    past, fresh, new_values, columns = [], [], [], []
    for i, j in work:
        wide = source[i, j * 16 : (j + 1) * 16].astype(jnp.float32)
        zero = jnp.zeros_like(wide)
        both = jnp.concatenate([jnp.where(upper, wide, zero), jnp.where(upper, zero, wide)], axis=1)
        column = pl.ds(pl.multiple_of((2 * chip + i) * 2 * width, 2 * width), 2 * width)
        columns.append(column)
        scores = lax.dot_general(
            both.astype(jnp.bfloat16),
            keys[j, :, column],
            (((1,), (1,)), ((), ())),
            preferred_element_type=jnp.float32,
        )
        past.append(jnp.where(place < lengths[j], scores * scaling, -1e30))
        new_key = jnp.where(upper, wide[heads : heads + 1], wide[heads + 2 : heads + 3])
        new_values.append(jnp.where(upper, wide[heads + 1 : heads + 2], wide[heads + 3 : heads + 4]))
        fresh.append(wide * new_key)
    past = jnp.concatenate(past, axis=0)
    fresh = jnp.sum(jnp.concatenate(fresh, axis=0), axis=1, keepdims=True) * scaling
    highest = jnp.maximum(jnp.max(past, axis=1, keepdims=True), fresh)
    past_exp = jnp.exp(past - highest)
    fresh_exp = jnp.exp(fresh - highest)
    inverse = 1.0 / (jnp.sum(past_exp, axis=1, keepdims=True) + fresh_exp)
    weights = (past_exp * inverse).astype(jnp.bfloat16)
    fresh_weight = (fresh_exp * inverse).astype(jnp.bfloat16).astype(jnp.float32)
    for index, (i, j) in enumerate(work):
        lines = slice(index * 16, (index + 1) * 16)
        mixed = jnp.dot(weights[lines], values[j, :, columns[index]], preferred_element_type=jnp.float32)
        mixed = jnp.where(upper, mixed[:, :width], mixed[:, width:]) + fresh_weight[lines] * new_values[index]
        for h in range(heads):
            target[first + i, j : j + 1, h * width : (h + 1) * width] = mixed[h : h + 1]


def attend_near_kernel(per_device, heads, lengths, source, keys, values, assign, out, order):
    shape = order.shape
    slots = jnp.broadcast_to(group_slots(shape[0], assign), shape)
    line = lax.broadcasted_iota(jnp.int32, shape, 0)
    match = jnp.where(line == slots, 1.0, 0.0).astype(jnp.bfloat16)
    same = jnp.where(line == lax.broadcasted_iota(jnp.int32, shape, 1), 1.0, 0.0).astype(jnp.bfloat16)
    order[...] = lax.dot_general(
        match, same, (((0,), (0,)), ((), ())), preferred_element_type=jnp.float32
    ).astype(jnp.bfloat16)
    out[...] = jnp.zeros_like(out)
    attend_blocks(per_device, heads, lengths, lax.axis_index("sec") >> 1, source, keys, values, out, 0)


def attend_far_kernel(per_device, heads, lengths, source, near, keys, values, own, first, second, third, total):
    chip = lax.axis_index("sec") >> 1
    tp = lax.axis_index("tp")
    total[...] = jnp.zeros_like(total)
    total[2 * chip] = near[0]
    total[2 * chip + 1] = near[1]
    attend_blocks(per_device, heads, lengths, 1 - chip, source, keys, values, total, 2 * (1 - chip))
    for step, target in enumerate((own, first, second, third)):
        target[...] = total[tp ^ step, 0:4].astype(jnp.bfloat16)


def gather_kernel(third, second, first, own, out, rows):
    for step, part in enumerate((own, first, second, third)):
        rows[4 * step : 4 * step + 4] = part[...].astype(jnp.float32)
    out[...] = rows[...].astype(jnp.bfloat16)


def project_kernel(far, per_device, first, second, assign, resid, weight, keep, send):
    sec, tp = lax.axis_index("sec"), lax.axis_index("tp")
    base = sec ^ (3 * far)
    share = 2 * per_device
    count = keep.shape[0]
    lines = jnp.concatenate([first[...], second[...]], axis=0)
    shape = (count, lines.shape[0])
    line = lax.broadcasted_iota(jnp.int32, shape, 1)
    place, index = (line >> 2) & 3, line & 3
    from_sec = base ^ (line >> 4) ^ jnp.where(place > 0, 1, 0)
    row = (tp ^ place) * share + (from_sec & 1) * per_device + index
    match = (lax.broadcasted_iota(jnp.int32, shape, 0) == row) & (index < per_device)
    match = jnp.where(match, 1.0, 0.0).astype(jnp.bfloat16)
    ordered = jnp.dot(match, lines, preferred_element_type=jnp.float32).astype(jnp.bfloat16)
    total = jnp.dot(ordered, weight[...], preferred_element_type=jnp.float32)
    group = resid.shape[0]
    slots = jnp.broadcast_to(group_slots(group, assign), (count, group)) - share * (base >> 1)
    match = lax.broadcasted_iota(jnp.int32, (count, group), 0) == slots + tp * share
    match = jnp.where(match & (slots >= 0) & (slots < share), 1.0, 0.0).astype(jnp.bfloat16)
    total = total + jnp.dot(match, resid[...], preferred_element_type=jnp.float32)
    keep[...] = total
    send[...] = total.astype(jnp.bfloat16)


def add_kernel(mine, other, keep, send):
    total = mine[...] + other[...].astype(jnp.float32)
    keep[...] = total
    send[...] = total.astype(jnp.bfloat16)


def row_half():
    sec = lax.axis_index("sec")
    return (sec ^ (sec >> 1)) & 1


def products(features, gate, up, unit, units, chunk, keep, send):
    half = keep.shape[0]
    for kind, weight in enumerate((gate, up)):
        for start in range(0, units, chunk):
            column = slice(unit + start, unit + start + chunk)
            product = jnp.dot(features, weight[:, column], preferred_element_type=jnp.float32)
            at = kind * units + start
            keep[:, at : at + chunk] = product[:half]
            send[:, at : at + chunk] = product[half:].astype(jnp.bfloat16)


def to_groups(first, second, groups):
    share = first.shape[0] // groups.shape[0]
    for index in range(groups.shape[0]):
        lines = slice(index * share, (index + 1) * share)
        groups[index, 0:share] = first[lines]
        groups[index, share : 2 * share] = second[lines]


def gate_up_first_kernel(
    chunk, near, near_other, far, far_other, gain, gate, up, keep, send, features, stream, halves, groups
):
    sec, tp = lax.axis_index("sec"), lax.axis_index("tp")
    chip = sec >> 1
    half = near.shape[0]
    halves[chip] = near[...] + near_other[...].astype(jnp.float32)
    halves[1 - chip] = far[...] + far_other[...].astype(jnp.float32)
    to_groups(halves[0], halves[1], groups)
    stream[...] = groups[tp, 0 : stream.shape[0]]
    first = row_half()
    total = jnp.concatenate([halves[first], halves[1 - first]], axis=0)
    squares = jnp.sum(total * total, axis=1, keepdims=True)
    scaled = (total * gain[...].astype(jnp.float32)).astype(jnp.bfloat16)
    features[...] = scaled
    units = (keep.shape[1] - 128) // 2
    products(scaled, gate, up, 0, units, chunk, keep, send)
    keep[:, 2 * units :] = jnp.broadcast_to(squares[:half], (half, 128))
    send[:, 2 * units :] = two_terms(squares[half:])


def gate_up_more_kernel(chunk, unit, features, gate, up, earlier, keep, send):
    products(features[...], gate, up, unit, keep.shape[1] // 2, chunk, keep, send)


def two_terms(column):
    shape = (column.shape[0], 128)
    column = jnp.broadcast_to(column, shape)
    coarse = column.astype(jnp.bfloat16).astype(jnp.float32)
    lane = lax.broadcasted_iota(jnp.int32, shape, 1)
    return jnp.where(lane < 64, coarse, column - coarse).astype(jnp.bfloat16)


def one_column(terms):
    return terms[:, 0:1].astype(jnp.float32) + terms[:, 64:65].astype(jnp.float32)


def pair_sum_first_kernel(mine, other, keep, send):
    width = mine.shape[1] - 128
    total = mine[:, :width] + other[:, :width].astype(jnp.float32)
    both = mine[:, width:] + one_column(other[:, width:])
    keep[:, :width] = total
    keep[:, width:] = both
    send[:, :width] = total.astype(jnp.bfloat16)
    send[:, width:] = two_terms(both[:, 0:1])


def pair_sum_kernel(mine, other, earlier, keep, send):
    total = mine[...] + other[...].astype(jnp.float32)
    width = total.shape[1]
    keep[...] = total
    send[:, :width] = total.astype(jnp.bfloat16)
    if send.shape[1] > width:
        send[:, width:] = jnp.zeros_like(send[:, width:])


def gated(mine, other, factor, hidden):
    width = hidden.shape[1]
    gate = (mine[:, :width] + other[:, :width].astype(jnp.float32)) * factor
    up = (mine[:, width : 2 * width] + other[:, width : 2 * width].astype(jnp.float32)) * factor
    hidden[...] = (gate / (1.0 + jnp.exp(-gate)) * up).astype(jnp.bfloat16)


def hidden_first_kernel(features, mine, other, earlier, hidden, scale):
    width = mine.shape[1] - 128
    total = mine[:, width : width + 1] + one_column(other[:, width:])
    factor = lax.rsqrt(total / features + 1e-06)
    scale[...] = jnp.broadcast_to(factor, scale.shape)
    gated(mine, other, factor, hidden)


def hidden_kernel(mine, other, scale, hidden):
    gated(mine, other, scale[:, 0:1], hidden)


def down_product(unit, mine, other, weight):
    lines = jnp.concatenate([mine[...].astype(jnp.float32), other[...].astype(jnp.float32)], axis=0)
    rows = weight[unit : unit + lines.shape[1], :]
    return jnp.dot(lines.astype(jnp.bfloat16), rows, preferred_element_type=jnp.float32)


def down_first_kernel(mine, other, weight, out):
    out[...] = down_product(0, mine, other, weight)


def down_more_kernel(unit, before, mine, other, weight, out):
    out[...] = before[...] + down_product(unit, mine, other, weight)


def down_last_kernel(unit, before, mine, other, weight, keep, first, second, third, groups):
    tp = lax.axis_index("tp")
    product = before[...] + down_product(unit, mine, other, weight)
    group = keep.shape[0]
    half = product.shape[0] // 2
    swapped = row_half() == 1
    lower, upper = product[:half], product[half:]
    to_groups(jnp.where(swapped, upper, lower), jnp.where(swapped, lower, upper), groups)
    keep[...] = groups[tp, 0:group]
    for step, target in enumerate((first, second, third)):
        target[...] = groups[tp ^ (step + 1), 0:group].astype(jnp.bfloat16)


def finish_kernel(third, second, first, stream, mine, order, out):
    total = stream[...] + mine[...]
    for other in (first, second, third):
        total = total + other[...].astype(jnp.float32)
    coarse = total.astype(jnp.bfloat16)
    fine = (total - coarse.astype(jnp.float32)).astype(jnp.bfloat16)
    ordered = [jnp.dot(order[...], term, preferred_element_type=jnp.float32) for term in (coarse, fine)]
    out[...] = (ordered[0] + ordered[1]).astype(jnp.bfloat16)


def local_pairs(
    resid,
    query,
    new_kv,
    key_cache,
    cached_value_rows,
    cache_len,
    assign,
    out_weight,
    norm_gain,
    gate_weight,
    up_weight,
    down_weight,
):
    f32, bf16 = jnp.float32, jnp.bfloat16
    group, features = resid.shape
    per_device = key_cache.shape[0]
    heads = query.shape[1] // HEAD_WIDTH
    head_block = out_weight.shape[0]
    width = gate_weight.shape[1]
    half = 2 * group
    assign = assign.reshape(1, -1)
    gain = norm_gain.reshape(1, -1)

    query_b, pairs_b = swap(query, "sec", 1), swap(new_kv, "sec", 1)
    block = (2, 16 * per_device, HEAD_WIDTH)
    own, picker = call(
        functools.partial(pick_own_kernel, per_device, group),
        [(block, bf16), ((16, group), bf16)],
        (query, new_kv, assign),
        [
            pltpu.VMEM(query.shape, bf16),
            pltpu.VMEM(new_kv.shape, bf16),
            pltpu.VMEM(assign.shape, jnp.int32),
            pltpu.VMEM(block, f32),
            pltpu.SemaphoreType.DMA((3,)),
        ],
        remote=(0, 1, 2),
    )
    mine, away = call(
        functools.partial(pick_other_kernel, per_device),
        [(block, bf16)] * 2,
        (own, picker, query_b, pairs_b),
        [pltpu.VMEM(block, f32)],
    )
    other = swap(away, "sec", 3)
    caches = (key_cache, cached_value_rows)
    near, order = call(
        functools.partial(attend_near_kernel, per_device, heads),
        [((2, 4, head_block), f32), ((group, group), bf16)],
        (cache_len, mine, *caches, assign),
        smem=(0,),
        resident=(2, 3),
    )
    own, *parts = call(
        functools.partial(attend_far_kernel, per_device, heads),
        [((4, head_block), bf16)] * 4,
        (cache_len, other, near, *caches),
        [pltpu.VMEM((4, 4, head_block), f32)],
        smem=(0,),
        resident=(3, 4),
    )

    parts = [swap(parts[step - 1], ("sec", "tp"), (1, step)) for step in (3, 2, 1)]
    (own,) = call(gather_kernel, [((16, head_block), bf16)], (*parts, own), [pltpu.VMEM((16, head_block), f32)])
    across = swap(own, "sec", 3)
    beside = swap(own, "sec", 1)

    pair = [((half, features), f32), ((half, features), bf16)]

    def project(far, *lines):
        return call(
            functools.partial(project_kernel, far, per_device), pair, (*lines, assign, resid, out_weight), resident=(4,), nanos=0 if far else 2000
        )

    def tp_sum(mine, away):
        mine, away = call(add_kernel, pair, (mine, swap(away, "tp", 1)))
        return mine, swap(away, "tp", 2)

    near = project(0, own, beside)
    corner = swap(after(across, near[1]), "sec", 1)
    far = project(1, across, corner)
    sums = tp_sum(*near) + tp_sum(*far)

    count = 4
    units = width // count
    chunk = min(512, units)
    weights = (gate_weight, up_weight)
    wide = [((half, 2 * units + 128), f32), ((half, 2 * units + 128), bf16)]
    plain = [((half, 2 * units), f32), ((half, 2 * units), bf16)]
    *product, lines, stream = call(
        functools.partial(gate_up_first_kernel, chunk),
        wide + [((2 * half, features), bf16), ((group, features), f32)],
        (*sums, gain, *weights),
        [pltpu.VMEM((2, half, features), f32), pltpu.VMEM((4, 16, features), f32)],
        resident=(5, 6),
        nanos=2000,
    )
    products_made = [product]

    def more_products(index, earlier):
        return call(
            functools.partial(gate_up_more_kernel, chunk, index * units),
            plain,
            (lines, *weights, earlier),
            resident=(1, 2),
            free=(3,),
            nanos=0,
        )

    def pair_sum(index, earlier):
        mine, away = products_made[index]
        other = swap(away, "sec", 1)
        if index == 0:
            return call(pair_sum_first_kernel, wide, (mine, other), nanos=0)
        outs = [plain[0], wide[1]] if index in (1,) else plain
        return call(pair_sum_kernel, outs, (mine, other, earlier), free=(2,), nanos=0)

    products_made.append(more_products(1, product[1]))
    chip_sums = [pair_sum(0, None)]
    chip_sums.append(pair_sum(1, chip_sums[0][1]))
    products_made.append(more_products(2, chip_sums[1][1]))
    products_made.append(more_products(3, products_made[2][1]))
    chip_sums.append(pair_sum(2, products_made[3][1]))
    chip_sums.append(pair_sum(3, chip_sums[2][1]))
    total = [((2 * half, features), f32)]
    before = scale = None
    for index, (mine, away) in enumerate(chip_sums):
        other = swap(away, "sec", 3)
        if index == 0:
            hidden, scale = call(
                functools.partial(hidden_first_kernel, features * lax.axis_size("sec")),
                [((half, units), bf16), ((half, 128), f32)],
                (mine, other, chip_sums[-1][1]),
                free=(2,),
                nanos=0,
            )
        else:
            (hidden,) = call(hidden_kernel, [((half, units), bf16)], (mine, other, scale), nanos=1000)
        beside = swap(hidden, "sec", 1)
        if index == 0:
            (before,) = call(down_first_kernel, total, (hidden, beside, down_weight), resident=(2,), nanos=1000)
        elif index < count - 1:
            (before,) = call(
                functools.partial(down_more_kernel, index * units),
                total,
                (before, hidden, beside, down_weight),
                resident=(3,),
                nanos=1000,
            )
        else:
            mine, *parts = call(
                functools.partial(down_last_kernel, index * units),
                [((group, features), f32)] + [((group, features), bf16)] * 3,
                (before, hidden, beside, down_weight),
                [pltpu.VMEM((4, 16, features), f32)],
                resident=(3,),
            )
    parts = [swap(parts[step - 1], "tp", step) for step in (3, 2, 1)]
    (out,) = call(finish_kernel, [((group, features), bf16)], (*parts, stream, mine, order))
    return out


def solution(mesh):
    small = mesh.shape["sec"] == 4 and mesh.shape["tp"] == 4
    return jax.shard_map(
        local_pairs if small else local,
        mesh=mesh,
        in_specs=(
            P(("rep", "tp"), "sec"),
            P(("rep", "tp"), "sec"),
            P(("rep", "tp"), "sec"),
            P(("rep", "sec", "tp"), None, None),
            P(("rep", "sec", "tp"), None, None),
            P(("rep", "sec", "tp")),
            P("rep"),
            P("tp", "sec"),
            P("sec"),
            P("sec", "tp"),
            P("sec", "tp"),
            P("tp", "sec"),
        ),
        out_specs=P(("rep", "tp"), "sec"),
        check_vma=False,
    )
```

```python
import functools
import math

import jax
import jax.numpy as jnp
from jax import lax
from jax.experimental import pallas as pl
from jax.experimental.pallas import tpu as pltpu
from jax.sharding import PartitionSpec as P

D = 5120
QUERY_HEADS = 40
KEY_VALUE_HEADS = 8
HEAD_WIDTH = 128
CACHE_SLOTS = 224


def attend_slots(query_rows, key_value_pairs, stored_keys, stored_values, lengths):
    cache_slots = query_rows.shape[0]
    group_query = QUERY_HEADS // KEY_VALUE_HEADS
    query_head_rows = query_rows.reshape(cache_slots, KEY_VALUE_HEADS, group_query, HEAD_WIDTH)
    paired_heads = key_value_pairs.reshape(cache_slots, KEY_VALUE_HEADS, 2, HEAD_WIDTH)
    fresh_keys = paired_heads[:, :, 0]
    fresh_values = paired_heads[:, :, 1]
    earlier_keys = stored_keys.reshape(cache_slots, CACHE_SLOTS, KEY_VALUE_HEADS, HEAD_WIDTH)
    earlier_values = stored_values.reshape(cache_slots, CACHE_SLOTS, KEY_VALUE_HEADS, HEAD_WIDTH)
    scaling = 1.0 / math.sqrt(HEAD_WIDTH)
    past_scores = (
        jnp.einsum(
            "rkgd,rlkd->rkgl", query_head_rows, earlier_keys, preferred_element_type=jnp.float32
        )
        * scaling
    )
    fresh_scores = (
        jnp.einsum("rkgd,rkd->rkg", query_head_rows, fresh_keys, preferred_element_type=jnp.float32)
        * scaling
    )
    valid = lax.broadcasted_iota(jnp.int32, (cache_slots, CACHE_SLOTS), 1) < lengths[:, None]
    past_scores = jnp.where(valid[:, None, None, :], past_scores, -1e30)
    highest = jnp.maximum(jnp.max(past_scores, axis=-1), fresh_scores)
    past_exp = jnp.exp(past_scores - highest[..., None])
    fresh_exp = jnp.exp(fresh_scores - highest)
    denominator = jnp.sum(past_exp, axis=-1) + fresh_exp
    past_weights = (past_exp / denominator[..., None]).astype(jnp.bfloat16)
    fresh_weights = (fresh_exp / denominator).astype(jnp.bfloat16)
    mixed = jnp.einsum(
        "rkgl,rlkd->rkgd", past_weights, earlier_values, preferred_element_type=jnp.float32
    )
    mixed = (
        mixed
        + fresh_weights.astype(jnp.float32)[..., None]
        * fresh_values.astype(jnp.float32)[:, :, None, :]
    )
    return mixed.reshape(cache_slots, QUERY_HEADS * HEAD_WIDTH).astype(jnp.bfloat16)


def gated_units(values, width):
    return (jax.nn.silu(values[:, :width]) * values[:, width:]).astype(jnp.bfloat16)


def received(blocks, axis):
    count = lax.axis_size(axis)
    result = [blocks[0]]
    for step in range(1, count):
        result.append(lax.ppermute(blocks[step], axis, [(i, i ^ step) for i in range(count)]))
    return result


def local(
    resid,
    query,
    new_kv,
    key_cache,
    cached_value_rows,
    cache_len,
    assign,
    out_weight,
    norm_gain,
    gate_weight,
    up_weight,
    down_weight,
):
    group = query.shape[0]
    per_device = key_cache.shape[0]
    tp_index = lax.axis_index("tp")
    sec_index = lax.axis_index("sec")
    tp_count = lax.axis_size("tp")
    sec_count = lax.axis_size("sec")
    local_slots = lax.dynamic_slice_in_dim(assign, tp_index * group, group)
    resid_f32 = resid.astype(jnp.float32)
    features = resid.shape[1]
    width = gate_weight.shape[1]
    rows = group * tp_count // sec_count

    tokens = jnp.concatenate([query, new_kv], axis=1)
    blocks = []
    for step in range(sec_count):
        wanted = (sec_index ^ step) * per_device + lax.iota(jnp.int32, per_device)
        picker = (local_slots[None, :] == wanted[:, None]).astype(jnp.bfloat16)
        blocks.append(jnp.dot(picker, tokens, preferred_element_type=jnp.float32).astype(jnp.bfloat16))
    pieces = jnp.stack(received(blocks, "sec"))
    pieces = jnp.take(pieces, sec_index ^ lax.iota(jnp.int32, sec_count), axis=0)
    my_query = pieces[:, :, : query.shape[1]].transpose(1, 0, 2).reshape(per_device, -1)
    my_pairs = pieces[:, :, query.shape[1] :].transpose(1, 0, 2).reshape(per_device, -1)
    attended = attend_slots(my_query, my_pairs, key_cache, cached_value_rows, cache_len)

    head_block = out_weight.shape[0]
    blocks = [
        lax.dynamic_slice_in_dim(attended, (tp_index ^ step) * head_block, head_block, 1)
        for step in range(tp_count)
    ]
    mine = jnp.stack(received(blocks, "tp"))
    everyone = jnp.stack(received([mine] * sec_count, "sec"))
    everyone = jnp.take(everyone, sec_index ^ lax.iota(jnp.int32, sec_count), axis=0)
    everyone = everyone.transpose(1, 0, 2, 3).reshape(tp_count, group, head_block)
    parts = jnp.dot(everyone.reshape(tp_count * group, head_block), out_weight, preferred_element_type=jnp.float32)
    parts = parts.astype(jnp.bfloat16).reshape(tp_count, group, features)
    shares = received([parts[step] for step in range(tp_count)], "tp")
    attn_out = sum(share.astype(jnp.float32) for share in shares)
    attn_out = jnp.take(attn_out, local_slots, axis=0)
    stream = resid_f32 + attn_out

    scaled = (stream * norm_gain.astype(jnp.float32)[None, :]).astype(jnp.bfloat16)
    squares = jnp.broadcast_to(jnp.sum(stream * stream, axis=1, keepdims=True), (group, 128))
    piece = jnp.concatenate(received([scaled] * tp_count, "tp"), axis=0)
    square_parts = jnp.concatenate(received([squares] * tp_count, "tp"), axis=0)
    square_parts = square_parts.reshape(sec_count, rows, 128)
    gate_part = jnp.dot(piece, gate_weight, preferred_element_type=jnp.float32)
    up_part = jnp.dot(piece, up_weight, preferred_element_type=jnp.float32)
    projected = jnp.concatenate([gate_part, up_part], axis=1).astype(jnp.bfloat16)
    projected = projected.reshape(sec_count, rows, 2 * width)
    blocks = [lax.dynamic_index_in_dim(projected, sec_index ^ step, 0, False) for step in range(sec_count)]
    share = sum(block.astype(jnp.float32) for block in received(blocks, "sec"))
    blocks = [lax.dynamic_index_in_dim(square_parts, sec_index ^ step, 0, False) for step in range(sec_count)]
    total = sum(received(blocks, "sec"))
    inverse = lax.rsqrt(total[:, :1] / D + 1e-06)
    hidden = gated_units(share * inverse, width)
    hidden = jnp.stack(received([hidden] * sec_count, "sec"))
    hidden = jnp.take(hidden, sec_index ^ lax.iota(jnp.int32, sec_count), axis=0).reshape(-1, width)
    parts = jnp.dot(hidden, down_weight, preferred_element_type=jnp.float32).astype(jnp.bfloat16)
    parts = parts.reshape(tp_count, group, features)
    shares = received([parts[step] for step in range(tp_count)], "tp")
    ff_out = sum(share.astype(jnp.float32) for share in shares)
    return (stream + ff_out).astype(jnp.bfloat16)


MIB = 1024 * 1024


def call(kernel, outs, operands, scratch=(), smem=(), resident=(), remote=(), free=(), nanos=2000, limit=8):
    specs = []
    placed = []
    for place, operand in enumerate(operands):
        space = pltpu.SMEM if place in smem else pltpu.HBM if place in remote else pltpu.VMEM
        space = pl.ANY if place in free else space
        specs.append(pl.BlockSpec(memory_space=space))
        if place in resident or place in remote:
            operand = constrained(operand, space)
        placed.append(operand)
    return pl.pallas_call(
        kernel,
        out_shape=[jax.ShapeDtypeStruct(shape, dtype) for shape, dtype in outs],
        in_specs=specs,
        out_specs=[pl.BlockSpec(memory_space=pltpu.VMEM) for _ in outs],
        scratch_shapes=list(scratch),
        compiler_params=pltpu.CompilerParams(vmem_limit_bytes=limit * MIB),
        cost_estimate=pl.CostEstimate(flops=nanos * 10**6, bytes_accessed=0, transcendentals=0),
    )(*placed)


def copy_kernel(value, earlier, out):
    out[...] = value[...]


def after(value, earlier):
    (value,) = call(copy_kernel, [(value.shape, value.dtype)], (value, earlier), free=(1,), nanos=0)
    return value


def constrained(operand, space):
    return pltpu.with_memory_space_constraint(operand, space)


def swap(value, axis, step):
    if isinstance(axis, tuple):
        count = lax.axis_size(axis[1])
        total = lax.axis_size(axis[0]) * count
        step = step[0] * count + step[1]
    else:
        total = lax.axis_size(axis)
    return lax.ppermute(value, axis, [(i, i ^ step) for i in range(total)])


def group_slots(group, assign):
    tp = lax.axis_index("tp")
    slots = jnp.zeros((1, group), jnp.int32)
    for index in range(assign.shape[1] // group):
        slots = jnp.where(tp == index, assign[:, index * group : (index + 1) * group], slots)
    return slots


def slot_picker(per_device, slots):
    sec = lax.axis_index("sec")
    group = slots.shape[1]
    line = lax.broadcasted_iota(jnp.int32, (16, group), 0)
    wanted = jnp.where(line < 8, sec * per_device + line, (sec ^ 3) * per_device + line - 8)
    inside = (line & 7) < per_device
    return jnp.where(inside & (jnp.broadcast_to(slots, (16, group)) == wanted), 1.0, 0.0).astype(jnp.bfloat16)


def split_heads(per_device, picker, query, pairs, rows):
    queries = jnp.dot(picker, query[...], preferred_element_type=jnp.float32)
    others = jnp.dot(picker, pairs[...], preferred_element_type=jnp.float32)
    width = HEAD_WIDTH
    heads = query.shape[1] // width
    rows[...] = jnp.zeros_like(rows)
    for side in range(2):
        for j in range(per_device):
            line = side * 8 + j
            for h in range(heads):
                rows[side, j * 16 + h : j * 16 + h + 1, :] = queries[line : line + 1, h * width : (h + 1) * width]
            for h in range(pairs.shape[1] // width):
                at = j * 16 + heads + h
                rows[side, at : at + 1, :] = others[line : line + 1, h * width : (h + 1) * width]


def pick_own_kernel(
    per_device, group, query, pairs, assign, out, picker, query_here, pairs_here, assign_here, rows, sems
):
    copies = [
        pltpu.make_async_copy(source, target, sems.at[index])
        for index, (source, target) in enumerate(
            ((query, query_here), (pairs, pairs_here), (assign, assign_here))
        )
    ]
    for copy in copies:
        copy.start()
    copies[2].wait()
    picker[...] = slot_picker(per_device, group_slots(group, assign_here))
    copies[0].wait()
    copies[1].wait()
    split_heads(per_device, picker[...], query_here, pairs_here, rows)
    out[...] = rows[...].astype(jnp.bfloat16)


def pick_other_kernel(per_device, own, picker, query, pairs, keep, send, rows):
    split_heads(per_device, picker[...], query, pairs, rows)
    here = lax.axis_index("sec") & 1
    keep[here] = own[0]
    keep[1 - here] = rows[0].astype(jnp.bfloat16)
    send[here] = own[1]
    send[1 - here] = rows[1].astype(jnp.bfloat16)


def attend_blocks(per_device, heads, lengths, chip, source, keys, values, target, first):
    share = heads // 2
    slots = keys.shape[1]
    width = HEAD_WIDTH
    scaling = 1.0 / math.sqrt(width)
    line = lax.broadcasted_iota(jnp.int32, (16, width), 0)
    upper = line < share
    place = lax.broadcasted_iota(jnp.int32, (16, slots), 1)
    work = [(i, j) for i in range(2) for j in range(per_device)]
    past, fresh, new_values, columns = [], [], [], []
    for i, j in work:
        wide = source[i, j * 16 : (j + 1) * 16].astype(jnp.float32)
        zero = jnp.zeros_like(wide)
        both = jnp.concatenate([jnp.where(upper, wide, zero), jnp.where(upper, zero, wide)], axis=1)
        column = pl.ds(pl.multiple_of((2 * chip + i) * 2 * width, 2 * width), 2 * width)
        columns.append(column)
        scores = lax.dot_general(
            both.astype(jnp.bfloat16),
            keys[j, :, column],
            (((1,), (1,)), ((), ())),
            preferred_element_type=jnp.float32,
        )
        past.append(jnp.where(place < lengths[j], scores * scaling, -1e30))
        new_key = jnp.where(upper, wide[heads : heads + 1], wide[heads + 2 : heads + 3])
        new_values.append(jnp.where(upper, wide[heads + 1 : heads + 2], wide[heads + 3 : heads + 4]))
        fresh.append(wide * new_key)
    past = jnp.concatenate(past, axis=0)
    fresh = jnp.sum(jnp.concatenate(fresh, axis=0), axis=1, keepdims=True) * scaling
    highest = jnp.maximum(jnp.max(past, axis=1, keepdims=True), fresh)
    past_exp = jnp.exp(past - highest)
    fresh_exp = jnp.exp(fresh - highest)
    inverse = 1.0 / (jnp.sum(past_exp, axis=1, keepdims=True) + fresh_exp)
    weights = (past_exp * inverse).astype(jnp.bfloat16)
    fresh_weight = (fresh_exp * inverse).astype(jnp.bfloat16).astype(jnp.float32)
    for index, (i, j) in enumerate(work):
        lines = slice(index * 16, (index + 1) * 16)
        mixed = jnp.dot(weights[lines], values[j, :, columns[index]], preferred_element_type=jnp.float32)
        mixed = jnp.where(upper, mixed[:, :width], mixed[:, width:]) + fresh_weight[lines] * new_values[index]
        for h in range(heads):
            target[first + i, j : j + 1, h * width : (h + 1) * width] = mixed[h : h + 1]


def attend_near_kernel(per_device, heads, lengths, source, keys, values, assign, out, order):
    shape = order.shape
    slots = jnp.broadcast_to(group_slots(shape[0], assign), shape)
    line = lax.broadcasted_iota(jnp.int32, shape, 0)
    match = jnp.where(line == slots, 1.0, 0.0).astype(jnp.bfloat16)
    same = jnp.where(line == lax.broadcasted_iota(jnp.int32, shape, 1), 1.0, 0.0).astype(jnp.bfloat16)
    order[...] = lax.dot_general(
        match, same, (((0,), (0,)), ((), ())), preferred_element_type=jnp.float32
    ).astype(jnp.bfloat16)
    out[...] = jnp.zeros_like(out)
    attend_blocks(per_device, heads, lengths, lax.axis_index("sec") >> 1, source, keys, values, out, 0)


def attend_far_kernel(per_device, heads, lengths, source, near, keys, values, own, first, second, third, total):
    chip = lax.axis_index("sec") >> 1
    tp = lax.axis_index("tp")
    total[...] = jnp.zeros_like(total)
    total[2 * chip] = near[0]
    total[2 * chip + 1] = near[1]
    attend_blocks(per_device, heads, lengths, 1 - chip, source, keys, values, total, 2 * (1 - chip))
    for step, target in enumerate((own, first, second, third)):
        target[...] = total[tp ^ step, 0:4].astype(jnp.bfloat16)


def gather_kernel(third, second, first, own, out, rows):
    for step, part in enumerate((own, first, second, third)):
        rows[4 * step : 4 * step + 4] = part[...].astype(jnp.float32)
    out[...] = rows[...].astype(jnp.bfloat16)


def project_kernel(far, per_device, first, second, assign, resid, weight, keep, send):
    sec, tp = lax.axis_index("sec"), lax.axis_index("tp")
    base = sec ^ (3 * far)
    share = 2 * per_device
    count = keep.shape[0]
    lines = jnp.concatenate([first[...], second[...]], axis=0)
    shape = (count, lines.shape[0])
    line = lax.broadcasted_iota(jnp.int32, shape, 1)
    place, index = (line >> 2) & 3, line & 3
    from_sec = base ^ (line >> 4) ^ jnp.where(place > 0, 1, 0)
    row = (tp ^ place) * share + (from_sec & 1) * per_device + index
    match = (lax.broadcasted_iota(jnp.int32, shape, 0) == row) & (index < per_device)
    match = jnp.where(match, 1.0, 0.0).astype(jnp.bfloat16)
    ordered = jnp.dot(match, lines, preferred_element_type=jnp.float32).astype(jnp.bfloat16)
    total = jnp.dot(ordered, weight[...], preferred_element_type=jnp.float32)
    group = resid.shape[0]
    slots = jnp.broadcast_to(group_slots(group, assign), (count, group)) - share * (base >> 1)
    match = lax.broadcasted_iota(jnp.int32, (count, group), 0) == slots + tp * share
    match = jnp.where(match & (slots >= 0) & (slots < share), 1.0, 0.0).astype(jnp.bfloat16)
    total = total + jnp.dot(match, resid[...], preferred_element_type=jnp.float32)
    keep[...] = total
    send[...] = total.astype(jnp.bfloat16)


def add_kernel(mine, other, keep, send):
    total = mine[...] + other[...].astype(jnp.float32)
    keep[...] = total
    send[...] = total.astype(jnp.bfloat16)


def row_half():
    sec = lax.axis_index("sec")
    return (sec ^ (sec >> 1)) & 1


def products(features, gate, up, unit, units, chunk, keep, send):
    half = keep.shape[0]
    for kind, weight in enumerate((gate, up)):
        for start in range(0, units, chunk):
            column = slice(unit + start, unit + start + chunk)
            product = jnp.dot(features, weight[:, column], preferred_element_type=jnp.float32)
            at = kind * units + start
            keep[:, at : at + chunk] = product[:half]
            send[:, at : at + chunk] = product[half:].astype(jnp.bfloat16)


def to_groups(first, second, groups):
    share = first.shape[0] // groups.shape[0]
    for index in range(groups.shape[0]):
        lines = slice(index * share, (index + 1) * share)
        groups[index, 0:share] = first[lines]
        groups[index, share : 2 * share] = second[lines]


def gate_up_first_kernel(
    chunk, near, near_other, far, far_other, gain, gate, up, keep, send, features, stream, halves, groups
):
    sec, tp = lax.axis_index("sec"), lax.axis_index("tp")
    chip = sec >> 1
    half = near.shape[0]
    halves[chip] = near[...] + near_other[...].astype(jnp.float32)
    halves[1 - chip] = far[...] + far_other[...].astype(jnp.float32)
    to_groups(halves[0], halves[1], groups)
    stream[...] = groups[tp, 0 : stream.shape[0]]
    first = row_half()
    total = jnp.concatenate([halves[first], halves[1 - first]], axis=0)
    squares = jnp.sum(total * total, axis=1, keepdims=True)
    scaled = (total * gain[...].astype(jnp.float32)).astype(jnp.bfloat16)
    features[...] = scaled
    units = (keep.shape[1] - 128) // 2
    products(scaled, gate, up, 0, units, chunk, keep, send)
    keep[:, 2 * units :] = jnp.broadcast_to(squares[:half], (half, 128))
    send[:, 2 * units :] = two_terms(squares[half:])


def gate_up_more_kernel(chunk, unit, features, gate, up, earlier, keep, send):
    products(features[...], gate, up, unit, keep.shape[1] // 2, chunk, keep, send)


def two_terms(column):
    shape = (column.shape[0], 128)
    column = jnp.broadcast_to(column, shape)
    coarse = column.astype(jnp.bfloat16).astype(jnp.float32)
    lane = lax.broadcasted_iota(jnp.int32, shape, 1)
    return jnp.where(lane < 64, coarse, column - coarse).astype(jnp.bfloat16)


def one_column(terms):
    return terms[:, 0:1].astype(jnp.float32) + terms[:, 64:65].astype(jnp.float32)


def pair_sum_first_kernel(mine, other, keep, send):
    width = mine.shape[1] - 128
    total = mine[:, :width] + other[:, :width].astype(jnp.float32)
    both = mine[:, width:] + one_column(other[:, width:])
    keep[:, :width] = total
    keep[:, width:] = both
    send[:, :width] = total.astype(jnp.bfloat16)
    send[:, width:] = two_terms(both[:, 0:1])


def pair_sum_kernel(mine, other, earlier, keep, send):
    total = mine[...] + other[...].astype(jnp.float32)
    keep[...] = total
    send[...] = total.astype(jnp.bfloat16)


def gated(mine, other, factor, hidden):
    width = hidden.shape[1]
    gate = (mine[:, :width] + other[:, :width].astype(jnp.float32)) * factor
    up = (mine[:, width : 2 * width] + other[:, width : 2 * width].astype(jnp.float32)) * factor
    hidden[...] = (gate / (1.0 + jnp.exp(-gate)) * up).astype(jnp.bfloat16)


def hidden_first_kernel(features, mine, other, earlier, hidden, scale):
    width = mine.shape[1] - 128
    total = mine[:, width : width + 1] + one_column(other[:, width:])
    factor = lax.rsqrt(total / features + 1e-06)
    scale[...] = jnp.broadcast_to(factor, scale.shape)
    gated(mine, other, factor, hidden)


def hidden_kernel(mine, other, scale, earlier, hidden):
    gated(mine, other, scale[:, 0:1], hidden)


def down_product(unit, mine, other, weight):
    lines = jnp.concatenate([mine[...].astype(jnp.float32), other[...].astype(jnp.float32)], axis=0)
    rows = weight[unit : unit + lines.shape[1], :]
    return jnp.dot(lines.astype(jnp.bfloat16), rows, preferred_element_type=jnp.float32)


def down_first_kernel(mine, other, weight, out):
    out[...] = down_product(0, mine, other, weight)


def down_more_kernel(unit, before, mine, other, weight, out):
    out[...] = before[...] + down_product(unit, mine, other, weight)


def down_last_kernel(unit, before, mine, other, weight, keep, first, second, third, groups):
    tp = lax.axis_index("tp")
    product = before[...] + down_product(unit, mine, other, weight)
    group = keep.shape[0]
    half = product.shape[0] // 2
    swapped = row_half() == 1
    lower, upper = product[:half], product[half:]
    to_groups(jnp.where(swapped, upper, lower), jnp.where(swapped, lower, upper), groups)
    keep[...] = groups[tp, 0:group]
    for step, target in enumerate((first, second, third)):
        target[...] = groups[tp ^ (step + 1), 0:group].astype(jnp.bfloat16)


def finish_kernel(third, second, first, stream, mine, order, out):
    total = stream[...] + mine[...]
    for other in (first, second, third):
        total = total + other[...].astype(jnp.float32)
    coarse = total.astype(jnp.bfloat16)
    fine = (total - coarse.astype(jnp.float32)).astype(jnp.bfloat16)
    ordered = [jnp.dot(order[...], term, preferred_element_type=jnp.float32) for term in (coarse, fine)]
    out[...] = (ordered[0] + ordered[1]).astype(jnp.bfloat16)


def local_pairs(
    resid,
    query,
    new_kv,
    key_cache,
    cached_value_rows,
    cache_len,
    assign,
    out_weight,
    norm_gain,
    gate_weight,
    up_weight,
    down_weight,
):
    f32, bf16 = jnp.float32, jnp.bfloat16
    group, features = resid.shape
    per_device = key_cache.shape[0]
    heads = query.shape[1] // HEAD_WIDTH
    head_block = out_weight.shape[0]
    width = gate_weight.shape[1]
    half = 2 * group
    assign = assign.reshape(1, -1)
    gain = norm_gain.reshape(1, -1)

    query_b, pairs_b = swap(query, "sec", 1), swap(new_kv, "sec", 1)
    block = (2, 16 * per_device, HEAD_WIDTH)
    own, picker = call(
        functools.partial(pick_own_kernel, per_device, group),
        [(block, bf16), ((16, group), bf16)],
        (query, new_kv, assign),
        [
            pltpu.VMEM(query.shape, bf16),
            pltpu.VMEM(new_kv.shape, bf16),
            pltpu.VMEM(assign.shape, jnp.int32),
            pltpu.VMEM(block, f32),
            pltpu.SemaphoreType.DMA((3,)),
        ],
        remote=(0, 1, 2),
    )
    mine, away = call(
        functools.partial(pick_other_kernel, per_device),
        [(block, bf16)] * 2,
        (own, picker, query_b, pairs_b),
        [pltpu.VMEM(block, f32)],
    )
    other = swap(away, "sec", 3)
    caches = (key_cache, cached_value_rows)
    near, order = call(
        functools.partial(attend_near_kernel, per_device, heads),
        [((2, 4, head_block), f32), ((group, group), bf16)],
        (cache_len, mine, *caches, assign),
        smem=(0,),
        resident=(2, 3),
    )
    own, *parts = call(
        functools.partial(attend_far_kernel, per_device, heads),
        [((4, head_block), bf16)] * 4,
        (cache_len, other, near, *caches),
        [pltpu.VMEM((4, 4, head_block), f32)],
        smem=(0,),
        resident=(3, 4),
    )

    parts = [swap(parts[step - 1], ("sec", "tp"), (1, step)) for step in (3, 2, 1)]
    (own,) = call(gather_kernel, [((16, head_block), bf16)], (*parts, own), [pltpu.VMEM((16, head_block), f32)])
    across = swap(own, "sec", 3)
    beside = swap(own, "sec", 1)

    pair = [((half, features), f32), ((half, features), bf16)]

    def project(far, *lines):
        return call(
            functools.partial(project_kernel, far, per_device), pair, (*lines, assign, resid, out_weight), resident=(4,), nanos=0 if far else 2000
        )

    def tp_sum(mine, away):
        mine, away = call(add_kernel, pair, (mine, swap(away, "tp", 1)))
        return mine, swap(away, "tp", 2)

    near = project(0, own, beside)
    corner = swap(after(across, near[1]), "sec", 1)
    far = project(1, across, corner)
    sums = tp_sum(*near) + tp_sum(*far)

    sizes = [width * sixteenths // 16 for sixteenths in (5, 5, 3, 3)]
    starts = [sum(sizes[:index]) for index in range(len(sizes))]
    chunk = width // 16
    weights = (gate_weight, up_weight)

    def sums_of(index, extra=0):
        shape = (half, 2 * sizes[index] + extra)
        return [(shape, f32), (shape, bf16)]

    *product, lines, stream = call(
        functools.partial(gate_up_first_kernel, chunk),
        sums_of(0, 128) + [((2 * half, features), bf16), ((group, features), f32)],
        (*sums, gain, *weights),
        [pltpu.VMEM((2, half, features), f32), pltpu.VMEM((4, 16, features), f32)],
        resident=(5, 6),
        nanos=2000,
    )
    products_made = [product]

    def more_products(index, earlier):
        return call(
            functools.partial(gate_up_more_kernel, chunk, starts[index]),
            sums_of(index),
            (lines, *weights, earlier),
            resident=(1, 2),
            free=(3,),
            nanos=0,
        )

    def pair_sum(index, earlier):
        mine, away = products_made[index]
        other = swap(away, "sec", 1)
        if index == 0:
            return call(pair_sum_first_kernel, sums_of(0, 128), (mine, other), nanos=0)
        return call(pair_sum_kernel, sums_of(index), (mine, other, earlier), free=(2,), nanos=0)

    products_made.append(more_products(1, product[1]))
    chip_sums = [pair_sum(0, None)]
    chip_sums.append(pair_sum(1, chip_sums[0][1]))
    products_made.append(more_products(2, chip_sums[1][1]))
    products_made.append(more_products(3, products_made[2][1]))
    chip_sums.append(pair_sum(2, products_made[3][1]))
    chip_sums.append(pair_sum(3, chip_sums[2][1]))
    total = [((2 * half, features), f32)]
    before = scale = None
    parts_done = []
    for index, (mine, away) in enumerate(chip_sums):
        other = swap(away, "sec", 3)
        if index == 0:
            hidden, scale = call(
                functools.partial(hidden_first_kernel, features * lax.axis_size("sec")),
                [((half, sizes[0]), bf16), ((half, 128), f32)],
                (mine, other, chip_sums[-1][1]),
                free=(2,),
                nanos=0,
            )
        else:
            earlier = parts_done[max(index - 2, 0)] if index > 1 else hidden
            (hidden,) = call(
                hidden_kernel, [((half, sizes[index]), bf16)], (mine, other, scale, earlier), free=(3,), nanos=1000
            )
        beside = swap(hidden, "sec", 1)
        if index == 0:
            (before,) = call(down_first_kernel, total, (hidden, beside, down_weight), resident=(2,), nanos=1000)
            parts_done.append(before)
        elif index < len(sizes) - 1:
            (before,) = call(
                functools.partial(down_more_kernel, starts[index]),
                total,
                (before, hidden, beside, down_weight),
                resident=(3,),
                nanos=1000,
            )
            parts_done.append(before)
        else:
            mine, *parts = call(
                functools.partial(down_last_kernel, starts[index]),
                [((group, features), f32)] + [((group, features), bf16)] * 3,
                (before, hidden, beside, down_weight),
                [pltpu.VMEM((4, 16, features), f32)],
                resident=(3,),
            )
    parts = [swap(parts[step - 1], "tp", step) for step in (3, 2, 1)]
    (out,) = call(finish_kernel, [((group, features), bf16)], (*parts, stream, mine, order))
    return out


def solution(mesh):
    small = mesh.shape["sec"] == 4 and mesh.shape["tp"] == 4
    return jax.shard_map(
        local_pairs if small else local,
        mesh=mesh,
        in_specs=(
            P(("rep", "tp"), "sec"),
            P(("rep", "tp"), "sec"),
            P(("rep", "tp"), "sec"),
            P(("rep", "sec", "tp"), None, None),
            P(("rep", "sec", "tp"), None, None),
            P(("rep", "sec", "tp")),
            P("rep"),
            P("tp", "sec"),
            P("sec"),
            P("sec", "tp"),
            P("sec", "tp"),
            P("tp", "sec"),
        ),
        out_specs=P(("rep", "tp"), "sec"),
        check_vma=False,
    )
```

```python
import functools
import math

import jax
import jax.numpy as jnp
from jax import lax
from jax.experimental import pallas as pl
from jax.experimental.pallas import tpu as pltpu
from jax.sharding import PartitionSpec as P

D = 5120
QUERY_HEADS = 40
KEY_VALUE_HEADS = 8
HEAD_WIDTH = 128
CACHE_SLOTS = 224


def attend_slots(query_rows, key_value_pairs, stored_keys, stored_values, lengths):
    cache_slots = query_rows.shape[0]
    group_query = QUERY_HEADS // KEY_VALUE_HEADS
    query_head_rows = query_rows.reshape(cache_slots, KEY_VALUE_HEADS, group_query, HEAD_WIDTH)
    paired_heads = key_value_pairs.reshape(cache_slots, KEY_VALUE_HEADS, 2, HEAD_WIDTH)
    fresh_keys = paired_heads[:, :, 0]
    fresh_values = paired_heads[:, :, 1]
    earlier_keys = stored_keys.reshape(cache_slots, CACHE_SLOTS, KEY_VALUE_HEADS, HEAD_WIDTH)
    earlier_values = stored_values.reshape(cache_slots, CACHE_SLOTS, KEY_VALUE_HEADS, HEAD_WIDTH)
    scaling = 1.0 / math.sqrt(HEAD_WIDTH)
    past_scores = (
        jnp.einsum(
            "rkgd,rlkd->rkgl", query_head_rows, earlier_keys, preferred_element_type=jnp.float32
        )
        * scaling
    )
    fresh_scores = (
        jnp.einsum("rkgd,rkd->rkg", query_head_rows, fresh_keys, preferred_element_type=jnp.float32)
        * scaling
    )
    valid = lax.broadcasted_iota(jnp.int32, (cache_slots, CACHE_SLOTS), 1) < lengths[:, None]
    past_scores = jnp.where(valid[:, None, None, :], past_scores, -1e30)
    highest = jnp.maximum(jnp.max(past_scores, axis=-1), fresh_scores)
    past_exp = jnp.exp(past_scores - highest[..., None])
    fresh_exp = jnp.exp(fresh_scores - highest)
    denominator = jnp.sum(past_exp, axis=-1) + fresh_exp
    past_weights = (past_exp / denominator[..., None]).astype(jnp.bfloat16)
    fresh_weights = (fresh_exp / denominator).astype(jnp.bfloat16)
    mixed = jnp.einsum(
        "rkgl,rlkd->rkgd", past_weights, earlier_values, preferred_element_type=jnp.float32
    )
    mixed = (
        mixed
        + fresh_weights.astype(jnp.float32)[..., None]
        * fresh_values.astype(jnp.float32)[:, :, None, :]
    )
    return mixed.reshape(cache_slots, QUERY_HEADS * HEAD_WIDTH).astype(jnp.bfloat16)


def gated_units(values, width):
    return (jax.nn.silu(values[:, :width]) * values[:, width:]).astype(jnp.bfloat16)


def received(blocks, axis):
    count = lax.axis_size(axis)
    result = [blocks[0]]
    for step in range(1, count):
        result.append(lax.ppermute(blocks[step], axis, [(i, i ^ step) for i in range(count)]))
    return result


def local(
    resid,
    query,
    new_kv,
    key_cache,
    cached_value_rows,
    cache_len,
    assign,
    out_weight,
    norm_gain,
    gate_weight,
    up_weight,
    down_weight,
):
    group = query.shape[0]
    per_device = key_cache.shape[0]
    tp_index = lax.axis_index("tp")
    sec_index = lax.axis_index("sec")
    tp_count = lax.axis_size("tp")
    sec_count = lax.axis_size("sec")
    local_slots = lax.dynamic_slice_in_dim(assign, tp_index * group, group)
    resid_f32 = resid.astype(jnp.float32)
    features = resid.shape[1]
    width = gate_weight.shape[1]
    rows = group * tp_count // sec_count

    tokens = jnp.concatenate([query, new_kv], axis=1)
    blocks = []
    for step in range(sec_count):
        wanted = (sec_index ^ step) * per_device + lax.iota(jnp.int32, per_device)
        picker = (local_slots[None, :] == wanted[:, None]).astype(jnp.bfloat16)
        blocks.append(jnp.dot(picker, tokens, preferred_element_type=jnp.float32).astype(jnp.bfloat16))
    pieces = jnp.stack(received(blocks, "sec"))
    pieces = jnp.take(pieces, sec_index ^ lax.iota(jnp.int32, sec_count), axis=0)
    my_query = pieces[:, :, : query.shape[1]].transpose(1, 0, 2).reshape(per_device, -1)
    my_pairs = pieces[:, :, query.shape[1] :].transpose(1, 0, 2).reshape(per_device, -1)
    attended = attend_slots(my_query, my_pairs, key_cache, cached_value_rows, cache_len)

    head_block = out_weight.shape[0]
    blocks = [
        lax.dynamic_slice_in_dim(attended, (tp_index ^ step) * head_block, head_block, 1)
        for step in range(tp_count)
    ]
    mine = jnp.stack(received(blocks, "tp"))
    everyone = jnp.stack(received([mine] * sec_count, "sec"))
    everyone = jnp.take(everyone, sec_index ^ lax.iota(jnp.int32, sec_count), axis=0)
    everyone = everyone.transpose(1, 0, 2, 3).reshape(tp_count, group, head_block)
    parts = jnp.dot(everyone.reshape(tp_count * group, head_block), out_weight, preferred_element_type=jnp.float32)
    parts = parts.astype(jnp.bfloat16).reshape(tp_count, group, features)
    shares = received([parts[step] for step in range(tp_count)], "tp")
    attn_out = sum(share.astype(jnp.float32) for share in shares)
    attn_out = jnp.take(attn_out, local_slots, axis=0)
    stream = resid_f32 + attn_out

    scaled = (stream * norm_gain.astype(jnp.float32)[None, :]).astype(jnp.bfloat16)
    squares = jnp.broadcast_to(jnp.sum(stream * stream, axis=1, keepdims=True), (group, 128))
    piece = jnp.concatenate(received([scaled] * tp_count, "tp"), axis=0)
    square_parts = jnp.concatenate(received([squares] * tp_count, "tp"), axis=0)
    square_parts = square_parts.reshape(sec_count, rows, 128)
    gate_part = jnp.dot(piece, gate_weight, preferred_element_type=jnp.float32)
    up_part = jnp.dot(piece, up_weight, preferred_element_type=jnp.float32)
    projected = jnp.concatenate([gate_part, up_part], axis=1).astype(jnp.bfloat16)
    projected = projected.reshape(sec_count, rows, 2 * width)
    blocks = [lax.dynamic_index_in_dim(projected, sec_index ^ step, 0, False) for step in range(sec_count)]
    share = sum(block.astype(jnp.float32) for block in received(blocks, "sec"))
    blocks = [lax.dynamic_index_in_dim(square_parts, sec_index ^ step, 0, False) for step in range(sec_count)]
    total = sum(received(blocks, "sec"))
    inverse = lax.rsqrt(total[:, :1] / D + 1e-06)
    hidden = gated_units(share * inverse, width)
    hidden = jnp.stack(received([hidden] * sec_count, "sec"))
    hidden = jnp.take(hidden, sec_index ^ lax.iota(jnp.int32, sec_count), axis=0).reshape(-1, width)
    parts = jnp.dot(hidden, down_weight, preferred_element_type=jnp.float32).astype(jnp.bfloat16)
    parts = parts.reshape(tp_count, group, features)
    shares = received([parts[step] for step in range(tp_count)], "tp")
    ff_out = sum(share.astype(jnp.float32) for share in shares)
    return (stream + ff_out).astype(jnp.bfloat16)


MIB = 1024 * 1024


def call(kernel, outs, operands, scratch=(), smem=(), resident=(), remote=(), free=(), nanos=2000, limit=8):
    specs = []
    placed = []
    for place, operand in enumerate(operands):
        space = pltpu.SMEM if place in smem else pltpu.HBM if place in remote else pltpu.VMEM
        space = pl.ANY if place in free else space
        specs.append(pl.BlockSpec(memory_space=space))
        if place in resident or place in remote:
            operand = constrained(operand, space)
        placed.append(operand)
    return pl.pallas_call(
        kernel,
        out_shape=[jax.ShapeDtypeStruct(shape, dtype) for shape, dtype in outs],
        in_specs=specs,
        out_specs=[pl.BlockSpec(memory_space=pltpu.VMEM) for _ in outs],
        scratch_shapes=list(scratch),
        compiler_params=pltpu.CompilerParams(vmem_limit_bytes=limit * MIB),
        cost_estimate=pl.CostEstimate(flops=nanos * 10**6, bytes_accessed=0, transcendentals=0),
    )(*placed)


def copy_kernel(value, earlier, out):
    out[...] = value[...]


def after(value, earlier):
    (value,) = call(copy_kernel, [(value.shape, value.dtype)], (value, earlier), free=(1,), nanos=0)
    return value


def constrained(operand, space):
    return pltpu.with_memory_space_constraint(operand, space)


def swap(value, axis, step):
    if isinstance(axis, tuple):
        count = lax.axis_size(axis[1])
        total = lax.axis_size(axis[0]) * count
        step = step[0] * count + step[1]
    else:
        total = lax.axis_size(axis)
    return lax.ppermute(value, axis, [(i, i ^ step) for i in range(total)])


def group_slots(group, assign):
    tp = lax.axis_index("tp")
    slots = jnp.zeros((1, group), jnp.int32)
    for index in range(assign.shape[1] // group):
        slots = jnp.where(tp == index, assign[:, index * group : (index + 1) * group], slots)
    return slots


def slot_picker(per_device, slots):
    sec = lax.axis_index("sec")
    group = slots.shape[1]
    line = lax.broadcasted_iota(jnp.int32, (16, group), 0)
    wanted = jnp.where(line < 8, sec * per_device + line, (sec ^ 3) * per_device + line - 8)
    inside = (line & 7) < per_device
    return jnp.where(inside & (jnp.broadcast_to(slots, (16, group)) == wanted), 1.0, 0.0).astype(jnp.bfloat16)


def split_heads(per_device, picker, query, pairs, rows):
    queries = jnp.dot(picker, query[...], preferred_element_type=jnp.float32)
    others = jnp.dot(picker, pairs[...], preferred_element_type=jnp.float32)
    width = HEAD_WIDTH
    heads = query.shape[1] // width
    rows[...] = jnp.zeros_like(rows)
    for side in range(2):
        for j in range(per_device):
            line = side * 8 + j
            for h in range(heads):
                rows[side, j * 16 + h : j * 16 + h + 1, :] = queries[line : line + 1, h * width : (h + 1) * width]
            for h in range(pairs.shape[1] // width):
                at = j * 16 + heads + h
                rows[side, at : at + 1, :] = others[line : line + 1, h * width : (h + 1) * width]


def pick_own_kernel(
    per_device, group, query, pairs, assign, out, picker, query_here, pairs_here, assign_here, rows, sems
):
    copies = [
        pltpu.make_async_copy(source, target, sems.at[index])
        for index, (source, target) in enumerate(
            ((query, query_here), (pairs, pairs_here), (assign, assign_here))
        )
    ]
    for copy in copies:
        copy.start()
    copies[2].wait()
    picker[...] = slot_picker(per_device, group_slots(group, assign_here))
    copies[0].wait()
    copies[1].wait()
    split_heads(per_device, picker[...], query_here, pairs_here, rows)
    out[...] = rows[...].astype(jnp.bfloat16)


def pick_other_kernel(per_device, own, picker, query, pairs, keep, send, rows):
    split_heads(per_device, picker[...], query, pairs, rows)
    here = lax.axis_index("sec") & 1
    keep[here] = own[0]
    keep[1 - here] = rows[0].astype(jnp.bfloat16)
    send[here] = own[1]
    send[1 - here] = rows[1].astype(jnp.bfloat16)


def attend_blocks(per_device, heads, lengths, chip, source, keys, values, target, first):
    share = heads // 2
    slots = keys.shape[1]
    width = HEAD_WIDTH
    scaling = 1.0 / math.sqrt(width)
    line = lax.broadcasted_iota(jnp.int32, (32, width), 0)
    kind = 2 * (line >> 4) + jnp.where((line & 15) < share, 0, 1)
    upper = (lax.broadcasted_iota(jnp.int32, (16, width), 0)) < share
    place = lax.broadcasted_iota(jnp.int32, (32, slots), 1)
    columns = pl.ds(pl.multiple_of(chip * 4 * width, 4 * width), 4 * width)
    past, fresh, new_values = [], [], []
    for j in range(per_device):
        blocks = [source[i, j * 16 : (j + 1) * 16].astype(jnp.float32) for i in range(2)]
        wide = jnp.concatenate(blocks, axis=0)
        zero = jnp.zeros_like(wide)
        spread = jnp.concatenate([jnp.where(kind == c, wide, zero) for c in range(4)], axis=1)
        scores = lax.dot_general(
            spread.astype(jnp.bfloat16),
            keys[j, :, columns],
            (((1,), (1,)), ((), ())),
            preferred_element_type=jnp.float32,
        )
        past.append(jnp.where(place < lengths[j], scores * scaling, -1e30))
        new_key, new_value = [
            jnp.concatenate(
                [jnp.where(upper, block[heads + at : heads + at + 1], block[heads + at + 2 : heads + at + 3]) for block in blocks],
                axis=0,
            )
            for at in range(2)
        ]
        new_values.append(new_value)
        fresh.append(wide * new_key)
    past = jnp.concatenate(past, axis=0)
    fresh = jnp.sum(jnp.concatenate(fresh, axis=0), axis=1, keepdims=True) * scaling
    highest = jnp.maximum(jnp.max(past, axis=1, keepdims=True), fresh)
    past_exp = jnp.exp(past - highest)
    fresh_exp = jnp.exp(fresh - highest)
    inverse = 1.0 / (jnp.sum(past_exp, axis=1, keepdims=True) + fresh_exp)
    weights = (past_exp * inverse).astype(jnp.bfloat16)
    fresh_weight = (fresh_exp * inverse).astype(jnp.bfloat16).astype(jnp.float32)
    for j in range(per_device):
        lines = slice(j * 32, (j + 1) * 32)
        product = jnp.dot(weights[lines], values[j, :, columns], preferred_element_type=jnp.float32)
        mixed = fresh_weight[lines] * new_values[j]
        for c in range(4):
            mixed = mixed + jnp.where(kind == c, product[:, c * width : (c + 1) * width], 0.0)
        for i in range(2):
            for h in range(heads):
                target[first + i, j : j + 1, h * width : (h + 1) * width] = mixed[i * 16 + h : i * 16 + h + 1]


def attend_near_kernel(per_device, heads, lengths, source, keys, values, assign, out, order):
    shape = order.shape
    slots = jnp.broadcast_to(group_slots(shape[0], assign), shape)
    line = lax.broadcasted_iota(jnp.int32, shape, 0)
    match = jnp.where(line == slots, 1.0, 0.0).astype(jnp.bfloat16)
    same = jnp.where(line == lax.broadcasted_iota(jnp.int32, shape, 1), 1.0, 0.0).astype(jnp.bfloat16)
    order[...] = lax.dot_general(
        match, same, (((0,), (0,)), ((), ())), preferred_element_type=jnp.float32
    ).astype(jnp.bfloat16)
    out[...] = jnp.zeros_like(out)
    attend_blocks(per_device, heads, lengths, lax.axis_index("sec") >> 1, source, keys, values, out, 0)


def attend_far_kernel(per_device, heads, lengths, source, near, keys, values, own, first, second, third, total):
    chip = lax.axis_index("sec") >> 1
    tp = lax.axis_index("tp")
    total[...] = jnp.zeros_like(total)
    total[2 * chip] = near[0]
    total[2 * chip + 1] = near[1]
    attend_blocks(per_device, heads, lengths, 1 - chip, source, keys, values, total, 2 * (1 - chip))
    for step, target in enumerate((own, first, second, third)):
        target[...] = total[tp ^ step, 0:4].astype(jnp.bfloat16)


def gather_kernel(third, second, first, own, out, rows):
    for step, part in enumerate((own, first, second, third)):
        rows[4 * step : 4 * step + 4] = part[...].astype(jnp.float32)
    out[...] = rows[...].astype(jnp.bfloat16)


def slot_rows(far, per_device, count):
    sec, tp = lax.axis_index("sec"), lax.axis_index("tp")
    share = 2 * per_device
    shape = (count, 32)
    line = lax.broadcasted_iota(jnp.int32, shape, 1)
    place, index = (line >> 2) & 3, line & 3
    from_sec = sec ^ (3 * far) ^ (line >> 4) ^ jnp.where(place > 0, 1, 0)
    row = (tp ^ place) * share + (from_sec & 1) * per_device + index
    match = (lax.broadcasted_iota(jnp.int32, shape, 0) == row) & (index < per_device)
    return jnp.where(match, 1.0, 0.0).astype(jnp.bfloat16)


def resid_rows(far, per_device, count, assign, resid):
    sec, tp = lax.axis_index("sec"), lax.axis_index("tp")
    share = 2 * per_device
    group = resid.shape[0]
    chip = (sec ^ (3 * far)) >> 1
    slots = jnp.broadcast_to(group_slots(group, assign), (count, group)) - share * chip
    match = lax.broadcasted_iota(jnp.int32, (count, group), 0) == slots + tp * share
    match = jnp.where(match & (slots >= 0) & (slots < share), 1.0, 0.0).astype(jnp.bfloat16)
    return jnp.dot(match, resid[...], preferred_element_type=jnp.float32)


def project(match, first, second, resid, weight, keep, send):
    lines = jnp.concatenate([first[...], second[...]], axis=0)
    ordered = jnp.dot(match, lines, preferred_element_type=jnp.float32).astype(jnp.bfloat16)
    total = resid + jnp.dot(ordered, weight[...], preferred_element_type=jnp.float32)
    keep[...] = total
    send[...] = total.astype(jnp.bfloat16)


def project_near_kernel(per_device, first, second, assign, resid, weight, keep, send, far_match, far_resid):
    count = keep.shape[0]
    near = resid_rows(0, per_device, count, assign, resid)
    project(slot_rows(0, per_device, count), first, second, near, weight, keep, send)
    far_match[...] = slot_rows(1, per_device, count)
    far_resid[...] = resid_rows(1, per_device, count, assign, resid)


def project_far_kernel(first, second, match, resid, weight, keep, send):
    project(match[...], first, second, resid[...], weight, keep, send)


def add_kernel(mine, other, keep, send):
    total = mine[...] + other[...].astype(jnp.float32)
    keep[...] = total
    send[...] = total.astype(jnp.bfloat16)


def row_half():
    sec = lax.axis_index("sec")
    return (sec ^ (sec >> 1)) & 1


def products(features, gate, up, unit, units, chunk, keep, send):
    half = keep.shape[0]
    for kind, weight in enumerate((gate, up)):
        for start in range(0, units, chunk):
            column = slice(unit + start, unit + start + chunk)
            product = jnp.dot(features, weight[:, column], preferred_element_type=jnp.float32)
            at = kind * units + start
            keep[:, at : at + chunk] = product[:half]
            send[:, at : at + chunk] = product[half:].astype(jnp.bfloat16)


def to_groups(first, second, groups):
    share = first.shape[0] // groups.shape[0]
    for index in range(groups.shape[0]):
        lines = slice(index * share, (index + 1) * share)
        groups[index, 0:share] = first[lines]
        groups[index, share : 2 * share] = second[lines]


def gate_up_first_kernel(
    chunk, near, near_other, far, far_other, gain, gate, up, keep, send, features, stream, halves, groups
):
    sec, tp = lax.axis_index("sec"), lax.axis_index("tp")
    chip = sec >> 1
    half = near.shape[0]
    halves[chip] = near[...] + near_other[...].astype(jnp.float32)
    halves[1 - chip] = far[...] + far_other[...].astype(jnp.float32)
    to_groups(halves[0], halves[1], groups)
    stream[...] = groups[tp, 0 : stream.shape[0]]
    first = row_half()
    total = jnp.concatenate([halves[first], halves[1 - first]], axis=0)
    squares = jnp.sum(total * total, axis=1, keepdims=True)
    scaled = (total * gain[...].astype(jnp.float32)).astype(jnp.bfloat16)
    features[...] = scaled
    units = (keep.shape[1] - 128) // 2
    products(scaled, gate, up, 0, units, chunk, keep, send)
    keep[:, 2 * units :] = jnp.broadcast_to(squares[:half], (half, 128))
    send[:, 2 * units :] = two_terms(squares[half:])


def gate_up_more_kernel(chunk, unit, features, gate, up, earlier, keep, send):
    products(features[...], gate, up, unit, keep.shape[1] // 2, chunk, keep, send)


def two_terms(column):
    shape = (column.shape[0], 128)
    column = jnp.broadcast_to(column, shape)
    coarse = column.astype(jnp.bfloat16).astype(jnp.float32)
    lane = lax.broadcasted_iota(jnp.int32, shape, 1)
    return jnp.where(lane < 64, coarse, column - coarse).astype(jnp.bfloat16)


def one_column(terms):
    return terms[:, 0:1].astype(jnp.float32) + terms[:, 64:65].astype(jnp.float32)


def pair_sum_first_kernel(mine, other, keep, send):
    width = mine.shape[1] - 128
    total = mine[:, :width] + other[:, :width].astype(jnp.float32)
    both = mine[:, width:] + one_column(other[:, width:])
    keep[:, :width] = total
    keep[:, width:] = both
    send[:, :width] = total.astype(jnp.bfloat16)
    send[:, width:] = two_terms(both[:, 0:1])


def pair_sum_kernel(mine, other, earlier, keep, send):
    total = mine[...] + other[...].astype(jnp.float32)
    keep[...] = total
    send[...] = total.astype(jnp.bfloat16)


def gated(mine, other, factor, hidden):
    width = hidden.shape[1]
    gate = (mine[:, :width] + other[:, :width].astype(jnp.float32)) * factor
    up = (mine[:, width : 2 * width] + other[:, width : 2 * width].astype(jnp.float32)) * factor
    hidden[...] = (gate / (1.0 + jnp.exp(-gate)) * up).astype(jnp.bfloat16)


def hidden_first_kernel(features, mine, other, earlier, hidden, scale):
    width = mine.shape[1] - 128
    total = mine[:, width : width + 1] + one_column(other[:, width:])
    factor = lax.rsqrt(total / features + 1e-06)
    scale[...] = jnp.broadcast_to(factor, scale.shape)
    gated(mine, other, factor, hidden)


def hidden_kernel(mine, other, scale, earlier, hidden):
    gated(mine, other, scale[:, 0:1], hidden)


def down_product(unit, mine, other, weight):
    lines = jnp.concatenate([mine[...].astype(jnp.float32), other[...].astype(jnp.float32)], axis=0)
    rows = weight[unit : unit + lines.shape[1], :]
    return jnp.dot(lines.astype(jnp.bfloat16), rows, preferred_element_type=jnp.float32)


def down_first_kernel(mine, other, weight, out):
    out[...] = down_product(0, mine, other, weight)


def down_more_kernel(unit, before, mine, other, weight, out):
    out[...] = before[...] + down_product(unit, mine, other, weight)


def down_last_kernel(unit, before, mine, other, weight, keep, first, second, third, groups):
    tp = lax.axis_index("tp")
    product = before[...] + down_product(unit, mine, other, weight)
    group = keep.shape[0]
    half = product.shape[0] // 2
    swapped = row_half() == 1
    lower, upper = product[:half], product[half:]
    to_groups(jnp.where(swapped, upper, lower), jnp.where(swapped, lower, upper), groups)
    keep[...] = groups[tp, 0:group]
    for step, target in enumerate((first, second, third)):
        target[...] = groups[tp ^ (step + 1), 0:group].astype(jnp.bfloat16)


def finish_kernel(third, second, first, stream, mine, order, out):
    total = stream[...] + mine[...]
    for other in (first, second, third):
        total = total + other[...].astype(jnp.float32)
    coarse = total.astype(jnp.bfloat16)
    fine = (total - coarse.astype(jnp.float32)).astype(jnp.bfloat16)
    ordered = [jnp.dot(order[...], term, preferred_element_type=jnp.float32) for term in (coarse, fine)]
    out[...] = (ordered[0] + ordered[1]).astype(jnp.bfloat16)


def local_pairs(
    resid,
    query,
    new_kv,
    key_cache,
    cached_value_rows,
    cache_len,
    assign,
    out_weight,
    norm_gain,
    gate_weight,
    up_weight,
    down_weight,
):
    f32, bf16 = jnp.float32, jnp.bfloat16
    group, features = resid.shape
    per_device = key_cache.shape[0]
    heads = query.shape[1] // HEAD_WIDTH
    head_block = out_weight.shape[0]
    width = gate_weight.shape[1]
    half = 2 * group
    assign = assign.reshape(1, -1)
    gain = norm_gain.reshape(1, -1)

    query_b, pairs_b = swap(query, "sec", 1), swap(new_kv, "sec", 1)
    block = (2, 16 * per_device, HEAD_WIDTH)
    own, picker = call(
        functools.partial(pick_own_kernel, per_device, group),
        [(block, bf16), ((16, group), bf16)],
        (query, new_kv, assign),
        [
            pltpu.VMEM(query.shape, bf16),
            pltpu.VMEM(new_kv.shape, bf16),
            pltpu.VMEM(assign.shape, jnp.int32),
            pltpu.VMEM(block, f32),
            pltpu.SemaphoreType.DMA((3,)),
        ],
        remote=(0, 1, 2),
    )
    mine, away = call(
        functools.partial(pick_other_kernel, per_device),
        [(block, bf16)] * 2,
        (own, picker, query_b, pairs_b),
        [pltpu.VMEM(block, f32)],
    )
    other = swap(away, "sec", 3)
    caches = (key_cache, cached_value_rows)
    near, order = call(
        functools.partial(attend_near_kernel, per_device, heads),
        [((2, 4, head_block), f32), ((group, group), bf16)],
        (cache_len, mine, *caches, assign),
        smem=(0,),
        resident=(2, 3),
    )
    own, *parts = call(
        functools.partial(attend_far_kernel, per_device, heads),
        [((4, head_block), bf16)] * 4,
        (cache_len, other, near, *caches),
        [pltpu.VMEM((4, 4, head_block), f32)],
        smem=(0,),
        resident=(3, 4),
    )

    parts = [swap(parts[step - 1], ("sec", "tp"), (1, step)) for step in (3, 2, 1)]
    (own,) = call(gather_kernel, [((16, head_block), bf16)], (*parts, own), [pltpu.VMEM((16, head_block), f32)])
    across = swap(own, "sec", 3)
    beside = swap(own, "sec", 1)

    pair = [((half, features), f32), ((half, features), bf16)]

    def tp_sum(mine, away):
        mine, away = call(add_kernel, pair, (mine, swap(away, "tp", 1)))
        return mine, swap(away, "tp", 2)

    *near, match, rows = call(
        functools.partial(project_near_kernel, per_device),
        pair + [((half, 32), bf16), ((half, features), f32)],
        (own, beside, assign, resid, out_weight),
        resident=(4,),
    )
    corner = swap(after(across, near[1]), "sec", 1)
    far = call(project_far_kernel, pair, (across, corner, match, rows, out_weight), resident=(4,), nanos=0)
    sums = tp_sum(*near) + tp_sum(*far)

    sizes = [width * sixteenths // 16 for sixteenths in (5, 5, 3, 3)]
    starts = [sum(sizes[:index]) for index in range(len(sizes))]
    chunk = width // 16
    weights = (gate_weight, up_weight)

    def sums_of(index, extra=0):
        shape = (half, 2 * sizes[index] + extra)
        return [(shape, f32), (shape, bf16)]

    *product, lines, stream = call(
        functools.partial(gate_up_first_kernel, chunk),
        sums_of(0, 128) + [((2 * half, features), bf16), ((group, features), f32)],
        (*sums, gain, *weights),
        [pltpu.VMEM((2, half, features), f32), pltpu.VMEM((4, 16, features), f32)],
        resident=(5, 6),
        nanos=2000,
    )
    products_made = [product]

    def more_products(index, earlier):
        return call(
            functools.partial(gate_up_more_kernel, chunk, starts[index]),
            sums_of(index),
            (lines, *weights, earlier),
            resident=(1, 2),
            free=(3,),
            nanos=0,
        )

    def pair_sum(index, earlier):
        mine, away = products_made[index]
        other = swap(away, "sec", 1)
        if index == 0:
            return call(pair_sum_first_kernel, sums_of(0, 128), (mine, other), nanos=0)
        return call(pair_sum_kernel, sums_of(index), (mine, other, earlier), free=(2,), nanos=0)

    products_made.append(more_products(1, product[1]))
    chip_sums = [pair_sum(0, None)]
    chip_sums.append(pair_sum(1, chip_sums[0][1]))
    products_made.append(more_products(2, chip_sums[1][1]))
    products_made.append(more_products(3, products_made[2][1]))
    chip_sums.append(pair_sum(2, products_made[3][1]))
    chip_sums.append(pair_sum(3, chip_sums[2][1]))
    total = [((2 * half, features), f32)]
    before = scale = None
    parts_done = []
    for index, (mine, away) in enumerate(chip_sums):
        other = swap(away, "sec", 3)
        if index == 0:
            hidden, scale = call(
                functools.partial(hidden_first_kernel, features * lax.axis_size("sec")),
                [((half, sizes[0]), bf16), ((half, 128), f32)],
                (mine, other, chip_sums[-1][1]),
                free=(2,),
                nanos=0,
            )
        else:
            earlier = parts_done[max(index - 2, 0)] if index > 1 else hidden
            (hidden,) = call(
                hidden_kernel, [((half, sizes[index]), bf16)], (mine, other, scale, earlier), free=(3,), nanos=1000
            )
        beside = swap(hidden, "sec", 1)
        if index == 0:
            (before,) = call(down_first_kernel, total, (hidden, beside, down_weight), resident=(2,), nanos=1000)
            parts_done.append(before)
        elif index < len(sizes) - 1:
            (before,) = call(
                functools.partial(down_more_kernel, starts[index]),
                total,
                (before, hidden, beside, down_weight),
                resident=(3,),
                nanos=1000,
            )
            parts_done.append(before)
        else:
            mine, *parts = call(
                functools.partial(down_last_kernel, starts[index]),
                [((group, features), f32)] + [((group, features), bf16)] * 3,
                (before, hidden, beside, down_weight),
                [pltpu.VMEM((4, 16, features), f32)],
                resident=(3,),
            )
    parts = [swap(parts[step - 1], "tp", step) for step in (3, 2, 1)]
    (out,) = call(finish_kernel, [((group, features), bf16)], (*parts, stream, mine, order))
    return out


def solution(mesh):
    small = mesh.shape["sec"] == 4 and mesh.shape["tp"] == 4
    return jax.shard_map(
        local_pairs if small else local,
        mesh=mesh,
        in_specs=(
            P(("rep", "tp"), "sec"),
            P(("rep", "tp"), "sec"),
            P(("rep", "tp"), "sec"),
            P(("rep", "sec", "tp"), None, None),
            P(("rep", "sec", "tp"), None, None),
            P(("rep", "sec", "tp")),
            P("rep"),
            P("tp", "sec"),
            P("sec"),
            P("sec", "tp"),
            P("sec", "tp"),
            P("tp", "sec"),
        ),
        out_specs=P(("rep", "tp"), "sec"),
        check_vma=False,
    )
```

```python
import functools
import math

import jax
import jax.numpy as jnp
from jax import lax
from jax.experimental import pallas as pl
from jax.experimental.pallas import tpu as pltpu
from jax.sharding import PartitionSpec as P

D = 5120
QUERY_HEADS = 40
KEY_VALUE_HEADS = 8
HEAD_WIDTH = 128
CACHE_SLOTS = 224


def attend_slots(query_rows, key_value_pairs, stored_keys, stored_values, lengths):
    cache_slots = query_rows.shape[0]
    group_query = QUERY_HEADS // KEY_VALUE_HEADS
    query_head_rows = query_rows.reshape(cache_slots, KEY_VALUE_HEADS, group_query, HEAD_WIDTH)
    paired_heads = key_value_pairs.reshape(cache_slots, KEY_VALUE_HEADS, 2, HEAD_WIDTH)
    fresh_keys = paired_heads[:, :, 0]
    fresh_values = paired_heads[:, :, 1]
    earlier_keys = stored_keys.reshape(cache_slots, CACHE_SLOTS, KEY_VALUE_HEADS, HEAD_WIDTH)
    earlier_values = stored_values.reshape(cache_slots, CACHE_SLOTS, KEY_VALUE_HEADS, HEAD_WIDTH)
    scaling = 1.0 / math.sqrt(HEAD_WIDTH)
    past_scores = (
        jnp.einsum(
            "rkgd,rlkd->rkgl", query_head_rows, earlier_keys, preferred_element_type=jnp.float32
        )
        * scaling
    )
    fresh_scores = (
        jnp.einsum("rkgd,rkd->rkg", query_head_rows, fresh_keys, preferred_element_type=jnp.float32)
        * scaling
    )
    valid = lax.broadcasted_iota(jnp.int32, (cache_slots, CACHE_SLOTS), 1) < lengths[:, None]
    past_scores = jnp.where(valid[:, None, None, :], past_scores, -1e30)
    highest = jnp.maximum(jnp.max(past_scores, axis=-1), fresh_scores)
    past_exp = jnp.exp(past_scores - highest[..., None])
    fresh_exp = jnp.exp(fresh_scores - highest)
    denominator = jnp.sum(past_exp, axis=-1) + fresh_exp
    past_weights = (past_exp / denominator[..., None]).astype(jnp.bfloat16)
    fresh_weights = (fresh_exp / denominator).astype(jnp.bfloat16)
    mixed = jnp.einsum(
        "rkgl,rlkd->rkgd", past_weights, earlier_values, preferred_element_type=jnp.float32
    )
    mixed = (
        mixed
        + fresh_weights.astype(jnp.float32)[..., None]
        * fresh_values.astype(jnp.float32)[:, :, None, :]
    )
    return mixed.reshape(cache_slots, QUERY_HEADS * HEAD_WIDTH).astype(jnp.bfloat16)


def gated_units(values, width):
    return (jax.nn.silu(values[:, :width]) * values[:, width:]).astype(jnp.bfloat16)


def received(blocks, axis):
    count = lax.axis_size(axis)
    result = [blocks[0]]
    for step in range(1, count):
        result.append(lax.ppermute(blocks[step], axis, [(i, i ^ step) for i in range(count)]))
    return result


def local(
    resid,
    query,
    new_kv,
    key_cache,
    cached_value_rows,
    cache_len,
    assign,
    out_weight,
    norm_gain,
    gate_weight,
    up_weight,
    down_weight,
):
    group = query.shape[0]
    per_device = key_cache.shape[0]
    tp_index = lax.axis_index("tp")
    sec_index = lax.axis_index("sec")
    tp_count = lax.axis_size("tp")
    sec_count = lax.axis_size("sec")
    local_slots = lax.dynamic_slice_in_dim(assign, tp_index * group, group)
    resid_f32 = resid.astype(jnp.float32)
    features = resid.shape[1]
    width = gate_weight.shape[1]
    rows = group * tp_count // sec_count

    tokens = jnp.concatenate([query, new_kv], axis=1)
    blocks = []
    for step in range(sec_count):
        wanted = (sec_index ^ step) * per_device + lax.iota(jnp.int32, per_device)
        picker = (local_slots[None, :] == wanted[:, None]).astype(jnp.bfloat16)
        blocks.append(jnp.dot(picker, tokens, preferred_element_type=jnp.float32).astype(jnp.bfloat16))
    pieces = jnp.stack(received(blocks, "sec"))
    pieces = jnp.take(pieces, sec_index ^ lax.iota(jnp.int32, sec_count), axis=0)
    my_query = pieces[:, :, : query.shape[1]].transpose(1, 0, 2).reshape(per_device, -1)
    my_pairs = pieces[:, :, query.shape[1] :].transpose(1, 0, 2).reshape(per_device, -1)
    attended = attend_slots(my_query, my_pairs, key_cache, cached_value_rows, cache_len)

    head_block = out_weight.shape[0]
    blocks = [
        lax.dynamic_slice_in_dim(attended, (tp_index ^ step) * head_block, head_block, 1)
        for step in range(tp_count)
    ]
    mine = jnp.stack(received(blocks, "tp"))
    everyone = jnp.stack(received([mine] * sec_count, "sec"))
    everyone = jnp.take(everyone, sec_index ^ lax.iota(jnp.int32, sec_count), axis=0)
    everyone = everyone.transpose(1, 0, 2, 3).reshape(tp_count, group, head_block)
    parts = jnp.dot(everyone.reshape(tp_count * group, head_block), out_weight, preferred_element_type=jnp.float32)
    parts = parts.astype(jnp.bfloat16).reshape(tp_count, group, features)
    shares = received([parts[step] for step in range(tp_count)], "tp")
    attn_out = sum(share.astype(jnp.float32) for share in shares)
    attn_out = jnp.take(attn_out, local_slots, axis=0)
    stream = resid_f32 + attn_out

    scaled = (stream * norm_gain.astype(jnp.float32)[None, :]).astype(jnp.bfloat16)
    squares = jnp.broadcast_to(jnp.sum(stream * stream, axis=1, keepdims=True), (group, 128))
    piece = jnp.concatenate(received([scaled] * tp_count, "tp"), axis=0)
    square_parts = jnp.concatenate(received([squares] * tp_count, "tp"), axis=0)
    square_parts = square_parts.reshape(sec_count, rows, 128)
    gate_part = jnp.dot(piece, gate_weight, preferred_element_type=jnp.float32)
    up_part = jnp.dot(piece, up_weight, preferred_element_type=jnp.float32)
    projected = jnp.concatenate([gate_part, up_part], axis=1).astype(jnp.bfloat16)
    projected = projected.reshape(sec_count, rows, 2 * width)
    blocks = [lax.dynamic_index_in_dim(projected, sec_index ^ step, 0, False) for step in range(sec_count)]
    share = sum(block.astype(jnp.float32) for block in received(blocks, "sec"))
    blocks = [lax.dynamic_index_in_dim(square_parts, sec_index ^ step, 0, False) for step in range(sec_count)]
    total = sum(received(blocks, "sec"))
    inverse = lax.rsqrt(total[:, :1] / D + 1e-06)
    hidden = gated_units(share * inverse, width)
    hidden = jnp.stack(received([hidden] * sec_count, "sec"))
    hidden = jnp.take(hidden, sec_index ^ lax.iota(jnp.int32, sec_count), axis=0).reshape(-1, width)
    parts = jnp.dot(hidden, down_weight, preferred_element_type=jnp.float32).astype(jnp.bfloat16)
    parts = parts.reshape(tp_count, group, features)
    shares = received([parts[step] for step in range(tp_count)], "tp")
    ff_out = sum(share.astype(jnp.float32) for share in shares)
    return (stream + ff_out).astype(jnp.bfloat16)


MIB = 1024 * 1024


def call(kernel, outs, operands, scratch=(), smem=(), resident=(), remote=(), free=(), nanos=2000, limit=8):
    specs = []
    placed = []
    for place, operand in enumerate(operands):
        space = pltpu.SMEM if place in smem else pltpu.HBM if place in remote else pltpu.VMEM
        space = pl.ANY if place in free else space
        specs.append(pl.BlockSpec(memory_space=space))
        if place in resident or place in remote:
            operand = constrained(operand, space)
        placed.append(operand)
    return pl.pallas_call(
        kernel,
        out_shape=[jax.ShapeDtypeStruct(shape, dtype) for shape, dtype in outs],
        in_specs=specs,
        out_specs=[pl.BlockSpec(memory_space=pltpu.VMEM) for _ in outs],
        scratch_shapes=list(scratch),
        compiler_params=pltpu.CompilerParams(vmem_limit_bytes=limit * MIB),
        cost_estimate=pl.CostEstimate(flops=nanos * 10**6, bytes_accessed=0, transcendentals=0),
    )(*placed)


def copy_kernel(value, earlier, out):
    out[...] = value[...]


def after(value, earlier):
    (value,) = call(copy_kernel, [(value.shape, value.dtype)], (value, earlier), free=(1,), nanos=0)
    return value


def constrained(operand, space):
    return pltpu.with_memory_space_constraint(operand, space)


def swap(value, axis, step):
    if isinstance(axis, tuple):
        count = lax.axis_size(axis[1])
        total = lax.axis_size(axis[0]) * count
        step = step[0] * count + step[1]
    else:
        total = lax.axis_size(axis)
    return lax.ppermute(value, axis, [(i, i ^ step) for i in range(total)])


def group_slots(group, assign):
    tp = lax.axis_index("tp")
    slots = jnp.zeros((1, group), jnp.int32)
    for index in range(assign.shape[1] // group):
        slots = jnp.where(tp == index, assign[:, index * group : (index + 1) * group], slots)
    return slots


def slot_picker(per_device, slots):
    sec = lax.axis_index("sec")
    group = slots.shape[1]
    line = lax.broadcasted_iota(jnp.int32, (16, group), 0)
    wanted = jnp.where(line < 8, sec * per_device + line, (sec ^ 3) * per_device + line - 8)
    inside = (line & 7) < per_device
    return jnp.where(inside & (jnp.broadcast_to(slots, (16, group)) == wanted), 1.0, 0.0).astype(jnp.bfloat16)


def split_heads(per_device, picker, query, pairs, rows):
    queries = jnp.dot(picker, query[...], preferred_element_type=jnp.float32)
    others = jnp.dot(picker, pairs[...], preferred_element_type=jnp.float32)
    width = HEAD_WIDTH
    heads = query.shape[1] // width
    rows[...] = jnp.zeros_like(rows)
    for side in range(2):
        for j in range(per_device):
            line = side * 8 + j
            for h in range(heads):
                rows[side, j * 16 + h : j * 16 + h + 1, :] = queries[line : line + 1, h * width : (h + 1) * width]
            for h in range(pairs.shape[1] // width):
                at = j * 16 + heads + h
                rows[side, at : at + 1, :] = others[line : line + 1, h * width : (h + 1) * width]


def pick_own_kernel(
    per_device, group, query, pairs, assign, out, picker, query_here, pairs_here, assign_here, rows, sems
):
    copies = [
        pltpu.make_async_copy(source, target, sems.at[index])
        for index, (source, target) in enumerate(
            ((query, query_here), (pairs, pairs_here), (assign, assign_here))
        )
    ]
    for copy in copies:
        copy.start()
    copies[2].wait()
    picker[...] = slot_picker(per_device, group_slots(group, assign_here))
    copies[0].wait()
    copies[1].wait()
    split_heads(per_device, picker[...], query_here, pairs_here, rows)
    out[...] = rows[...].astype(jnp.bfloat16)


def pick_other_kernel(per_device, own, picker, query, pairs, keep, send, rows):
    split_heads(per_device, picker[...], query, pairs, rows)
    here = lax.axis_index("sec") & 1
    keep[here] = own[0]
    keep[1 - here] = rows[0].astype(jnp.bfloat16)
    send[here] = own[1]
    send[1 - here] = rows[1].astype(jnp.bfloat16)


def attend_blocks(per_device, heads, lengths, chip, source, keys, values, target, first):
    share = heads // 2
    slots = keys.shape[1]
    width = HEAD_WIDTH
    scaling = 1.0 / math.sqrt(width)
    line = lax.broadcasted_iota(jnp.int32, (16, width), 0)
    upper = line < share
    place = lax.broadcasted_iota(jnp.int32, (16, slots), 1)
    work = [(i, j) for i in range(2) for j in range(per_device)]
    past, fresh, new_values, columns = [], [], [], []
    for i, j in work:
        wide = source[i, j * 16 : (j + 1) * 16].astype(jnp.float32)
        zero = jnp.zeros_like(wide)
        both = jnp.concatenate([jnp.where(upper, wide, zero), jnp.where(upper, zero, wide)], axis=1)
        column = pl.ds(pl.multiple_of((2 * chip + i) * 2 * width, 2 * width), 2 * width)
        columns.append(column)
        scores = lax.dot_general(
            both.astype(jnp.bfloat16),
            keys[j, :, column],
            (((1,), (1,)), ((), ())),
            preferred_element_type=jnp.float32,
        )
        past.append(jnp.where(place < lengths[j], scores * scaling, -1e30))
        new_key = jnp.where(upper, wide[heads : heads + 1], wide[heads + 2 : heads + 3])
        new_values.append(jnp.where(upper, wide[heads + 1 : heads + 2], wide[heads + 3 : heads + 4]))
        fresh.append(wide * new_key)
    past = jnp.concatenate(past, axis=0)
    fresh = jnp.sum(jnp.concatenate(fresh, axis=0), axis=1, keepdims=True) * scaling
    highest = jnp.maximum(jnp.max(past, axis=1, keepdims=True), fresh)
    past_exp = jnp.exp(past - highest)
    fresh_exp = jnp.exp(fresh - highest)
    inverse = 1.0 / (jnp.sum(past_exp, axis=1, keepdims=True) + fresh_exp)
    weights = (past_exp * inverse).astype(jnp.bfloat16)
    fresh_weight = (fresh_exp * inverse).astype(jnp.bfloat16).astype(jnp.float32)
    for index, (i, j) in enumerate(work):
        lines = slice(index * 16, (index + 1) * 16)
        mixed = jnp.dot(weights[lines], values[j, :, columns[index]], preferred_element_type=jnp.float32)
        mixed = jnp.where(upper, mixed[:, :width], mixed[:, width:]) + fresh_weight[lines] * new_values[index]
        for h in range(heads):
            target[first + i, j : j + 1, h * width : (h + 1) * width] = mixed[h : h + 1]


def attend_near_kernel(per_device, heads, lengths, source, keys, values, assign, out, order):
    group = order.shape[0]
    slots = jnp.broadcast_to(group_slots(group, assign), (group, group))
    line = lax.broadcasted_iota(jnp.int32, (group, group), 0)
    match = jnp.where(line == slots, 1.0, 0.0).astype(jnp.bfloat16)
    line = lax.broadcasted_iota(jnp.int32, order.shape, 0)
    same = line == (lax.broadcasted_iota(jnp.int32, order.shape, 1) & 15)
    same = jnp.where(same, 1.0, 0.0).astype(jnp.bfloat16)
    order[...] = lax.dot_general(
        match, same, (((0,), (0,)), ((), ())), preferred_element_type=jnp.float32
    ).astype(jnp.bfloat16)
    out[...] = jnp.zeros_like(out)
    attend_blocks(per_device, heads, lengths, lax.axis_index("sec") >> 1, source, keys, values, out, 0)


def attend_far_kernel(per_device, heads, lengths, source, near, keys, values, own, first, second, third, total):
    chip = lax.axis_index("sec") >> 1
    tp = lax.axis_index("tp")
    total[...] = jnp.zeros_like(total)
    total[2 * chip] = near[0]
    total[2 * chip + 1] = near[1]
    attend_blocks(per_device, heads, lengths, 1 - chip, source, keys, values, total, 2 * (1 - chip))
    for step, target in enumerate((own, first, second, third)):
        target[...] = total[tp ^ step, 0:4].astype(jnp.bfloat16)


def gather_kernel(third, second, first, own, out, rows):
    for step, part in enumerate((own, first, second, third)):
        rows[4 * step : 4 * step + 4] = part[...].astype(jnp.float32)
    out[...] = rows[...].astype(jnp.bfloat16)


def slot_rows(far, per_device, count):
    sec, tp = lax.axis_index("sec"), lax.axis_index("tp")
    share = 2 * per_device
    shape = (count, 32)
    line = lax.broadcasted_iota(jnp.int32, shape, 1)
    place, index = (line >> 2) & 3, line & 3
    from_sec = sec ^ (3 * far) ^ (line >> 4) ^ jnp.where(place > 0, 1, 0)
    row = (tp ^ place) * share + (from_sec & 1) * per_device + index
    match = (lax.broadcasted_iota(jnp.int32, shape, 0) == row) & (index < per_device)
    return jnp.where(match, 1.0, 0.0).astype(jnp.bfloat16)


def resid_rows(far, per_device, count, assign, resid):
    sec, tp = lax.axis_index("sec"), lax.axis_index("tp")
    share = 2 * per_device
    group = resid.shape[0]
    chip = (sec ^ (3 * far)) >> 1
    slots = jnp.broadcast_to(group_slots(group, assign), (count, group)) - share * chip
    match = lax.broadcasted_iota(jnp.int32, (count, group), 0) == slots + tp * share
    match = jnp.where(match & (slots >= 0) & (slots < share), 1.0, 0.0).astype(jnp.bfloat16)
    return jnp.dot(match, resid[...], preferred_element_type=jnp.float32)


def project(match, first, second, resid, weight, keep, send):
    lines = jnp.concatenate([first[...], second[...]], axis=0)
    ordered = jnp.dot(match, lines, preferred_element_type=jnp.float32).astype(jnp.bfloat16)
    total = resid + jnp.dot(ordered, weight[...], preferred_element_type=jnp.float32)
    keep[...] = total
    send[...] = total.astype(jnp.bfloat16)


def project_near_kernel(per_device, first, second, assign, resid, weight, keep, send, far_match, far_resid):
    count = keep.shape[0]
    near = resid_rows(0, per_device, count, assign, resid)
    project(slot_rows(0, per_device, count), first, second, near, weight, keep, send)
    far_match[...] = slot_rows(1, per_device, count)
    far_resid[...] = resid_rows(1, per_device, count, assign, resid)


def project_far_kernel(first, second, match, resid, weight, keep, send):
    project(match[...], first, second, resid[...], weight, keep, send)


def add_kernel(mine, other, keep, send):
    total = mine[...] + other[...].astype(jnp.float32)
    keep[...] = total
    send[...] = total.astype(jnp.bfloat16)


def row_half():
    sec = lax.axis_index("sec")
    return (sec ^ (sec >> 1)) & 1


def products(features, gate, up, unit, units, chunk, keep, send):
    half = keep.shape[0]
    for kind, weight in enumerate((gate, up)):
        for start in range(0, units, chunk):
            column = slice(unit + start, unit + start + chunk)
            product = jnp.dot(features, weight[:, column], preferred_element_type=jnp.float32)
            at = kind * units + start
            keep[:, at : at + chunk] = product[:half]
            send[:, at : at + chunk] = product[half:].astype(jnp.bfloat16)


def to_groups(first, second, groups):
    share = first.shape[0] // groups.shape[0]
    for index in range(groups.shape[0]):
        lines = slice(index * share, (index + 1) * share)
        groups[index, 0:share] = first[lines]
        groups[index, share : 2 * share] = second[lines]


def gate_up_first_kernel(
    chunk, near, near_other, far, far_other, gain, gate, up, keep, send, features, stream, halves, groups
):
    sec, tp = lax.axis_index("sec"), lax.axis_index("tp")
    chip = sec >> 1
    half = near.shape[0]
    halves[chip] = near[...] + near_other[...].astype(jnp.float32)
    halves[1 - chip] = far[...] + far_other[...].astype(jnp.float32)
    to_groups(halves[0], halves[1], groups)
    stream[...] = groups[tp, 0 : stream.shape[0]]
    first = row_half()
    total = jnp.concatenate([halves[first], halves[1 - first]], axis=0)
    squares = jnp.sum(total * total, axis=1, keepdims=True)
    scaled = (total * gain[...].astype(jnp.float32)).astype(jnp.bfloat16)
    features[...] = scaled
    units = (keep.shape[1] - 128) // 2
    products(scaled, gate, up, 0, units, chunk, keep, send)
    keep[:, 2 * units :] = jnp.broadcast_to(squares[:half], (half, 128))
    send[:, 2 * units :] = two_terms(squares[half:])


def gate_up_more_kernel(chunk, unit, features, gate, up, earlier, keep, send):
    products(features[...], gate, up, unit, keep.shape[1] // 2, chunk, keep, send)


def two_terms(column):
    shape = (column.shape[0], 128)
    column = jnp.broadcast_to(column, shape)
    coarse = column.astype(jnp.bfloat16).astype(jnp.float32)
    lane = lax.broadcasted_iota(jnp.int32, shape, 1)
    return jnp.where(lane < 64, coarse, column - coarse).astype(jnp.bfloat16)


def one_column(terms):
    return terms[:, 0:1].astype(jnp.float32) + terms[:, 64:65].astype(jnp.float32)


def pair_sum_first_kernel(mine, other, keep, send):
    width = mine.shape[1] - 128
    total = mine[:, :width] + other[:, :width].astype(jnp.float32)
    both = mine[:, width:] + one_column(other[:, width:])
    keep[:, :width] = total
    keep[:, width:] = both
    send[:, :width] = total.astype(jnp.bfloat16)
    send[:, width:] = two_terms(both[:, 0:1])


def pair_sum_kernel(mine, other, earlier, keep, send):
    total = mine[...] + other[...].astype(jnp.float32)
    keep[...] = total
    send[...] = total.astype(jnp.bfloat16)


def gated(mine, other, factor, hidden):
    width = hidden.shape[1]
    gate = (mine[:, :width] + other[:, :width].astype(jnp.float32)) * factor
    up = (mine[:, width : 2 * width] + other[:, width : 2 * width].astype(jnp.float32)) * factor
    hidden[...] = (gate / (1.0 + jnp.exp(-gate)) * up).astype(jnp.bfloat16)


def hidden_first_kernel(features, mine, other, earlier, hidden, scale):
    width = mine.shape[1] - 128
    total = mine[:, width : width + 1] + one_column(other[:, width:])
    factor = lax.rsqrt(total / features + 1e-06)
    scale[...] = jnp.broadcast_to(factor, scale.shape)
    gated(mine, other, factor, hidden)


def hidden_kernel(mine, other, scale, earlier, hidden):
    gated(mine, other, scale[:, 0:1], hidden)


def down_product(unit, mine, other, weight):
    lines = jnp.concatenate([mine[...].astype(jnp.float32), other[...].astype(jnp.float32)], axis=0)
    rows = weight[unit : unit + lines.shape[1], :]
    return jnp.dot(lines.astype(jnp.bfloat16), rows, preferred_element_type=jnp.float32)


def down_first_kernel(mine, other, weight, out):
    out[...] = down_product(0, mine, other, weight)


def down_more_kernel(unit, before, mine, other, weight, out):
    out[...] = before[...] + down_product(unit, mine, other, weight)


def down_last_kernel(unit, before, mine, other, weight, keep, first, second, third, groups):
    tp = lax.axis_index("tp")
    product = before[...] + down_product(unit, mine, other, weight)
    group = keep.shape[0]
    half = product.shape[0] // 2
    swapped = row_half() == 1
    lower, upper = product[:half], product[half:]
    to_groups(jnp.where(swapped, upper, lower), jnp.where(swapped, lower, upper), groups)
    keep[...] = groups[tp, 0:group]
    for step, target in enumerate((first, second, third)):
        part = groups[tp ^ (step + 1), 0:group]
        columns = target.shape[1]
        target[...] = jnp.concatenate([part[:, :columns], part[:, columns:]], axis=0).astype(jnp.bfloat16)


def finish_kernel(third, second, first, stream, mine, order, out, terms):
    total = stream[...] + mine[...]
    group = out.shape[0]
    for other in (first, second, third):
        halves = other[...].astype(jnp.float32)
        total = total + jnp.concatenate([halves[:group], halves[group:]], axis=1)
    coarse = total.astype(jnp.bfloat16).astype(jnp.float32)
    terms[...] = jnp.zeros_like(terms)
    terms[0:group] = coarse
    terms[16 : 16 + group] = total - coarse
    ordered = jnp.dot(order[...], terms[...].astype(jnp.bfloat16), preferred_element_type=jnp.float32)
    out[...] = ordered.astype(jnp.bfloat16)


def local_pairs(
    resid,
    query,
    new_kv,
    key_cache,
    cached_value_rows,
    cache_len,
    assign,
    out_weight,
    norm_gain,
    gate_weight,
    up_weight,
    down_weight,
):
    f32, bf16 = jnp.float32, jnp.bfloat16
    group, features = resid.shape
    per_device = key_cache.shape[0]
    heads = query.shape[1] // HEAD_WIDTH
    head_block = out_weight.shape[0]
    width = gate_weight.shape[1]
    half = 2 * group
    assign = assign.reshape(1, -1)
    gain = norm_gain.reshape(1, -1)

    query_b, pairs_b = swap(query, "sec", 1), swap(new_kv, "sec", 1)
    block = (2, 16 * per_device, HEAD_WIDTH)
    own, picker = call(
        functools.partial(pick_own_kernel, per_device, group),
        [(block, bf16), ((16, group), bf16)],
        (query, new_kv, assign),
        [
            pltpu.VMEM(query.shape, bf16),
            pltpu.VMEM(new_kv.shape, bf16),
            pltpu.VMEM(assign.shape, jnp.int32),
            pltpu.VMEM(block, f32),
            pltpu.SemaphoreType.DMA((3,)),
        ],
        remote=(0, 1, 2),
    )
    mine, away = call(
        functools.partial(pick_other_kernel, per_device),
        [(block, bf16)] * 2,
        (own, picker, query_b, pairs_b),
        [pltpu.VMEM(block, f32)],
    )
    other = swap(away, "sec", 3)
    caches = (key_cache, cached_value_rows)
    near, order = call(
        functools.partial(attend_near_kernel, per_device, heads),
        [((2, 4, head_block), f32), ((group, 32), bf16)],
        (cache_len, mine, *caches, assign),
        smem=(0,),
        resident=(2, 3),
    )
    own, *parts = call(
        functools.partial(attend_far_kernel, per_device, heads),
        [((4, head_block), bf16)] * 4,
        (cache_len, other, near, *caches),
        [pltpu.VMEM((4, 4, head_block), f32)],
        smem=(0,),
        resident=(3, 4),
    )

    parts = [swap(parts[step - 1], ("sec", "tp"), (1, step)) for step in (3, 2, 1)]
    (own,) = call(gather_kernel, [((16, head_block), bf16)], (*parts, own), [pltpu.VMEM((16, head_block), f32)])
    across = swap(own, "sec", 3)
    beside = swap(own, "sec", 1)

    pair = [((half, features), f32), ((half, features), bf16)]

    def tp_sum(mine, away):
        mine, away = call(add_kernel, pair, (mine, swap(away, "tp", 1)))
        return mine, swap(away, "tp", 2)

    *near, match, rows = call(
        functools.partial(project_near_kernel, per_device),
        pair + [((half, 32), bf16), ((half, features), f32)],
        (own, beside, assign, resid, out_weight),
        resident=(4,),
    )
    corner = swap(after(across, near[1]), "sec", 1)
    far = call(project_far_kernel, pair, (across, corner, match, rows, out_weight), resident=(4,), nanos=0)
    sums = tp_sum(*near) + tp_sum(*far)

    sizes = [width * sixteenths // 16 for sixteenths in (5, 5, 3, 3)]
    starts = [sum(sizes[:index]) for index in range(len(sizes))]
    chunk = width // 16
    weights = (gate_weight, up_weight)

    def sums_of(index, extra=0):
        shape = (half, 2 * sizes[index] + extra)
        return [(shape, f32), (shape, bf16)]

    *product, lines, stream = call(
        functools.partial(gate_up_first_kernel, chunk),
        sums_of(0, 128) + [((2 * half, features), bf16), ((group, features), f32)],
        (*sums, gain, *weights),
        [pltpu.VMEM((2, half, features), f32), pltpu.VMEM((4, 16, features), f32)],
        resident=(5, 6),
        nanos=2000,
    )
    products_made = [product]

    def more_products(index, earlier):
        return call(
            functools.partial(gate_up_more_kernel, chunk, starts[index]),
            sums_of(index),
            (lines, *weights, earlier),
            resident=(1, 2),
            free=(3,),
            nanos=0,
        )

    def pair_sum(index, earlier):
        mine, away = products_made[index]
        other = swap(away, "sec", 1)
        if index == 0:
            return call(pair_sum_first_kernel, sums_of(0, 128), (mine, other), nanos=0)
        return call(pair_sum_kernel, sums_of(index), (mine, other, earlier), free=(2,), nanos=0)

    products_made.append(more_products(1, product[1]))
    chip_sums = [pair_sum(0, None)]
    chip_sums.append(pair_sum(1, chip_sums[0][1]))
    products_made.append(more_products(2, chip_sums[1][1]))
    products_made.append(more_products(3, products_made[2][1]))
    chip_sums.append(pair_sum(2, products_made[3][1]))
    chip_sums.append(pair_sum(3, chip_sums[2][1]))
    total = [((2 * half, features), f32)]
    before = scale = None
    parts_done = []
    for index, (mine, away) in enumerate(chip_sums):
        other = swap(away, "sec", 3)
        if index == 0:
            hidden, scale = call(
                functools.partial(hidden_first_kernel, features * lax.axis_size("sec")),
                [((half, sizes[0]), bf16), ((half, 128), f32)],
                (mine, other, chip_sums[-1][1]),
                free=(2,),
                nanos=0,
            )
        else:
            earlier = parts_done[max(index - 2, 0)] if index > 1 else hidden
            (hidden,) = call(
                hidden_kernel, [((half, sizes[index]), bf16)], (mine, other, scale, earlier), free=(3,), nanos=1000
            )
        beside = swap(hidden, "sec", 1)
        if index == 0:
            (before,) = call(down_first_kernel, total, (hidden, beside, down_weight), resident=(2,), nanos=1000)
            parts_done.append(before)
        elif index < len(sizes) - 1:
            (before,) = call(
                functools.partial(down_more_kernel, starts[index]),
                total,
                (before, hidden, beside, down_weight),
                resident=(3,),
                nanos=1000,
            )
            parts_done.append(before)
        else:
            mine, *parts = call(
                functools.partial(down_last_kernel, starts[index]),
                [((group, features), f32)] + [((half, features // 2), bf16)] * 3,
                (before, hidden, beside, down_weight),
                [pltpu.VMEM((4, 16, features), f32)],
                resident=(3,),
            )
    parts = [swap(parts[step - 1], "tp", step) for step in (3, 2, 1)]
    (out,) = call(
        finish_kernel,
        [((group, features), bf16)],
        (*parts, stream, mine, order),
        [pltpu.VMEM((32, features), f32)],
    )
    return out


def solution(mesh):
    small = mesh.shape["sec"] == 4 and mesh.shape["tp"] == 4
    return jax.shard_map(
        local_pairs if small else local,
        mesh=mesh,
        in_specs=(
            P(("rep", "tp"), "sec"),
            P(("rep", "tp"), "sec"),
            P(("rep", "tp"), "sec"),
            P(("rep", "sec", "tp"), None, None),
            P(("rep", "sec", "tp"), None, None),
            P(("rep", "sec", "tp")),
            P("rep"),
            P("tp", "sec"),
            P("sec"),
            P("sec", "tp"),
            P("sec", "tp"),
            P("tp", "sec"),
        ),
        out_specs=P(("rep", "tp"), "sec"),
        check_vma=False,
    )
```

```python
import functools
import math

import jax
import jax.numpy as jnp
from jax import lax
from jax.experimental import pallas as pl
from jax.experimental.pallas import tpu as pltpu
from jax.sharding import PartitionSpec as P

D = 5120
QUERY_HEADS = 40
KEY_VALUE_HEADS = 8
HEAD_WIDTH = 128
CACHE_SLOTS = 224


def attend_slots(query_rows, key_value_pairs, stored_keys, stored_values, lengths):
    cache_slots = query_rows.shape[0]
    group_query = QUERY_HEADS // KEY_VALUE_HEADS
    query_head_rows = query_rows.reshape(cache_slots, KEY_VALUE_HEADS, group_query, HEAD_WIDTH)
    paired_heads = key_value_pairs.reshape(cache_slots, KEY_VALUE_HEADS, 2, HEAD_WIDTH)
    fresh_keys = paired_heads[:, :, 0]
    fresh_values = paired_heads[:, :, 1]
    earlier_keys = stored_keys.reshape(cache_slots, CACHE_SLOTS, KEY_VALUE_HEADS, HEAD_WIDTH)
    earlier_values = stored_values.reshape(cache_slots, CACHE_SLOTS, KEY_VALUE_HEADS, HEAD_WIDTH)
    scaling = 1.0 / math.sqrt(HEAD_WIDTH)
    past_scores = (
        jnp.einsum(
            "rkgd,rlkd->rkgl", query_head_rows, earlier_keys, preferred_element_type=jnp.float32
        )
        * scaling
    )
    fresh_scores = (
        jnp.einsum("rkgd,rkd->rkg", query_head_rows, fresh_keys, preferred_element_type=jnp.float32)
        * scaling
    )
    valid = lax.broadcasted_iota(jnp.int32, (cache_slots, CACHE_SLOTS), 1) < lengths[:, None]
    past_scores = jnp.where(valid[:, None, None, :], past_scores, -1e30)
    highest = jnp.maximum(jnp.max(past_scores, axis=-1), fresh_scores)
    past_exp = jnp.exp(past_scores - highest[..., None])
    fresh_exp = jnp.exp(fresh_scores - highest)
    denominator = jnp.sum(past_exp, axis=-1) + fresh_exp
    past_weights = (past_exp / denominator[..., None]).astype(jnp.bfloat16)
    fresh_weights = (fresh_exp / denominator).astype(jnp.bfloat16)
    mixed = jnp.einsum(
        "rkgl,rlkd->rkgd", past_weights, earlier_values, preferred_element_type=jnp.float32
    )
    mixed = (
        mixed
        + fresh_weights.astype(jnp.float32)[..., None]
        * fresh_values.astype(jnp.float32)[:, :, None, :]
    )
    return mixed.reshape(cache_slots, QUERY_HEADS * HEAD_WIDTH).astype(jnp.bfloat16)


def gated_units(values, width):
    return (jax.nn.silu(values[:, :width]) * values[:, width:]).astype(jnp.bfloat16)


def received(blocks, axis):
    count = lax.axis_size(axis)
    result = [blocks[0]]
    for step in range(1, count):
        result.append(lax.ppermute(blocks[step], axis, [(i, i ^ step) for i in range(count)]))
    return result


def local(
    resid,
    query,
    new_kv,
    key_cache,
    cached_value_rows,
    cache_len,
    assign,
    out_weight,
    norm_gain,
    gate_weight,
    up_weight,
    down_weight,
):
    group = query.shape[0]
    per_device = key_cache.shape[0]
    tp_index = lax.axis_index("tp")
    sec_index = lax.axis_index("sec")
    tp_count = lax.axis_size("tp")
    sec_count = lax.axis_size("sec")
    local_slots = lax.dynamic_slice_in_dim(assign, tp_index * group, group)
    resid_f32 = resid.astype(jnp.float32)
    features = resid.shape[1]
    width = gate_weight.shape[1]
    rows = group * tp_count // sec_count

    tokens = jnp.concatenate([query, new_kv], axis=1)
    blocks = []
    for step in range(sec_count):
        wanted = (sec_index ^ step) * per_device + lax.iota(jnp.int32, per_device)
        picker = (local_slots[None, :] == wanted[:, None]).astype(jnp.bfloat16)
        blocks.append(jnp.dot(picker, tokens, preferred_element_type=jnp.float32).astype(jnp.bfloat16))
    pieces = jnp.stack(received(blocks, "sec"))
    pieces = jnp.take(pieces, sec_index ^ lax.iota(jnp.int32, sec_count), axis=0)
    my_query = pieces[:, :, : query.shape[1]].transpose(1, 0, 2).reshape(per_device, -1)
    my_pairs = pieces[:, :, query.shape[1] :].transpose(1, 0, 2).reshape(per_device, -1)
    attended = attend_slots(my_query, my_pairs, key_cache, cached_value_rows, cache_len)

    head_block = out_weight.shape[0]
    blocks = [
        lax.dynamic_slice_in_dim(attended, (tp_index ^ step) * head_block, head_block, 1)
        for step in range(tp_count)
    ]
    mine = jnp.stack(received(blocks, "tp"))
    everyone = jnp.stack(received([mine] * sec_count, "sec"))
    everyone = jnp.take(everyone, sec_index ^ lax.iota(jnp.int32, sec_count), axis=0)
    everyone = everyone.transpose(1, 0, 2, 3).reshape(tp_count, group, head_block)
    parts = jnp.dot(everyone.reshape(tp_count * group, head_block), out_weight, preferred_element_type=jnp.float32)
    parts = parts.astype(jnp.bfloat16).reshape(tp_count, group, features)
    shares = received([parts[step] for step in range(tp_count)], "tp")
    attn_out = sum(share.astype(jnp.float32) for share in shares)
    attn_out = jnp.take(attn_out, local_slots, axis=0)
    stream = resid_f32 + attn_out

    scaled = (stream * norm_gain.astype(jnp.float32)[None, :]).astype(jnp.bfloat16)
    squares = jnp.broadcast_to(jnp.sum(stream * stream, axis=1, keepdims=True), (group, 128))
    piece = jnp.concatenate(received([scaled] * tp_count, "tp"), axis=0)
    square_parts = jnp.concatenate(received([squares] * tp_count, "tp"), axis=0)
    square_parts = square_parts.reshape(sec_count, rows, 128)
    gate_part = jnp.dot(piece, gate_weight, preferred_element_type=jnp.float32)
    up_part = jnp.dot(piece, up_weight, preferred_element_type=jnp.float32)
    projected = jnp.concatenate([gate_part, up_part], axis=1).astype(jnp.bfloat16)
    projected = projected.reshape(sec_count, rows, 2 * width)
    blocks = [lax.dynamic_index_in_dim(projected, sec_index ^ step, 0, False) for step in range(sec_count)]
    share = sum(block.astype(jnp.float32) for block in received(blocks, "sec"))
    blocks = [lax.dynamic_index_in_dim(square_parts, sec_index ^ step, 0, False) for step in range(sec_count)]
    total = sum(received(blocks, "sec"))
    inverse = lax.rsqrt(total[:, :1] / D + 1e-06)
    hidden = gated_units(share * inverse, width)
    hidden = jnp.stack(received([hidden] * sec_count, "sec"))
    hidden = jnp.take(hidden, sec_index ^ lax.iota(jnp.int32, sec_count), axis=0).reshape(-1, width)
    parts = jnp.dot(hidden, down_weight, preferred_element_type=jnp.float32).astype(jnp.bfloat16)
    parts = parts.reshape(tp_count, group, features)
    shares = received([parts[step] for step in range(tp_count)], "tp")
    ff_out = sum(share.astype(jnp.float32) for share in shares)
    return (stream + ff_out).astype(jnp.bfloat16)


MIB = 1024 * 1024


def call(kernel, outs, operands, scratch=(), smem=(), resident=(), remote=(), free=(), nanos=2000, limit=8):
    specs = []
    placed = []
    for place, operand in enumerate(operands):
        space = pltpu.SMEM if place in smem else pltpu.HBM if place in remote else pltpu.VMEM
        space = pl.ANY if place in free else space
        specs.append(pl.BlockSpec(memory_space=space))
        if place in resident or place in remote:
            operand = constrained(operand, space)
        placed.append(operand)
    return pl.pallas_call(
        kernel,
        out_shape=[jax.ShapeDtypeStruct(shape, dtype) for shape, dtype in outs],
        in_specs=specs,
        out_specs=[pl.BlockSpec(memory_space=pltpu.VMEM) for _ in outs],
        scratch_shapes=list(scratch),
        compiler_params=pltpu.CompilerParams(vmem_limit_bytes=limit * MIB),
        cost_estimate=pl.CostEstimate(flops=nanos * 10**6, bytes_accessed=0, transcendentals=0),
    )(*placed)


def copy_kernel(value, earlier, out):
    out[...] = value[...]


def after(value, earlier):
    (value,) = call(copy_kernel, [(value.shape, value.dtype)], (value, earlier), free=(1,), nanos=0)
    return value


def constrained(operand, space):
    return pltpu.with_memory_space_constraint(operand, space)


def swap(value, axis, step):
    if isinstance(axis, tuple):
        count = lax.axis_size(axis[1])
        total = lax.axis_size(axis[0]) * count
        step = step[0] * count + step[1]
    else:
        total = lax.axis_size(axis)
    return lax.ppermute(value, axis, [(i, i ^ step) for i in range(total)])


def group_slots(group, assign):
    tp = lax.axis_index("tp")
    slots = jnp.zeros((1, group), jnp.int32)
    for index in range(assign.shape[1] // group):
        slots = jnp.where(tp == index, assign[:, index * group : (index + 1) * group], slots)
    return slots


def slot_picker(per_device, slots):
    sec = lax.axis_index("sec")
    group = slots.shape[1]
    line = lax.broadcasted_iota(jnp.int32, (16, group), 0)
    wanted = jnp.where(line < 8, sec * per_device + line, (sec ^ 3) * per_device + line - 8)
    inside = (line & 7) < per_device
    return jnp.where(inside & (jnp.broadcast_to(slots, (16, group)) == wanted), 1.0, 0.0).astype(jnp.bfloat16)


def split_heads(per_device, picker, query, pairs, rows):
    queries = jnp.dot(picker, query[...], preferred_element_type=jnp.float32)
    others = jnp.dot(picker, pairs[...], preferred_element_type=jnp.float32)
    width = HEAD_WIDTH
    heads = query.shape[1] // width
    rows[...] = jnp.zeros_like(rows)
    for side in range(2):
        for j in range(per_device):
            line = side * 8 + j
            for h in range(heads):
                rows[side, j * 16 + h : j * 16 + h + 1, :] = queries[line : line + 1, h * width : (h + 1) * width]
            for h in range(pairs.shape[1] // width):
                at = j * 16 + heads + h
                rows[side, at : at + 1, :] = others[line : line + 1, h * width : (h + 1) * width]


def pick_own_kernel(
    per_device, group, query, pairs, assign, out, picker, query_here, pairs_here, assign_here, rows, sems
):
    copies = [
        pltpu.make_async_copy(source, target, sems.at[index])
        for index, (source, target) in enumerate(
            ((query, query_here), (pairs, pairs_here), (assign, assign_here))
        )
    ]
    for copy in copies:
        copy.start()
    copies[2].wait()
    picker[...] = slot_picker(per_device, group_slots(group, assign_here))
    copies[0].wait()
    copies[1].wait()
    split_heads(per_device, picker[...], query_here, pairs_here, rows)
    out[...] = rows[...].astype(jnp.bfloat16)


def pick_other_kernel(per_device, own, picker, query, pairs, keep, send, rows):
    split_heads(per_device, picker[...], query, pairs, rows)
    here = lax.axis_index("sec") & 1
    keep[here] = own[0]
    keep[1 - here] = rows[0].astype(jnp.bfloat16)
    send[here] = own[1]
    send[1 - here] = rows[1].astype(jnp.bfloat16)


def attend_blocks(per_device, heads, lengths, chip, source, keys, values, target, first):
    share = heads // 2
    slots = keys.shape[1]
    width = HEAD_WIDTH
    scaling = 1.0 / math.sqrt(width)
    line = lax.broadcasted_iota(jnp.int32, (16, width), 0)
    upper = line < share
    place = lax.broadcasted_iota(jnp.int32, (16, slots), 1)
    work = [(i, j) for i in range(2) for j in range(per_device)]
    past, fresh, new_values, columns = [], [], [], []
    for i, j in work:
        wide = source[i, j * 16 : (j + 1) * 16].astype(jnp.float32)
        zero = jnp.zeros_like(wide)
        both = jnp.concatenate([jnp.where(upper, wide, zero), jnp.where(upper, zero, wide)], axis=1)
        column = pl.ds(pl.multiple_of((2 * chip + i) * 2 * width, 2 * width), 2 * width)
        columns.append(column)
        scores = lax.dot_general(
            both.astype(jnp.bfloat16),
            keys[j, :, column],
            (((1,), (1,)), ((), ())),
            preferred_element_type=jnp.float32,
        )
        past.append(jnp.where(place < lengths[j], scores * scaling, -1e30))
        new_key = jnp.where(upper, wide[heads : heads + 1], wide[heads + 2 : heads + 3])
        new_values.append(jnp.where(upper, wide[heads + 1 : heads + 2], wide[heads + 3 : heads + 4]))
        fresh.append(wide * new_key)
    past = jnp.concatenate(past, axis=0)
    fresh = jnp.sum(jnp.concatenate(fresh, axis=0), axis=1, keepdims=True) * scaling
    highest = jnp.maximum(jnp.max(past, axis=1, keepdims=True), fresh)
    past_exp = jnp.exp(past - highest)
    fresh_exp = jnp.exp(fresh - highest)
    inverse = 1.0 / (jnp.sum(past_exp, axis=1, keepdims=True) + fresh_exp)
    weights = (past_exp * inverse).astype(jnp.bfloat16)
    fresh_weight = (fresh_exp * inverse).astype(jnp.bfloat16).astype(jnp.float32)
    for index, (i, j) in enumerate(work):
        lines = slice(index * 16, (index + 1) * 16)
        mixed = jnp.dot(weights[lines], values[j, :, columns[index]], preferred_element_type=jnp.float32)
        mixed = jnp.where(upper, mixed[:, :width], mixed[:, width:]) + fresh_weight[lines] * new_values[index]
        for h in range(heads):
            target[first + i, j : j + 1, h * width : (h + 1) * width] = mixed[h : h + 1]


def attend_near_kernel(per_device, heads, lengths, source, keys, values, assign, out, order):
    group = order.shape[0] // 2
    slots = jnp.broadcast_to(group_slots(group, assign), (group, group))
    line = lax.broadcasted_iota(jnp.int32, (group, group), 0)
    match = jnp.where(line == slots, 1.0, 0.0).astype(jnp.bfloat16)
    shape = (group, order.shape[1])
    column = lax.broadcasted_iota(jnp.int32, shape, 1) & 31
    column = jnp.where(column < group, column, jnp.where(column < 2 * group, column - group, group))
    same = jnp.where(lax.broadcasted_iota(jnp.int32, shape, 0) == column, 1.0, 0.0).astype(jnp.bfloat16)
    ordered = lax.dot_general(match, same, (((0,), (0,)), ((), ())), preferred_element_type=jnp.float32)
    line = lax.broadcasted_iota(jnp.int32, (2 * group, group), 0)
    line = jnp.where(line < group, line, line - group)
    twice = jnp.where(line == lax.broadcasted_iota(jnp.int32, (2 * group, group), 1), 1.0, 0.0).astype(jnp.bfloat16)
    ordered = jnp.dot(twice, ordered.astype(jnp.bfloat16), preferred_element_type=jnp.float32)
    lower = lax.broadcasted_iota(jnp.int32, order.shape, 0) < group
    first = (lax.broadcasted_iota(jnp.int32, order.shape, 1) & 31) < group
    order[...] = jnp.where(lower == first, ordered, 0.0).astype(jnp.bfloat16)
    out[...] = jnp.zeros_like(out)
    attend_blocks(per_device, heads, lengths, lax.axis_index("sec") >> 1, source, keys, values, out, 0)


def attend_far_kernel(per_device, heads, lengths, source, near, keys, values, own, first, second, third, total):
    chip = lax.axis_index("sec") >> 1
    tp = lax.axis_index("tp")
    total[...] = jnp.zeros_like(total)
    total[2 * chip] = near[0]
    total[2 * chip + 1] = near[1]
    attend_blocks(per_device, heads, lengths, 1 - chip, source, keys, values, total, 2 * (1 - chip))
    for step, target in enumerate((own, first, second, third)):
        target[...] = total[tp ^ step, 0:4].astype(jnp.bfloat16)


def gather_kernel(third, second, first, own, out, rows):
    for step, part in enumerate((own, first, second, third)):
        rows[4 * step : 4 * step + 4] = part[...].astype(jnp.float32)
    out[...] = rows[...].astype(jnp.bfloat16)


def slot_rows(far, per_device, count):
    sec, tp = lax.axis_index("sec"), lax.axis_index("tp")
    share = 2 * per_device
    shape = (count, 32)
    line = lax.broadcasted_iota(jnp.int32, shape, 1)
    place, index = (line >> 2) & 3, line & 3
    from_sec = sec ^ (3 * far) ^ (line >> 4) ^ jnp.where(place > 0, 1, 0)
    row = (tp ^ place) * share + (from_sec & 1) * per_device + index
    match = (lax.broadcasted_iota(jnp.int32, shape, 0) == row) & (index < per_device)
    return jnp.where(match, 1.0, 0.0).astype(jnp.bfloat16)


def resid_rows(far, per_device, count, assign, resid):
    sec, tp = lax.axis_index("sec"), lax.axis_index("tp")
    share = 2 * per_device
    group = resid.shape[0]
    chip = (sec ^ (3 * far)) >> 1
    slots = jnp.broadcast_to(group_slots(group, assign), (count, group)) - share * chip
    match = lax.broadcasted_iota(jnp.int32, (count, group), 0) == slots + tp * share
    match = jnp.where(match & (slots >= 0) & (slots < share), 1.0, 0.0).astype(jnp.bfloat16)
    return jnp.dot(match, resid[...], preferred_element_type=jnp.float32)


def project(match, first, second, resid, weight, keep, send):
    lines = jnp.concatenate([first[...], second[...]], axis=0)
    ordered = jnp.dot(match, lines, preferred_element_type=jnp.float32).astype(jnp.bfloat16)
    total = resid + jnp.dot(ordered, weight[...], preferred_element_type=jnp.float32)
    keep[...] = total
    send[...] = total.astype(jnp.bfloat16)


def project_near_kernel(per_device, first, second, assign, resid, weight, keep, send, far_match, far_resid):
    count = keep.shape[0]
    near = resid_rows(0, per_device, count, assign, resid)
    project(slot_rows(0, per_device, count), first, second, near, weight, keep, send)
    far_match[...] = slot_rows(1, per_device, count)
    far_resid[...] = resid_rows(1, per_device, count, assign, resid)


def project_far_kernel(first, second, match, resid, weight, keep, send):
    project(match[...], first, second, resid[...], weight, keep, send)


def add_kernel(mine, other, keep, send):
    total = mine[...] + other[...].astype(jnp.float32)
    keep[...] = total
    send[...] = total.astype(jnp.bfloat16)


def row_half():
    sec = lax.axis_index("sec")
    return (sec ^ (sec >> 1)) & 1


def products(features, gate, up, unit, units, chunk, keep, send):
    half = keep.shape[0]
    for kind, weight in enumerate((gate, up)):
        for start in range(0, units, chunk):
            column = slice(unit + start, unit + start + chunk)
            product = jnp.dot(features, weight[:, column], preferred_element_type=jnp.float32)
            at = kind * units + start
            keep[:, at : at + chunk] = product[:half]
            send[:, at : at + chunk] = product[half:].astype(jnp.bfloat16)


def to_groups(first, second, groups):
    share = first.shape[0] // groups.shape[0]
    for index in range(groups.shape[0]):
        lines = slice(index * share, (index + 1) * share)
        groups[index, 0:share] = first[lines]
        groups[index, share : 2 * share] = second[lines]


def gate_up_first_kernel(
    chunk, near, near_other, far, far_other, gain, gate, up, keep, send, features, stream, halves, groups
):
    sec, tp = lax.axis_index("sec"), lax.axis_index("tp")
    chip = sec >> 1
    half = near.shape[0]
    halves[chip] = near[...] + near_other[...].astype(jnp.float32)
    halves[1 - chip] = far[...] + far_other[...].astype(jnp.float32)
    to_groups(halves[0], halves[1], groups)
    stream[...] = groups[tp, 0 : stream.shape[0]]
    first = row_half()
    total = jnp.concatenate([halves[first], halves[1 - first]], axis=0)
    squares = jnp.sum(total * total, axis=1, keepdims=True)
    scaled = (total * gain[...].astype(jnp.float32)).astype(jnp.bfloat16)
    features[...] = scaled
    units = (keep.shape[1] - 128) // 2
    products(scaled, gate, up, 0, units, chunk, keep, send)
    keep[:, 2 * units :] = jnp.broadcast_to(squares[:half], (half, 128))
    send[:, 2 * units :] = two_terms(squares[half:])


def gate_up_more_kernel(chunk, unit, features, gate, up, earlier, keep, send):
    products(features[...], gate, up, unit, keep.shape[1] // 2, chunk, keep, send)


def two_terms(column):
    shape = (column.shape[0], 128)
    column = jnp.broadcast_to(column, shape)
    coarse = column.astype(jnp.bfloat16).astype(jnp.float32)
    lane = lax.broadcasted_iota(jnp.int32, shape, 1)
    return jnp.where(lane < 64, coarse, column - coarse).astype(jnp.bfloat16)


def one_column(terms):
    return terms[:, 0:1].astype(jnp.float32) + terms[:, 64:65].astype(jnp.float32)


def pair_sum_first_kernel(mine, other, keep, send):
    width = mine.shape[1] - 128
    total = mine[:, :width] + other[:, :width].astype(jnp.float32)
    both = mine[:, width:] + one_column(other[:, width:])
    keep[:, :width] = total
    keep[:, width:] = both
    send[:, :width] = total.astype(jnp.bfloat16)
    send[:, width:] = two_terms(both[:, 0:1])


def pair_sum_kernel(mine, other, earlier, keep, send):
    total = mine[...] + other[...].astype(jnp.float32)
    keep[...] = total
    send[...] = total.astype(jnp.bfloat16)


def gated(mine, other, factor, hidden):
    width = hidden.shape[1]
    gate = (mine[:, :width] + other[:, :width].astype(jnp.float32)) * factor
    up = (mine[:, width : 2 * width] + other[:, width : 2 * width].astype(jnp.float32)) * factor
    hidden[...] = (gate / (1.0 + jnp.exp(-gate)) * up).astype(jnp.bfloat16)


def hidden_first_kernel(features, mine, other, earlier, hidden, scale):
    width = mine.shape[1] - 128
    total = mine[:, width : width + 1] + one_column(other[:, width:])
    factor = lax.rsqrt(total / features + 1e-06)
    scale[...] = jnp.broadcast_to(factor, scale.shape)
    gated(mine, other, factor, hidden)


def hidden_kernel(mine, other, scale, earlier, hidden):
    gated(mine, other, scale[:, 0:1], hidden)


def down_product(unit, mine, other, weight):
    lines = jnp.concatenate([mine[...].astype(jnp.float32), other[...].astype(jnp.float32)], axis=0)
    rows = weight[unit : unit + lines.shape[1], :]
    return jnp.dot(lines.astype(jnp.bfloat16), rows, preferred_element_type=jnp.float32)


def column_halves(rows):
    columns = rows.shape[1] // 2
    return jnp.concatenate([rows[:, :columns], rows[:, columns:]], axis=0)


def down_first_kernel(mine, other, weight, stream, out, stream_halves):
    out[...] = down_product(0, mine, other, weight)
    stream_halves[...] = column_halves(stream[...])


def down_more_kernel(unit, before, mine, other, weight, out):
    out[...] = before[...] + down_product(unit, mine, other, weight)


def down_last_kernel(unit, before, mine, other, weight, keep, first, second, third, groups):
    tp = lax.axis_index("tp")
    product = before[...] + down_product(unit, mine, other, weight)
    group = keep.shape[0] // 2
    half = product.shape[0] // 2
    swapped = row_half() == 1
    lower, upper = product[:half], product[half:]
    to_groups(jnp.where(swapped, upper, lower), jnp.where(swapped, lower, upper), groups)
    for step, target in enumerate((keep, first, second, third)):
        target[...] = column_halves(groups[tp ^ step, 0:group]).astype(target.dtype)


def finish_kernel(third, second, first, stream, mine, order, out, terms):
    total = stream[...] + mine[...]
    for other in (first, second, third):
        total = total + other[...].astype(jnp.float32)
    lines, columns = total.shape
    coarse = total.astype(jnp.bfloat16).astype(jnp.float32)
    terms[...] = jnp.zeros_like(terms)
    terms[0:lines] = coarse
    terms[32 : 32 + lines] = total - coarse
    ordered = jnp.dot(order[...], terms[...].astype(jnp.bfloat16), preferred_element_type=jnp.float32)
    group = lines // 2
    out[:, :columns] = ordered[:group].astype(jnp.bfloat16)
    out[:, columns:] = ordered[group:].astype(jnp.bfloat16)


def local_pairs(
    resid,
    query,
    new_kv,
    key_cache,
    cached_value_rows,
    cache_len,
    assign,
    out_weight,
    norm_gain,
    gate_weight,
    up_weight,
    down_weight,
):
    f32, bf16 = jnp.float32, jnp.bfloat16
    group, features = resid.shape
    per_device = key_cache.shape[0]
    heads = query.shape[1] // HEAD_WIDTH
    head_block = out_weight.shape[0]
    width = gate_weight.shape[1]
    half = 2 * group
    assign = assign.reshape(1, -1)
    gain = norm_gain.reshape(1, -1)

    query_b, pairs_b = swap(query, "sec", 1), swap(new_kv, "sec", 1)
    block = (2, 16 * per_device, HEAD_WIDTH)
    own, picker = call(
        functools.partial(pick_own_kernel, per_device, group),
        [(block, bf16), ((16, group), bf16)],
        (query, new_kv, assign),
        [
            pltpu.VMEM(query.shape, bf16),
            pltpu.VMEM(new_kv.shape, bf16),
            pltpu.VMEM(assign.shape, jnp.int32),
            pltpu.VMEM(block, f32),
            pltpu.SemaphoreType.DMA((3,)),
        ],
        remote=(0, 1, 2),
    )
    mine, away = call(
        functools.partial(pick_other_kernel, per_device),
        [(block, bf16)] * 2,
        (own, picker, query_b, pairs_b),
        [pltpu.VMEM(block, f32)],
    )
    other = swap(away, "sec", 3)
    caches = (key_cache, cached_value_rows)
    near, order = call(
        functools.partial(attend_near_kernel, per_device, heads),
        [((2, 4, head_block), f32), ((half, 64), bf16)],
        (cache_len, mine, *caches, assign),
        smem=(0,),
        resident=(2, 3),
    )
    own, *parts = call(
        functools.partial(attend_far_kernel, per_device, heads),
        [((4, head_block), bf16)] * 4,
        (cache_len, other, near, *caches),
        [pltpu.VMEM((4, 4, head_block), f32)],
        smem=(0,),
        resident=(3, 4),
    )

    parts = [swap(parts[step - 1], ("sec", "tp"), (1, step)) for step in (3, 2, 1)]
    (own,) = call(gather_kernel, [((16, head_block), bf16)], (*parts, own), [pltpu.VMEM((16, head_block), f32)])
    across = swap(own, "sec", 3)
    beside = swap(own, "sec", 1)

    pair = [((half, features), f32), ((half, features), bf16)]

    def tp_sum(mine, away):
        mine, away = call(add_kernel, pair, (mine, swap(away, "tp", 1)))
        return mine, swap(away, "tp", 2)

    *near, match, rows = call(
        functools.partial(project_near_kernel, per_device),
        pair + [((half, 32), bf16), ((half, features), f32)],
        (own, beside, assign, resid, out_weight),
        resident=(4,),
    )
    corner = swap(after(across, near[1]), "sec", 1)
    far = call(project_far_kernel, pair, (across, corner, match, rows, out_weight), resident=(4,), nanos=0)
    sums = tp_sum(*near) + tp_sum(*far)

    sizes = [width * sixteenths // 16 for sixteenths in (5, 5, 4, 2)]
    starts = [sum(sizes[:index]) for index in range(len(sizes))]
    chunk = width // 16
    weights = (gate_weight, up_weight)

    def sums_of(index, extra=0):
        shape = (half, 2 * sizes[index] + extra)
        return [(shape, f32), (shape, bf16)]

    *product, lines, stream = call(
        functools.partial(gate_up_first_kernel, chunk),
        sums_of(0, 128) + [((2 * half, features), bf16), ((group, features), f32)],
        (*sums, gain, *weights),
        [pltpu.VMEM((2, half, features), f32), pltpu.VMEM((4, 16, features), f32)],
        resident=(5, 6),
        nanos=2000,
    )
    products_made = [product]

    def more_products(index, earlier):
        return call(
            functools.partial(gate_up_more_kernel, chunk, starts[index]),
            sums_of(index),
            (lines, *weights, earlier),
            resident=(1, 2),
            free=(3,),
            nanos=0,
        )

    def pair_sum(index, earlier):
        mine, away = products_made[index]
        other = swap(away, "sec", 1)
        if index == 0:
            return call(pair_sum_first_kernel, sums_of(0, 128), (mine, other), nanos=0)
        return call(pair_sum_kernel, sums_of(index), (mine, other, earlier), free=(2,), nanos=0)

    products_made.append(more_products(1, product[1]))
    chip_sums = [pair_sum(0, None)]
    chip_sums.append(pair_sum(1, chip_sums[0][1]))
    products_made.append(more_products(2, chip_sums[1][1]))
    products_made.append(more_products(3, products_made[2][1]))
    chip_sums.append(pair_sum(2, products_made[3][1]))
    chip_sums.append(pair_sum(3, chip_sums[2][1]))
    total = [((2 * half, features), f32)]
    before = scale = None
    parts_done = []
    for index, (mine, away) in enumerate(chip_sums):
        other = swap(away, "sec", 3)
        if index == 0:
            hidden, scale = call(
                functools.partial(hidden_first_kernel, features * lax.axis_size("sec")),
                [((half, sizes[0]), bf16), ((half, 128), f32)],
                (mine, other, chip_sums[-1][1]),
                free=(2,),
                nanos=0,
            )
        else:
            earlier = parts_done[max(index - 2, 0)] if index > 1 else hidden
            (hidden,) = call(
                hidden_kernel, [((half, sizes[index]), bf16)], (mine, other, scale, earlier), free=(3,), nanos=1000
            )
        beside = swap(hidden, "sec", 1)
        if index == 0:
            before, stream = call(
                down_first_kernel,
                total + [((half, features // 2), f32)],
                (hidden, beside, down_weight, stream),
                resident=(2,),
                nanos=1000,
            )
            parts_done.append(before)
        elif index < len(sizes) - 1:
            (before,) = call(
                functools.partial(down_more_kernel, starts[index]),
                total,
                (before, hidden, beside, down_weight),
                resident=(3,),
                nanos=1000,
            )
            parts_done.append(before)
        else:
            mine, *parts = call(
                functools.partial(down_last_kernel, starts[index]),
                [((half, features // 2), f32)] + [((half, features // 2), bf16)] * 3,
                (before, hidden, beside, down_weight),
                [pltpu.VMEM((4, 16, features), f32)],
                resident=(3,),
            )
    parts = [swap(parts[step - 1], "tp", step) for step in (3, 2, 1)]
    (out,) = call(
        finish_kernel,
        [((group, features), bf16)],
        (*parts, stream, mine, order),
        [pltpu.VMEM((64, features // 2), f32)],
    )
    return out


def solution(mesh):
    small = mesh.shape["sec"] == 4 and mesh.shape["tp"] == 4
    return jax.shard_map(
        local_pairs if small else local,
        mesh=mesh,
        in_specs=(
            P(("rep", "tp"), "sec"),
            P(("rep", "tp"), "sec"),
            P(("rep", "tp"), "sec"),
            P(("rep", "sec", "tp"), None, None),
            P(("rep", "sec", "tp"), None, None),
            P(("rep", "sec", "tp")),
            P("rep"),
            P("tp", "sec"),
            P("sec"),
            P("sec", "tp"),
            P("sec", "tp"),
            P("tp", "sec"),
        ),
        out_specs=P(("rep", "tp"), "sec"),
        check_vma=False,
    )
```

```python
import functools
import math

import jax
import jax.numpy as jnp
from jax import lax
from jax.experimental import pallas as pl
from jax.experimental.pallas import tpu as pltpu
from jax.sharding import PartitionSpec as P

D = 5120
QUERY_HEADS = 40
KEY_VALUE_HEADS = 8
HEAD_WIDTH = 128
CACHE_SLOTS = 224


def attend_slots(query_rows, key_value_pairs, stored_keys, stored_values, lengths):
    cache_slots = query_rows.shape[0]
    group_query = QUERY_HEADS // KEY_VALUE_HEADS
    query_head_rows = query_rows.reshape(cache_slots, KEY_VALUE_HEADS, group_query, HEAD_WIDTH)
    paired_heads = key_value_pairs.reshape(cache_slots, KEY_VALUE_HEADS, 2, HEAD_WIDTH)
    fresh_keys = paired_heads[:, :, 0]
    fresh_values = paired_heads[:, :, 1]
    earlier_keys = stored_keys.reshape(cache_slots, CACHE_SLOTS, KEY_VALUE_HEADS, HEAD_WIDTH)
    earlier_values = stored_values.reshape(cache_slots, CACHE_SLOTS, KEY_VALUE_HEADS, HEAD_WIDTH)
    scaling = 1.0 / math.sqrt(HEAD_WIDTH)
    past_scores = (
        jnp.einsum(
            "rkgd,rlkd->rkgl", query_head_rows, earlier_keys, preferred_element_type=jnp.float32
        )
        * scaling
    )
    fresh_scores = (
        jnp.einsum("rkgd,rkd->rkg", query_head_rows, fresh_keys, preferred_element_type=jnp.float32)
        * scaling
    )
    valid = lax.broadcasted_iota(jnp.int32, (cache_slots, CACHE_SLOTS), 1) < lengths[:, None]
    past_scores = jnp.where(valid[:, None, None, :], past_scores, -1e30)
    highest = jnp.maximum(jnp.max(past_scores, axis=-1), fresh_scores)
    past_exp = jnp.exp(past_scores - highest[..., None])
    fresh_exp = jnp.exp(fresh_scores - highest)
    denominator = jnp.sum(past_exp, axis=-1) + fresh_exp
    past_weights = (past_exp / denominator[..., None]).astype(jnp.bfloat16)
    fresh_weights = (fresh_exp / denominator).astype(jnp.bfloat16)
    mixed = jnp.einsum(
        "rkgl,rlkd->rkgd", past_weights, earlier_values, preferred_element_type=jnp.float32
    )
    mixed = (
        mixed
        + fresh_weights.astype(jnp.float32)[..., None]
        * fresh_values.astype(jnp.float32)[:, :, None, :]
    )
    return mixed.reshape(cache_slots, QUERY_HEADS * HEAD_WIDTH).astype(jnp.bfloat16)


def gated_units(values, width):
    return (jax.nn.silu(values[:, :width]) * values[:, width:]).astype(jnp.bfloat16)


def received(blocks, axis):
    count = lax.axis_size(axis)
    result = [blocks[0]]
    for step in range(1, count):
        result.append(lax.ppermute(blocks[step], axis, [(i, i ^ step) for i in range(count)]))
    return result


def local(
    resid,
    query,
    new_kv,
    key_cache,
    cached_value_rows,
    cache_len,
    assign,
    out_weight,
    norm_gain,
    gate_weight,
    up_weight,
    down_weight,
):
    group = query.shape[0]
    per_device = key_cache.shape[0]
    tp_index = lax.axis_index("tp")
    sec_index = lax.axis_index("sec")
    tp_count = lax.axis_size("tp")
    sec_count = lax.axis_size("sec")
    local_slots = lax.dynamic_slice_in_dim(assign, tp_index * group, group)
    resid_f32 = resid.astype(jnp.float32)
    features = resid.shape[1]
    width = gate_weight.shape[1]
    rows = group * tp_count // sec_count

    tokens = jnp.concatenate([query, new_kv], axis=1)
    blocks = []
    for step in range(sec_count):
        wanted = (sec_index ^ step) * per_device + lax.iota(jnp.int32, per_device)
        picker = (local_slots[None, :] == wanted[:, None]).astype(jnp.bfloat16)
        blocks.append(jnp.dot(picker, tokens, preferred_element_type=jnp.float32).astype(jnp.bfloat16))
    pieces = jnp.stack(received(blocks, "sec"))
    pieces = jnp.take(pieces, sec_index ^ lax.iota(jnp.int32, sec_count), axis=0)
    my_query = pieces[:, :, : query.shape[1]].transpose(1, 0, 2).reshape(per_device, -1)
    my_pairs = pieces[:, :, query.shape[1] :].transpose(1, 0, 2).reshape(per_device, -1)
    attended = attend_slots(my_query, my_pairs, key_cache, cached_value_rows, cache_len)

    head_block = out_weight.shape[0]
    blocks = [
        lax.dynamic_slice_in_dim(attended, (tp_index ^ step) * head_block, head_block, 1)
        for step in range(tp_count)
    ]
    mine = jnp.stack(received(blocks, "tp"))
    everyone = jnp.stack(received([mine] * sec_count, "sec"))
    everyone = jnp.take(everyone, sec_index ^ lax.iota(jnp.int32, sec_count), axis=0)
    everyone = everyone.transpose(1, 0, 2, 3).reshape(tp_count, group, head_block)
    parts = jnp.dot(everyone.reshape(tp_count * group, head_block), out_weight, preferred_element_type=jnp.float32)
    parts = parts.astype(jnp.bfloat16).reshape(tp_count, group, features)
    shares = received([parts[step] for step in range(tp_count)], "tp")
    attn_out = sum(share.astype(jnp.float32) for share in shares)
    attn_out = jnp.take(attn_out, local_slots, axis=0)
    stream = resid_f32 + attn_out

    scaled = (stream * norm_gain.astype(jnp.float32)[None, :]).astype(jnp.bfloat16)
    squares = jnp.broadcast_to(jnp.sum(stream * stream, axis=1, keepdims=True), (group, 128))
    piece = jnp.concatenate(received([scaled] * tp_count, "tp"), axis=0)
    square_parts = jnp.concatenate(received([squares] * tp_count, "tp"), axis=0)
    square_parts = square_parts.reshape(sec_count, rows, 128)
    gate_part = jnp.dot(piece, gate_weight, preferred_element_type=jnp.float32)
    up_part = jnp.dot(piece, up_weight, preferred_element_type=jnp.float32)
    projected = jnp.concatenate([gate_part, up_part], axis=1).astype(jnp.bfloat16)
    projected = projected.reshape(sec_count, rows, 2 * width)
    blocks = [lax.dynamic_index_in_dim(projected, sec_index ^ step, 0, False) for step in range(sec_count)]
    share = sum(block.astype(jnp.float32) for block in received(blocks, "sec"))
    blocks = [lax.dynamic_index_in_dim(square_parts, sec_index ^ step, 0, False) for step in range(sec_count)]
    total = sum(received(blocks, "sec"))
    inverse = lax.rsqrt(total[:, :1] / D + 1e-06)
    hidden = gated_units(share * inverse, width)
    hidden = jnp.stack(received([hidden] * sec_count, "sec"))
    hidden = jnp.take(hidden, sec_index ^ lax.iota(jnp.int32, sec_count), axis=0).reshape(-1, width)
    parts = jnp.dot(hidden, down_weight, preferred_element_type=jnp.float32).astype(jnp.bfloat16)
    parts = parts.reshape(tp_count, group, features)
    shares = received([parts[step] for step in range(tp_count)], "tp")
    ff_out = sum(share.astype(jnp.float32) for share in shares)
    return (stream + ff_out).astype(jnp.bfloat16)


MIB = 1024 * 1024


def call(kernel, outs, operands, scratch=(), smem=(), resident=(), remote=(), free=(), nanos=2000, limit=8):
    specs = []
    placed = []
    for place, operand in enumerate(operands):
        space = pltpu.SMEM if place in smem else pltpu.HBM if place in remote else pltpu.VMEM
        space = pl.ANY if place in free else space
        specs.append(pl.BlockSpec(memory_space=space))
        if place in resident or place in remote:
            operand = constrained(operand, space)
        placed.append(operand)
    return pl.pallas_call(
        kernel,
        out_shape=[jax.ShapeDtypeStruct(shape, dtype) for shape, dtype in outs],
        in_specs=specs,
        out_specs=[pl.BlockSpec(memory_space=pltpu.VMEM) for _ in outs],
        scratch_shapes=list(scratch),
        compiler_params=pltpu.CompilerParams(vmem_limit_bytes=limit * MIB),
        cost_estimate=pl.CostEstimate(flops=nanos * 10**6, bytes_accessed=0, transcendentals=0),
    )(*placed)


def copy_kernel(value, earlier, out):
    out[...] = value[...]


def after(value, earlier):
    (value,) = call(copy_kernel, [(value.shape, value.dtype)], (value, earlier), free=(1,), nanos=0)
    return value


def constrained(operand, space):
    return pltpu.with_memory_space_constraint(operand, space)


def swap(value, axis, step):
    if isinstance(axis, tuple):
        count = lax.axis_size(axis[1])
        total = lax.axis_size(axis[0]) * count
        step = step[0] * count + step[1]
    else:
        total = lax.axis_size(axis)
    return lax.ppermute(value, axis, [(i, i ^ step) for i in range(total)])


def group_slots(group, assign):
    tp = lax.axis_index("tp")
    slots = jnp.zeros((1, group), jnp.int32)
    for index in range(assign.shape[1] // group):
        slots = jnp.where(tp == index, assign[:, index * group : (index + 1) * group], slots)
    return slots


def slot_picker(per_device, slots):
    sec = lax.axis_index("sec")
    group = slots.shape[1]
    line = lax.broadcasted_iota(jnp.int32, (16, group), 0)
    wanted = jnp.where(line < 8, sec * per_device + line, (sec ^ 3) * per_device + line - 8)
    inside = (line & 7) < per_device
    return jnp.where(inside & (jnp.broadcast_to(slots, (16, group)) == wanted), 1.0, 0.0).astype(jnp.bfloat16)


def split_heads(per_device, picker, query, pairs, rows):
    queries = jnp.dot(picker, query[...], preferred_element_type=jnp.float32)
    others = jnp.dot(picker, pairs[...], preferred_element_type=jnp.float32)
    width = HEAD_WIDTH
    heads = query.shape[1] // width
    rows[...] = jnp.zeros_like(rows)
    for side in range(2):
        for j in range(per_device):
            line = side * 8 + j
            for h in range(heads):
                rows[side, j * 16 + h : j * 16 + h + 1, :] = queries[line : line + 1, h * width : (h + 1) * width]
            for h in range(pairs.shape[1] // width):
                at = j * 16 + heads + h
                rows[side, at : at + 1, :] = others[line : line + 1, h * width : (h + 1) * width]


def pick_own_kernel(
    per_device, group, query, pairs, assign, out, picker, query_here, pairs_here, assign_here, rows, sems
):
    copies = [
        pltpu.make_async_copy(source, target, sems.at[index])
        for index, (source, target) in enumerate(
            ((query, query_here), (pairs, pairs_here), (assign, assign_here))
        )
    ]
    for copy in copies:
        copy.start()
    copies[2].wait()
    picker[...] = slot_picker(per_device, group_slots(group, assign_here))
    copies[0].wait()
    copies[1].wait()
    split_heads(per_device, picker[...], query_here, pairs_here, rows)
    out[...] = rows[...].astype(jnp.bfloat16)


def pick_other_kernel(per_device, own, picker, query, pairs, keep, send, rows):
    split_heads(per_device, picker[...], query, pairs, rows)
    here = lax.axis_index("sec") & 1
    keep[here] = own[0]
    keep[1 - here] = rows[0].astype(jnp.bfloat16)
    send[here] = own[1]
    send[1 - here] = rows[1].astype(jnp.bfloat16)


def attend_blocks(per_device, heads, lengths, chip, source, keys, values, target, first):
    share = heads // 2
    slots = keys.shape[1]
    width = HEAD_WIDTH
    scaling = 1.0 / math.sqrt(width)
    line = lax.broadcasted_iota(jnp.int32, (16, width), 0)
    upper = line < share
    place = lax.broadcasted_iota(jnp.int32, (16, slots), 1)
    work = [(i, j) for i in range(2) for j in range(per_device)]
    past, fresh, new_values, columns = [], [], [], []
    for i, j in work:
        wide = source[i, j * 16 : (j + 1) * 16].astype(jnp.float32)
        zero = jnp.zeros_like(wide)
        both = jnp.concatenate([jnp.where(upper, wide, zero), jnp.where(upper, zero, wide)], axis=1)
        column = pl.ds(pl.multiple_of((2 * chip + i) * 2 * width, 2 * width), 2 * width)
        columns.append(column)
        scores = lax.dot_general(
            both.astype(jnp.bfloat16),
            keys[j, :, column],
            (((1,), (1,)), ((), ())),
            preferred_element_type=jnp.float32,
        )
        past.append(jnp.where(place < lengths[j], scores * scaling, -1e30))
        new_key = jnp.where(upper, wide[heads : heads + 1], wide[heads + 2 : heads + 3])
        new_values.append(jnp.where(upper, wide[heads + 1 : heads + 2], wide[heads + 3 : heads + 4]))
        fresh.append(wide * new_key)
    past = jnp.concatenate(past, axis=0)
    fresh = jnp.sum(jnp.concatenate(fresh, axis=0), axis=1, keepdims=True) * scaling
    highest = jnp.maximum(jnp.max(past, axis=1, keepdims=True), fresh)
    past_exp = jnp.exp(past - highest)
    fresh_exp = jnp.exp(fresh - highest)
    inverse = 1.0 / (jnp.sum(past_exp, axis=1, keepdims=True) + fresh_exp)
    weights = (past_exp * inverse).astype(jnp.bfloat16)
    fresh_weight = (fresh_exp * inverse).astype(jnp.bfloat16).astype(jnp.float32)
    for index, (i, j) in enumerate(work):
        lines = slice(index * 16, (index + 1) * 16)
        mixed = jnp.dot(weights[lines], values[j, :, columns[index]], preferred_element_type=jnp.float32)
        mixed = jnp.where(upper, mixed[:, :width], mixed[:, width:]) + fresh_weight[lines] * new_values[index]
        for h in range(heads):
            target[first + i, j : j + 1, h * width : (h + 1) * width] = mixed[h : h + 1]


def attend_near_kernel(per_device, heads, lengths, source, keys, values, assign, out, order):
    group = order.shape[0] // 2
    slots = jnp.broadcast_to(group_slots(group, assign), (group, group))
    line = lax.broadcasted_iota(jnp.int32, (group, group), 0)
    match = jnp.where(line == slots, 1.0, 0.0).astype(jnp.bfloat16)
    shape = (group, order.shape[1])
    column = lax.broadcasted_iota(jnp.int32, shape, 1) & 31
    column = jnp.where(column < group, column, jnp.where(column < 2 * group, column - group, group))
    same = jnp.where(lax.broadcasted_iota(jnp.int32, shape, 0) == column, 1.0, 0.0).astype(jnp.bfloat16)
    ordered = lax.dot_general(match, same, (((0,), (0,)), ((), ())), preferred_element_type=jnp.float32)
    line = lax.broadcasted_iota(jnp.int32, (2 * group, group), 0)
    line = jnp.where(line < group, line, line - group)
    twice = jnp.where(line == lax.broadcasted_iota(jnp.int32, (2 * group, group), 1), 1.0, 0.0).astype(jnp.bfloat16)
    ordered = jnp.dot(twice, ordered.astype(jnp.bfloat16), preferred_element_type=jnp.float32)
    lower = lax.broadcasted_iota(jnp.int32, order.shape, 0) < group
    first = (lax.broadcasted_iota(jnp.int32, order.shape, 1) & 31) < group
    order[...] = jnp.where(lower == first, ordered, 0.0).astype(jnp.bfloat16)
    out[...] = jnp.zeros_like(out)
    attend_blocks(per_device, heads, lengths, lax.axis_index("sec") >> 1, source, keys, values, out, 0)


def attend_far_kernel(per_device, heads, lengths, source, near, keys, values, own, first, second, third, total):
    chip = lax.axis_index("sec") >> 1
    tp = lax.axis_index("tp")
    total[...] = jnp.zeros_like(total)
    total[2 * chip] = near[0]
    total[2 * chip + 1] = near[1]
    attend_blocks(per_device, heads, lengths, 1 - chip, source, keys, values, total, 2 * (1 - chip))
    for step, target in enumerate((own, first, second, third)):
        target[...] = total[tp ^ step, 0:4].astype(jnp.bfloat16)


def gather_kernel(third, second, first, own, out, rows):
    for step, part in enumerate((own, first, second, third)):
        rows[4 * step : 4 * step + 4] = part[...].astype(jnp.float32)
    out[...] = rows[...].astype(jnp.bfloat16)


def slot_rows(far, per_device, count):
    sec, tp = lax.axis_index("sec"), lax.axis_index("tp")
    share = 2 * per_device
    shape = (count, 32)
    line = lax.broadcasted_iota(jnp.int32, shape, 1)
    place, index = (line >> 2) & 3, line & 3
    from_sec = sec ^ (3 * far) ^ (line >> 4) ^ jnp.where(place > 0, 1, 0)
    row = (tp ^ place) * share + (from_sec & 1) * per_device + index
    match = (lax.broadcasted_iota(jnp.int32, shape, 0) == row) & (index < per_device)
    return jnp.where(match, 1.0, 0.0).astype(jnp.bfloat16)


def resid_rows(far, per_device, count, assign, resid):
    sec, tp = lax.axis_index("sec"), lax.axis_index("tp")
    share = 2 * per_device
    group = resid.shape[0]
    chip = (sec ^ (3 * far)) >> 1
    slots = jnp.broadcast_to(group_slots(group, assign), (count, group)) - share * chip
    match = lax.broadcasted_iota(jnp.int32, (count, group), 0) == slots + tp * share
    match = jnp.where(match & (slots >= 0) & (slots < share), 1.0, 0.0).astype(jnp.bfloat16)
    return jnp.dot(match, resid[...], preferred_element_type=jnp.float32)


def project(match, first, second, resid, weight, keep, send):
    lines = jnp.concatenate([first[...], second[...]], axis=0)
    ordered = jnp.dot(match, lines, preferred_element_type=jnp.float32).astype(jnp.bfloat16)
    total = resid + jnp.dot(ordered, weight[...], preferred_element_type=jnp.float32)
    keep[...] = total
    send[...] = total.astype(jnp.bfloat16)


def project_near_kernel(per_device, first, second, assign, resid, weight, keep, send, far_match, far_resid):
    count = keep.shape[0]
    near = resid_rows(0, per_device, count, assign, resid)
    project(slot_rows(0, per_device, count), first, second, near, weight, keep, send)
    far_match[...] = slot_rows(1, per_device, count)
    far_resid[...] = resid_rows(1, per_device, count, assign, resid)


def project_far_kernel(first, second, match, resid, weight, keep, send):
    project(match[...], first, second, resid[...], weight, keep, send)


def add_kernel(mine, other, keep, send):
    total = mine[...] + other[...].astype(jnp.float32)
    keep[...] = total
    send[...] = total.astype(jnp.bfloat16)


def row_half():
    sec = lax.axis_index("sec")
    return (sec ^ (sec >> 1)) & 1


def products(features, gate, up, unit, units, chunk, keep, send):
    half = keep.shape[0]
    for kind, weight in enumerate((gate, up)):
        for start in range(0, units, chunk):
            column = slice(unit + start, unit + start + chunk)
            product = jnp.dot(features, weight[:, column], preferred_element_type=jnp.float32)
            at = kind * units + start
            keep[:, at : at + chunk] = product[:half]
            send[:, at : at + chunk] = product[half:].astype(jnp.bfloat16)


def to_groups(first, second, groups):
    share = first.shape[0] // groups.shape[0]
    for index in range(groups.shape[0]):
        lines = slice(index * share, (index + 1) * share)
        groups[index, 0:share] = first[lines]
        groups[index, share : 2 * share] = second[lines]


def gate_up_first_kernel(
    chunk, near, near_other, far, far_other, gain, gate, up, keep, send, features, stream, halves, groups
):
    sec, tp = lax.axis_index("sec"), lax.axis_index("tp")
    chip = sec >> 1
    half = near.shape[0]
    halves[chip] = near[...] + near_other[...].astype(jnp.float32)
    halves[1 - chip] = far[...] + far_other[...].astype(jnp.float32)
    to_groups(halves[0], halves[1], groups)
    stream[...] = groups[tp, 0 : stream.shape[0]]
    first = row_half()
    total = jnp.concatenate([halves[first], halves[1 - first]], axis=0)
    squares = jnp.sum(total * total, axis=1, keepdims=True)
    scaled = (total * gain[...].astype(jnp.float32)).astype(jnp.bfloat16)
    features[...] = scaled
    units = (keep.shape[1] - 128) // 2
    products(scaled, gate, up, 0, units, chunk, keep, send)
    keep[:, 2 * units :] = jnp.broadcast_to(squares[:half], (half, 128))
    send[:, 2 * units :] = two_terms(squares[half:])


def gate_up_more_kernel(chunk, unit, features, gate, up, earlier, keep, send):
    products(features[...], gate, up, unit, keep.shape[1] // 2, chunk, keep, send)


def two_terms(column):
    shape = (column.shape[0], 128)
    column = jnp.broadcast_to(column, shape)
    coarse = column.astype(jnp.bfloat16).astype(jnp.float32)
    lane = lax.broadcasted_iota(jnp.int32, shape, 1)
    return jnp.where(lane < 64, coarse, column - coarse).astype(jnp.bfloat16)


def one_column(terms):
    return terms[:, 0:1].astype(jnp.float32) + terms[:, 64:65].astype(jnp.float32)


def pair_sum_first_kernel(mine, other, keep, send):
    width = mine.shape[1] - 128
    total = mine[:, :width] + other[:, :width].astype(jnp.float32)
    both = mine[:, width:] + one_column(other[:, width:])
    keep[:, :width] = total
    keep[:, width:] = both
    send[:, :width] = total.astype(jnp.bfloat16)
    send[:, width:] = two_terms(both[:, 0:1])


def pair_sum_kernel(mine, other, earlier, keep, send):
    total = mine[...] + other[...].astype(jnp.float32)
    keep[...] = total
    send[...] = total.astype(jnp.bfloat16)


def gated(mine, other, factor, hidden):
    width = hidden.shape[1]
    gate = (mine[:, :width] + other[:, :width].astype(jnp.float32)) * factor
    up = (mine[:, width : 2 * width] + other[:, width : 2 * width].astype(jnp.float32)) * factor
    hidden[...] = (gate / (1.0 + jnp.exp(-gate)) * up).astype(jnp.bfloat16)


def hidden_first_kernel(features, mine, other, earlier, hidden, scale):
    width = mine.shape[1] - 128
    total = mine[:, width : width + 1] + one_column(other[:, width:])
    factor = lax.rsqrt(total / features + 1e-06)
    scale[...] = jnp.broadcast_to(factor, scale.shape)
    gated(mine, other, factor, hidden)


def hidden_kernel(mine, other, scale, earlier, hidden):
    gated(mine, other, scale[:, 0:1], hidden)


def down_product(unit, mine, other, weight):
    lines = jnp.concatenate([mine[...].astype(jnp.float32), other[...].astype(jnp.float32)], axis=0)
    rows = weight[unit : unit + lines.shape[1], :]
    return jnp.dot(lines.astype(jnp.bfloat16), rows, preferred_element_type=jnp.float32)


def column_halves(rows):
    columns = rows.shape[1] // 2
    return jnp.concatenate([rows[:, :columns], rows[:, columns:]], axis=0)


def down_first_kernel(mine, other, weight, stream, out, stream_halves):
    out[...] = down_product(0, mine, other, weight)
    stream_halves[...] = column_halves(stream[...])


def down_more_kernel(unit, before, mine, other, weight, out):
    out[...] = before[...] + down_product(unit, mine, other, weight)


def down_last_kernel(unit, before, mine, other, weight, keep, first, second, third, groups):
    tp = lax.axis_index("tp")
    product = before[...] + down_product(unit, mine, other, weight)
    group = keep.shape[0] // 2
    half = product.shape[0] // 2
    swapped = row_half() == 1
    lower, upper = product[:half], product[half:]
    to_groups(jnp.where(swapped, upper, lower), jnp.where(swapped, lower, upper), groups)
    for step, target in enumerate((keep, first, second, third)):
        target[...] = column_halves(groups[tp ^ step, 0:group]).astype(target.dtype)


def finish_kernel(third, second, first, stream, mine, order, out, terms):
    total = stream[...] + mine[...]
    for other in (first, second, third):
        total = total + other[...].astype(jnp.float32)
    lines, columns = total.shape
    coarse = total.astype(jnp.bfloat16).astype(jnp.float32)
    terms[...] = jnp.zeros_like(terms)
    terms[0:lines] = coarse
    terms[32 : 32 + lines] = total - coarse
    ordered = jnp.dot(order[...], terms[...].astype(jnp.bfloat16), preferred_element_type=jnp.float32)
    group = lines // 2
    out[:, :columns] = ordered[:group].astype(jnp.bfloat16)
    out[:, columns:] = ordered[group:].astype(jnp.bfloat16)


def local_pairs(
    resid,
    query,
    new_kv,
    key_cache,
    cached_value_rows,
    cache_len,
    assign,
    out_weight,
    norm_gain,
    gate_weight,
    up_weight,
    down_weight,
):
    f32, bf16 = jnp.float32, jnp.bfloat16
    group, features = resid.shape
    per_device = key_cache.shape[0]
    heads = query.shape[1] // HEAD_WIDTH
    head_block = out_weight.shape[0]
    width = gate_weight.shape[1]
    half = 2 * group
    assign = assign.reshape(1, -1)
    gain = norm_gain.reshape(1, -1)

    query_b, pairs_b = swap(query, "sec", 1), swap(new_kv, "sec", 1)
    block = (2, 16 * per_device, HEAD_WIDTH)
    own, picker = call(
        functools.partial(pick_own_kernel, per_device, group),
        [(block, bf16), ((16, group), bf16)],
        (query, new_kv, assign),
        [
            pltpu.VMEM(query.shape, bf16),
            pltpu.VMEM(new_kv.shape, bf16),
            pltpu.VMEM(assign.shape, jnp.int32),
            pltpu.VMEM(block, f32),
            pltpu.SemaphoreType.DMA((3,)),
        ],
        remote=(0, 1, 2),
    )
    mine, away = call(
        functools.partial(pick_other_kernel, per_device),
        [(block, bf16)] * 2,
        (own, picker, query_b, pairs_b),
        [pltpu.VMEM(block, f32)],
    )
    other = swap(away, "sec", 3)
    caches = (key_cache, cached_value_rows)
    near, order = call(
        functools.partial(attend_near_kernel, per_device, heads),
        [((2, 4, head_block), f32), ((half, 64), bf16)],
        (cache_len, mine, *caches, assign),
        smem=(0,),
        resident=(2, 3),
    )
    own, *parts = call(
        functools.partial(attend_far_kernel, per_device, heads),
        [((4, head_block), bf16)] * 4,
        (cache_len, other, near, *caches),
        [pltpu.VMEM((4, 4, head_block), f32)],
        smem=(0,),
        resident=(3, 4),
    )

    parts = [swap(parts[step - 1], ("sec", "tp"), (1, step)) for step in (3, 2, 1)]
    (own,) = call(gather_kernel, [((16, head_block), bf16)], (*parts, own), [pltpu.VMEM((16, head_block), f32)])
    across = swap(own, "sec", 3)
    beside = swap(own, "sec", 1)

    pair = [((half, features), f32), ((half, features), bf16)]

    def tp_sum(mine, away, first, second):
        mine, away = call(add_kernel, pair, (mine, swap(away, "tp", first)))
        return mine, swap(away, "tp", second)

    *near, match, rows = call(
        functools.partial(project_near_kernel, per_device),
        pair + [((half, 32), bf16), ((half, features), f32)],
        (own, beside, assign, resid, out_weight),
        resident=(4,),
    )
    corner = swap(after(across, near[1]), "sec", 1)
    far = call(project_far_kernel, pair, (across, corner, match, rows, out_weight), resident=(4,), nanos=0)
    sums = tp_sum(*near, 2, 1) + tp_sum(*far, 1, 2)

    sizes = [width * sixteenths // 16 for sixteenths in (5, 5, 4, 2)]
    starts = [sum(sizes[:index]) for index in range(len(sizes))]
    chunk = width // 16
    weights = (gate_weight, up_weight)

    def sums_of(index, extra=0):
        shape = (half, 2 * sizes[index] + extra)
        return [(shape, f32), (shape, bf16)]

    *product, lines, stream = call(
        functools.partial(gate_up_first_kernel, chunk),
        sums_of(0, 128) + [((2 * half, features), bf16), ((group, features), f32)],
        (*sums, gain, *weights),
        [pltpu.VMEM((2, half, features), f32), pltpu.VMEM((4, 16, features), f32)],
        resident=(5, 6),
        nanos=2000,
    )
    products_made = [product]

    def more_products(index, earlier):
        return call(
            functools.partial(gate_up_more_kernel, chunk, starts[index]),
            sums_of(index),
            (lines, *weights, earlier),
            resident=(1, 2),
            free=(3,),
            nanos=0,
        )

    def pair_sum(index, earlier):
        mine, away = products_made[index]
        other = swap(away, "sec", 1)
        if index == 0:
            return call(pair_sum_first_kernel, sums_of(0, 128), (mine, other), nanos=0)
        return call(pair_sum_kernel, sums_of(index), (mine, other, earlier), free=(2,), nanos=0)

    products_made.append(more_products(1, product[1]))
    chip_sums = [pair_sum(0, None)]
    chip_sums.append(pair_sum(1, chip_sums[0][1]))
    products_made.append(more_products(2, chip_sums[1][1]))
    products_made.append(more_products(3, products_made[2][1]))
    chip_sums.append(pair_sum(2, products_made[3][1]))
    chip_sums.append(pair_sum(3, chip_sums[2][1]))
    total = [((2 * half, features), f32)]
    before = scale = None
    parts_done = []
    for index, (mine, away) in enumerate(chip_sums):
        other = swap(away, "sec", 3)
        if index == 0:
            hidden, scale = call(
                functools.partial(hidden_first_kernel, features * lax.axis_size("sec")),
                [((half, sizes[0]), bf16), ((half, 128), f32)],
                (mine, other, chip_sums[-1][1]),
                free=(2,),
                nanos=0,
            )
        else:
            earlier = parts_done[max(index - 2, 0)] if index > 1 else hidden
            (hidden,) = call(
                hidden_kernel, [((half, sizes[index]), bf16)], (mine, other, scale, earlier), free=(3,), nanos=1000
            )
        beside = swap(hidden, "sec", 1)
        if index == 0:
            before, stream = call(
                down_first_kernel,
                total + [((half, features // 2), f32)],
                (hidden, beside, down_weight, stream),
                resident=(2,),
                nanos=1000,
            )
            parts_done.append(before)
        elif index < len(sizes) - 1:
            (before,) = call(
                functools.partial(down_more_kernel, starts[index]),
                total,
                (before, hidden, beside, down_weight),
                resident=(3,),
                nanos=1000,
            )
            parts_done.append(before)
        else:
            mine, *parts = call(
                functools.partial(down_last_kernel, starts[index]),
                [((half, features // 2), f32)] + [((half, features // 2), bf16)] * 3,
                (before, hidden, beside, down_weight),
                [pltpu.VMEM((4, 16, features), f32)],
                resident=(3,),
            )
    parts = [swap(parts[step - 1], "tp", step) for step in (3, 2, 1)]
    (out,) = call(
        finish_kernel,
        [((group, features), bf16)],
        (*parts, stream, mine, order),
        [pltpu.VMEM((64, features // 2), f32)],
    )
    return out


def solution(mesh):
    small = mesh.shape["sec"] == 4 and mesh.shape["tp"] == 4
    return jax.shard_map(
        local_pairs if small else local,
        mesh=mesh,
        in_specs=(
            P(("rep", "tp"), "sec"),
            P(("rep", "tp"), "sec"),
            P(("rep", "tp"), "sec"),
            P(("rep", "sec", "tp"), None, None),
            P(("rep", "sec", "tp"), None, None),
            P(("rep", "sec", "tp")),
            P("rep"),
            P("tp", "sec"),
            P("sec"),
            P("sec", "tp"),
            P("sec", "tp"),
            P("tp", "sec"),
        ),
        out_specs=P(("rep", "tp"), "sec"),
        check_vma=False,
    )
```

```python
import functools
import math

import jax
import jax.numpy as jnp
from jax import lax
from jax.experimental import pallas as pl
from jax.experimental.pallas import tpu as pltpu
from jax.sharding import PartitionSpec as P

D = 5120
QUERY_HEADS = 40
KEY_VALUE_HEADS = 8
HEAD_WIDTH = 128
CACHE_SLOTS = 224


def attend_slots(query_rows, key_value_pairs, stored_keys, stored_values, lengths):
    cache_slots = query_rows.shape[0]
    group_query = QUERY_HEADS // KEY_VALUE_HEADS
    query_head_rows = query_rows.reshape(cache_slots, KEY_VALUE_HEADS, group_query, HEAD_WIDTH)
    paired_heads = key_value_pairs.reshape(cache_slots, KEY_VALUE_HEADS, 2, HEAD_WIDTH)
    fresh_keys = paired_heads[:, :, 0]
    fresh_values = paired_heads[:, :, 1]
    earlier_keys = stored_keys.reshape(cache_slots, CACHE_SLOTS, KEY_VALUE_HEADS, HEAD_WIDTH)
    earlier_values = stored_values.reshape(cache_slots, CACHE_SLOTS, KEY_VALUE_HEADS, HEAD_WIDTH)
    scaling = 1.0 / math.sqrt(HEAD_WIDTH)
    past_scores = (
        jnp.einsum(
            "rkgd,rlkd->rkgl", query_head_rows, earlier_keys, preferred_element_type=jnp.float32
        )
        * scaling
    )
    fresh_scores = (
        jnp.einsum("rkgd,rkd->rkg", query_head_rows, fresh_keys, preferred_element_type=jnp.float32)
        * scaling
    )
    valid = lax.broadcasted_iota(jnp.int32, (cache_slots, CACHE_SLOTS), 1) < lengths[:, None]
    past_scores = jnp.where(valid[:, None, None, :], past_scores, -1e30)
    highest = jnp.maximum(jnp.max(past_scores, axis=-1), fresh_scores)
    past_exp = jnp.exp(past_scores - highest[..., None])
    fresh_exp = jnp.exp(fresh_scores - highest)
    denominator = jnp.sum(past_exp, axis=-1) + fresh_exp
    past_weights = (past_exp / denominator[..., None]).astype(jnp.bfloat16)
    fresh_weights = (fresh_exp / denominator).astype(jnp.bfloat16)
    mixed = jnp.einsum(
        "rkgl,rlkd->rkgd", past_weights, earlier_values, preferred_element_type=jnp.float32
    )
    mixed = (
        mixed
        + fresh_weights.astype(jnp.float32)[..., None]
        * fresh_values.astype(jnp.float32)[:, :, None, :]
    )
    return mixed.reshape(cache_slots, QUERY_HEADS * HEAD_WIDTH).astype(jnp.bfloat16)


def gated_units(values, width):
    return (jax.nn.silu(values[:, :width]) * values[:, width:]).astype(jnp.bfloat16)


def received(blocks, axis):
    count = lax.axis_size(axis)
    result = [blocks[0]]
    for step in range(1, count):
        result.append(lax.ppermute(blocks[step], axis, [(i, i ^ step) for i in range(count)]))
    return result


def local(
    resid,
    query,
    new_kv,
    key_cache,
    cached_value_rows,
    cache_len,
    assign,
    out_weight,
    norm_gain,
    gate_weight,
    up_weight,
    down_weight,
):
    group = query.shape[0]
    per_device = key_cache.shape[0]
    tp_index = lax.axis_index("tp")
    sec_index = lax.axis_index("sec")
    tp_count = lax.axis_size("tp")
    sec_count = lax.axis_size("sec")
    local_slots = lax.dynamic_slice_in_dim(assign, tp_index * group, group)
    resid_f32 = resid.astype(jnp.float32)
    features = resid.shape[1]
    width = gate_weight.shape[1]
    rows = group * tp_count // sec_count

    tokens = jnp.concatenate([query, new_kv], axis=1)
    blocks = []
    for step in range(sec_count):
        wanted = (sec_index ^ step) * per_device + lax.iota(jnp.int32, per_device)
        picker = (local_slots[None, :] == wanted[:, None]).astype(jnp.bfloat16)
        blocks.append(jnp.dot(picker, tokens, preferred_element_type=jnp.float32).astype(jnp.bfloat16))
    pieces = jnp.stack(received(blocks, "sec"))
    pieces = jnp.take(pieces, sec_index ^ lax.iota(jnp.int32, sec_count), axis=0)
    my_query = pieces[:, :, : query.shape[1]].transpose(1, 0, 2).reshape(per_device, -1)
    my_pairs = pieces[:, :, query.shape[1] :].transpose(1, 0, 2).reshape(per_device, -1)
    attended = attend_slots(my_query, my_pairs, key_cache, cached_value_rows, cache_len)

    head_block = out_weight.shape[0]
    blocks = [
        lax.dynamic_slice_in_dim(attended, (tp_index ^ step) * head_block, head_block, 1)
        for step in range(tp_count)
    ]
    mine = jnp.stack(received(blocks, "tp"))
    everyone = jnp.stack(received([mine] * sec_count, "sec"))
    everyone = jnp.take(everyone, sec_index ^ lax.iota(jnp.int32, sec_count), axis=0)
    everyone = everyone.transpose(1, 0, 2, 3).reshape(tp_count, group, head_block)
    parts = jnp.dot(everyone.reshape(tp_count * group, head_block), out_weight, preferred_element_type=jnp.float32)
    parts = parts.astype(jnp.bfloat16).reshape(tp_count, group, features)
    shares = received([parts[step] for step in range(tp_count)], "tp")
    attn_out = sum(share.astype(jnp.float32) for share in shares)
    attn_out = jnp.take(attn_out, local_slots, axis=0)
    stream = resid_f32 + attn_out

    scaled = (stream * norm_gain.astype(jnp.float32)[None, :]).astype(jnp.bfloat16)
    squares = jnp.broadcast_to(jnp.sum(stream * stream, axis=1, keepdims=True), (group, 128))
    piece = jnp.concatenate(received([scaled] * tp_count, "tp"), axis=0)
    square_parts = jnp.concatenate(received([squares] * tp_count, "tp"), axis=0)
    square_parts = square_parts.reshape(sec_count, rows, 128)
    gate_part = jnp.dot(piece, gate_weight, preferred_element_type=jnp.float32)
    up_part = jnp.dot(piece, up_weight, preferred_element_type=jnp.float32)
    projected = jnp.concatenate([gate_part, up_part], axis=1).astype(jnp.bfloat16)
    projected = projected.reshape(sec_count, rows, 2 * width)
    blocks = [lax.dynamic_index_in_dim(projected, sec_index ^ step, 0, False) for step in range(sec_count)]
    share = sum(block.astype(jnp.float32) for block in received(blocks, "sec"))
    blocks = [lax.dynamic_index_in_dim(square_parts, sec_index ^ step, 0, False) for step in range(sec_count)]
    total = sum(received(blocks, "sec"))
    inverse = lax.rsqrt(total[:, :1] / D + 1e-06)
    hidden = gated_units(share * inverse, width)
    hidden = jnp.stack(received([hidden] * sec_count, "sec"))
    hidden = jnp.take(hidden, sec_index ^ lax.iota(jnp.int32, sec_count), axis=0).reshape(-1, width)
    parts = jnp.dot(hidden, down_weight, preferred_element_type=jnp.float32).astype(jnp.bfloat16)
    parts = parts.reshape(tp_count, group, features)
    shares = received([parts[step] for step in range(tp_count)], "tp")
    ff_out = sum(share.astype(jnp.float32) for share in shares)
    return (stream + ff_out).astype(jnp.bfloat16)


MIB = 1024 * 1024


def call(kernel, outs, operands, scratch=(), smem=(), resident=(), remote=(), free=(), nanos=2000, limit=8):
    specs = []
    placed = []
    for place, operand in enumerate(operands):
        space = pltpu.SMEM if place in smem else pltpu.HBM if place in remote else pltpu.VMEM
        space = pl.ANY if place in free else space
        specs.append(pl.BlockSpec(memory_space=space))
        if place in resident or place in remote:
            operand = constrained(operand, space)
        placed.append(operand)
    return pl.pallas_call(
        kernel,
        out_shape=[jax.ShapeDtypeStruct(shape, dtype) for shape, dtype in outs],
        in_specs=specs,
        out_specs=[pl.BlockSpec(memory_space=pltpu.VMEM) for _ in outs],
        scratch_shapes=list(scratch),
        compiler_params=pltpu.CompilerParams(vmem_limit_bytes=limit * MIB),
        cost_estimate=pl.CostEstimate(flops=nanos * 10**6, bytes_accessed=0, transcendentals=0),
    )(*placed)


def constrained(operand, space):
    return pltpu.with_memory_space_constraint(operand, space)


def swap(value, axis, step):
    if isinstance(axis, tuple):
        count = lax.axis_size(axis[1])
        total = lax.axis_size(axis[0]) * count
        step = step[0] * count + step[1]
    else:
        total = lax.axis_size(axis)
    return lax.ppermute(value, axis, [(i, i ^ step) for i in range(total)])


def group_slots(group, assign):
    tp = lax.axis_index("tp")
    slots = jnp.zeros((1, group), jnp.int32)
    for index in range(assign.shape[1] // group):
        slots = jnp.where(tp == index, assign[:, index * group : (index + 1) * group], slots)
    return slots


def slot_picker(per_device, slots):
    sec = lax.axis_index("sec")
    group = slots.shape[1]
    line = lax.broadcasted_iota(jnp.int32, (16, group), 0)
    wanted = jnp.where(line < 8, sec * per_device + line, (sec ^ 3) * per_device + line - 8)
    inside = (line & 7) < per_device
    return jnp.where(inside & (jnp.broadcast_to(slots, (16, group)) == wanted), 1.0, 0.0).astype(jnp.bfloat16)


def split_heads(per_device, picker, query, pairs, rows):
    queries = jnp.dot(picker, query[...], preferred_element_type=jnp.float32)
    others = jnp.dot(picker, pairs[...], preferred_element_type=jnp.float32)
    width = HEAD_WIDTH
    heads = query.shape[1] // width
    rows[...] = jnp.zeros_like(rows)
    for side in range(2):
        for j in range(per_device):
            line = side * 8 + j
            for h in range(heads):
                rows[side, j * 16 + h : j * 16 + h + 1, :] = queries[line : line + 1, h * width : (h + 1) * width]
            for h in range(pairs.shape[1] // width):
                at = j * 16 + heads + h
                rows[side, at : at + 1, :] = others[line : line + 1, h * width : (h + 1) * width]


def pick_own_kernel(
    per_device, group, query, pairs, assign, out, picker, query_here, pairs_here, assign_here, rows, sems
):
    copies = [
        pltpu.make_async_copy(source, target, sems.at[index])
        for index, (source, target) in enumerate(
            ((query, query_here), (pairs, pairs_here), (assign, assign_here))
        )
    ]
    for copy in copies:
        copy.start()
    copies[2].wait()
    picker[...] = slot_picker(per_device, group_slots(group, assign_here))
    copies[0].wait()
    copies[1].wait()
    split_heads(per_device, picker[...], query_here, pairs_here, rows)
    out[...] = rows[...].astype(jnp.bfloat16)


def pick_other_kernel(per_device, own, picker, query, pairs, keep, send, rows):
    split_heads(per_device, picker[...], query, pairs, rows)
    here = lax.axis_index("sec") & 1
    keep[here] = own[0]
    keep[1 - here] = rows[0].astype(jnp.bfloat16)
    send[here] = own[1]
    send[1 - here] = rows[1].astype(jnp.bfloat16)


def attend_blocks(per_device, heads, lengths, chip, source, keys, values, target, first):
    share = heads // 2
    slots = keys.shape[1]
    width = HEAD_WIDTH
    scaling = 1.0 / math.sqrt(width)
    line = lax.broadcasted_iota(jnp.int32, (16, width), 0)
    upper = line < share
    place = lax.broadcasted_iota(jnp.int32, (16, slots), 1)
    work = [(i, j) for i in range(2) for j in range(per_device)]
    past, fresh, new_values, columns = [], [], [], []
    for i, j in work:
        wide = source[i, j * 16 : (j + 1) * 16].astype(jnp.float32)
        zero = jnp.zeros_like(wide)
        both = jnp.concatenate([jnp.where(upper, wide, zero), jnp.where(upper, zero, wide)], axis=1)
        column = pl.ds(pl.multiple_of((2 * chip + i) * 2 * width, 2 * width), 2 * width)
        columns.append(column)
        scores = lax.dot_general(
            both.astype(jnp.bfloat16),
            keys[j, :, column],
            (((1,), (1,)), ((), ())),
            preferred_element_type=jnp.float32,
        )
        past.append(jnp.where(place < lengths[j], scores * scaling, -1e30))
        new_key = jnp.where(upper, wide[heads : heads + 1], wide[heads + 2 : heads + 3])
        new_values.append(jnp.where(upper, wide[heads + 1 : heads + 2], wide[heads + 3 : heads + 4]))
        fresh.append(wide * new_key)
    past = jnp.concatenate(past, axis=0)
    fresh = jnp.sum(jnp.concatenate(fresh, axis=0), axis=1, keepdims=True) * scaling
    highest = jnp.maximum(jnp.max(past, axis=1, keepdims=True), fresh)
    past_exp = jnp.exp(past - highest)
    fresh_exp = jnp.exp(fresh - highest)
    inverse = 1.0 / (jnp.sum(past_exp, axis=1, keepdims=True) + fresh_exp)
    weights = (past_exp * inverse).astype(jnp.bfloat16)
    fresh_weight = (fresh_exp * inverse).astype(jnp.bfloat16).astype(jnp.float32)
    for index, (i, j) in enumerate(work):
        lines = slice(index * 16, (index + 1) * 16)
        mixed = jnp.dot(weights[lines], values[j, :, columns[index]], preferred_element_type=jnp.float32)
        mixed = jnp.where(upper, mixed[:, :width], mixed[:, width:]) + fresh_weight[lines] * new_values[index]
        for h in range(heads):
            target[first + i, j : j + 1, h * width : (h + 1) * width] = mixed[h : h + 1]


def attend_near_kernel(per_device, heads, lengths, source, keys, values, assign, out, order):
    group = order.shape[0] // 2
    slots = jnp.broadcast_to(group_slots(group, assign), (group, group))
    line = lax.broadcasted_iota(jnp.int32, (group, group), 0)
    match = jnp.where(line == slots, 1.0, 0.0).astype(jnp.bfloat16)
    shape = (group, order.shape[1])
    column = lax.broadcasted_iota(jnp.int32, shape, 1) & 31
    column = jnp.where(column < group, column, jnp.where(column < 2 * group, column - group, group))
    same = jnp.where(lax.broadcasted_iota(jnp.int32, shape, 0) == column, 1.0, 0.0).astype(jnp.bfloat16)
    ordered = lax.dot_general(match, same, (((0,), (0,)), ((), ())), preferred_element_type=jnp.float32)
    line = lax.broadcasted_iota(jnp.int32, (2 * group, group), 0)
    line = jnp.where(line < group, line, line - group)
    twice = jnp.where(line == lax.broadcasted_iota(jnp.int32, (2 * group, group), 1), 1.0, 0.0).astype(jnp.bfloat16)
    ordered = jnp.dot(twice, ordered.astype(jnp.bfloat16), preferred_element_type=jnp.float32)
    lower = lax.broadcasted_iota(jnp.int32, order.shape, 0) < group
    first = (lax.broadcasted_iota(jnp.int32, order.shape, 1) & 31) < group
    order[...] = jnp.where(lower == first, ordered, 0.0).astype(jnp.bfloat16)
    out[...] = jnp.zeros_like(out)
    attend_blocks(per_device, heads, lengths, lax.axis_index("sec") >> 1, source, keys, values, out, 0)


def attend_far_kernel(per_device, heads, lengths, source, near, keys, values, own, first, second, third, total):
    chip = lax.axis_index("sec") >> 1
    tp = lax.axis_index("tp")
    total[...] = jnp.zeros_like(total)
    total[2 * chip] = near[0]
    total[2 * chip + 1] = near[1]
    attend_blocks(per_device, heads, lengths, 1 - chip, source, keys, values, total, 2 * (1 - chip))
    for step, target in enumerate((own, first, second, third)):
        target[...] = total[tp ^ step, 0:4].astype(jnp.bfloat16)


def gather_kernel(third, second, first, own, out, rows):
    for step, part in enumerate((own, first, second, third)):
        rows[4 * step : 4 * step + 4] = part[...].astype(jnp.float32)
    out[...] = rows[...].astype(jnp.bfloat16)


def slot_rows(far, per_device, count):
    sec, tp = lax.axis_index("sec"), lax.axis_index("tp")
    share = 2 * per_device
    shape = (count, 32)
    line = lax.broadcasted_iota(jnp.int32, shape, 1)
    place, index = (line >> 2) & 3, line & 3
    from_sec = sec ^ (3 * far) ^ (line >> 4) ^ jnp.where(place > 0, 1, 0)
    row = (tp ^ place) * share + (from_sec & 1) * per_device + index
    match = (lax.broadcasted_iota(jnp.int32, shape, 0) == row) & (index < per_device)
    return jnp.where(match, 1.0, 0.0).astype(jnp.bfloat16)


def resid_rows(far, per_device, count, assign, resid):
    sec, tp = lax.axis_index("sec"), lax.axis_index("tp")
    share = 2 * per_device
    group = resid.shape[0]
    chip = (sec ^ (3 * far)) >> 1
    slots = jnp.broadcast_to(group_slots(group, assign), (count, group)) - share * chip
    match = lax.broadcasted_iota(jnp.int32, (count, group), 0) == slots + tp * share
    match = jnp.where(match & (slots >= 0) & (slots < share), 1.0, 0.0).astype(jnp.bfloat16)
    return jnp.dot(match, resid[...], preferred_element_type=jnp.float32)


def project(match, first, second, resid, weight, keep, send):
    lines = jnp.concatenate([first[...], second[...]], axis=0)
    ordered = jnp.dot(match, lines, preferred_element_type=jnp.float32).astype(jnp.bfloat16)
    total = resid + jnp.dot(ordered, weight[...], preferred_element_type=jnp.float32)
    keep[...] = total
    send[...] = total.astype(jnp.bfloat16)


def project_near_kernel(per_device, first, second, assign, resid, weight, keep, send, far_match, far_resid):
    count = keep.shape[0]
    near = resid_rows(0, per_device, count, assign, resid)
    project(slot_rows(0, per_device, count), first, second, near, weight, keep, send)
    far_match[...] = slot_rows(1, per_device, count)
    far_resid[...] = resid_rows(1, per_device, count, assign, resid)


def project_far_kernel(first, second, match, resid, weight, keep, send):
    project(match[...], first, second, resid[...], weight, keep, send)


def add_kernel(mine, other, keep, send):
    total = mine[...] + other[...].astype(jnp.float32)
    keep[...] = total
    send[...] = total.astype(jnp.bfloat16)


def row_half():
    sec = lax.axis_index("sec")
    return (sec ^ (sec >> 1)) & 1


def products(features, gate, up, unit, units, chunk, keep, send):
    half = keep.shape[0]
    for kind, weight in enumerate((gate, up)):
        for start in range(0, units, chunk):
            column = slice(unit + start, unit + start + chunk)
            product = jnp.dot(features, weight[:, column], preferred_element_type=jnp.float32)
            at = kind * units + start
            keep[:, at : at + chunk] = product[:half]
            send[:, at : at + chunk] = product[half:].astype(jnp.bfloat16)


def to_groups(first, second, groups):
    share = first.shape[0] // groups.shape[0]
    for index in range(groups.shape[0]):
        lines = slice(index * share, (index + 1) * share)
        groups[index, 0:share] = first[lines]
        groups[index, share : 2 * share] = second[lines]


def gate_up_first_kernel(
    chunk, near, near_other, far, far_other, gain, gate, up, keep, send, features, stream, halves, groups
):
    sec, tp = lax.axis_index("sec"), lax.axis_index("tp")
    chip = sec >> 1
    half = near.shape[0]
    halves[chip] = near[...] + near_other[...].astype(jnp.float32)
    halves[1 - chip] = far[...] + far_other[...].astype(jnp.float32)
    to_groups(halves[0], halves[1], groups)
    stream[...] = groups[tp, 0 : stream.shape[0]]
    first = row_half()
    total = jnp.concatenate([halves[first], halves[1 - first]], axis=0)
    squares = jnp.sum(total * total, axis=1, keepdims=True)
    scaled = (total * gain[...].astype(jnp.float32)).astype(jnp.bfloat16)
    features[...] = scaled
    units = (keep.shape[1] - 128) // 2
    products(scaled, gate, up, 0, units, chunk, keep, send)
    keep[:, 2 * units :] = jnp.broadcast_to(squares[:half], (half, 128))
    send[:, 2 * units :] = two_terms(squares[half:])


def gate_up_more_kernel(chunk, unit, features, gate, up, earlier, keep, send):
    products(features[...], gate, up, unit, keep.shape[1] // 2, chunk, keep, send)


def two_terms(column):
    shape = (column.shape[0], 128)
    column = jnp.broadcast_to(column, shape)
    coarse = column.astype(jnp.bfloat16).astype(jnp.float32)
    lane = lax.broadcasted_iota(jnp.int32, shape, 1)
    return jnp.where(lane < 64, coarse, column - coarse).astype(jnp.bfloat16)


def one_column(terms):
    return terms[:, 0:1].astype(jnp.float32) + terms[:, 64:65].astype(jnp.float32)


def pair_sum_first_kernel(mine, other, keep, send):
    width = mine.shape[1] - 128
    total = mine[:, :width] + other[:, :width].astype(jnp.float32)
    both = mine[:, width:] + one_column(other[:, width:])
    keep[:, :width] = total
    keep[:, width:] = both
    send[:, :width] = total.astype(jnp.bfloat16)
    send[:, width:] = two_terms(both[:, 0:1])


def pair_sum_kernel(mine, other, earlier, keep, send):
    total = mine[...] + other[...].astype(jnp.float32)
    keep[...] = total
    send[...] = total.astype(jnp.bfloat16)


def gated(mine, other, factor, hidden):
    width = hidden.shape[1]
    gate = (mine[:, :width] + other[:, :width].astype(jnp.float32)) * factor
    up = (mine[:, width : 2 * width] + other[:, width : 2 * width].astype(jnp.float32)) * factor
    hidden[...] = (gate / (1.0 + jnp.exp(-gate)) * up).astype(jnp.bfloat16)


def hidden_first_kernel(features, mine, other, earlier, hidden, scale):
    width = mine.shape[1] - 128
    total = mine[:, width : width + 1] + one_column(other[:, width:])
    factor = lax.rsqrt(total / features + 1e-06)
    scale[...] = jnp.broadcast_to(factor, scale.shape)
    gated(mine, other, factor, hidden)


def hidden_kernel(mine, other, scale, earlier, hidden):
    gated(mine, other, scale[:, 0:1], hidden)


def down_product(unit, mine, other, weight):
    lines = jnp.concatenate([mine[...].astype(jnp.float32), other[...].astype(jnp.float32)], axis=0)
    rows = weight[unit : unit + lines.shape[1], :]
    return jnp.dot(lines.astype(jnp.bfloat16), rows, preferred_element_type=jnp.float32)


def column_halves(rows):
    columns = rows.shape[1] // 2
    return jnp.concatenate([rows[:, :columns], rows[:, columns:]], axis=0)


def down_first_kernel(mine, other, weight, stream, out, stream_halves):
    out[...] = down_product(0, mine, other, weight)
    stream_halves[...] = column_halves(stream[...])


def down_more_kernel(unit, before, mine, other, weight, out):
    out[...] = before[...] + down_product(unit, mine, other, weight)


def down_last_kernel(unit, before, mine, other, weight, keep, first, second, third, groups):
    tp = lax.axis_index("tp")
    product = before[...] + down_product(unit, mine, other, weight)
    group = keep.shape[0] // 2
    half = product.shape[0] // 2
    swapped = row_half() == 1
    lower, upper = product[:half], product[half:]
    to_groups(jnp.where(swapped, upper, lower), jnp.where(swapped, lower, upper), groups)
    for step, target in enumerate((keep, first, second, third)):
        target[...] = column_halves(groups[tp ^ step, 0:group]).astype(target.dtype)


def finish_kernel(third, second, first, stream, mine, order, out, terms):
    total = stream[...] + mine[...]
    for other in (first, second, third):
        total = total + other[...].astype(jnp.float32)
    lines, columns = total.shape
    coarse = total.astype(jnp.bfloat16).astype(jnp.float32)
    terms[...] = jnp.zeros_like(terms)
    terms[0:lines] = coarse
    terms[32 : 32 + lines] = total - coarse
    ordered = jnp.dot(order[...], terms[...].astype(jnp.bfloat16), preferred_element_type=jnp.float32)
    group = lines // 2
    out[:, :columns] = ordered[:group].astype(jnp.bfloat16)
    out[:, columns:] = ordered[group:].astype(jnp.bfloat16)


def local_pairs(
    resid,
    query,
    new_kv,
    key_cache,
    cached_value_rows,
    cache_len,
    assign,
    out_weight,
    norm_gain,
    gate_weight,
    up_weight,
    down_weight,
):
    f32, bf16 = jnp.float32, jnp.bfloat16
    group, features = resid.shape
    per_device = key_cache.shape[0]
    heads = query.shape[1] // HEAD_WIDTH
    head_block = out_weight.shape[0]
    width = gate_weight.shape[1]
    half = 2 * group
    assign = assign.reshape(1, -1)
    gain = norm_gain.reshape(1, -1)

    query_b, pairs_b = swap(query, "sec", 1), swap(new_kv, "sec", 1)
    block = (2, 16 * per_device, HEAD_WIDTH)
    own, picker = call(
        functools.partial(pick_own_kernel, per_device, group),
        [(block, bf16), ((16, group), bf16)],
        (query, new_kv, assign),
        [
            pltpu.VMEM(query.shape, bf16),
            pltpu.VMEM(new_kv.shape, bf16),
            pltpu.VMEM(assign.shape, jnp.int32),
            pltpu.VMEM(block, f32),
            pltpu.SemaphoreType.DMA((3,)),
        ],
        remote=(0, 1, 2),
    )
    mine, away = call(
        functools.partial(pick_other_kernel, per_device),
        [(block, bf16)] * 2,
        (own, picker, query_b, pairs_b),
        [pltpu.VMEM(block, f32)],
    )
    other = swap(away, "sec", 3)
    caches = (key_cache, cached_value_rows)
    near, order = call(
        functools.partial(attend_near_kernel, per_device, heads),
        [((2, 4, head_block), f32), ((half, 64), bf16)],
        (cache_len, mine, *caches, assign),
        smem=(0,),
        resident=(2, 3),
    )
    own, *parts = call(
        functools.partial(attend_far_kernel, per_device, heads),
        [((4, head_block), bf16)] * 4,
        (cache_len, other, near, *caches),
        [pltpu.VMEM((4, 4, head_block), f32)],
        smem=(0,),
        resident=(3, 4),
    )

    parts = [swap(parts[step - 1], ("sec", "tp"), (1, step)) for step in (3, 2, 1)]
    (own,) = call(gather_kernel, [((16, head_block), bf16)], (*parts, own), [pltpu.VMEM((16, head_block), f32)])
    across = swap(own, "sec", 3)
    beside = swap(own, "sec", 1)

    pair = [((half, features), f32), ((half, features), bf16)]

    def tp_sum(mine, away, first, second):
        mine, away = call(add_kernel, pair, (mine, swap(away, "tp", first)))
        return mine, swap(away, "tp", second)

    *near, match, rows = call(
        functools.partial(project_near_kernel, per_device),
        pair + [((half, 32), bf16), ((half, features), f32)],
        (own, beside, assign, resid, out_weight),
        resident=(4,),
    )
    corner = swap(own, "sec", 2)
    far = call(project_far_kernel, pair, (across, corner, match, rows, out_weight), resident=(4,), nanos=0)
    sums = tp_sum(*near, 2, 1) + tp_sum(*far, 1, 2)

    sizes = [width * sixteenths // 16 for sixteenths in (5, 5, 4, 2)]
    starts = [sum(sizes[:index]) for index in range(len(sizes))]
    chunk = width // 16
    weights = (gate_weight, up_weight)

    def sums_of(index, extra=0):
        shape = (half, 2 * sizes[index] + extra)
        return [(shape, f32), (shape, bf16)]

    *product, lines, stream = call(
        functools.partial(gate_up_first_kernel, chunk),
        sums_of(0, 128) + [((2 * half, features), bf16), ((group, features), f32)],
        (*sums, gain, *weights),
        [pltpu.VMEM((2, half, features), f32), pltpu.VMEM((4, 16, features), f32)],
        resident=(5, 6),
        nanos=2000,
    )
    products_made = [product]

    def more_products(index, earlier):
        return call(
            functools.partial(gate_up_more_kernel, chunk, starts[index]),
            sums_of(index),
            (lines, *weights, earlier),
            resident=(1, 2),
            free=(3,),
            nanos=0,
        )

    def pair_sum(index, earlier):
        mine, away = products_made[index]
        other = swap(away, "sec", 1)
        if index == 0:
            return call(pair_sum_first_kernel, sums_of(0, 128), (mine, other), nanos=0)
        return call(pair_sum_kernel, sums_of(index), (mine, other, earlier), free=(2,), nanos=0)

    products_made.append(more_products(1, product[1]))
    chip_sums = [pair_sum(0, None)]
    chip_sums.append(pair_sum(1, chip_sums[0][1]))
    products_made.append(more_products(2, chip_sums[1][1]))
    products_made.append(more_products(3, products_made[2][1]))
    chip_sums.append(pair_sum(2, products_made[3][1]))
    chip_sums.append(pair_sum(3, chip_sums[2][1]))
    total = [((2 * half, features), f32)]
    before = scale = None
    parts_done = []
    for index, (mine, away) in enumerate(chip_sums):
        other = swap(away, "sec", 3)
        if index == 0:
            hidden, scale = call(
                functools.partial(hidden_first_kernel, features * lax.axis_size("sec")),
                [((half, sizes[0]), bf16), ((half, 128), f32)],
                (mine, other, chip_sums[-1][1]),
                free=(2,),
                nanos=0,
            )
        else:
            earlier = parts_done[max(index - 2, 0)] if index > 1 else hidden
            (hidden,) = call(
                hidden_kernel, [((half, sizes[index]), bf16)], (mine, other, scale, earlier), free=(3,), nanos=1000
            )
        beside = swap(hidden, "sec", 1)
        if index == 0:
            before, stream = call(
                down_first_kernel,
                total + [((half, features // 2), f32)],
                (hidden, beside, down_weight, stream),
                resident=(2,),
                nanos=1000,
            )
            parts_done.append(before)
        elif index < len(sizes) - 1:
            (before,) = call(
                functools.partial(down_more_kernel, starts[index]),
                total,
                (before, hidden, beside, down_weight),
                resident=(3,),
                nanos=1000,
            )
            parts_done.append(before)
        else:
            mine, *parts = call(
                functools.partial(down_last_kernel, starts[index]),
                [((half, features // 2), f32)] + [((half, features // 2), bf16)] * 3,
                (before, hidden, beside, down_weight),
                [pltpu.VMEM((4, 16, features), f32)],
                resident=(3,),
            )
    parts = [swap(parts[step - 1], "tp", step) for step in (3, 2, 1)]
    (out,) = call(
        finish_kernel,
        [((group, features), bf16)],
        (*parts, stream, mine, order),
        [pltpu.VMEM((64, features // 2), f32)],
    )
    return out


def solution(mesh):
    small = mesh.shape["sec"] == 4 and mesh.shape["tp"] == 4
    return jax.shard_map(
        local_pairs if small else local,
        mesh=mesh,
        in_specs=(
            P(("rep", "tp"), "sec"),
            P(("rep", "tp"), "sec"),
            P(("rep", "tp"), "sec"),
            P(("rep", "sec", "tp"), None, None),
            P(("rep", "sec", "tp"), None, None),
            P(("rep", "sec", "tp")),
            P("rep"),
            P("tp", "sec"),
            P("sec"),
            P("sec", "tp"),
            P("sec", "tp"),
            P("tp", "sec"),
        ),
        out_specs=P(("rep", "tp"), "sec"),
        check_vma=False,
    )
```
